32 devices in a mesh: col: 4 (over z), hgt: 8 (over y, x, core).
Axes of the slice: x: 2, y: 2, z: 4, core: 2. Of those that a mesh axis runs over, the one named last changes fastest.
Arguments:
- efield_lattice_vector: float32 [3, 64, 192, 1024], P(None, 'col', 'hgt'), may hold values from -6 to 6
- hfield_lattice_vector: float32 [3, 64, 192, 1024], P(None, 'col', 'hgt'), may hold values from -6 to 6
- cell_temp: float32 [64, 192, 1024], P('col', 'hgt'), may hold values from -3 to 1
- region_tags: int32 [64, 192, 1024], P('col', 'hgt'), may hold values from 0 to 2
- block_owner: int32 [4, 8, 16, 24, 8, 1], P('col', 'hgt'), may hold values from 0 to 31; in each aligned block of 3072 rows (0 to 3071, 3072 to 6143, ..., all dimensions but the last counted through in order) at most 192 rows name the same one
- block_node: int32 [4, 8, 16, 24, 8], P('col', 'hgt'), may hold values from 0 to 383
- node_enthalpy: float32 [12288, 128], P(('col', 'hgt')), may hold values from -1.5 to 2.5
Outputs:
- e_out: float32 [3, 64, 192, 1024], P(None, 'col', 'hgt')
- h_out: float32 [3, 64, 192, 1024], P(None, 'col', 'hgt')
- node_temp: float32 [12288, 128], P(('col', 'hgt'))
The draws below stay inside these ranges and needn't reach their ends.
Inputs may be any that keep to these rules, and one draw needn't show every extreme that they name: `block_owner`: among the margin blocks of one device, no partition is named by more than 192 blocks, a bound that the blocks of some device reach.
All inputs are finite; a program needn't handle non-finite values.
Results may differ from the reference program's by a relative error of at most 0.0003.
Values sent between devices are 32-bit elements; how exact they have to be, the bound alone decides.
No kernel may reach another device: no remote copies, remote signals or barrier semaphores. Data moves between devices by JAX's collectives and lax.ppermute only.
A program may use at most 320 MiB of HBM per device.

```python
import math
import jax
import jax.numpy as jnp
import numpy as np

CX = 16
CZ = 24
NY = 1024
PTS = 128
STEPS = 4
NX = 64
NZ = 192
CAP = 192
NODES = 384
N_COL = 4
N_HGT = 8
DEVICES = 32


def touch_ends(values, key, smallest, top_value):
    extent = values.shape
    index_at = [jax.random.randint(jax.random.fold_in(key, axis), (), 0, extent[axis]) for axis in range(len(extent))]
    values = values.at[tuple(index_at)].set(smallest)
    longest = extent.index(max(extent))
    index_at[longest] = (index_at[longest] + 1) % extent[longest]
    return values.at[tuple(index_at)].set(top_value)


def block_scale(rng, shape, shards, least, high):
    factor_of, own = 1.0, jax.random.fold_in(rng, 6)
    for dim, parts in shards:
        heights = jnp.exp(jax.random.uniform(jax.random.fold_in(own, dim), (parts,), jnp.float32, least / len(shards), high / len(shards)))
        factor_of = factor_of * jnp.repeat(heights, shape[dim] // parts).reshape([-1 if axis == dim else 1 for axis in range(len(shape))])
    return factor_of


def routed_block(own_key, own, number, rows, number_of, top, limit, slope):
    sequence = jax.random.permutation(own_key, number_of)
    packed, usual = portions_of(number_of, rows * top, limit, slope, True), portions_of(number_of, rows * top, limit, slope, False)
    places = jnp.arange(number_of)

    def named(tallies, rotation):
        used = int((tallies > 0).sum())
        fixed = max(1, used // 4)
        moved = fixed + (places - fixed + rotation * (used - fixed)) % max(1, number_of - fixed)
        return jnp.zeros((number_of,), jnp.int32).at[sequence[jnp.where(places < fixed, places, moved)]].set(jnp.asarray(tallies, jnp.int32))

    tallies = jnp.where(number % 4 == 0, named(packed, number // 4), named(usual, number - number // 4 - 1))
    mixed = jax.random.permutation(jax.random.fold_in(own, 3), number_of)
    giver, receiver = mixed[0:number_of // 2 * 2:2], mixed[1:number_of // 2 * 2:2]
    margin = jnp.minimum(tallies[giver] - 1, limit - tallies[receiver]) // 2
    margin = jnp.where((giver == sequence[0]) | (receiver == sequence[0]) | (tallies[receiver] == 0), 0, jnp.maximum(margin, 0))
    moved = jax.random.randint(jax.random.fold_in(own, 4), (number_of // 2,), 0, 1 << 20) % (margin + 1)
    tallies = tallies.at[giver].add(-moved).at[receiver].add(moved)
    labels = jnp.searchsorted(jnp.cumsum(tallies), jnp.arange(rows * top), side="right").astype(jnp.int32)
    grid = labels.reshape(top, rows).T
    grid = grid[jax.random.permutation(jax.random.fold_in(own, 1), rows)]
    rotation = jax.random.randint(jax.random.fold_in(own, 2), (rows, 1), 0, top)
    return jnp.take_along_axis(grid, (jnp.arange(top)[None, :] + rotation) % top, axis=1)


def portions_of(amount, total, reach, slope, full):
    portions = [(1 << 20) // math.isqrt(grade ** slope) + 1 for grade in range(1, amount + 1)]
    largest = reach if full else min(reach, max(-(-total // amount), total * portions[0] // sum(portions)))
    least = 1 if total - largest >= amount - 1 else 0
    holding, rest = [largest] + [least] * (amount - 1), total - largest - least * (amount - 1)
    while rest > 0:
        free = [i for i in range(1, amount) if holding[i] < largest] or [i for i in range(1, amount) if holding[i] < reach]
        whole, left = sum([portions[i] for i in free]), rest
        for i in free:
            more = min(reach - holding[i], max(1, left * portions[i] // whole), rest)
            holding[i] = holding[i] + more
            rest = rest - more
    return np.array(holding)


def centred(stream_key, dims, width, reach, cuts=(), dtype=jnp.bfloat16):
    result = jax.random.normal(stream_key, dims, jnp.float32) * width
    if len(cuts) > 0:
        result = block_scale(stream_key, dims, cuts, -0.22, 0.18) * result
    return jnp.clip(result, min=-reach, max=reach).astype(dtype)


def setup_inputs(seed: int = 0) -> dict:
    key_list = jax.random.split(jax.random.key(seed), 8)
    efield_lattice_vector = centred(key_list[0], (3, NX, NZ, NY), 1.0, 6.0, ((1, 4), (2, 8)), jnp.float32)
    hfield_lattice_vector = centred(key_list[1], (3, NX, NZ, NY), 1.0, 6.0, ((1, 4), (2, 8)), jnp.float32)
    cell_temp = jnp.clip(-3.0 + 4.0 * jax.random.uniform(key_list[2], (NX, NZ, NY), jnp.float32) ** block_scale(key_list[2], (NX, NZ, NY), ((0, 4), (1, 8)), -0.2, 0.2), -3.0, 1.0)
    region_tags = touch_ends(jax.random.randint(key_list[3], (NX, NZ, NY), 0, 3), jax.random.fold_in(key_list[3], 1), 0, 2).astype(jnp.int32)
    block_owner_keys = jax.random.split(jax.random.fold_in(key_list[4], 1), N_COL * N_HGT * CX * CZ * (NY // PTS) // (CX * CZ * (NY // PTS)))
    block_owner_turns = jax.random.permutation(jax.random.fold_in(key_list[4], 3), N_COL * N_HGT * CX * CZ * (NY // PTS) // (CX * CZ * (NY // PTS)))
    block_owner = jax.vmap(lambda own, number: routed_block(jax.random.fold_in(key_list[4], 2), own, number, CX * CZ * (NY // PTS), DEVICES, 1, CAP, 2))(block_owner_keys, block_owner_turns).reshape((N_COL, N_HGT, CX, CZ, NY // PTS, 1))
    block_node = touch_ends(jax.random.randint(key_list[5], (N_COL, N_HGT, CX, CZ, NY // PTS), 0, NODES), jax.random.fold_in(key_list[5], 1), 0, NODES - 1).astype(jnp.int32)
    node_enthalpy = jnp.clip(-1.5 + 4.0 * jax.random.uniform(key_list[6], (DEVICES * NODES, PTS), jnp.float32) ** block_scale(key_list[6], (DEVICES * NODES, PTS), ((0, 32),), -0.2, 0.2), -1.5, 2.5)
    return {"efield_lattice_vector": efield_lattice_vector, "hfield_lattice_vector": hfield_lattice_vector, "cell_temp": cell_temp, "region_tags": region_tags, "block_owner": block_owner, "block_node": block_node, "node_enthalpy": node_enthalpy}


def coefficients(cell_temp, region_tags):
    frac = jax.nn.sigmoid(2.0 * cell_temp)
    lean = region_tags == 0
    fat = region_tags == 1
    eps_frozen = jnp.where(lean, 4.0, jnp.where(fat, 2.5, 5.0))
    eps_thawed = jnp.where(lean, 50.0, jnp.where(fat, 6.0, 10.0))
    sig_frozen = jnp.where(lean, 0.2, jnp.where(fat, 0.05, 0.1))
    melted_conductance = jnp.where(lean, 8.0, jnp.where(fat, 0.4, 1.0))
    eps = eps_frozen + (eps_thawed - eps_frozen) * frac
    sigma = sig_frozen + (melted_conductance - sig_frozen) * frac
    loss = sigma * 0.55 / (2.0 * eps)
    ca = (1.0 - loss) / (1.0 + loss)
    cb = 0.55 / (eps * (1.0 + loss))
    return sigma, ca, cb


def forward(field, plane, axis):
    size = field.shape[axis]
    return jnp.concatenate([jax.lax.slice_in_dim(field, 1, size, axis=axis), plane], axis) - field


def backward(field, plane, axis):
    size = field.shape[axis]
    return field - jnp.concatenate([plane, jax.lax.slice_in_dim(field, 0, size - 1, axis=axis)], axis)


def curl(diff, comps, planes_x, planes_z, plane_y):
    fx, fy, fz = comps
    dx_y = diff(fy, planes_x[0], 0)
    dx_z = diff(fz, planes_x[1], 0)
    dz_x = diff(fx, planes_z[0], 1)
    dz_y = diff(fy, planes_z[1], 1)
    dy_x = diff(fx, plane_y, 2)
    dy_z = diff(fz, plane_y, 2)
    return jnp.stack([dy_z - dz_y, dz_x - dx_z, dx_y - dy_x])


def tissue_warmth_kelvin(heat_content_per_mass):
    return jnp.where(heat_content_per_mass < 0.0, heat_content_per_mass / 2.0, jnp.where(heat_content_per_mass > 1.0, (heat_content_per_mass - 1.0) / 3.0, 0.0))


def reference(efield_lattice_vector, hfield_lattice_vector, cell_temp, region_tags, block_owner, block_node, node_enthalpy):
    sigma, ca, cb = coefficients(cell_temp, region_tags)
    zeros_x = jnp.zeros((2, 1, NZ, NY), jnp.float32)
    zeros_z = jnp.zeros((2, NX, 1, NY), jnp.float32)
    empty_height_plane = jnp.zeros((NX, NZ, 1), jnp.float32)
    power = jnp.zeros((NX, NZ, NY), jnp.float32)
    for step in range(STEPS):
        hfield_lattice_vector = hfield_lattice_vector - 0.55 * curl(forward, (efield_lattice_vector[0], efield_lattice_vector[1], efield_lattice_vector[2]), zeros_x, zeros_z, empty_height_plane)
        efield_lattice_vector = ca * efield_lattice_vector + cb * curl(backward, (hfield_lattice_vector[0], hfield_lattice_vector[1], hfield_lattice_vector[2]), zeros_x, zeros_z, empty_height_plane)
        power = power + sigma * (efield_lattice_vector[0] * efield_lattice_vector[0] + efield_lattice_vector[1] * efield_lattice_vector[1] + efield_lattice_vector[2] * efield_lattice_vector[2])
    absorbed = power / STEPS
    blocks = absorbed.reshape(N_COL, CX, N_HGT, CZ, NY // PTS, PTS).transpose(0, 2, 1, 3, 4, 5).reshape(-1, PTS)
    desired_result = block_owner.reshape(-1) * NODES + block_node.reshape(-1)
    heat = jax.ops.segment_sum(blocks, desired_result, num_segments=DEVICES * NODES)
    heat_content_per_mass = node_enthalpy + 0.25 * heat
    return efield_lattice_vector, hfield_lattice_vector, tissue_warmth_kelvin(heat_content_per_mass)
```

```python
import functools

import jax
import jax.numpy as jnp
from jax import lax
from jax.experimental import pallas as pl
from jax.experimental.pallas import tpu as pltpu
from jax.sharding import PartitionSpec as P

PTS = 128
STEPS = 4
COURANT = 0.55
LANES = 128
ROWS = 8
F32 = jnp.float32
VMEM_MIB = 16

WHOLE = pl.BlockSpec(memory_space=pltpu.VMEM)
SCALARS = pl.BlockSpec(memory_space=pltpu.SMEM)
FAR = pl.BlockSpec(memory_space=pltpu.HBM)


def vmem(*shape):
    return pltpu.VMEM(shape, F32)


def far(x):
    return pltpu.with_memory_space_constraint(x, pltpu.HBM)


def params(mib):
    return pltpu.CompilerParams(vmem_limit_bytes=mib << 20)


def cost(flops, moved):
    return pl.CostEstimate(flops=flops, bytes_accessed=moved, transcendentals=0)


def after_y(f):
    lane = lax.broadcasted_iota(jnp.int32, (ROWS, LANES), 1)
    n = f.shape[1] // LANES
    turned = [pltpu.roll(f[:, k * LANES : (k + 1) * LANES], LANES - 1, 1) for k in range(n)]
    turned.append(jnp.zeros((ROWS, LANES), F32))
    return jnp.concatenate([jnp.where(lane < LANES - 1, turned[k], turned[k + 1]) for k in range(n)], 1)


def before_y(f):
    lane = lax.broadcasted_iota(jnp.int32, (ROWS, LANES), 1)
    n = f.shape[1] // LANES
    turned = [jnp.zeros((ROWS, LANES), F32)]
    turned += [pltpu.roll(f[:, k * LANES : (k + 1) * LANES], 1, 1) for k in range(n)]
    return jnp.concatenate([jnp.where(lane > 0, turned[k + 1], turned[k]) for k in range(n)], 1)


def after_row(f, row):
    place = lax.broadcasted_iota(jnp.int32, f.shape, 0)
    return jnp.where(place < ROWS - 1, pltpu.roll(f, ROWS - 1, 0), jnp.broadcast_to(row, f.shape))


def before_row(f, row):
    place = lax.broadcasted_iota(jnp.int32, f.shape, 0)
    return jnp.where(place > 0, pltpu.roll(f, 1, 0), jnp.broadcast_to(row, f.shape))


def edges_kernel(e, h, fwd, back, sems):
    last = e.shape[1] - 1
    copies = [
        pltpu.make_async_copy(e.at[:, last], fwd.at[pl.ds(0, 3)], sems.at[0]),
        pltpu.make_async_copy(h.at[pl.ds(1, 2), last], fwd.at[pl.ds(3, 2)], sems.at[1]),
        pltpu.make_async_copy(e.at[pl.ds(1, 2), 0], back, sems.at[2]),
    ]
    for copy in copies:
        copy.start()
    for copy in copies:
        copy.wait()


def load_kernel(e_in, h_in, place, inside, e, h, fwd, back, diag_fwd, diag_back, sems):
    nx, nz = e_in.shape[1:3]
    e_copy = pltpu.make_async_copy(e_in, e.at[:, pl.ds(0, nx)], sems.at[0])
    h_copy = pltpu.make_async_copy(h_in, h.at[:, pl.ds(1, nx)], sems.at[1])
    e_copy.start()
    h_copy.start()
    e_copy.wait()
    h_copy.wait()

    def rows(x, carry):
        for comp in range(3):
            fwd[comp, pl.ds(x, 1), :] = e[comp, x, nz - 1 : nz, :]
        for comp in range(2):
            fwd[3 + comp, pl.ds(x, 1), :] = h[comp, x + 1, nz - 1 : nz, :]
            back[comp, pl.ds(x, 1), :] = e[comp, x, 0:1, :]
        return carry

    lax.fori_loop(0, nx, rows, 0)
    diag_fwd[...] = e[0, nx - 1, 0:1, :]
    diag_back[...] = e[2, 0, nz - 1 : nz, :]


def coefficients_kernel(temp_far, tags_far, ca, cb, sigma_out, temp, tags, sems):
    nx, nz, _ = temp.shape
    parts = 4
    size = nx // parts
    copies = []
    for part in range(parts):
        here = pl.ds(part * size, size)
        copies.append(pltpu.make_async_copy(temp_far.at[here], temp.at[here], sems.at[0, part]))
        copies.append(pltpu.make_async_copy(tags_far.at[here], tags.at[here], sems.at[1, part]))
    for copy in copies:
        copy.start()

    def plane(x, carry):
        for z in range(0, nz, ROWS):
            tag = tags[x, z : z + ROWS, :]
            lean = tag == 0
            fat = tag == 1
            frac = 1.0 / (1.0 + jnp.exp(-2.0 * temp[x, z : z + ROWS, :]))
            eps_low = jnp.where(lean, 4.0, jnp.where(fat, 2.5, 5.0))
            eps_rise = jnp.where(lean, 46.0, jnp.where(fat, 3.5, 5.0))
            sig_low = jnp.where(lean, 0.2, jnp.where(fat, 0.05, 0.1))
            sig_rise = jnp.where(lean, 7.8, jnp.where(fat, 0.35, 0.9))
            eps = eps_low + eps_rise * frac
            sigma = sig_low + sig_rise * frac
            half = (0.5 * COURANT) * sigma
            inverse = 1.0 / (eps + half)
            ca[x, z : z + ROWS, :] = (eps - half) * inverse
            cb[x, z : z + ROWS, :] = COURANT * inverse
            sigma_out[x, z : z + ROWS, :] = sigma
        return carry

    for part in range(parts):
        copies[2 * part].wait()
        copies[2 * part + 1].wait()
        lax.fori_loop(part * size, (part + 1) * size, plane, 0)


def step_kernel(first, last, *refs):
    inside, e_old, h_old, ca, cb, sigma = refs[:6]
    col_fwd, col_back, hgt_fwd, hgt_back, corner_x, corner_z, own_rows = refs[6:13]
    refs = refs[13:]
    if first:
        low_old = None
    else:
        low_old, power_old = refs[:2]
        refs = refs[2:]
    if last:
        e, h, power, low = refs
    else:
        e, h, power, low, to_fwd, to_back, rows_fwd, rows_back, diag_fwd, diag_back = refs
    nx = e.shape[1] - 1
    nz = e.shape[2]
    behind = inside[0]
    below = inside[1]

    for z in range(0, nz, ROWS):
        here = slice(z, z + ROWS)
        ex, ey, ez = (col_fwd[comp, here, :] for comp in range(3))
        row = col_fwd[0, z + ROWS : z + ROWS + 1, :] if z + ROWS < nz else corner_x[...]
        hy = col_fwd[3, here, :] if first else h[1, 0, here, :]
        hz = col_fwd[4, here, :] if first else h[2, 0, here, :]
        hy = hy - (COURANT * behind) * ((after_row(ex, row) - ex) - (e[2, 0, here, :] - ez))
        hz = hz - (COURANT * behind) * ((e[1, 0, here, :] - ey) - (after_y(ex) - ex))
        h[1, 0, here, :] = hy
        h[2, 0, here, :] = hz
        for comp in (1, 2):
            e[comp, nx, here, :] = col_back[comp - 1, here, :]

    for x in range(0, nx, ROWS):
        here = slice(x, x + ROWS)
        ex, ey, ez = (hgt_fwd[comp, here, :] for comp in range(3))
        row = hgt_fwd[2, x + ROWS : x + ROWS + 1, :] if x + ROWS < nx else corner_z[...]
        hx = hgt_fwd[3, here, :] if first else low_old[0, here, :]
        hy = hgt_fwd[4, here, :] if first else low_old[1, here, :]
        hx = hx - (COURANT * below) * ((after_y(ez) - ez) - (own_rows[1, here, :] - ey))
        hy = hy - (COURANT * below) * ((own_rows[0, here, :] - ex) - (after_row(ez, row) - ez))
        low[0, here, :] = hx
        low[1, here, :] = hy

    def plane(x, carry):
        here_x = pl.ds(x, 1)
        for z in range(0, nz, ROWS):
            here = slice(z, z + ROWS)
            ex, ey, ez = (e[comp, x, here, :] for comp in range(3))
            if z + ROWS < nz:
                row_x, row_y = (e[comp, x, z + ROWS : z + ROWS + 1, :] for comp in range(2))
            else:
                row_x, row_y = (hgt_back[comp, here_x, :] for comp in range(2))
            hx = h[0, x + 1, here, :] - COURANT * ((after_y(ez) - ez) - (after_row(ey, row_y) - ey))
            hy = h[1, x + 1, here, :] - COURANT * ((after_row(ex, row_x) - ex) - (e[2, x + 1, here, :] - ez))
            hz = h[2, x + 1, here, :] - COURANT * ((e[1, x + 1, here, :] - ey) - (after_y(ex) - ex))
            if z > 0:
                low_x, low_y = (h[comp, x + 1, z - 1 : z, :] for comp in range(2))
            else:
                low_x, low_y = (low[comp, here_x, :] for comp in range(2))
            h[0, x + 1, here, :] = hx
            h[1, x + 1, here, :] = hy
            h[2, x + 1, here, :] = hz
            keep = ca[x, here, :]
            drive = cb[x, here, :]
            ex = keep * ex + drive * ((hz - before_y(hz)) - (hy - before_row(hy, low_y)))
            ey = keep * ey + drive * ((hx - before_row(hx, low_x)) - (hz - h[2, x, here, :]))
            ez = keep * ez + drive * ((hy - h[1, x, here, :]) - (hx - before_y(hx)))
            e[0, x, here, :] = ex
            e[1, x, here, :] = ey
            e[2, x, here, :] = ez
            heat = sigma[x, here, :] * (ex * ex + ey * ey + ez * ez)
            power[x, here, :] = heat if first else power_old[x, here, :] + heat
        if not last:
            for comp in range(3):
                rows_fwd[comp, here_x, :] = e[comp, x, nz - 1 : nz, :]
            for comp in range(2):
                rows_back[comp, here_x, :] = e[comp, x, 0:1, :]
        return carry

    lax.fori_loop(0, nx, plane, 0)
    if not last:
        to_fwd[...] = e[:, nx - 1]
        to_back[...] = e[1:3, 0]
        diag_fwd[...] = e[0, nx - 1, 0:1, :]
        diag_back[...] = e[2, 0, nz - 1 : nz, :]


def places_kernel(n_col, n_hgt, cap, extra, owner, node, place, nodes_out):
    n_dev = n_col * n_hgt
    count = owner.shape[1]
    width = 256
    rows = lax.broadcasted_iota(jnp.int32, (n_dev, width), 0)
    before = lax.broadcasted_iota(jnp.int32, (width, width), 0)
    after = lax.broadcasted_iota(jnp.int32, (width, width), 1)
    upper = jnp.where(before <= after, 1.0, 0.0).astype(jnp.bfloat16)
    room_for = nodes_out.shape[0] // n_dev * LANES
    room = lax.broadcasted_iota(jnp.int32, (room_for, width), 0)
    total = jnp.zeros((n_dev, 1), F32)
    high = jnp.zeros((n_dev, room_for), F32)
    low = jnp.zeros((n_dev, room_for), F32)
    nt = (((1,), (1,)), ((), ()))
    for start in range(0, count, width):
        own = owner[:, start : start + width]
        target = lax.rem(own, n_hgt) * n_col + lax.div(own, n_hgt)
        hit = jnp.where(rows == target, 1.0, 0.0)
        running = total + jnp.dot(hit.astype(jnp.bfloat16), upper, preferred_element_type=F32)
        total = running[:, width - 1 : width]
        rank = jnp.sum(hit * running, axis=0, keepdims=True).astype(jnp.int32) - 1
        group = lax.div(target, n_col)
        place[:, start : start + width] = target * cap + group * extra + rank
        number = node[:, start : start + width]
        upper_part = lax.div(number, 16)
        lower_part = number - 16 * upper_part
        seat = jnp.where(room == rank, 1.0, 0.0).astype(jnp.bfloat16)
        high = high + lax.dot_general(
            (hit * upper_part.astype(F32)).astype(jnp.bfloat16), seat, nt, preferred_element_type=F32
        )
        low = low + lax.dot_general(
            (hit * lower_part.astype(F32)).astype(jnp.bfloat16), seat, nt, preferred_element_type=F32
        )
    taken = lax.broadcasted_iota(jnp.int32, (n_dev, room_for), 1).astype(F32) < total
    table = jnp.where(taken, 16.0 * high + low, -1.0)
    parts = room_for // LANES
    for part in range(parts):
        nodes_out[pl.ds(part, n_dev, stride=parts), :] = table[:, part * LANES : (part + 1) * LANES]


def pack_kernel(place, power, nodes, e, h, out, e_out, h_out, sems):
    nx, nz, ny = power.shape
    e_copy = pltpu.make_async_copy(e.at[:, pl.ds(0, nx)], e_out, sems.at[0])
    h_copy = pltpu.make_async_copy(h.at[:, pl.ds(1, nx)], h_out, sems.at[1])
    e_copy.start()
    h_copy.start()
    n_group, rows, _ = out.shape
    per_row = ny // PTS
    extra = nodes.shape[0] // n_group
    flat = out.reshape(n_group * rows, PTS)

    def clear(group, carry):
        out[group] = jnp.zeros((rows, PTS), F32)
        out[group, rows - extra : rows, :] = nodes[pl.ds(pl.multiple_of(group * extra, ROWS), extra), :]
        return carry

    lax.fori_loop(0, n_group, clear, 0)

    def plane(x, carry):
        for z in range(nz):
            for k in range(per_row):
                spot = place[x * (nz * per_row) + z * per_row + k]
                flat[pl.ds(spot, 1), :] = power[x, z : z + 1, k * PTS : (k + 1) * PTS]
        return carry

    lax.fori_loop(0, nx, plane, 0)
    e_copy.wait()
    h_copy.wait()


def collect_kernel(cap, blocks, out, chosen, split):
    n_from, rows, pts = blocks.shape
    n_part, node_count, _ = out.shape
    room = chosen.shape[1] // n_from
    parts = room // LANES
    ids = lax.broadcasted_iota(jnp.int32, (node_count, LANES), 0).astype(F32)
    split[...] = jnp.zeros(split.shape, split.dtype)
    for part in range(n_part):
        for source in range(n_from):
            for piece in range(parts):
                row = n_part * cap + part * parts + piece
                lanes = slice(source * room + piece * LANES, source * room + (piece + 1) * LANES)
                hit = ids == blocks[source, row : row + 1, :]
                chosen[:, lanes] = jnp.where(hit, 1.0, 0.0).astype(jnp.bfloat16)
            values = blocks[source, part * cap : (part + 1) * cap, :]
            high = values.astype(jnp.bfloat16)
            here = slice(source * room, source * room + cap)
            split[here, 0:pts] = high
            split[here, pts : 2 * pts] = (values - high.astype(F32)).astype(jnp.bfloat16)
        both = jnp.dot(chosen[...], split[...], preferred_element_type=F32)
        out[part] = both[:, 0:pts] + both[:, pts : 2 * pts]


def shifted(block, d_col, d_hgt):
    n_col = lax.axis_size("col")
    n_hgt = lax.axis_size("hgt")
    route = [
        (c * n_hgt + h, (c + d_col) * n_hgt + h + d_hgt)
        for c in range(n_col)
        for h in range(n_hgt)
        if 0 <= c + d_col < n_col and 0 <= h + d_hgt < n_hgt
    ]
    return lax.ppermute(block, ("col", "hgt"), route)


def tissue_warmth_kelvin(heat_content_per_mass):
    return jnp.where(
        heat_content_per_mass < 0.0,
        heat_content_per_mass / 2.0,
        jnp.where(heat_content_per_mass > 1.0, (heat_content_per_mass - 1.0) / 3.0, 0.0),
    )


def per_device(
    efield_lattice_vector,
    hfield_lattice_vector,
    cell_temp,
    region_tags,
    block_owner,
    block_node,
    node_enthalpy,
):
    nx, nz, ny = cell_temp.shape
    n_col = lax.axis_size("col")
    n_hgt = lax.axis_size("hgt")
    n_dev = n_col * n_hgt
    count = nx * nz * ny // PTS
    cap = 2 * count // n_dev
    node_count = node_enthalpy.shape[0]
    cells = nx * nz * ny
    sem = pltpu.SemaphoreType.DMA

    e_start = far(efield_lattice_vector)
    h_start = far(hfield_lattice_vector)
    to_fwd, to_back = pl.pallas_call(
        edges_kernel,
        out_shape=(vmem(5, nz, ny), vmem(2, nz, ny)),
        in_specs=[FAR, FAR],
        out_specs=(WHOLE, WHOLE),
        scratch_shapes=[sem((3,))],
        compiler_params=params(VMEM_MIB),
        cost_estimate=cost(0, 7 * nz * ny * 8),
        name="edges",
    )(e_start, h_start)
    col_fwd = shifted(to_fwd, 1, 0)
    col_back = shifted(to_back, -1, 0)
    room_for = -(-cap // LANES) * LANES
    extra = -(-(n_col * room_for // LANES) // ROWS) * ROWS
    place, send_nodes = pl.pallas_call(
        functools.partial(places_kernel, n_col, n_hgt, cap, extra),
        out_shape=(
            jax.ShapeDtypeStruct((1, count), jnp.int32),
            jax.ShapeDtypeStruct((n_hgt * extra, PTS), F32),
        ),
        in_specs=[WHOLE, WHOLE],
        out_specs=(WHOLE, WHOLE),
        compiler_params=params(VMEM_MIB),
        cost_estimate=cost(count * n_dev * 8, count * 16),
        name="places",
    )(block_owner.reshape(1, count), block_node.reshape(1, count))
    place = place.reshape(count)
    inside = jnp.stack([lax.axis_index("col") > 0, lax.axis_index("hgt") > 0]).astype(F32)
    e, h, rows_fwd, rows_back, diag_fwd, diag_back = pl.pallas_call(
        load_kernel,
        out_shape=(
            vmem(3, nx + 1, nz, ny),
            vmem(3, nx + 1, nz, ny),
            vmem(5, nx, ny),
            vmem(2, nx, ny),
            vmem(1, ny),
            vmem(1, ny),
        ),
        in_specs=[FAR, FAR, SCALARS, SCALARS],
        out_specs=(WHOLE,) * 6,
        scratch_shapes=[sem((2,))],
        compiler_params=params(VMEM_MIB),
        cost_estimate=cost(0, cells * 24),
        name="load",
    )(e_start, h_start, place, inside)
    hgt_fwd = shifted(rows_fwd, 0, 1)
    hgt_back = shifted(rows_back, 0, -1)
    corner_x = shifted(diag_fwd, 1, -1)
    corner_z = shifted(diag_back, -1, 1)

    ca, cb, sigma = pl.pallas_call(
        coefficients_kernel,
        out_shape=(vmem(nx, nz, ny),) * 3,
        in_specs=[FAR, FAR],
        out_specs=(WHOLE,) * 3,
        scratch_shapes=[
            pltpu.VMEM((nx, nz, ny), F32),
            pltpu.VMEM((nx, nz, ny), jnp.int32),
            sem((2, 4)),
        ],
        compiler_params=params(VMEM_MIB),
        cost_estimate=cost(cells * 40, cells * 20),
        name="coefficients",
    )(far(cell_temp), far(region_tags))
    low = power = None
    for step in range(STEPS):
        first = step == 0
        last = step == STEPS - 1
        out_shape = [vmem(3, nx + 1, nz, ny), vmem(3, nx + 1, nz, ny), vmem(nx, nz, ny), vmem(2, nx, ny)]
        if not last:
            out_shape += [
                vmem(3, nz, ny),
                vmem(2, nz, ny),
                vmem(3, nx, ny),
                vmem(2, nx, ny),
                vmem(1, ny),
                vmem(1, ny),
            ]
        args = [inside, e, h, ca, cb, sigma, col_fwd, col_back, hgt_fwd, hgt_back, corner_x, corner_z, rows_back]
        aliases = {1: 0, 2: 1}
        if not first:
            args += [low, power]
            aliases.update({13: 3, 14: 2})
        outs = pl.pallas_call(
            functools.partial(step_kernel, first, last),
            out_shape=tuple(out_shape),
            in_specs=[SCALARS] + [WHOLE] * (len(args) - 1),
            out_specs=(WHOLE,) * len(out_shape),
            input_output_aliases=aliases,
            compiler_params=params(VMEM_MIB),
            cost_estimate=cost(cells * 60, cells * 40),
            name=f"yee_step_{step}",
        )(*args)
        e, h, power, low = outs[:4]
        if not last:
            to_fwd, to_back, rows_fwd, rows_back, diag_fwd, diag_back = outs[4:]
            col_fwd = shifted(to_fwd, 1, 0)
            col_back = shifted(to_back, -1, 0)
            hgt_fwd = shifted(rows_fwd, 0, 1)
            hgt_back = shifted(rows_back, 0, -1)
            corner_x = shifted(diag_fwd, 1, -1)
            corner_z = shifted(diag_back, -1, 1)

    send, e_out, h_out = pl.pallas_call(
        pack_kernel,
        out_shape=(
            jax.ShapeDtypeStruct((n_hgt, n_col * cap + extra, PTS), F32),
            pltpu.HBM((3, nx, nz, ny), F32),
            pltpu.HBM((3, nx, nz, ny), F32),
        ),
        in_specs=[SCALARS, WHOLE, WHOLE, WHOLE, WHOLE],
        out_specs=(WHOLE, FAR, FAR),
        scratch_shapes=[sem((2,))],
        compiler_params=params(VMEM_MIB),
        cost_estimate=cost(cells, cells * 36),
        name="pack",
    )(place, power, send_nodes, e, h)
    blocks = lax.all_to_all(send, "hgt", split_axis=0, concat_axis=0, tiled=True)
    partial = pl.pallas_call(
        functools.partial(collect_kernel, cap),
        out_shape=jax.ShapeDtypeStruct((n_col, node_count, PTS), F32),
        in_specs=[WHOLE],
        out_specs=WHOLE,
        scratch_shapes=[
            pltpu.VMEM((node_count, n_hgt * room_for), jnp.bfloat16),
            pltpu.VMEM((n_hgt * room_for, 2 * PTS), jnp.bfloat16),
        ],
        compiler_params=params(VMEM_MIB),
        cost_estimate=cost(n_col * node_count * n_hgt * room_for * PTS * 4, cells * 8),
        name="collect",
    )(blocks)
    parts = lax.all_to_all(partial, "col", split_axis=0, concat_axis=0, tiled=True)
    heat = jnp.sum(parts, axis=0)
    heat_content_per_mass = node_enthalpy + (0.25 / STEPS) * heat
    return e_out, h_out, tissue_warmth_kelvin(heat_content_per_mass)


def solution(mesh):
    placed = (
        P(None, "col", "hgt", None),
        P(None, "col", "hgt", None),
        P("col", "hgt", None),
        P("col", "hgt", None),
        P("col", "hgt", None, None, None, None),
        P("col", "hgt", None, None, None),
        P(("col", "hgt"), None),
    )
    return jax.shard_map(
        per_device,
        mesh=mesh,
        in_specs=placed,
        out_specs=(
            P(None, "col", "hgt", None),
            P(None, "col", "hgt", None),
            P(("col", "hgt"), None),
        ),
        check_vma=False,
    )
```

```python
import functools

import jax
import jax.numpy as jnp
from jax import lax
from jax.experimental import pallas as pl
from jax.experimental.pallas import tpu as pltpu
from jax.sharding import PartitionSpec as P

PTS = 128
STEPS = 4
COURANT = 0.55
LANES = 128
ROWS = 8
F32 = jnp.float32
VMEM_MIB = 16

WHOLE = pl.BlockSpec(memory_space=pltpu.VMEM)
SCALARS = pl.BlockSpec(memory_space=pltpu.SMEM)
FAR = pl.BlockSpec(memory_space=pltpu.HBM)


def vmem(*shape):
    return pltpu.VMEM(shape, F32)


def far(x):
    return pltpu.with_memory_space_constraint(x, pltpu.HBM)


def params(mib):
    return pltpu.CompilerParams(vmem_limit_bytes=mib << 20)


def cost(flops, moved):
    return pl.CostEstimate(flops=flops, bytes_accessed=moved, transcendentals=0)


def after_y(f):
    lane = lax.broadcasted_iota(jnp.int32, (ROWS, LANES), 1)
    n = f.shape[1] // LANES
    turned = [pltpu.roll(f[:, k * LANES : (k + 1) * LANES], LANES - 1, 1) for k in range(n)]
    turned.append(jnp.zeros((ROWS, LANES), F32))
    return jnp.concatenate([jnp.where(lane < LANES - 1, turned[k], turned[k + 1]) for k in range(n)], 1)


def before_y(f):
    lane = lax.broadcasted_iota(jnp.int32, (ROWS, LANES), 1)
    n = f.shape[1] // LANES
    turned = [jnp.zeros((ROWS, LANES), F32)]
    turned += [pltpu.roll(f[:, k * LANES : (k + 1) * LANES], 1, 1) for k in range(n)]
    return jnp.concatenate([jnp.where(lane > 0, turned[k + 1], turned[k]) for k in range(n)], 1)


def after_row(f, row):
    place = lax.broadcasted_iota(jnp.int32, f.shape, 0)
    return jnp.where(place < ROWS - 1, pltpu.roll(f, ROWS - 1, 0), jnp.broadcast_to(row, f.shape))


def before_row(f, row):
    place = lax.broadcasted_iota(jnp.int32, f.shape, 0)
    return jnp.where(place > 0, pltpu.roll(f, 1, 0), jnp.broadcast_to(row, f.shape))


def edge_kernel(e, back, sem):
    copy = pltpu.make_async_copy(e.at[pl.ds(1, 2), 0], back, sem)
    copy.start()
    copy.wait()


def load_kernel(e_in, order, e, back, sem):
    nx = e.shape[1]
    copy = pltpu.make_async_copy(e_in, e, sem)
    copy.start()
    copy.wait()

    def rows(x, carry):
        for comp in range(2):
            back[comp, pl.ds(x, 1), :] = e[comp, x, 0:1, :]
        return carry

    lax.fori_loop(0, nx, rows, 0)


def coefficients_kernel(temp_far, tags_far, h_far, ca, cb, sigma_out, h, temp, tags, sems):
    nx, nz, _ = temp.shape
    parts = 4
    size = nx // parts
    copies = []
    for part in range(parts):
        here = pl.ds(part * size, size)
        copies.append(pltpu.make_async_copy(temp_far.at[here], temp.at[here], sems.at[0, part]))
        copies.append(pltpu.make_async_copy(tags_far.at[here], tags.at[here], sems.at[1, part]))
    h_copy = pltpu.make_async_copy(h_far, h, sems.at[2, 0])
    for copy in copies:
        copy.start()
    h_copy.start()

    def plane(x, carry):
        for z in range(0, nz, ROWS):
            tag = tags[x, z : z + ROWS, :]
            lean = tag == 0
            fat = tag == 1
            frac = 1.0 / (1.0 + jnp.exp(-2.0 * temp[x, z : z + ROWS, :]))
            eps_low = jnp.where(lean, 4.0, jnp.where(fat, 2.5, 5.0))
            eps_rise = jnp.where(lean, 46.0, jnp.where(fat, 3.5, 5.0))
            sig_low = jnp.where(lean, 0.2, jnp.where(fat, 0.05, 0.1))
            sig_rise = jnp.where(lean, 7.8, jnp.where(fat, 0.35, 0.9))
            eps = eps_low + eps_rise * frac
            sigma = sig_low + sig_rise * frac
            half = (0.5 * COURANT) * sigma
            inverse = 1.0 / (eps + half)
            ca[x, z : z + ROWS, :] = (eps - half) * inverse
            cb[x, z : z + ROWS, :] = COURANT * inverse
            sigma_out[x, z : z + ROWS, :] = sigma
        return carry

    for part in range(parts):
        copies[2 * part].wait()
        copies[2 * part + 1].wait()
        lax.fori_loop(part * size, (part + 1) * size, plane, 0)
    h_copy.wait()


def over(first, stop, body):
    if stop - first == 1:
        body(first)
    else:

        def step(x, carry):
            body(x)
            return carry

        lax.fori_loop(first, stop, step, 0)


def h_tile(e, h, col, hgt, x, z):
    nz = e.shape[2]
    here = slice(z, z + ROWS)
    ex, ey, ez = (e[comp, x, here, :] for comp in range(3))
    if z + ROWS < nz:
        row_x, row_y = (e[comp, x, z + ROWS : z + ROWS + 1, :] for comp in range(2))
    else:
        row_x, row_y = (hgt[comp, pl.ds(x, 1), :] for comp in range(2))
    if col is None:
        next_y, next_z = (e[comp, x + 1, here, :] for comp in (1, 2))
    else:
        next_y, next_z = (col[comp, here, :] for comp in range(2))
    h[0, x, here, :] = h[0, x, here, :] - COURANT * ((after_y(ez) - ez) - (after_row(ey, row_y) - ey))
    hy = h[1, x, here, :] - COURANT * ((after_row(ex, row_x) - ex) - (next_z - ez))
    hz = h[2, x, here, :] - COURANT * ((next_y - ey) - (after_y(ex) - ex))
    h[1, x, here, :] = hy
    h[2, x, here, :] = hz
    return hy, hz


def e_tile(first, h, e, power, ca, cb, sigma, col, hgt, x, z):
    here = slice(z, z + ROWS)
    hx, hy, hz = (h[comp, x, here, :] for comp in range(3))
    if z > 0:
        row_x, row_y = (h[comp, x, z - 1 : z, :] for comp in range(2))
    else:
        row_x, row_y = (hgt[comp, pl.ds(x, 1), :] for comp in range(2))
    if col is None:
        past_y, past_z = (h[comp, x - 1, here, :] for comp in (1, 2))
    else:
        past_y, past_z = (col[comp, here, :] for comp in range(2))
    keep = ca[x, here, :]
    drive = cb[x, here, :]
    ex = keep * e[0, x, here, :] + drive * ((hz - before_y(hz)) - (hy - before_row(hy, row_y)))
    ey = keep * e[1, x, here, :] + drive * ((hx - before_row(hx, row_x)) - (hz - past_z))
    ez = keep * e[2, x, here, :] + drive * ((hy - past_y) - (hx - before_y(hx)))
    e[0, x, here, :] = ex
    e[1, x, here, :] = ey
    e[2, x, here, :] = ez
    heat = sigma[x, here, :] * (ex * ex + ey * ey + ez * ez)
    power[x, here, :] = heat if first else power[x, here, :] + heat
    return ey, ez


def h_inner_kernel(e, h_old, h):
    nx, nz = e.shape[1:3]

    def plane(x):
        for z in range(0, nz - ROWS, ROWS):
            h_tile(e, h, None, None, x, z)

    over(0, nx - 1, plane)


def h_plane_kernel(e, col, hgt, h_old, h, send):
    nx, nz = e.shape[1:3]
    for z in range(0, nz, ROWS):
        hy, hz = h_tile(e, h, col, hgt, nx - 1, z)
        send[0, z : z + ROWS, :] = hy
        send[1, z : z + ROWS, :] = hz


def h_rows_kernel(e, hgt, h_old, h, send):
    nx, nz = e.shape[1:3]

    def keep(x):
        for comp in range(2):
            send[comp, pl.ds(x, 1), :] = h[comp, x, nz - 1 : nz, :]

    def plane(x):
        h_tile(e, h, None, hgt, x, nz - ROWS)
        keep(x)

    over(0, nx - 1, plane)
    keep(nx - 1)


def e_inner_kernel(first, h, ca, cb, sigma, *refs):
    e, power = refs[-2:]
    nx, nz = e.shape[1:3]

    def plane(x):
        for z in range(ROWS, nz, ROWS):
            e_tile(first, h, e, power, ca, cb, sigma, None, None, x, z)

    over(1, nx, plane)


def e_plane_kernel(first, h, ca, cb, sigma, col, hgt, e_old, power_old, e, power, *send):
    nz = e.shape[2]
    for z in range(0, nz, ROWS):
        ey, ez = e_tile(first, h, e, power, ca, cb, sigma, col, hgt, 0, z)
        if send:
            send[0][0, z : z + ROWS, :] = ey
            send[0][1, z : z + ROWS, :] = ez


def e_rows_kernel(first, h, ca, cb, sigma, hgt, e_old, power_old, e, power, *send):
    nx = e.shape[1]

    def keep(x):
        if send:
            for comp in range(2):
                send[0][comp, pl.ds(x, 1), :] = e[comp, x, 0:1, :]

    def plane(x):
        e_tile(first, h, e, power, ca, cb, sigma, None, hgt, x, 0)
        keep(x)

    keep(0)
    over(1, nx, plane)


def places_kernel(n_col, n_hgt, cap, extra, owner, node, place, nodes_out):
    n_dev = n_col * n_hgt
    count = owner.shape[1]
    width = 256
    rows = lax.broadcasted_iota(jnp.int32, (n_dev, width), 0)
    before = lax.broadcasted_iota(jnp.int32, (width, width), 0)
    after = lax.broadcasted_iota(jnp.int32, (width, width), 1)
    upper = jnp.where(before <= after, 1.0, 0.0).astype(jnp.bfloat16)
    room_for = nodes_out.shape[0] // n_dev * LANES
    room = lax.broadcasted_iota(jnp.int32, (room_for, width), 0)
    total = jnp.zeros((n_dev, 1), F32)
    high = jnp.zeros((n_dev, room_for), F32)
    low = jnp.zeros((n_dev, room_for), F32)
    nt = (((1,), (1,)), ((), ()))
    for start in range(0, count, width):
        own = owner[:, start : start + width]
        target = lax.rem(own, n_hgt) * n_col + lax.div(own, n_hgt)
        hit = jnp.where(rows == target, 1.0, 0.0)
        running = total + jnp.dot(hit.astype(jnp.bfloat16), upper, preferred_element_type=F32)
        total = running[:, width - 1 : width]
        rank = jnp.sum(hit * running, axis=0, keepdims=True).astype(jnp.int32) - 1
        group = lax.div(target, n_col)
        place[:, start : start + width] = target * cap + group * extra + rank
        number = node[:, start : start + width]
        upper_part = lax.div(number, 16)
        lower_part = number - 16 * upper_part
        seat = jnp.where(room == rank, 1.0, 0.0).astype(jnp.bfloat16)
        high = high + lax.dot_general(
            (hit * upper_part.astype(F32)).astype(jnp.bfloat16), seat, nt, preferred_element_type=F32
        )
        low = low + lax.dot_general(
            (hit * lower_part.astype(F32)).astype(jnp.bfloat16), seat, nt, preferred_element_type=F32
        )
    taken = lax.broadcasted_iota(jnp.int32, (n_dev, room_for), 1).astype(F32) < total
    table = jnp.where(taken, 16.0 * high + low, -1.0)
    parts = room_for // LANES
    for part in range(parts):
        nodes_out[pl.ds(part, n_dev, stride=parts), :] = table[:, part * LANES : (part + 1) * LANES]


def pack_kernel(place, power, nodes, e, h, out, e_out, h_out, sems):
    nx, nz, ny = power.shape
    e_copy = pltpu.make_async_copy(e, e_out, sems.at[0])
    h_copy = pltpu.make_async_copy(h, h_out, sems.at[1])
    e_copy.start()
    h_copy.start()
    n_group, rows, _ = out.shape
    per_row = ny // PTS
    extra = nodes.shape[0] // n_group
    flat = out.reshape(n_group * rows, PTS)

    def clear(group, carry):
        out[group] = jnp.zeros((rows, PTS), F32)
        out[group, rows - extra : rows, :] = nodes[pl.ds(pl.multiple_of(group * extra, ROWS), extra), :]
        return carry

    lax.fori_loop(0, n_group, clear, 0)

    def plane(x, carry):
        for z in range(nz):
            for k in range(per_row):
                spot = place[x * (nz * per_row) + z * per_row + k]
                flat[pl.ds(spot, 1), :] = power[x, z : z + 1, k * PTS : (k + 1) * PTS]
        return carry

    lax.fori_loop(0, nx, plane, 0)
    e_copy.wait()
    h_copy.wait()


def collect_kernel(cap, blocks, out, chosen, split):
    n_from, rows, pts = blocks.shape
    n_part, node_count, _ = out.shape
    room = chosen.shape[1] // n_from
    parts = room // LANES
    ids = lax.broadcasted_iota(jnp.int32, (node_count, LANES), 0).astype(F32)
    split[...] = jnp.zeros(split.shape, split.dtype)
    for part in range(n_part):
        for source in range(n_from):
            for piece in range(parts):
                row = n_part * cap + part * parts + piece
                lanes = slice(source * room + piece * LANES, source * room + (piece + 1) * LANES)
                hit = ids == blocks[source, row : row + 1, :]
                chosen[:, lanes] = jnp.where(hit, 1.0, 0.0).astype(jnp.bfloat16)
            values = blocks[source, part * cap : (part + 1) * cap, :]
            high = values.astype(jnp.bfloat16)
            here = slice(source * room, source * room + cap)
            split[here, 0:pts] = high
            split[here, pts : 2 * pts] = (values - high.astype(F32)).astype(jnp.bfloat16)
        both = jnp.dot(chosen[...], split[...], preferred_element_type=F32)
        out[part] = both[:, 0:pts] + both[:, pts : 2 * pts]


def shifted(block, d_col, d_hgt):
    n_col = lax.axis_size("col")
    n_hgt = lax.axis_size("hgt")
    route = [
        (c * n_hgt + h, (c + d_col) * n_hgt + h + d_hgt)
        for c in range(n_col)
        for h in range(n_hgt)
        if 0 <= c + d_col < n_col and 0 <= h + d_hgt < n_hgt
    ]
    return lax.ppermute(block, ("col", "hgt"), route)


def tissue_warmth_kelvin(heat_content_per_mass):
    return jnp.where(
        heat_content_per_mass < 0.0,
        heat_content_per_mass / 2.0,
        jnp.where(heat_content_per_mass > 1.0, (heat_content_per_mass - 1.0) / 3.0, 0.0),
    )


def per_device(
    efield_lattice_vector,
    hfield_lattice_vector,
    cell_temp,
    region_tags,
    block_owner,
    block_node,
    node_enthalpy,
):
    nx, nz, ny = cell_temp.shape
    n_col = lax.axis_size("col")
    n_hgt = lax.axis_size("hgt")
    n_dev = n_col * n_hgt
    count = nx * nz * ny // PTS
    cap = 2 * count // n_dev
    node_count = node_enthalpy.shape[0]
    cells = nx * nz * ny
    sem = pltpu.SemaphoreType.DMA

    def kernel(body, outs, ins, args, name, work, aliases=None, scratch=()):
        return pl.pallas_call(
            body,
            out_shape=outs,
            in_specs=ins,
            out_specs=jax.tree.map(lambda out: WHOLE, outs),
            input_output_aliases=aliases or {},
            scratch_shapes=scratch,
            compiler_params=params(VMEM_MIB),
            cost_estimate=cost(work * cells, work * cells),
            name=name,
        )(*args)

    e_start = far(efield_lattice_vector)
    h_start = far(hfield_lattice_vector)
    owners = block_owner.reshape(1, count)
    nodes = block_node.reshape(1, count)
    field = vmem(3, nx, nz, ny)
    whole = vmem(nx, nz, ny)
    planes = vmem(2, nz, ny)
    rows = vmem(2, nx, ny)

    to_col = kernel(edge_kernel, planes, [FAR], [e_start], "edge", 1, scratch=[sem])
    col = shifted(to_col, -1, 0)
    e, to_hgt = kernel(load_kernel, (field, rows), [FAR, WHOLE], [e_start, owners + nodes], "load", 24, scratch=[sem])
    hgt = shifted(to_hgt, 0, -1)
    ca, cb, sigma, h = kernel(
        coefficients_kernel,
        (whole, whole, whole, field),
        [FAR] * 3,
        [far(cell_temp), far(region_tags), h_start],
        "coefficients",
        40,
        scratch=[pltpu.VMEM((nx, nz, ny), F32), pltpu.VMEM((nx, nz, ny), jnp.int32), sem((3, 4))],
    )
    room_for = -(-cap // LANES) * LANES
    extra = -(-(n_col * room_for // LANES) // ROWS) * ROWS
    place, send_nodes = kernel(
        functools.partial(places_kernel, n_col, n_hgt, cap, extra),
        (jax.ShapeDtypeStruct((1, count), jnp.int32), jax.ShapeDtypeStruct((n_hgt * extra, PTS), F32)),
        [WHOLE] * 2,
        [owners, nodes],
        "places",
        8,
    )
    power = None
    for step in range(STEPS):
        first = step == 0
        last = step == STEPS - 1
        h = kernel(h_inner_kernel, field, [WHOLE] * 2, [e, h], f"h_inner_{step}", 25, {1: 0})
        h, to_col = kernel(
            h_plane_kernel, (field, planes), [WHOLE] * 4, [e, col, hgt, h], f"h_plane_{step}", 2, {3: 0}
        )
        col = shifted(to_col, 1, 0)
        h, to_hgt = kernel(h_rows_kernel, (field, rows), [WHOLE] * 3, [e, hgt, h], f"h_rows_{step}", 12, {2: 0})
        hgt = shifted(to_hgt, 0, 1)
        media = [h, ca, cb, sigma]
        if first:
            e, power = kernel(
                functools.partial(e_inner_kernel, first),
                (field, whole),
                [WHOLE] * 5,
                media + [e],
                f"e_inner_{step}",
                30,
                {4: 0},
            )
        else:
            e, power = kernel(
                functools.partial(e_inner_kernel, first),
                (field, whole),
                [WHOLE] * 6,
                media + [e, power],
                f"e_inner_{step}",
                30,
                {4: 0, 5: 1},
            )
        outs = kernel(
            functools.partial(e_plane_kernel, first),
            (field, whole) if last else (field, whole, planes),
            [WHOLE] * 8,
            media + [col, hgt, e, power],
            f"e_plane_{step}",
            3,
            {6: 0, 7: 1},
        )
        e, power = outs[:2]
        if not last:
            col = shifted(outs[2], -1, 0)
        outs = kernel(
            functools.partial(e_rows_kernel, first),
            (field, whole) if last else (field, whole, rows),
            [WHOLE] * 7,
            media + [hgt, e, power],
            f"e_rows_{step}",
            15,
            {5: 0, 6: 1},
        )
        e, power = outs[:2]
        if not last:
            hgt = shifted(outs[2], 0, -1)

    send, e_out, h_out = pl.pallas_call(
        pack_kernel,
        out_shape=(
            jax.ShapeDtypeStruct((n_hgt, n_col * cap + extra, PTS), F32),
            pltpu.HBM((3, nx, nz, ny), F32),
            pltpu.HBM((3, nx, nz, ny), F32),
        ),
        in_specs=[SCALARS, WHOLE, WHOLE, WHOLE, WHOLE],
        out_specs=(WHOLE, FAR, FAR),
        scratch_shapes=[sem((2,))],
        compiler_params=params(VMEM_MIB),
        cost_estimate=cost(cells, cells * 36),
        name="pack",
    )(place.reshape(count), power, send_nodes, e, h)
    blocks = lax.all_to_all(send, "hgt", split_axis=0, concat_axis=0, tiled=True)
    partial = pl.pallas_call(
        functools.partial(collect_kernel, cap),
        out_shape=jax.ShapeDtypeStruct((n_col, node_count, PTS), F32),
        in_specs=[WHOLE],
        out_specs=WHOLE,
        scratch_shapes=[
            pltpu.VMEM((node_count, n_hgt * room_for), jnp.bfloat16),
            pltpu.VMEM((n_hgt * room_for, 2 * PTS), jnp.bfloat16),
        ],
        compiler_params=params(VMEM_MIB),
        cost_estimate=cost(n_col * node_count * n_hgt * room_for * PTS * 4, cells * 8),
        name="collect",
    )(blocks)
    parts = lax.all_to_all(partial, "col", split_axis=0, concat_axis=0, tiled=True)
    heat = jnp.sum(parts, axis=0)
    heat_content_per_mass = node_enthalpy + (0.25 / STEPS) * heat
    return e_out, h_out, tissue_warmth_kelvin(heat_content_per_mass)


def solution(mesh):
    placed = (
        P(None, "col", "hgt", None),
        P(None, "col", "hgt", None),
        P("col", "hgt", None),
        P("col", "hgt", None),
        P("col", "hgt", None, None, None, None),
        P("col", "hgt", None, None, None),
        P(("col", "hgt"), None),
    )
    return jax.shard_map(
        per_device,
        mesh=mesh,
        in_specs=placed,
        out_specs=(
            P(None, "col", "hgt", None),
            P(None, "col", "hgt", None),
            P(("col", "hgt"), None),
        ),
        check_vma=False,
    )
```

```python
import functools

import jax
import jax.numpy as jnp
from jax import lax
from jax.experimental import pallas as pl
from jax.experimental.pallas import tpu as pltpu
from jax.sharding import PartitionSpec as P

PTS = 128
STEPS = 4
COURANT = 0.55
LANES = 128
ROWS = 8
F32 = jnp.float32
VMEM_MIB = 16

WHOLE = pl.BlockSpec(memory_space=pltpu.VMEM)
SCALARS = pl.BlockSpec(memory_space=pltpu.SMEM)
FAR = pl.BlockSpec(memory_space=pltpu.HBM)


def vmem(*shape):
    return pltpu.VMEM(shape, F32)


def far(x):
    return pltpu.with_memory_space_constraint(x, pltpu.HBM)


def params(mib):
    return pltpu.CompilerParams(vmem_limit_bytes=mib << 20)


def cost(flops, moved):
    return pl.CostEstimate(flops=flops, bytes_accessed=moved, transcendentals=0)


def after_y(f):
    lane = lax.broadcasted_iota(jnp.int32, (ROWS, LANES), 1)
    n = f.shape[1] // LANES
    turned = [pltpu.roll(f[:, k * LANES : (k + 1) * LANES], LANES - 1, 1) for k in range(n)]
    turned.append(jnp.zeros((ROWS, LANES), F32))
    return jnp.concatenate([jnp.where(lane < LANES - 1, turned[k], turned[k + 1]) for k in range(n)], 1)


def before_y(f):
    lane = lax.broadcasted_iota(jnp.int32, (ROWS, LANES), 1)
    n = f.shape[1] // LANES
    turned = [jnp.zeros((ROWS, LANES), F32)]
    turned += [pltpu.roll(f[:, k * LANES : (k + 1) * LANES], 1, 1) for k in range(n)]
    return jnp.concatenate([jnp.where(lane > 0, turned[k + 1], turned[k]) for k in range(n)], 1)


def after_row(f, row):
    place = lax.broadcasted_iota(jnp.int32, f.shape, 0)
    return jnp.where(place < ROWS - 1, pltpu.roll(f, ROWS - 1, 0), jnp.broadcast_to(row, f.shape))


def before_row(f, row):
    place = lax.broadcasted_iota(jnp.int32, f.shape, 0)
    return jnp.where(place > 0, pltpu.roll(f, 1, 0), jnp.broadcast_to(row, f.shape))


def edge_kernel(e, to_col, to_hgt, low, sems):
    nx = e.shape[1]
    col_copy = pltpu.make_async_copy(e.at[pl.ds(1, 2), 0], to_col, sems.at[0])
    low_copy = pltpu.make_async_copy(e.at[pl.ds(0, 2), :, pl.ds(0, ROWS)], low, sems.at[1])
    low_copy.start()
    col_copy.start()
    low_copy.wait()
    for x in range(nx):
        for comp in range(2):
            to_hgt[comp, x : x + 1, :] = low[comp, x, 0:1, :]
    col_copy.wait()


def load_kernel(
    temp_far, tags_far, e_far, h_far, order, ca, cb, sigma_out, e, h, media_rows, e_rows, h_rows, temp, tags, sems
):
    nx, nz, _ = temp.shape
    parts = 4
    size = nx // parts
    copies = []
    for part in range(parts):
        here = pl.ds(part * size, size)
        copies.append(pltpu.make_async_copy(temp_far.at[here], temp.at[here], sems.at[0, part]))
        copies.append(pltpu.make_async_copy(tags_far.at[here], tags.at[here], sems.at[1, part]))
    e_copy = pltpu.make_async_copy(e_far, e, sems.at[2, 0])
    h_copy = pltpu.make_async_copy(h_far, h, sems.at[2, 1])
    for copy in copies:
        copy.start()
    e_copy.start()
    h_copy.start()

    def plane(x, carry):
        for z in range(0, nz, ROWS):
            tag = tags[x, z : z + ROWS, :]
            lean = tag == 0
            fat = tag == 1
            frac = 1.0 / (1.0 + jnp.exp(-2.0 * temp[x, z : z + ROWS, :]))
            eps_low = jnp.where(lean, 4.0, jnp.where(fat, 2.5, 5.0))
            eps_rise = jnp.where(lean, 46.0, jnp.where(fat, 3.5, 5.0))
            sig_low = jnp.where(lean, 0.2, jnp.where(fat, 0.05, 0.1))
            sig_rise = jnp.where(lean, 7.8, jnp.where(fat, 0.35, 0.9))
            eps = eps_low + eps_rise * frac
            sigma = sig_low + sig_rise * frac
            half = (0.5 * COURANT) * sigma
            inverse = 1.0 / (eps + half)
            ca[x, z : z + ROWS, :] = (eps - half) * inverse
            cb[x, z : z + ROWS, :] = COURANT * inverse
            sigma_out[x, z : z + ROWS, :] = sigma
        media_rows[0, pl.ds(x, 1), :] = ca[x, 0:1, :]
        media_rows[1, pl.ds(x, 1), :] = cb[x, 0:1, :]
        return carry

    for part in range(parts):
        copies[2 * part].wait()
        copies[2 * part + 1].wait()
        lax.fori_loop(part * size, (part + 1) * size, plane, 0)
    e_copy.wait()
    h_copy.wait()

    def rows(x, carry):
        for comp in range(3):
            e_rows[comp, pl.ds(x, 1), :] = e[comp, x, nz - 1 : nz, :]
        for comp in range(2):
            h_rows[comp, pl.ds(x, 1), :] = h[comp, x, nz - 1 : nz, :]
        return carry

    lax.fori_loop(0, nx, rows, 0)


def over(first, stop, body):
    if stop - first == 1:
        body(first)
    else:

        def step(x, carry):
            body(x)
            return carry

        lax.fori_loop(first, stop, step, 0)


def h_tile(e, h, col, hgt, x, z):
    nz = e.shape[2]
    here = slice(z, z + ROWS)
    ex, ey, ez = (e[comp, x, here, :] for comp in range(3))
    if z + ROWS < nz:
        row_x, row_y = (e[comp, x, z + ROWS : z + ROWS + 1, :] for comp in range(2))
    else:
        row_x, row_y = (hgt[comp, pl.ds(x, 1), :] for comp in range(2))
    if col is None:
        next_y, next_z = (e[comp, x + 1, here, :] for comp in (1, 2))
    else:
        next_y, next_z = (col[comp, here, :] for comp in range(2))
    h[0, x, here, :] = h[0, x, here, :] - COURANT * ((after_y(ez) - ez) - (after_row(ey, row_y) - ey))
    hy = h[1, x, here, :] - COURANT * ((after_row(ex, row_x) - ex) - (next_z - ez))
    hz = h[2, x, here, :] - COURANT * ((next_y - ey) - (after_y(ex) - ex))
    h[1, x, here, :] = hy
    h[2, x, here, :] = hz
    return hy, hz


def e_tile(first, h, e, power, ca, cb, sigma, col, hgt, x, z):
    here = slice(z, z + ROWS)
    hx, hy, hz = (h[comp, x, here, :] for comp in range(3))
    if z > 0:
        row_x, row_y = (h[comp, x, z - 1 : z, :] for comp in range(2))
    else:
        row_x, row_y = (hgt[comp, pl.ds(x, 1), :] for comp in range(2))
    if col is None:
        past_y, past_z = (h[comp, x - 1, here, :] for comp in (1, 2))
    else:
        past_y, past_z = (col[comp, here, :] for comp in range(2))
    keep = ca[x, here, :]
    drive = cb[x, here, :]
    ex = keep * e[0, x, here, :] + drive * ((hz - before_y(hz)) - (hy - before_row(hy, row_y)))
    ey = keep * e[1, x, here, :] + drive * ((hx - before_row(hx, row_x)) - (hz - past_z))
    ez = keep * e[2, x, here, :] + drive * ((hy - past_y) - (hx - before_y(hx)))
    e[0, x, here, :] = ex
    e[1, x, here, :] = ey
    e[2, x, here, :] = ez
    heat = sigma[x, here, :] * (ex * ex + ey * ey + ez * ez)
    power[x, here, :] = heat if first else power[x, here, :] + heat
    return ey, ez


def h_edge_kernel(e, col, hgt, e_rows, rows_old, h_old, h, to_col, to_hgt):
    nx, nz = e.shape[1:3]
    for z in range(0, nz, ROWS):
        hy, hz = h_tile(e, h, col, hgt, nx - 1, z)
        to_col[0, z : z + ROWS, :] = hy
        to_col[1, z : z + ROWS, :] = hz
    for x in range(0, nx, ROWS):
        here = slice(x, x + ROWS)
        ex, ey, ez = (e_rows[comp, here, :] for comp in range(3))
        row = e_rows[2, x + ROWS : x + ROWS + 1, :] if x + ROWS < nx else col[1, nz - 1 : nz, :]
        to_hgt[0, here, :] = rows_old[0, here, :] - COURANT * ((after_y(ez) - ez) - (hgt[1, here, :] - ey))
        to_hgt[1, here, :] = rows_old[1, here, :] - COURANT * ((hgt[0, here, :] - ex) - (after_row(ez, row) - ez))


def h_rest_kernel(e, hgt, h_old, h, rows):
    nx, nz = e.shape[1:3]

    def keep(x):
        for comp in range(3):
            rows[comp, pl.ds(x, 1), :] = h[comp, x, 0:1, :]

    def plane(x):
        for z in range(0, nz, ROWS):
            h_tile(e, h, None, hgt, x, z)
        keep(x)

    over(0, nx - 1, plane)
    keep(nx - 1)


def e_edge_kernel(first, h, ca, cb, sigma, col, hgt, media_rows, h_rows, rows_old, *refs):
    e, power, to_col, to_hgt = refs[-4:]
    nx, nz = e.shape[1:3]
    for z in range(0, nz, ROWS):
        ey, ez = e_tile(first, h, e, power, ca, cb, sigma, col, hgt, 0, z)
        to_col[0, z : z + ROWS, :] = ey
        to_col[1, z : z + ROWS, :] = ez
    for x in range(0, nx, ROWS):
        here = slice(x, x + ROWS)
        hx, hy, hz = (h_rows[comp, here, :] for comp in range(3))
        row = h_rows[2, x - 1 : x, :] if x > 0 else col[1, 0:1, :]
        keep = media_rows[0, here, :]
        drive = media_rows[1, here, :]
        to_hgt[0, here, :] = keep * rows_old[0, here, :] + drive * ((hz - before_y(hz)) - (hy - hgt[1, here, :]))
        to_hgt[1, here, :] = keep * rows_old[1, here, :] + drive * ((hx - hgt[0, here, :]) - (hz - before_row(hz, row)))


def e_rest_kernel(first, h, ca, cb, sigma, hgt, e_old, power_old, e, power, rows):
    nx, nz = e.shape[1:3]

    def keep(x):
        for comp in range(3):
            rows[comp, pl.ds(x, 1), :] = e[comp, x, nz - 1 : nz, :]

    def plane(x):
        for z in range(0, nz, ROWS):
            e_tile(first, h, e, power, ca, cb, sigma, None, hgt, x, z)
        keep(x)

    keep(0)
    over(1, nx, plane)


def e_last_kernel(first, h, ca, cb, sigma, col, hgt, e_old, power_old, e, power):
    nx, nz = e.shape[1:3]

    def plane(x):
        for z in range(0, nz, ROWS):
            e_tile(first, h, e, power, ca, cb, sigma, col if isinstance(x, int) else None, hgt, x, z)

    plane(0)
    over(1, nx, plane)


def places_kernel(n_col, n_hgt, cap, extra, owner, node, place, nodes_out):
    n_dev = n_col * n_hgt
    count = owner.shape[1]
    width = 256
    rows = lax.broadcasted_iota(jnp.int32, (n_dev, width), 0)
    before = lax.broadcasted_iota(jnp.int32, (width, width), 0)
    after = lax.broadcasted_iota(jnp.int32, (width, width), 1)
    upper = jnp.where(before <= after, 1.0, 0.0).astype(jnp.bfloat16)
    room_for = nodes_out.shape[0] // n_dev * LANES
    room = lax.broadcasted_iota(jnp.int32, (room_for, width), 0)
    total = jnp.zeros((n_dev, 1), F32)
    parts_of = jnp.zeros((2 * n_dev, room_for), F32)
    nt = (((1,), (1,)), ((), ()))
    for start in range(0, count, width):
        own = owner[:, start : start + width]
        target = lax.rem(own, n_hgt) * n_col + lax.div(own, n_hgt)
        hit = jnp.where(rows == target, 1.0, 0.0)
        running = total + jnp.dot(hit.astype(jnp.bfloat16), upper, preferred_element_type=F32)
        total = running[:, width - 1 : width]
        rank = jnp.sum(hit * running, axis=0, keepdims=True).astype(jnp.int32) - 1
        group = lax.div(target, n_col)
        place[:, start : start + width] = target * cap + group * extra + rank
        number = node[:, start : start + width]
        upper_part = lax.div(number, 16)
        lower_part = number - 16 * upper_part
        seat = jnp.where(room == rank, 1.0, 0.0).astype(jnp.bfloat16)
        both = jnp.concatenate([hit * upper_part.astype(F32), hit * lower_part.astype(F32)], 0)
        parts_of = parts_of + lax.dot_general(both.astype(jnp.bfloat16), seat, nt, preferred_element_type=F32)
    taken = lax.broadcasted_iota(jnp.int32, (n_dev, room_for), 1).astype(F32) < total
    table = jnp.where(taken, 16.0 * parts_of[:n_dev] + parts_of[n_dev:], -1.0)
    parts = room_for // LANES
    for part in range(parts):
        nodes_out[pl.ds(part, n_dev, stride=parts), :] = table[:, part * LANES : (part + 1) * LANES]


def pack_kernel(place, power, nodes, e, h, out, e_out, h_out, sems):
    nx, nz, ny = power.shape
    e_copy = pltpu.make_async_copy(e, e_out, sems.at[0])
    h_copy = pltpu.make_async_copy(h, h_out, sems.at[1])
    e_copy.start()
    h_copy.start()
    n_group, rows, _ = out.shape
    per_row = ny // PTS
    extra = nodes.shape[0] // n_group
    flat = out.reshape(n_group * rows, PTS)

    def clear(group, carry):
        out[group] = jnp.zeros((rows, PTS), F32)
        out[group, rows - extra : rows, :] = nodes[pl.ds(pl.multiple_of(group * extra, ROWS), extra), :]
        return carry

    lax.fori_loop(0, n_group, clear, 0)

    def plane(x, carry):
        for z in range(nz):
            for k in range(per_row):
                spot = place[x * (nz * per_row) + z * per_row + k]
                flat[pl.ds(spot, 1), :] = power[x, z : z + 1, k * PTS : (k + 1) * PTS]
        return carry

    lax.fori_loop(0, nx, plane, 0)
    e_copy.wait()
    h_copy.wait()


def collect_kernel(cap, blocks, out, chosen, split):
    n_from, rows, pts = blocks.shape
    n_part, node_count, _ = out.shape
    room = chosen.shape[1] // n_from
    parts = room // LANES
    ids = lax.broadcasted_iota(jnp.int32, (node_count, LANES), 0).astype(F32)
    split[...] = jnp.zeros(split.shape, split.dtype)
    for part in range(n_part):
        for source in range(n_from):
            for piece in range(parts):
                row = n_part * cap + part * parts + piece
                lanes = slice(source * room + piece * LANES, source * room + (piece + 1) * LANES)
                hit = ids == blocks[source, row : row + 1, :]
                chosen[:, lanes] = jnp.where(hit, 1.0, 0.0).astype(jnp.bfloat16)
            values = blocks[source, part * cap : (part + 1) * cap, :]
            high = values.astype(jnp.bfloat16)
            here = slice(source * room, source * room + cap)
            split[here, 0:pts] = high
            split[here, pts : 2 * pts] = (values - high.astype(F32)).astype(jnp.bfloat16)
        both = jnp.dot(chosen[...], split[...], preferred_element_type=F32)
        out[part] = both[:, 0:pts] + both[:, pts : 2 * pts]


def shifted(block, d_col, d_hgt):
    n_col = lax.axis_size("col")
    n_hgt = lax.axis_size("hgt")
    route = [
        (c * n_hgt + h, (c + d_col) * n_hgt + h + d_hgt)
        for c in range(n_col)
        for h in range(n_hgt)
        if 0 <= c + d_col < n_col and 0 <= h + d_hgt < n_hgt
    ]
    return lax.ppermute(block, ("col", "hgt"), route)


def tissue_warmth_kelvin(heat_content_per_mass):
    return jnp.where(
        heat_content_per_mass < 0.0,
        heat_content_per_mass / 2.0,
        jnp.where(heat_content_per_mass > 1.0, (heat_content_per_mass - 1.0) / 3.0, 0.0),
    )


def per_device(
    efield_lattice_vector,
    hfield_lattice_vector,
    cell_temp,
    region_tags,
    block_owner,
    block_node,
    node_enthalpy,
):
    nx, nz, ny = cell_temp.shape
    n_col = lax.axis_size("col")
    n_hgt = lax.axis_size("hgt")
    n_dev = n_col * n_hgt
    count = nx * nz * ny // PTS
    cap = 2 * count // n_dev
    node_count = node_enthalpy.shape[0]
    cells = nx * nz * ny
    sem = pltpu.SemaphoreType.DMA

    def kernel(body, outs, ins, args, name, work, aliases=None, scratch=()):
        return pl.pallas_call(
            body,
            out_shape=outs,
            in_specs=ins,
            out_specs=jax.tree.map(lambda out: WHOLE, outs),
            input_output_aliases=aliases or {},
            scratch_shapes=scratch,
            compiler_params=params(VMEM_MIB),
            cost_estimate=cost(work * cells, work * cells),
            name=name,
        )(*args)

    e_start = far(efield_lattice_vector)
    h_start = far(hfield_lattice_vector)
    owners = block_owner.reshape(1, count)
    nodes = block_node.reshape(1, count)
    field = vmem(3, nx, nz, ny)
    whole = vmem(nx, nz, ny)
    planes = vmem(2, nz, ny)
    two_rows = vmem(2, nx, ny)
    three_rows = vmem(3, nx, ny)

    to_col, e_low = kernel(
        edge_kernel, (planes, two_rows), [FAR], [e_start], "edge", 4, scratch=[vmem(2, nx, ROWS, ny), sem((2,))]
    )
    col = shifted(to_col, -1, 0)
    hgt = shifted(e_low, 0, -1)
    ca, cb, sigma, e, h, media_rows, e_rows, h_high = kernel(
        load_kernel,
        (whole, whole, whole, field, field, two_rows, three_rows, two_rows),
        [FAR] * 4 + [WHOLE],
        [far(cell_temp), far(region_tags), e_start, h_start, owners + nodes],
        "load",
        60,
        scratch=[vmem(nx, nz, ny), pltpu.VMEM((nx, nz, ny), jnp.int32), sem((3, 4))],
    )
    room_for = -(-cap // LANES) * LANES
    extra = -(-(n_col * room_for // LANES) // ROWS) * ROWS
    place, send_nodes = kernel(
        functools.partial(places_kernel, n_col, n_hgt, cap, extra),
        (jax.ShapeDtypeStruct((1, count), jnp.int32), jax.ShapeDtypeStruct((n_hgt * extra, PTS), F32)),
        [WHOLE] * 2,
        [owners, nodes],
        "places",
        8,
    )
    power = None
    for step in range(STEPS):
        first = step == 0
        h, to_col, h_high = kernel(
            h_edge_kernel,
            (field, planes, two_rows),
            [WHOLE] * 6,
            [e, col, hgt, e_rows, h_high, h],
            f"h_edge_{step}",
            4,
            {5: 0},
        )
        e_hgt = hgt
        col = shifted(to_col, 1, 0)
        hgt = shifted(h_high, 0, 1)
        h, h_rows = kernel(
            h_rest_kernel, (field, three_rows), [WHOLE] * 3, [e, e_hgt, h], f"h_rest_{step}", 40, {2: 0}
        )
        media = [h, ca, cb, sigma]
        if step == STEPS - 1:
            e, power = kernel(
                functools.partial(e_last_kernel, first),
                (field, whole),
                [WHOLE] * 8,
                media + [col, hgt, e, power],
                f"e_last_{step}",
                50,
                {6: 0, 7: 1},
            )
            break
        args = media + [col, hgt, media_rows, h_rows, e_low, e] + ([] if first else [power])
        e, power, to_col, e_low = kernel(
            functools.partial(e_edge_kernel, first),
            (field, whole, planes, two_rows),
            [WHOLE] * len(args),
            args,
            f"e_edge_{step}",
            5,
            {9: 0} if first else {9: 0, 10: 1},
        )
        h_hgt = hgt
        col = shifted(to_col, -1, 0)
        hgt = shifted(e_low, 0, -1)
        e, power, e_rows = kernel(
            functools.partial(e_rest_kernel, first),
            (field, whole, three_rows),
            [WHOLE] * 7,
            media + [h_hgt, e, power],
            f"e_rest_{step}",
            45,
            {5: 0, 6: 1},
        )

    send, e_out, h_out = pl.pallas_call(
        pack_kernel,
        out_shape=(
            jax.ShapeDtypeStruct((n_hgt, n_col * cap + extra, PTS), F32),
            pltpu.HBM((3, nx, nz, ny), F32),
            pltpu.HBM((3, nx, nz, ny), F32),
        ),
        in_specs=[SCALARS, WHOLE, WHOLE, WHOLE, WHOLE],
        out_specs=(WHOLE, FAR, FAR),
        scratch_shapes=[sem((2,))],
        compiler_params=params(VMEM_MIB),
        cost_estimate=cost(cells, cells * 36),
        name="pack",
    )(place.reshape(count), power, send_nodes, e, h)
    blocks = lax.all_to_all(send, "hgt", split_axis=0, concat_axis=0, tiled=True)
    partial = pl.pallas_call(
        functools.partial(collect_kernel, cap),
        out_shape=jax.ShapeDtypeStruct((n_col, node_count, PTS), F32),
        in_specs=[WHOLE],
        out_specs=WHOLE,
        scratch_shapes=[
            pltpu.VMEM((node_count, n_hgt * room_for), jnp.bfloat16),
            pltpu.VMEM((n_hgt * room_for, 2 * PTS), jnp.bfloat16),
        ],
        compiler_params=params(VMEM_MIB),
        cost_estimate=cost(n_col * node_count * n_hgt * room_for * PTS * 4, cells * 8),
        name="collect",
    )(blocks)
    parts = lax.all_to_all(partial, "col", split_axis=0, concat_axis=0, tiled=True)
    heat = jnp.sum(parts, axis=0)
    heat_content_per_mass = node_enthalpy + (0.25 / STEPS) * heat
    return e_out, h_out, tissue_warmth_kelvin(heat_content_per_mass)


def solution(mesh):
    placed = (
        P(None, "col", "hgt", None),
        P(None, "col", "hgt", None),
        P("col", "hgt", None),
        P("col", "hgt", None),
        P("col", "hgt", None, None, None, None),
        P("col", "hgt", None, None, None),
        P(("col", "hgt"), None),
    )
    return jax.shard_map(
        per_device,
        mesh=mesh,
        in_specs=placed,
        out_specs=(
            P(None, "col", "hgt", None),
            P(None, "col", "hgt", None),
            P(("col", "hgt"), None),
        ),
        check_vma=False,
    )
```

```python
import functools

import jax
import jax.numpy as jnp
from jax import lax
from jax.experimental import pallas as pl
from jax.experimental.pallas import tpu as pltpu
from jax.sharding import PartitionSpec as P

PTS = 128
STEPS = 4
COURANT = 0.55
LANES = 128
ROWS = 8
F32 = jnp.float32
VMEM_MIB = 16

WHOLE = pl.BlockSpec(memory_space=pltpu.VMEM)
SCALARS = pl.BlockSpec(memory_space=pltpu.SMEM)
FAR = pl.BlockSpec(memory_space=pltpu.HBM)


def vmem(*shape):
    return pltpu.VMEM(shape, F32)


def far(x):
    return pltpu.with_memory_space_constraint(x, pltpu.HBM)


def params(mib):
    return pltpu.CompilerParams(vmem_limit_bytes=mib << 20)


def cost(flops, moved):
    return pl.CostEstimate(flops=flops, bytes_accessed=moved, transcendentals=0)


def after_y(f):
    lane = lax.broadcasted_iota(jnp.int32, (ROWS, LANES), 1)
    n = f.shape[1] // LANES
    turned = [pltpu.roll(f[:, k * LANES : (k + 1) * LANES], LANES - 1, 1) for k in range(n)]
    turned.append(jnp.zeros((ROWS, LANES), F32))
    return jnp.concatenate([jnp.where(lane < LANES - 1, turned[k], turned[k + 1]) for k in range(n)], 1)


def before_y(f):
    lane = lax.broadcasted_iota(jnp.int32, (ROWS, LANES), 1)
    n = f.shape[1] // LANES
    turned = [jnp.zeros((ROWS, LANES), F32)]
    turned += [pltpu.roll(f[:, k * LANES : (k + 1) * LANES], 1, 1) for k in range(n)]
    return jnp.concatenate([jnp.where(lane > 0, turned[k + 1], turned[k]) for k in range(n)], 1)


def after_row(f, row):
    place = lax.broadcasted_iota(jnp.int32, f.shape, 0)
    return jnp.where(place < ROWS - 1, pltpu.roll(f, ROWS - 1, 0), jnp.broadcast_to(row, f.shape))


def before_row(f, row):
    place = lax.broadcasted_iota(jnp.int32, f.shape, 0)
    return jnp.where(place > 0, pltpu.roll(f, 1, 0), jnp.broadcast_to(row, f.shape))


def edge_kernel(e, to_col, to_hgt, low, sems):
    nx = e.shape[1]
    col_copy = pltpu.make_async_copy(e.at[pl.ds(1, 2), 0], to_col, sems.at[0])
    low_copy = pltpu.make_async_copy(e.at[pl.ds(0, 2), :, pl.ds(0, ROWS)], low, sems.at[1])
    low_copy.start()
    col_copy.start()
    low_copy.wait()
    for x in range(nx):
        for comp in range(2):
            to_hgt[comp, x : x + 1, :] = low[comp, x, 0:1, :]
    col_copy.wait()


def load_kernel(
    temp_far, tags_far, e_far, h_far, order, ca, cb, sigma_out, e, h, media_rows, e_rows, h_rows, temp, tags, sems
):
    nx, nz, _ = temp.shape
    parts = 4
    size = nx // parts
    copies = []
    for part in range(parts):
        here = pl.ds(part * size, size)
        copies.append(pltpu.make_async_copy(temp_far.at[here], temp.at[here], sems.at[0, part]))
        copies.append(pltpu.make_async_copy(tags_far.at[here], tags.at[here], sems.at[1, part]))
    e_copy = pltpu.make_async_copy(e_far, e, sems.at[2, 0])
    h_copy = pltpu.make_async_copy(h_far, h, sems.at[2, 1])
    for copy in copies:
        copy.start()
    e_copy.start()
    h_copy.start()

    def plane(x, carry):
        for z in range(0, nz, ROWS):
            tag = tags[x, z : z + ROWS, :]
            lean = tag == 0
            fat = tag == 1
            frac = 1.0 / (1.0 + jnp.exp(-2.0 * temp[x, z : z + ROWS, :]))
            eps_low = jnp.where(lean, 4.0, jnp.where(fat, 2.5, 5.0))
            eps_rise = jnp.where(lean, 46.0, jnp.where(fat, 3.5, 5.0))
            sig_low = jnp.where(lean, 0.2, jnp.where(fat, 0.05, 0.1))
            sig_rise = jnp.where(lean, 7.8, jnp.where(fat, 0.35, 0.9))
            eps = eps_low + eps_rise * frac
            sigma = sig_low + sig_rise * frac
            half = (0.5 * COURANT) * sigma
            inverse = 1.0 / (eps + half)
            ca[x, z : z + ROWS, :] = (eps - half) * inverse
            cb[x, z : z + ROWS, :] = COURANT * inverse
            sigma_out[x, z : z + ROWS, :] = sigma
        media_rows[0, pl.ds(x, 1), :] = ca[x, 0:1, :]
        media_rows[1, pl.ds(x, 1), :] = cb[x, 0:1, :]
        return carry

    for part in range(parts):
        copies[2 * part].wait()
        copies[2 * part + 1].wait()
        lax.fori_loop(part * size, (part + 1) * size, plane, 0)
    e_copy.wait()
    h_copy.wait()

    def rows(x, carry):
        for comp in range(3):
            e_rows[comp, pl.ds(x, 1), :] = e[comp, x, nz - 1 : nz, :]
        for comp in range(2):
            h_rows[comp, pl.ds(x, 1), :] = h[comp, x, nz - 1 : nz, :]
        return carry

    lax.fori_loop(0, nx, rows, 0)


def over(first, stop, body):
    if stop - first == 1:
        body(first)
    else:

        def step(x, carry):
            body(x)
            return carry

        lax.fori_loop(first, stop, step, 0)


def h_tile(e, h, col, hgt, x, z):
    nz = e.shape[2]
    here = slice(z, z + ROWS)
    ex, ey, ez = (e[comp, x, here, :] for comp in range(3))
    if z + ROWS < nz:
        row_x, row_y = (e[comp, x, z + ROWS : z + ROWS + 1, :] for comp in range(2))
    else:
        row_x, row_y = (hgt[comp, pl.ds(x, 1), :] for comp in range(2))
    if col is None:
        next_y, next_z = (e[comp, x + 1, here, :] for comp in (1, 2))
    else:
        next_y, next_z = (col[comp, here, :] for comp in range(2))
    h[0, x, here, :] = h[0, x, here, :] - COURANT * ((after_y(ez) - ez) - (after_row(ey, row_y) - ey))
    hy = h[1, x, here, :] - COURANT * ((after_row(ex, row_x) - ex) - (next_z - ez))
    hz = h[2, x, here, :] - COURANT * ((next_y - ey) - (after_y(ex) - ex))
    h[1, x, here, :] = hy
    h[2, x, here, :] = hz
    return hy, hz


def e_tile(first, h, e, power, ca, cb, sigma, col, hgt, x, z):
    here = slice(z, z + ROWS)
    hx, hy, hz = (h[comp, x, here, :] for comp in range(3))
    if z > 0:
        row_x, row_y = (h[comp, x, z - 1 : z, :] for comp in range(2))
    else:
        row_x, row_y = (hgt[comp, pl.ds(x, 1), :] for comp in range(2))
    if col is None:
        past_y, past_z = (h[comp, x - 1, here, :] for comp in (1, 2))
    else:
        past_y, past_z = (col[comp, here, :] for comp in range(2))
    keep = ca[x, here, :]
    drive = cb[x, here, :]
    ex = keep * e[0, x, here, :] + drive * ((hz - before_y(hz)) - (hy - before_row(hy, row_y)))
    ey = keep * e[1, x, here, :] + drive * ((hx - before_row(hx, row_x)) - (hz - past_z))
    ez = keep * e[2, x, here, :] + drive * ((hy - past_y) - (hx - before_y(hx)))
    e[0, x, here, :] = ex
    e[1, x, here, :] = ey
    e[2, x, here, :] = ez
    heat = sigma[x, here, :] * (ex * ex + ey * ey + ez * ez)
    power[x, here, :] = heat if first else power[x, here, :] + heat
    return ey, ez


def h_edge_kernel(e, col, hgt, e_rows, rows_old, h_old, h, to_col, to_hgt):
    nx, nz = e.shape[1:3]
    for z in range(0, nz, ROWS):
        hy, hz = h_tile(e, h, col, hgt, nx - 1, z)
        to_col[0, z : z + ROWS, :] = hy
        to_col[1, z : z + ROWS, :] = hz
    for x in range(0, nx, ROWS):
        here = slice(x, x + ROWS)
        ex, ey, ez = (e_rows[comp, here, :] for comp in range(3))
        row = e_rows[2, x + ROWS : x + ROWS + 1, :] if x + ROWS < nx else col[1, nz - 1 : nz, :]
        to_hgt[0, here, :] = rows_old[0, here, :] - COURANT * ((after_y(ez) - ez) - (hgt[1, here, :] - ey))
        to_hgt[1, here, :] = rows_old[1, here, :] - COURANT * ((hgt[0, here, :] - ex) - (after_row(ez, row) - ez))


def h_rest_kernel(e, hgt, h_old, h, rows):
    nx, nz = e.shape[1:3]

    def keep(x):
        for comp in range(3):
            rows[comp, pl.ds(x, 1), :] = h[comp, x, 0:1, :]

    def plane(x):
        for z in range(0, nz, ROWS):
            h_tile(e, h, None, hgt, x, z)
        keep(x)

    over(0, nx - 1, plane)
    keep(nx - 1)


def e_edge_kernel(first, h, ca, cb, sigma, col, hgt, media_rows, h_rows, rows_old, *refs):
    e, power, to_col, to_hgt = refs[-4:]
    nx, nz = e.shape[1:3]
    for z in range(0, nz, ROWS):
        ey, ez = e_tile(first, h, e, power, ca, cb, sigma, col, hgt, 0, z)
        to_col[0, z : z + ROWS, :] = ey
        to_col[1, z : z + ROWS, :] = ez
    for x in range(0, nx, ROWS):
        here = slice(x, x + ROWS)
        hx, hy, hz = (h_rows[comp, here, :] for comp in range(3))
        row = h_rows[2, x - 1 : x, :] if x > 0 else col[1, 0:1, :]
        keep = media_rows[0, here, :]
        drive = media_rows[1, here, :]
        to_hgt[0, here, :] = keep * rows_old[0, here, :] + drive * ((hz - before_y(hz)) - (hy - hgt[1, here, :]))
        to_hgt[1, here, :] = keep * rows_old[1, here, :] + drive * ((hx - hgt[0, here, :]) - (hz - before_row(hz, row)))


def e_rest_kernel(first, h, ca, cb, sigma, hgt, e_old, power_old, e, power, rows):
    nx, nz = e.shape[1:3]

    def keep(x):
        for comp in range(3):
            rows[comp, pl.ds(x, 1), :] = e[comp, x, nz - 1 : nz, :]

    def plane(x):
        for z in range(0, nz, ROWS):
            e_tile(first, h, e, power, ca, cb, sigma, None, hgt, x, z)
        keep(x)

    keep(0)
    over(1, nx, plane)


def e_last_kernel(first, h, ca, cb, sigma, col, hgt, e_old, power_old, e, power):
    nx, nz = e.shape[1:3]

    def plane(x):
        for z in range(0, nz, ROWS):
            e_tile(first, h, e, power, ca, cb, sigma, col if isinstance(x, int) else None, hgt, x, z)

    plane(0)
    over(1, nx, plane)


def places_kernel(n_col, n_hgt, near, far_cap, extra, my_col, owner, node, place, near_nodes, far_nodes):
    n_dev = n_col * n_hgt
    count = owner.shape[1]
    width = 256
    rows = lax.broadcasted_iota(jnp.int32, (n_dev, width), 0)
    before = lax.broadcasted_iota(jnp.int32, (width, width), 0)
    after = lax.broadcasted_iota(jnp.int32, (width, width), 1)
    upper = jnp.where(before <= after, 1.0, 0.0).astype(jnp.bfloat16)
    room_for = 2 * LANES
    near_rows = n_col * near + extra
    far_rows = n_hgt * far_cap + extra
    room = lax.broadcasted_iota(jnp.int32, (room_for, width), 0)
    total = jnp.zeros((n_dev, 1), F32)
    parts_of = jnp.zeros((2 * n_dev, room_for), F32)
    nt = (((1,), (1,)), ((), ()))
    for start in range(0, count, width):
        own = owner[:, start : start + width]
        own_col = lax.div(own, n_hgt)
        own_hgt = lax.rem(own, n_hgt)
        hit = jnp.where(rows == own, 1.0, 0.0)
        running = total + jnp.dot(hit.astype(jnp.bfloat16), upper, preferred_element_type=F32)
        total = running[:, width - 1 : width]
        rank = jnp.sum(hit * running, axis=0, keepdims=True).astype(jnp.int32) - 1
        place[:, start : start + width] = jnp.where(
            rank < near,
            own_hgt * near_rows + lax.rem(own_col - my_col[0] + n_col, n_col) * near + rank,
            n_hgt * near_rows + own_col * far_rows + own_hgt * far_cap + (rank - near),
        )
        rank = jnp.where(rank < near, rank, rank + (LANES - near))
        number = node[:, start : start + width]
        upper_part = lax.div(number, 16)
        lower_part = number - 16 * upper_part
        seat = jnp.where(room == rank, 1.0, 0.0).astype(jnp.bfloat16)
        both = jnp.concatenate([hit * upper_part.astype(F32), hit * lower_part.astype(F32)], 0)
        parts_of = parts_of + lax.dot_general(both.astype(jnp.bfloat16), seat, nt, preferred_element_type=F32)
    seat_of = lax.broadcasted_iota(jnp.int32, (n_dev, LANES), 1).astype(F32)
    table = 16.0 * parts_of[:n_dev] + parts_of[n_dev:]
    near_taken = (seat_of < near) & (seat_of < total)
    far_taken = (seat_of < far_cap) & (seat_of + near < total)
    near_table = jnp.where(near_taken, table[:, :LANES], -1.0)
    far_table = jnp.where(far_taken, table[:, LANES:], -1.0)
    near_nodes[...] = jnp.full(near_nodes.shape, -1.0, F32)
    far_nodes[...] = jnp.full(far_nodes.shape, -1.0, F32)
    for group in range(n_col):
        mine = slice(group * n_hgt, (group + 1) * n_hgt)
        far_nodes[group, 0:n_hgt, :] = far_table[mine, :]
        slot = lax.rem(group - my_col[0] + n_col, n_col)
        for part in range(n_hgt):
            near_nodes[part, pl.ds(slot, 1), :] = near_table[group * n_hgt + part : group * n_hgt + part + 1, :]


def pack_kernel(place, power, near_nodes, far_nodes, e, h, near_out, far_out, e_out, h_out, flat, sems):
    nx, nz, ny = power.shape
    e_copy = pltpu.make_async_copy(e, e_out, sems.at[0])
    h_copy = pltpu.make_async_copy(h, h_out, sems.at[1])
    e_copy.start()
    h_copy.start()
    per_row = ny // PTS
    begin = 0
    chunk = 8 * ROWS

    def clear(i, carry):
        flat[pl.ds(pl.multiple_of(i * chunk, chunk), chunk), :] = jnp.zeros((chunk, PTS), F32)
        return carry

    lax.fori_loop(0, flat.shape[0] // chunk, clear, 0)
    for at in range(flat.shape[0] // chunk * chunk, flat.shape[0], ROWS):
        flat[at : at + ROWS, :] = jnp.zeros((ROWS, PTS), F32)
    for table in (near_nodes, far_nodes):
        groups, extra, _ = table.shape
        rows = (near_out if table is near_nodes else far_out).shape[1]
        for group in range(groups):
            begin += rows
            flat[begin - extra : begin, :] = table[group]

    def plane(x, carry):
        for z in range(nz):
            for k in range(per_row):
                spot = place[x * (nz * per_row) + z * per_row + k]
                flat[pl.ds(spot, 1), :] = power[x, z : z + 1, k * PTS : (k + 1) * PTS]
        return carry

    lax.fori_loop(0, nx, plane, 0)
    begin = 0
    copies = []
    for out in (near_out, far_out):
        groups, rows, _ = out.shape
        first = 0 if out is near_out else near_out.shape[0] * near_out.shape[1]
        for group in range(groups):
            copies.append(
                pltpu.make_async_copy(flat.at[pl.ds(first + group * rows, rows)], out.at[group], sems.at[2 + len(copies)])
            )
    for copy in copies:
        copy.start()
    for copy in copies:
        copy.wait()
    e_copy.wait()
    h_copy.wait()


def summed(blocks, first, cap, node_row, chosen, split, node_count):
    ids = lax.broadcasted_iota(jnp.int32, (node_count, LANES), 0).astype(F32)
    n_from, _, pts = blocks.shape
    many = len(first)
    for source in range(n_from):
        for i in range(many):
            seat = (source * many + i) * LANES
            row = node_row[i]
            hit = ids == blocks[source, row : row + 1, :]
            chosen[:, seat : seat + LANES] = jnp.where(hit, 1.0, 0.0).astype(jnp.bfloat16)
            values = blocks[source, first[i] : first[i] + cap, :]
            high = values.astype(jnp.bfloat16)
            split[seat : seat + cap, 0:pts] = high
            split[seat : seat + cap, pts : 2 * pts] = (values - high.astype(F32)).astype(jnp.bfloat16)
    both = jnp.dot(chosen[...], split[...], preferred_element_type=F32)
    return both[:, 0:pts] + both[:, pts : 2 * pts]


def collect_kernel(cap, blocks, *refs):
    *outs, chosen, split = refs
    if cap < LANES:
        split[...] = jnp.zeros(split.shape, split.dtype)
    for part, out in enumerate(outs):
        out[...] = summed(blocks, [part * cap], cap, [len(outs) * cap + part], chosen, split, out.shape[0])


def regroup_kernel(cap, blocks, order, out):
    n_from = blocks.shape[0]
    n_part = out.shape[0]
    out[:, n_from * cap :, :] = jnp.full((n_part, out.shape[1] - n_from * cap, PTS), -1.0, F32)
    for source in range(n_from):
        for part in range(n_part):
            out[part, source * cap : (source + 1) * cap, :] = blocks[source, part * cap : (part + 1) * cap, :]
            row = n_part * cap + part
            out[part, n_from * cap + source : n_from * cap + source + 1, :] = blocks[source, row : row + 1, :]


def collect_far_kernel(cap, n_mid, blocks, out, chosen, split):
    split[...] = jnp.zeros(split.shape, split.dtype)
    first = [i * cap for i in range(n_mid)]
    node_row = [n_mid * cap + i for i in range(n_mid)]
    out[...] = summed(blocks, first, cap, node_row, chosen, split, out.shape[0])


def finish_kernel(enthalpy, *refs):
    *parts, out = refs
    heat = parts[0][...]
    for part in parts[1:]:
        heat = heat + part[...]
    content = enthalpy[...] + (0.25 / STEPS) * heat
    out[...] = jnp.where(content < 0.0, content / 2.0, jnp.where(content > 1.0, (content - 1.0) / 3.0, 0.0))


def shifted(block, d_col, d_hgt):
    n_col = lax.axis_size("col")
    n_hgt = lax.axis_size("hgt")
    route = [
        (c * n_hgt + h, (c + d_col) * n_hgt + h + d_hgt)
        for c in range(n_col)
        for h in range(n_hgt)
        if 0 <= c + d_col < n_col and 0 <= h + d_hgt < n_hgt
    ]
    return lax.ppermute(block, ("col", "hgt"), route)


def per_device(
    efield_lattice_vector,
    hfield_lattice_vector,
    cell_temp,
    region_tags,
    block_owner,
    block_node,
    node_enthalpy,
):
    nx, nz, ny = cell_temp.shape
    n_col = lax.axis_size("col")
    n_hgt = lax.axis_size("hgt")
    n_dev = n_col * n_hgt
    count = nx * nz * ny // PTS
    cap = 2 * count // n_dev
    node_count = node_enthalpy.shape[0]
    cells = nx * nz * ny
    sem = pltpu.SemaphoreType.DMA

    def kernel(body, outs, ins, args, name, work, aliases=None, scratch=()):
        return pl.pallas_call(
            body,
            out_shape=outs,
            in_specs=ins,
            out_specs=jax.tree.map(lambda out: WHOLE, outs),
            input_output_aliases=aliases or {},
            scratch_shapes=scratch,
            compiler_params=params(VMEM_MIB),
            cost_estimate=cost(work * cells, work * cells),
            name=name,
        )(*args)

    e_start = far(efield_lattice_vector)
    h_start = far(hfield_lattice_vector)
    my_col = lax.axis_index("col").astype(jnp.int32).reshape(1)
    owners = block_owner.reshape(1, count)
    nodes = block_node.reshape(1, count)
    field = vmem(3, nx, nz, ny)
    whole = vmem(nx, nz, ny)
    planes = vmem(2, nz, ny)
    two_rows = vmem(2, nx, ny)
    three_rows = vmem(3, nx, ny)

    to_col, e_low = kernel(
        edge_kernel, (planes, two_rows), [FAR], [e_start], "edge", 4, scratch=[vmem(2, nx, ROWS, ny), sem((2,))]
    )
    col = shifted(to_col, -1, 0)
    hgt = shifted(e_low, 0, -1)
    ca, cb, sigma, e, h, media_rows, e_rows, h_high = kernel(
        load_kernel,
        (whole, whole, whole, field, field, two_rows, three_rows, two_rows),
        [FAR] * 4 + [WHOLE],
        [far(cell_temp), far(region_tags), e_start, h_start, owners + nodes + my_col],
        "load",
        60,
        scratch=[vmem(nx, nz, ny), pltpu.VMEM((nx, nz, ny), jnp.int32), sem((3, 4))],
    )
    near = 2 * cap // 3 // ROWS * ROWS
    far_cap = -(-(cap - near) // ROWS) * ROWS
    extra = -(-max(n_col, n_hgt) // ROWS) * ROWS
    place, near_nodes, far_nodes = kernel(
        functools.partial(places_kernel, n_col, n_hgt, near, far_cap, extra),
        (jax.ShapeDtypeStruct((1, count), jnp.int32), vmem(n_hgt, extra, PTS), vmem(n_col, extra, PTS)),
        [SCALARS, WHOLE, WHOLE],
        [my_col, owners, nodes],
        "places",
        8,
    )
    power = None
    for step in range(STEPS):
        first = step == 0
        h, to_col, h_high = kernel(
            h_edge_kernel,
            (field, planes, two_rows),
            [WHOLE] * 6,
            [e, col, hgt, e_rows, h_high, h],
            f"h_edge_{step}",
            4,
            {5: 0},
        )
        e_hgt = hgt
        col = shifted(to_col, 1, 0)
        hgt = shifted(h_high, 0, 1)
        h, h_rows = kernel(
            h_rest_kernel, (field, three_rows), [WHOLE] * 3, [e, e_hgt, h], f"h_rest_{step}", 40, {2: 0}
        )
        media = [h, ca, cb, sigma]
        if step == STEPS - 1:
            e, power = kernel(
                functools.partial(e_last_kernel, first),
                (field, whole),
                [WHOLE] * 8,
                media + [col, hgt, e, power],
                f"e_last_{step}",
                50,
                {6: 0, 7: 1},
            )
            break
        args = media + [col, hgt, media_rows, h_rows, e_low, e] + ([] if first else [power])
        e, power, to_col, e_low = kernel(
            functools.partial(e_edge_kernel, first),
            (field, whole, planes, two_rows),
            [WHOLE] * len(args),
            args,
            f"e_edge_{step}",
            5,
            {9: 0} if first else {9: 0, 10: 1},
        )
        h_hgt = hgt
        col = shifted(to_col, -1, 0)
        hgt = shifted(e_low, 0, -1)
        e, power, e_rows = kernel(
            functools.partial(e_rest_kernel, first),
            (field, whole, three_rows),
            [WHOLE] * 7,
            media + [h_hgt, e, power],
            f"e_rest_{step}",
            45,
            {5: 0, 6: 1},
        )

    near_rows = n_col * near + extra
    far_rows = n_hgt * far_cap + extra
    near_send, far_send, e_out, h_out = pl.pallas_call(
        pack_kernel,
        out_shape=(
            pltpu.HBM((n_hgt, near_rows, PTS), F32),
            pltpu.HBM((n_col, far_rows, PTS), F32),
            pltpu.HBM((3, nx, nz, ny), F32),
            pltpu.HBM((3, nx, nz, ny), F32),
        ),
        in_specs=[SCALARS] + [WHOLE] * 5,
        out_specs=(FAR, FAR, FAR, FAR),
        scratch_shapes=[vmem(n_hgt * near_rows + n_col * far_rows, PTS), sem((2 + n_hgt + n_col,))],
        compiler_params=params(VMEM_MIB),
        cost_estimate=cost(cells, cells * 36),
        name="pack",
    )(place.reshape(count), power, near_nodes, far_nodes, e, h)

    def swap(x, axis):
        return lax.all_to_all(x, axis, split_axis=0, concat_axis=0, tiled=True)

    def one_hot_space(sources):
        return [
            pltpu.VMEM((node_count, sources * LANES), jnp.bfloat16),
            pltpu.VMEM((sources * LANES, 2 * PTS), jnp.bfloat16),
        ]

    near_blocks = swap(near_send, "hgt")
    far_blocks = swap(far_send, "col")
    node_rows = jax.ShapeDtypeStruct((node_count, PTS), F32)
    partial = kernel(
        functools.partial(collect_kernel, near),
        (node_rows,) * n_col,
        [WHOLE],
        [near_blocks],
        "collect",
        100,
        scratch=one_hot_space(n_hgt),
    )
    parts = [partial[0]]
    for turn in range(1, n_col):
        route = [(c, (c + turn) % n_col) for c in range(n_col)]
        parts.append(lax.ppermute(partial[turn], "col", route))
    far_again = kernel(
        functools.partial(regroup_kernel, far_cap),
        jax.ShapeDtypeStruct((n_hgt, n_col * far_cap + ROWS, PTS), F32),
        [WHOLE, FAR],
        [far_blocks, partial[0]],
        "regroup",
        0,
    )
    far_final = swap(far_again, "hgt")
    far_heat = kernel(
        functools.partial(collect_far_kernel, far_cap, n_col),
        node_rows,
        [WHOLE],
        [far_final],
        "collect_far",
        10,
        scratch=one_hot_space(n_dev),
    )
    node_temp = kernel(
        finish_kernel,
        node_rows,
        [WHOLE] * (2 + n_col),
        [node_enthalpy, *parts, far_heat],
        "finish",
        1,
    )
    return e_out, h_out, node_temp


def solution(mesh):
    placed = (
        P(None, "col", "hgt", None),
        P(None, "col", "hgt", None),
        P("col", "hgt", None),
        P("col", "hgt", None),
        P("col", "hgt", None, None, None, None),
        P("col", "hgt", None, None, None),
        P(("col", "hgt"), None),
    )
    return jax.shard_map(
        per_device,
        mesh=mesh,
        in_specs=placed,
        out_specs=(
            P(None, "col", "hgt", None),
            P(None, "col", "hgt", None),
            P(("col", "hgt"), None),
        ),
        check_vma=False,
    )
```

```python
import functools

import jax
import jax.numpy as jnp
from jax import lax
from jax.experimental import pallas as pl
from jax.experimental.pallas import tpu as pltpu
from jax.sharding import PartitionSpec as P

PTS = 128
STEPS = 4
COURANT = 0.55
LANES = 128
ROWS = 8
F32 = jnp.float32
VMEM_MIB = 20

WHOLE = pl.BlockSpec(memory_space=pltpu.VMEM)
SCALARS = pl.BlockSpec(memory_space=pltpu.SMEM)
FAR = pl.BlockSpec(memory_space=pltpu.HBM)


def vmem(*shape):
    return pltpu.VMEM(shape, F32)


def far(x):
    return pltpu.with_memory_space_constraint(x, pltpu.HBM)


def params(mib):
    return pltpu.CompilerParams(vmem_limit_bytes=mib << 20)


def cost(flops, moved):
    return pl.CostEstimate(flops=flops, bytes_accessed=moved, transcendentals=0)


def after_y(f):
    lane = lax.broadcasted_iota(jnp.int32, (ROWS, LANES), 1)
    n = f.shape[1] // LANES
    turned = [pltpu.roll(f[:, k * LANES : (k + 1) * LANES], LANES - 1, 1) for k in range(n)]
    turned.append(jnp.zeros((ROWS, LANES), F32))
    return jnp.concatenate([jnp.where(lane < LANES - 1, turned[k], turned[k + 1]) for k in range(n)], 1)


def before_y(f):
    lane = lax.broadcasted_iota(jnp.int32, (ROWS, LANES), 1)
    n = f.shape[1] // LANES
    turned = [jnp.zeros((ROWS, LANES), F32)]
    turned += [pltpu.roll(f[:, k * LANES : (k + 1) * LANES], 1, 1) for k in range(n)]
    return jnp.concatenate([jnp.where(lane > 0, turned[k + 1], turned[k]) for k in range(n)], 1)


def after_row(f, row):
    place = lax.broadcasted_iota(jnp.int32, f.shape, 0)
    return jnp.where(place < ROWS - 1, pltpu.roll(f, ROWS - 1, 0), jnp.broadcast_to(row, f.shape))


def before_row(f, row):
    place = lax.broadcasted_iota(jnp.int32, f.shape, 0)
    return jnp.where(place > 0, pltpu.roll(f, 1, 0), jnp.broadcast_to(row, f.shape))


def edge_kernel(e, to_col, to_hgt, low, sems):
    nx = e.shape[1]
    col_copy = pltpu.make_async_copy(e.at[pl.ds(1, 2), 0], to_col, sems.at[0])
    low_copy = pltpu.make_async_copy(e.at[pl.ds(0, 2), :, pl.ds(0, ROWS)], low, sems.at[1])
    low_copy.start()
    col_copy.start()
    low_copy.wait()
    for x in range(nx):
        for comp in range(2):
            to_hgt[comp, x : x + 1, :] = low[comp, x, 0:1, :]
    col_copy.wait()


def load_kernel(
    temp_far, tags_far, e_far, h_far, order, ca, cb, sigma_out, e, h, media_rows, e_rows, h_rows, temp, tags, sems
):
    nx, nz, _ = temp.shape
    parts = 4
    size = nx // parts
    copies = []
    for part in range(parts):
        here = pl.ds(part * size, size)
        copies.append(pltpu.make_async_copy(temp_far.at[here], temp.at[here], sems.at[0, part]))
        copies.append(pltpu.make_async_copy(tags_far.at[here], tags.at[here], sems.at[1, part]))
    e_copy = pltpu.make_async_copy(e_far, e, sems.at[2, 0])
    h_copy = pltpu.make_async_copy(h_far, h, sems.at[2, 1])
    for copy in copies:
        copy.start()
    e_copy.start()
    h_copy.start()

    def plane(x, carry):
        for z in range(0, nz, ROWS):
            tag = tags[x, z : z + ROWS, :]
            lean = tag == 0
            fat = tag == 1
            frac = 1.0 / (1.0 + jnp.exp(-2.0 * temp[x, z : z + ROWS, :]))
            eps_low = jnp.where(lean, 4.0, jnp.where(fat, 2.5, 5.0))
            eps_rise = jnp.where(lean, 46.0, jnp.where(fat, 3.5, 5.0))
            sig_low = jnp.where(lean, 0.2, jnp.where(fat, 0.05, 0.1))
            sig_rise = jnp.where(lean, 7.8, jnp.where(fat, 0.35, 0.9))
            eps = eps_low + eps_rise * frac
            sigma = sig_low + sig_rise * frac
            half = (0.5 * COURANT) * sigma
            inverse = 1.0 / (eps + half)
            ca[x, z : z + ROWS, :] = (eps - half) * inverse
            cb[x, z : z + ROWS, :] = COURANT * inverse
            sigma_out[x, z : z + ROWS, :] = sigma
        media_rows[0, pl.ds(x, 1), :] = ca[x, 0:1, :]
        media_rows[1, pl.ds(x, 1), :] = cb[x, 0:1, :]
        return carry

    for part in range(parts):
        copies[2 * part].wait()
        copies[2 * part + 1].wait()
        lax.fori_loop(part * size, (part + 1) * size, plane, 0)
    e_copy.wait()
    h_copy.wait()

    def rows(x, carry):
        for comp in range(3):
            e_rows[comp, pl.ds(x, 1), :] = e[comp, x, nz - 1 : nz, :]
        for comp in range(2):
            h_rows[comp, pl.ds(x, 1), :] = h[comp, x, nz - 1 : nz, :]
        return carry

    lax.fori_loop(0, nx, rows, 0)


def over(first, stop, body):
    if stop - first == 1:
        body(first)
    else:

        def step(x, carry):
            body(x)
            return carry

        lax.fori_loop(first, stop, step, 0)


def h_tile(e, h, col, hgt, x, z):
    nz = e.shape[2]
    here = slice(z, z + ROWS)
    ex, ey, ez = (e[comp, x, here, :] for comp in range(3))
    if z + ROWS < nz:
        row_x, row_y = (e[comp, x, z + ROWS : z + ROWS + 1, :] for comp in range(2))
    else:
        row_x, row_y = (hgt[comp, pl.ds(x, 1), :] for comp in range(2))
    if col is None:
        next_y, next_z = (e[comp, x + 1, here, :] for comp in (1, 2))
    else:
        next_y, next_z = (col[comp, here, :] for comp in range(2))
    h[0, x, here, :] = h[0, x, here, :] - COURANT * ((after_y(ez) - ez) - (after_row(ey, row_y) - ey))
    hy = h[1, x, here, :] - COURANT * ((after_row(ex, row_x) - ex) - (next_z - ez))
    hz = h[2, x, here, :] - COURANT * ((next_y - ey) - (after_y(ex) - ex))
    h[1, x, here, :] = hy
    h[2, x, here, :] = hz
    return hy, hz


def e_tile(first, h, e, power, ca, cb, sigma, col, hgt, x, z):
    here = slice(z, z + ROWS)
    hx, hy, hz = (h[comp, x, here, :] for comp in range(3))
    if z > 0:
        row_x, row_y = (h[comp, x, z - 1 : z, :] for comp in range(2))
    else:
        row_x, row_y = (hgt[comp, pl.ds(x, 1), :] for comp in range(2))
    if col is None:
        past_y, past_z = (h[comp, x - 1, here, :] for comp in (1, 2))
    else:
        past_y, past_z = (col[comp, here, :] for comp in range(2))
    keep = ca[x, here, :]
    drive = cb[x, here, :]
    ex = keep * e[0, x, here, :] + drive * ((hz - before_y(hz)) - (hy - before_row(hy, row_y)))
    ey = keep * e[1, x, here, :] + drive * ((hx - before_row(hx, row_x)) - (hz - past_z))
    ez = keep * e[2, x, here, :] + drive * ((hy - past_y) - (hx - before_y(hx)))
    e[0, x, here, :] = ex
    e[1, x, here, :] = ey
    e[2, x, here, :] = ez
    heat = sigma[x, here, :] * (ex * ex + ey * ey + ez * ez)
    power[x, here, :] = heat if first else power[x, here, :] + heat
    return ey, ez


def h_edge_kernel(e, col, hgt, e_rows, rows_old, h_old, h, to_col, to_hgt):
    nx, nz = e.shape[1:3]
    for z in range(0, nz, ROWS):
        hy, hz = h_tile(e, h, col, hgt, nx - 1, z)
        to_col[0, z : z + ROWS, :] = hy
        to_col[1, z : z + ROWS, :] = hz
    for x in range(0, nx, ROWS):
        here = slice(x, x + ROWS)
        ex, ey, ez = (e_rows[comp, here, :] for comp in range(3))
        row = e_rows[2, x + ROWS : x + ROWS + 1, :] if x + ROWS < nx else col[1, nz - 1 : nz, :]
        to_hgt[0, here, :] = rows_old[0, here, :] - COURANT * ((after_y(ez) - ez) - (hgt[1, here, :] - ey))
        to_hgt[1, here, :] = rows_old[1, here, :] - COURANT * ((hgt[0, here, :] - ex) - (after_row(ez, row) - ez))


def h_rest_kernel(e, hgt, h_old, h, rows):
    nx, nz = e.shape[1:3]

    def keep(x):
        for comp in range(3):
            rows[comp, pl.ds(x, 1), :] = h[comp, x, 0:1, :]

    def plane(x):
        for z in range(0, nz, ROWS):
            h_tile(e, h, None, hgt, x, z)
        keep(x)

    over(0, nx - 1, plane)
    keep(nx - 1)


def e_edge_kernel(first, h, ca, cb, sigma, col, hgt, media_rows, h_rows, rows_old, *refs):
    e, power, to_col, to_hgt = refs[-4:]
    nx, nz = e.shape[1:3]
    for z in range(0, nz, ROWS):
        ey, ez = e_tile(first, h, e, power, ca, cb, sigma, col, hgt, 0, z)
        to_col[0, z : z + ROWS, :] = ey
        to_col[1, z : z + ROWS, :] = ez
    for x in range(0, nx, ROWS):
        here = slice(x, x + ROWS)
        hx, hy, hz = (h_rows[comp, here, :] for comp in range(3))
        row = h_rows[2, x - 1 : x, :] if x > 0 else col[1, 0:1, :]
        keep = media_rows[0, here, :]
        drive = media_rows[1, here, :]
        to_hgt[0, here, :] = keep * rows_old[0, here, :] + drive * ((hz - before_y(hz)) - (hy - hgt[1, here, :]))
        to_hgt[1, here, :] = keep * rows_old[1, here, :] + drive * ((hx - hgt[0, here, :]) - (hz - before_row(hz, row)))


def e_rest_kernel(first, h, ca, cb, sigma, hgt, e_old, power_old, e, power, rows):
    nx, nz = e.shape[1:3]

    def keep(x):
        for comp in range(3):
            rows[comp, pl.ds(x, 1), :] = e[comp, x, nz - 1 : nz, :]

    def plane(x):
        for z in range(0, nz, ROWS):
            e_tile(first, h, e, power, ca, cb, sigma, None, hgt, x, z)
        keep(x)

    keep(0)
    over(1, nx, plane)


def e_last_kernel(first, h, ca, cb, sigma, col, hgt, e_old, power_old, e, power):
    nx, nz = e.shape[1:3]

    def plane(x):
        for z in range(0, nz, ROWS):
            e_tile(first, h, e, power, ca, cb, sigma, col if isinstance(x, int) else None, hgt, x, z)

    plane(0)
    over(1, nx, plane)


def places_kernel(n_col, n_hgt, cap, my_col, owner, node, place, mine_nodes, pair_nodes, other_nodes):
    n_dev = n_col * n_hgt
    count = owner.shape[1]
    width = 256
    rows = lax.broadcasted_iota(jnp.int32, (n_dev, width), 0)
    before = lax.broadcasted_iota(jnp.int32, (width, width), 0)
    after = lax.broadcasted_iota(jnp.int32, (width, width), 1)
    upper = jnp.where(before <= after, 1.0, 0.0).astype(jnp.bfloat16)
    per = -(-cap // LANES)
    room_for = per * LANES
    room = lax.broadcasted_iota(jnp.int32, (room_for, width), 0)
    total = jnp.zeros((n_dev, 1), F32)
    parts_of = jnp.zeros((2 * n_dev, room_for), F32)
    nt = (((1,), (1,)), ((), ()))
    begins, heights = starts_of(n_col, n_hgt, cap)
    for start in range(0, count, width):
        own = owner[:, start : start + width]
        hit = jnp.where(rows == own, 1.0, 0.0)
        running = total + jnp.dot(hit.astype(jnp.bfloat16), upper, preferred_element_type=F32)
        total = running[:, width - 1 : width]
        rank = jnp.sum(hit * running, axis=0, keepdims=True).astype(jnp.int32) - 1
        turn = lax.bitwise_xor(lax.div(own, n_hgt), my_col[0])
        own_hgt = lax.rem(own, n_hgt)
        begin = jnp.where(
            turn == 0,
            begins[0] + own_hgt * heights[0],
            jnp.where(
                turn == 1,
                begins[1] + own_hgt * heights[1],
                begins[2] + own_hgt * heights[2] + (turn - 2) * cap,
            ),
        )
        place[:, start : start + width] = begin + rank
        number = node[:, start : start + width]
        upper_part = lax.div(number, 16)
        lower_part = number - 16 * upper_part
        seat = jnp.where(room == rank, 1.0, 0.0).astype(jnp.bfloat16)
        both = jnp.concatenate([hit * upper_part.astype(F32), hit * lower_part.astype(F32)], 0)
        parts_of = parts_of + lax.dot_general(both.astype(jnp.bfloat16), seat, nt, preferred_element_type=F32)
    taken = lax.broadcasted_iota(jnp.int32, (n_dev, room_for), 1).astype(F32) < total
    table = jnp.where(taken, 16.0 * parts_of[:n_dev] + parts_of[n_dev:], -1.0)
    for ref in (mine_nodes, pair_nodes, other_nodes):
        ref[...] = jnp.full(ref.shape, -1.0, F32)
    for group in range(n_col):
        turn = lax.bitwise_xor(jnp.int32(group), my_col[0])
        for part in range(n_hgt):
            at = group * n_hgt + part
            for piece in range(per):
                row = table[at : at + 1, piece * LANES : (piece + 1) * LANES]

                @pl.when(turn == 0)
                def _():
                    mine_nodes[part, piece : piece + 1, :] = row

                @pl.when(turn == 1)
                def _():
                    pair_nodes[part, piece : piece + 1, :] = row

                @pl.when(turn > 1)
                def _():
                    other_nodes[part, pl.ds((turn - 2) * per + piece, 1), :] = row


def table_rows(parts, cap):
    return -(-parts * -(-cap // LANES) // ROWS) * ROWS


def starts_of(n_col, n_hgt, cap):
    one = cap + table_rows(1, cap)
    heights = [one, one, (n_col - 2) * cap + table_rows(n_col - 2, cap)]
    return [0, n_hgt * heights[0], n_hgt * (heights[0] + heights[1])], heights


def pack_kernel(cap, place, power, mine_nodes, pair_nodes, other_nodes, e, h, mine, pair, other, e_out, h_out, flat, sems):
    nx, nz, ny = power.shape
    e_copy = pltpu.make_async_copy(e, e_out, sems.at[0])
    h_copy = pltpu.make_async_copy(h, h_out, sems.at[1])
    e_copy.start()
    h_copy.start()
    per_row = ny // PTS
    outs = (mine, pair, other)
    chunk = 8 * ROWS

    def clear(i, carry):
        flat[pl.ds(pl.multiple_of(i * chunk, chunk), chunk), :] = jnp.zeros((chunk, PTS), F32)
        return carry

    lax.fori_loop(0, flat.shape[0] // chunk, clear, 0)
    for at in range(flat.shape[0] // chunk * chunk, flat.shape[0], ROWS):
        flat[at : at + ROWS, :] = jnp.zeros((ROWS, PTS), F32)
    begin = 0
    begins = []
    heights = [cap + mine_nodes.shape[1], pair.shape[1], other.shape[1]]
    for out, rows, table in zip(outs, heights, (mine_nodes, pair_nodes, other_nodes)):
        groups = out.shape[0]
        begins.append(begin)
        for group in range(groups):
            begin += rows
            flat[begin - table.shape[1] : begin, :] = table[group]

    def plane(x, carry):
        for z in range(nz):
            for k in range(per_row):
                spot = place[x * (nz * per_row) + z * per_row + k]
                flat[pl.ds(spot, 1), :] = power[x, z : z + 1, k * PTS : (k + 1) * PTS]
        return carry

    lax.fori_loop(0, nx, plane, 0)
    copies = []
    for out, rows, first in zip(outs, heights, begins):
        for group in range(out.shape[0]):
            source = flat.at[pl.ds(first + group * rows, rows)]
            target = out.at[group, pl.ds(0, rows)]
            copies.append(pltpu.make_async_copy(source, target, sems.at[2 + len(copies)]))
    for copy in copies:
        copy.start()
    for copy in copies:
        copy.wait()
    e_copy.wait()
    h_copy.wait()


def summed(blocks, first, cap, node_row, chosen, split, node_count):
    ids = lax.broadcasted_iota(jnp.int32, (node_count, LANES), 0).astype(F32)
    n_from, _, pts = blocks.shape
    per = -(-cap // LANES)
    many = len(first)
    for source in range(n_from):
        for i in range(many):
            seat = (source * many + i) * per * LANES
            for piece in range(per):
                row = node_row[i] + piece
                lanes = slice(seat + piece * LANES, seat + (piece + 1) * LANES)
                hit = ids == blocks[source, row : row + 1, :]
                chosen[:, lanes] = jnp.where(hit, 1.0, 0.0).astype(jnp.bfloat16)
            values = blocks[source, first[i] : first[i] + cap, :]
            high = values.astype(jnp.bfloat16)
            split[seat : seat + cap, 0:pts] = high
            split[seat : seat + cap, pts : 2 * pts] = (values - high.astype(F32)).astype(jnp.bfloat16)
    both = jnp.dot(chosen[...], split[...], preferred_element_type=F32)
    return both[:, 0:pts] + both[:, pts : 2 * pts]


def collect_kernel(cap, blocks, *refs):
    *outs, chosen, split = refs
    per = -(-cap // LANES)
    split[...] = jnp.zeros(split.shape, split.dtype)
    for part, out in enumerate(outs):
        out[...] = summed(blocks, [part * cap], cap, [len(outs) * cap + part * per], chosen, split, out.shape[0])


def merge_kernel(pair, order, mine_old, mine, sems):
    rows = pair.shape[1]
    copies = [
        pltpu.make_async_copy(pair.at[group], mine.at[group, pl.ds(rows, rows)], sems.at[group])
        for group in range(mine.shape[0])
    ]
    for copy in copies:
        copy.start()
    for copy in copies:
        copy.wait()


def collect_mine_kernel(cap, blocks, out, chosen, split):
    half = blocks.shape[1] // 2
    split[...] = jnp.zeros(split.shape, split.dtype)
    out[...] = summed(blocks, [0, half], cap, [cap, half + cap], chosen, split, out.shape[0])


def finish_kernel(enthalpy, *refs):
    *parts, out = refs
    heat = parts[0][...]
    for part in parts[1:]:
        heat = heat + part[...]
    content = enthalpy[...] + (0.25 / STEPS) * heat
    out[...] = jnp.where(content < 0.0, content / 2.0, jnp.where(content > 1.0, (content - 1.0) / 3.0, 0.0))


def shifted(block, d_col, d_hgt):
    n_col = lax.axis_size("col")
    n_hgt = lax.axis_size("hgt")
    route = [
        (c * n_hgt + h, (c + d_col) * n_hgt + h + d_hgt)
        for c in range(n_col)
        for h in range(n_hgt)
        if 0 <= c + d_col < n_col and 0 <= h + d_hgt < n_hgt
    ]
    return lax.ppermute(block, ("col", "hgt"), route)


def per_device(
    efield_lattice_vector,
    hfield_lattice_vector,
    cell_temp,
    region_tags,
    block_owner,
    block_node,
    node_enthalpy,
):
    nx, nz, ny = cell_temp.shape
    n_col = lax.axis_size("col")
    n_hgt = lax.axis_size("hgt")
    n_dev = n_col * n_hgt
    count = nx * nz * ny // PTS
    cap = 2 * count // n_dev
    node_count = node_enthalpy.shape[0]
    cells = nx * nz * ny
    sem = pltpu.SemaphoreType.DMA

    def kernel(body, outs, ins, args, name, work, aliases=None, scratch=()):
        return pl.pallas_call(
            body,
            out_shape=outs,
            in_specs=ins,
            out_specs=jax.tree.map(lambda out: WHOLE, outs),
            input_output_aliases=aliases or {},
            scratch_shapes=scratch,
            compiler_params=params(VMEM_MIB),
            cost_estimate=cost(work * cells, work * cells),
            name=name,
        )(*args)

    e_start = far(efield_lattice_vector)
    h_start = far(hfield_lattice_vector)
    my_col = lax.axis_index("col").astype(jnp.int32).reshape(1)
    owners = block_owner.reshape(1, count)
    nodes = block_node.reshape(1, count)
    field = vmem(3, nx, nz, ny)
    whole = vmem(nx, nz, ny)
    planes = vmem(2, nz, ny)
    two_rows = vmem(2, nx, ny)
    three_rows = vmem(3, nx, ny)

    to_col, e_low = kernel(
        edge_kernel, (planes, two_rows), [FAR], [e_start], "edge", 4, scratch=[vmem(2, nx, ROWS, ny), sem((2,))]
    )
    col = shifted(to_col, -1, 0)
    hgt = shifted(e_low, 0, -1)
    ca, cb, sigma, e, h, media_rows, e_rows, h_high = kernel(
        load_kernel,
        (whole, whole, whole, field, field, two_rows, three_rows, two_rows),
        [FAR] * 4 + [WHOLE],
        [far(cell_temp), far(region_tags), e_start, h_start, owners + nodes + my_col],
        "load",
        60,
        scratch=[vmem(nx, nz, ny), pltpu.VMEM((nx, nz, ny), jnp.int32), sem((3, 4))],
    )
    begins, heights = starts_of(n_col, n_hgt, cap)
    place, mine_nodes, pair_nodes, other_nodes = kernel(
        functools.partial(places_kernel, n_col, n_hgt, cap),
        (
            jax.ShapeDtypeStruct((1, count), jnp.int32),
            vmem(n_hgt, table_rows(1, cap), PTS),
            vmem(n_hgt, table_rows(1, cap), PTS),
            vmem(n_hgt, table_rows(n_col - 2, cap), PTS),
        ),
        [SCALARS, WHOLE, WHOLE],
        [my_col, owners, nodes],
        "places",
        8,
    )
    power = None
    for step in range(STEPS):
        first = step == 0
        h, to_col, h_high = kernel(
            h_edge_kernel,
            (field, planes, two_rows),
            [WHOLE] * 6,
            [e, col, hgt, e_rows, h_high, h],
            f"h_edge_{step}",
            4,
            {5: 0},
        )
        e_hgt = hgt
        col = shifted(to_col, 1, 0)
        hgt = shifted(h_high, 0, 1)
        h, h_rows = kernel(
            h_rest_kernel, (field, three_rows), [WHOLE] * 3, [e, e_hgt, h], f"h_rest_{step}", 40, {2: 0}
        )
        media = [h, ca, cb, sigma]
        if step == STEPS - 1:
            e, power = kernel(
                functools.partial(e_last_kernel, first),
                (field, whole),
                [WHOLE] * 8,
                media + [col, hgt, e, power],
                f"e_last_{step}",
                50,
                {6: 0, 7: 1},
            )
            break
        args = media + [col, hgt, media_rows, h_rows, e_low, e] + ([] if first else [power])
        e, power, to_col, e_low = kernel(
            functools.partial(e_edge_kernel, first),
            (field, whole, planes, two_rows),
            [WHOLE] * len(args),
            args,
            f"e_edge_{step}",
            5,
            {9: 0} if first else {9: 0, 10: 1},
        )
        h_hgt = hgt
        col = shifted(to_col, -1, 0)
        hgt = shifted(e_low, 0, -1)
        e, power, e_rows = kernel(
            functools.partial(e_rest_kernel, first),
            (field, whole, three_rows),
            [WHOLE] * 7,
            media + [h_hgt, e, power],
            f"e_rest_{step}",
            45,
            {5: 0, 6: 1},
        )

    mine, pair, other, e_out, h_out = pl.pallas_call(
        functools.partial(pack_kernel, cap),
        out_shape=(
            pltpu.HBM((n_hgt, 2 * heights[0], PTS), F32),
            pltpu.HBM((n_hgt, heights[1], PTS), F32),
            pltpu.HBM((n_hgt, heights[2], PTS), F32),
            pltpu.HBM((3, nx, nz, ny), F32),
            pltpu.HBM((3, nx, nz, ny), F32),
        ),
        in_specs=[SCALARS] + [WHOLE] * 6,
        out_specs=(FAR,) * 5,
        scratch_shapes=[vmem(n_hgt * sum(heights), PTS), sem((2 + 3 * n_hgt,))],
        compiler_params=params(VMEM_MIB),
        cost_estimate=cost(cells, cells * 36),
        name="pack",
    )(place.reshape(count), power, mine_nodes, pair_nodes, other_nodes, e, h)

    def swap(x, axis):
        return lax.all_to_all(x, axis, split_axis=0, concat_axis=0, tiled=True)

    def across(x, turn):
        return lax.ppermute(x, "col", [(c, c ^ turn) for c in range(n_col)])

    def one_hot_space(sources):
        seats = sources * -(-cap // LANES) * LANES
        return [pltpu.VMEM((node_count, seats), jnp.bfloat16), pltpu.VMEM((seats, 2 * PTS), jnp.bfloat16)]

    node_rows = jax.ShapeDtypeStruct((node_count, PTS), F32)
    from_pair = across(pair, 1)
    other_blocks = swap(other, "hgt")
    sums = kernel(
        functools.partial(collect_kernel, cap),
        (node_rows,) * (n_col - 2),
        [WHOLE],
        [other_blocks],
        "collect_other",
        1,
        scratch=one_hot_space(n_hgt),
    )
    parts = [across(sums[turn - 2], turn) for turn in range(2, n_col)]
    mine = pl.pallas_call(
        merge_kernel,
        out_shape=pltpu.HBM((n_hgt, 2 * heights[0], PTS), F32),
        in_specs=[pl.BlockSpec(memory_space=pl.ANY), pl.BlockSpec(memory_space=pl.ANY), FAR],
        out_specs=FAR,
        input_output_aliases={2: 0},
        scratch_shapes=[sem((n_hgt,))],
        compiler_params=params(VMEM_MIB),
        cost_estimate=cost(1, 1),
        name="merge",
    )(from_pair, sums[0], mine)
    mine_blocks = swap(mine, "hgt")
    own = kernel(
        functools.partial(collect_mine_kernel, cap),
        node_rows,
        [WHOLE],
        [mine_blocks],
        "collect_mine",
        1,
        scratch=one_hot_space(2 * n_hgt),
    )
    node_temp = kernel(
        finish_kernel, node_rows, [WHOLE] * (n_col), [node_enthalpy, own, *parts], "finish", 1
    )
    return e_out, h_out, node_temp


def solution(mesh):
    placed = (
        P(None, "col", "hgt", None),
        P(None, "col", "hgt", None),
        P("col", "hgt", None),
        P("col", "hgt", None),
        P("col", "hgt", None, None, None, None),
        P("col", "hgt", None, None, None),
        P(("col", "hgt"), None),
    )
    return jax.shard_map(
        per_device,
        mesh=mesh,
        in_specs=placed,
        out_specs=(
            P(None, "col", "hgt", None),
            P(None, "col", "hgt", None),
            P(("col", "hgt"), None),
        ),
        check_vma=False,
    )
```

```python
import functools

import jax
import jax.numpy as jnp
from jax import lax
from jax.experimental import pallas as pl
from jax.experimental.pallas import tpu as pltpu
from jax.sharding import PartitionSpec as P

PTS = 128
STEPS = 4
COURANT = 0.55
LANES = 128
ROWS = 8
F32 = jnp.float32
VMEM_MIB = 20

WHOLE = pl.BlockSpec(memory_space=pltpu.VMEM)
SCALARS = pl.BlockSpec(memory_space=pltpu.SMEM)
FAR = pl.BlockSpec(memory_space=pltpu.HBM)


def vmem(*shape):
    return pltpu.VMEM(shape, F32)


def far(x):
    return pltpu.with_memory_space_constraint(x, pltpu.HBM)


def params(mib):
    return pltpu.CompilerParams(vmem_limit_bytes=mib << 20)


def cost(flops, moved):
    return pl.CostEstimate(flops=flops, bytes_accessed=moved, transcendentals=0)


def after_y(f):
    lane = lax.broadcasted_iota(jnp.int32, (ROWS, LANES), 1)
    n = f.shape[1] // LANES
    turned = [pltpu.roll(f[:, k * LANES : (k + 1) * LANES], LANES - 1, 1) for k in range(n)]
    turned.append(jnp.zeros((ROWS, LANES), F32))
    return jnp.concatenate([jnp.where(lane < LANES - 1, turned[k], turned[k + 1]) for k in range(n)], 1)


def before_y(f):
    lane = lax.broadcasted_iota(jnp.int32, (ROWS, LANES), 1)
    n = f.shape[1] // LANES
    turned = [jnp.zeros((ROWS, LANES), F32)]
    turned += [pltpu.roll(f[:, k * LANES : (k + 1) * LANES], 1, 1) for k in range(n)]
    return jnp.concatenate([jnp.where(lane > 0, turned[k + 1], turned[k]) for k in range(n)], 1)


def after_row(f, row):
    place = lax.broadcasted_iota(jnp.int32, f.shape, 0)
    return jnp.where(place < ROWS - 1, pltpu.roll(f, ROWS - 1, 0), jnp.broadcast_to(row, f.shape))


def before_row(f, row):
    place = lax.broadcasted_iota(jnp.int32, f.shape, 0)
    return jnp.where(place > 0, pltpu.roll(f, 1, 0), jnp.broadcast_to(row, f.shape))


def edge_kernel(e, to_col, to_hgt, low, sems):
    nx = e.shape[1]
    col_copy = pltpu.make_async_copy(e.at[pl.ds(1, 2), 0], to_col, sems.at[0])
    low_copy = pltpu.make_async_copy(e.at[pl.ds(0, 2), :, pl.ds(0, ROWS)], low, sems.at[1])
    low_copy.start()
    col_copy.start()
    low_copy.wait()
    for x in range(nx):
        for comp in range(2):
            to_hgt[comp, x : x + 1, :] = low[comp, x, 0:1, :]
    col_copy.wait()


def load_kernel(
    temp_far, tags_far, e_far, h_far, order, ca, cb, sigma_out, e, h, media_rows, e_rows, h_rows, temp, tags, sems
):
    nx, nz, _ = temp.shape
    parts = 4
    size = nx // parts
    copies = []
    for part in range(parts):
        here = pl.ds(part * size, size)
        copies.append(pltpu.make_async_copy(temp_far.at[here], temp.at[here], sems.at[0, part]))
        copies.append(pltpu.make_async_copy(tags_far.at[here], tags.at[here], sems.at[1, part]))
    e_copy = pltpu.make_async_copy(e_far, e, sems.at[2, 0])
    h_copy = pltpu.make_async_copy(h_far, h, sems.at[2, 1])
    for copy in copies:
        copy.start()
    e_copy.start()
    h_copy.start()

    def plane(x, carry):
        for z in range(0, nz, ROWS):
            tag = tags[x, z : z + ROWS, :]
            lean = tag == 0
            fat = tag == 1
            frac = 1.0 / (1.0 + jnp.exp(-2.0 * temp[x, z : z + ROWS, :]))
            eps_low = jnp.where(lean, 4.0, jnp.where(fat, 2.5, 5.0))
            eps_rise = jnp.where(lean, 46.0, jnp.where(fat, 3.5, 5.0))
            sig_low = jnp.where(lean, 0.2, jnp.where(fat, 0.05, 0.1))
            sig_rise = jnp.where(lean, 7.8, jnp.where(fat, 0.35, 0.9))
            eps = eps_low + eps_rise * frac
            sigma = sig_low + sig_rise * frac
            half = (0.5 * COURANT) * sigma
            inverse = 1.0 / (eps + half)
            ca[x, z : z + ROWS, :] = (eps - half) * inverse
            cb[x, z : z + ROWS, :] = COURANT * inverse
            sigma_out[x, z : z + ROWS, :] = sigma
        media_rows[0, pl.ds(x, 1), :] = ca[x, 0:1, :]
        media_rows[1, pl.ds(x, 1), :] = cb[x, 0:1, :]
        return carry

    for part in range(parts):
        copies[2 * part].wait()
        copies[2 * part + 1].wait()
        lax.fori_loop(part * size, (part + 1) * size, plane, 0)
    e_copy.wait()
    h_copy.wait()

    def rows(x, carry):
        for comp in range(3):
            e_rows[comp, pl.ds(x, 1), :] = e[comp, x, nz - 1 : nz, :]
        for comp in range(2):
            h_rows[comp, pl.ds(x, 1), :] = h[comp, x, nz - 1 : nz, :]
        return carry

    lax.fori_loop(0, nx, rows, 0)


def over(first, stop, body):
    if stop - first == 1:
        body(first)
    else:

        def step(x, carry):
            body(x)
            return carry

        lax.fori_loop(first, stop, step, 0)


def h_tile(e, h, col, hgt, x, z):
    nz = e.shape[2]
    here = slice(z, z + ROWS)
    ex, ey, ez = (e[comp, x, here, :] for comp in range(3))
    if z + ROWS < nz:
        row_x, row_y = (e[comp, x, z + ROWS : z + ROWS + 1, :] for comp in range(2))
    else:
        row_x, row_y = (hgt[comp, pl.ds(x, 1), :] for comp in range(2))
    if col is None:
        next_y, next_z = (e[comp, x + 1, here, :] for comp in (1, 2))
    else:
        next_y, next_z = (col[comp, here, :] for comp in range(2))
    h[0, x, here, :] = h[0, x, here, :] - COURANT * ((after_y(ez) - ez) - (after_row(ey, row_y) - ey))
    hy = h[1, x, here, :] - COURANT * ((after_row(ex, row_x) - ex) - (next_z - ez))
    hz = h[2, x, here, :] - COURANT * ((next_y - ey) - (after_y(ex) - ex))
    h[1, x, here, :] = hy
    h[2, x, here, :] = hz
    return hy, hz


def e_tile(first, h, e, power, ca, cb, sigma, col, hgt, x, z):
    here = slice(z, z + ROWS)
    hx, hy, hz = (h[comp, x, here, :] for comp in range(3))
    if z > 0:
        row_x, row_y = (h[comp, x, z - 1 : z, :] for comp in range(2))
    else:
        row_x, row_y = (hgt[comp, pl.ds(x, 1), :] for comp in range(2))
    if col is None:
        past_y, past_z = (h[comp, x - 1, here, :] for comp in (1, 2))
    else:
        past_y, past_z = (col[comp, here, :] for comp in range(2))
    keep = ca[x, here, :]
    drive = cb[x, here, :]
    ex = keep * e[0, x, here, :] + drive * ((hz - before_y(hz)) - (hy - before_row(hy, row_y)))
    ey = keep * e[1, x, here, :] + drive * ((hx - before_row(hx, row_x)) - (hz - past_z))
    ez = keep * e[2, x, here, :] + drive * ((hy - past_y) - (hx - before_y(hx)))
    e[0, x, here, :] = ex
    e[1, x, here, :] = ey
    e[2, x, here, :] = ez
    heat = sigma[x, here, :] * (ex * ex + ey * ey + ez * ez)
    power[x, here, :] = heat if first else power[x, here, :] + heat
    return ey, ez


def h_edge_kernel(e, col, hgt, e_rows, rows_old, h_old, h, to_col, to_hgt):
    nx, nz = e.shape[1:3]
    for z in range(0, nz, ROWS):
        hy, hz = h_tile(e, h, col, hgt, nx - 1, z)
        to_col[0, z : z + ROWS, :] = hy
        to_col[1, z : z + ROWS, :] = hz
    for x in range(0, nx, ROWS):
        here = slice(x, x + ROWS)
        ex, ey, ez = (e_rows[comp, here, :] for comp in range(3))
        row = e_rows[2, x + ROWS : x + ROWS + 1, :] if x + ROWS < nx else col[1, nz - 1 : nz, :]
        to_hgt[0, here, :] = rows_old[0, here, :] - COURANT * ((after_y(ez) - ez) - (hgt[1, here, :] - ey))
        to_hgt[1, here, :] = rows_old[1, here, :] - COURANT * ((hgt[0, here, :] - ex) - (after_row(ez, row) - ez))


def h_rest_kernel(e, hgt, h_old, h, *rows):
    nx, nz = e.shape[1:3]

    def keep(x):
        if rows:
            for comp in range(3):
                rows[0][comp, pl.ds(x, 1), :] = h[comp, x, 0:1, :]

    def plane(x):
        for z in range(0, nz, ROWS):
            h_tile(e, h, None, hgt, x, z)
        keep(x)

    over(0, nx - 1, plane)
    keep(nx - 1)


def e_edge_kernel(first, h, ca, cb, sigma, col, hgt, media_rows, h_rows, rows_old, *refs):
    e, power, to_col, to_hgt = refs[-4:]
    nx, nz = e.shape[1:3]
    for z in range(0, nz, ROWS):
        ey, ez = e_tile(first, h, e, power, ca, cb, sigma, col, hgt, 0, z)
        to_col[0, z : z + ROWS, :] = ey
        to_col[1, z : z + ROWS, :] = ez
    for x in range(0, nx, ROWS):
        here = slice(x, x + ROWS)
        hx, hy, hz = (h_rows[comp, here, :] for comp in range(3))
        row = h_rows[2, x - 1 : x, :] if x > 0 else col[1, 0:1, :]
        keep = media_rows[0, here, :]
        drive = media_rows[1, here, :]
        to_hgt[0, here, :] = keep * rows_old[0, here, :] + drive * ((hz - before_y(hz)) - (hy - hgt[1, here, :]))
        to_hgt[1, here, :] = keep * rows_old[1, here, :] + drive * ((hx - hgt[0, here, :]) - (hz - before_row(hz, row)))


def e_rest_kernel(first, h, ca, cb, sigma, hgt, e_old, power_old, e, power, rows):
    nx, nz = e.shape[1:3]

    def keep(x):
        for comp in range(3):
            rows[comp, pl.ds(x, 1), :] = e[comp, x, nz - 1 : nz, :]

    def plane(x):
        for z in range(0, nz, ROWS):
            e_tile(first, h, e, power, ca, cb, sigma, None, hgt, x, z)
        keep(x)

    keep(0)
    over(1, nx, plane)


def e_last_kernel(first, h, ca, cb, sigma, col, hgt, e_old, power_old, e, power, h_out, sem):
    nx, nz = e.shape[1:3]
    copy = pltpu.make_async_copy(h, h_out, sem)
    copy.start()

    def plane(x):
        for z in range(0, nz, ROWS):
            e_tile(first, h, e, power, ca, cb, sigma, col if isinstance(x, int) else None, hgt, x, z)

    plane(0)
    over(1, nx, plane)
    copy.wait()


def places_kernel(n_col, n_hgt, cap, my_col, owner, node, place, flat):
    n_dev = n_col * n_hgt
    count = owner.shape[1]
    width = 256
    rows = lax.broadcasted_iota(jnp.int32, (n_dev, width), 0)
    before = lax.broadcasted_iota(jnp.int32, (width, width), 0)
    after = lax.broadcasted_iota(jnp.int32, (width, width), 1)
    upper = jnp.where(before <= after, 1.0, 0.0).astype(jnp.bfloat16)
    per = -(-cap // LANES)
    room_for = per * LANES
    room = lax.broadcasted_iota(jnp.int32, (room_for, width), 0)
    total = jnp.zeros((n_dev, 1), F32)
    parts_of = jnp.zeros((2 * n_dev, room_for), F32)
    nt = (((1,), (1,)), ((), ()))
    begins, heights = starts_of(n_col, n_hgt, cap)
    for start in range(0, count, width):
        own = owner[:, start : start + width]
        hit = jnp.where(rows == own, 1.0, 0.0)
        running = total + jnp.dot(hit.astype(jnp.bfloat16), upper, preferred_element_type=F32)
        total = running[:, width - 1 : width]
        rank = jnp.sum(hit * running, axis=0, keepdims=True).astype(jnp.int32) - 1
        turn = lax.bitwise_xor(lax.div(own, n_hgt), my_col[0])
        own_hgt = lax.rem(own, n_hgt)
        begin = jnp.where(
            turn == 0,
            begins[0] + own_hgt * heights[0],
            jnp.where(
                turn == 1,
                begins[1] + own_hgt * heights[1],
                begins[2] + own_hgt * heights[2] + (turn - 2) * cap,
            ),
        )
        place[:, start : start + width] = begin + rank
        number = node[:, start : start + width]
        upper_part = lax.div(number, 16)
        lower_part = number - 16 * upper_part
        seat = jnp.where(room == rank, 1.0, 0.0).astype(jnp.bfloat16)
        both = jnp.concatenate([hit * upper_part.astype(F32), hit * lower_part.astype(F32)], 0)
        parts_of = parts_of + lax.dot_general(both.astype(jnp.bfloat16), seat, nt, preferred_element_type=F32)
    taken = lax.broadcasted_iota(jnp.int32, (n_dev, room_for), 1).astype(F32) < total
    table = jnp.where(taken, 16.0 * parts_of[:n_dev] + parts_of[n_dev:], -1.0)
    chunk = 8 * ROWS

    def clear(i, carry):
        flat[pl.ds(pl.multiple_of(i * chunk, chunk), chunk), :] = jnp.zeros((chunk, PTS), F32)
        return carry

    lax.fori_loop(0, flat.shape[0] // chunk, clear, 0)
    for at in range(flat.shape[0] // chunk * chunk, flat.shape[0], ROWS):
        flat[at : at + ROWS, :] = jnp.zeros((ROWS, PTS), F32)
    behind = [cap, cap, (n_col - 2) * cap]
    for begin, height, skip in zip(begins, heights, behind):
        for part in range(n_hgt):
            at = begin + part * height
            flat[at + skip : at + height, :] = jnp.full((height - skip, PTS), -1.0, F32)
    for group in range(n_col):
        turn = lax.bitwise_xor(jnp.int32(group), my_col[0])
        kind = jnp.minimum(turn, 2)
        begin = jnp.where(kind == 0, begins[0], jnp.where(kind == 1, begins[1], begins[2]))
        height = jnp.where(kind == 2, heights[2], heights[0])
        skip = jnp.where(kind == 2, behind[2] + (turn - 2) * per, cap)
        for part in range(n_hgt):
            at = group * n_hgt + part
            for piece in range(per):
                row = table[at : at + 1, piece * LANES : (piece + 1) * LANES]
                flat[pl.ds(begin + part * height + skip + piece, 1), :] = row


def table_rows(parts, cap):
    return -(-parts * -(-cap // LANES) // ROWS) * ROWS


def starts_of(n_col, n_hgt, cap):
    one = cap + table_rows(1, cap)
    heights = [one, one, (n_col - 2) * cap + table_rows(n_col - 2, cap)]
    return [0, n_hgt * heights[0], n_hgt * (heights[0] + heights[1])], heights


def pack_kernel(heights, place, power, flat_old, e, mine, pair, other, e_out, flat, sems):
    nx, nz, ny = power.shape
    e_copy = pltpu.make_async_copy(e, e_out, sems.at[0])
    e_copy.start()
    per_row = ny // PTS

    def plane(x, carry):
        for z in range(nz):
            for k in range(per_row):
                spot = place[x * (nz * per_row) + z * per_row + k]
                flat[pl.ds(spot, 1), :] = power[x, z : z + 1, k * PTS : (k + 1) * PTS]
        return carry

    lax.fori_loop(0, nx, plane, 0)
    copies = []
    first = 0
    for out, rows in zip((mine, pair, other), heights):
        for group in range(out.shape[0]):
            target = out.at[group, pl.ds(0, rows)]
            copies.append(pltpu.make_async_copy(flat.at[pl.ds(first, rows)], target, sems.at[1 + len(copies)]))
            first += rows
    for copy in copies:
        copy.start()
    for copy in copies:
        copy.wait()
    e_copy.wait()


def summed(blocks, first, cap, node_row, chosen, split, node_count):
    ids = lax.broadcasted_iota(jnp.int32, (node_count, LANES), 0).astype(F32)
    n_from, _, pts = blocks.shape
    per = -(-cap // LANES)
    many = len(first)
    for source in range(n_from):
        for i in range(many):
            seat = (source * many + i) * per * LANES
            for piece in range(per):
                row = node_row[i] + piece
                lanes = slice(seat + piece * LANES, seat + (piece + 1) * LANES)
                hit = ids == blocks[source, row : row + 1, :]
                chosen[:, lanes] = jnp.where(hit, 1.0, 0.0).astype(jnp.bfloat16)
            values = blocks[source, first[i] : first[i] + cap, :]
            high = values.astype(jnp.bfloat16)
            split[seat : seat + cap, 0:pts] = high
            split[seat : seat + cap, pts : 2 * pts] = (values - high.astype(F32)).astype(jnp.bfloat16)
    both = jnp.dot(chosen[...], split[...], preferred_element_type=F32)
    return both[:, 0:pts] + both[:, pts : 2 * pts]


def collect_kernel(cap, blocks, *refs):
    *outs, chosen, split = refs
    per = -(-cap // LANES)
    split[...] = jnp.zeros(split.shape, split.dtype)
    for part, out in enumerate(outs):
        out[...] = summed(blocks, [part * cap], cap, [len(outs) * cap + part * per], chosen, split, out.shape[0])


def merge_kernel(pair, mine_old, mine, sems):
    rows = pair.shape[1]
    copies = [
        pltpu.make_async_copy(pair.at[group], mine.at[group, pl.ds(rows, rows)], sems.at[group])
        for group in range(mine.shape[0])
    ]
    for copy in copies:
        copy.start()
    for copy in copies:
        copy.wait()


def collect_mine_kernel(cap, blocks, out, chosen, split):
    half = blocks.shape[1] // 2
    split[...] = jnp.zeros(split.shape, split.dtype)
    out[...] = summed(blocks, [0, half], cap, [cap, half + cap], chosen, split, out.shape[0])


def finish_kernel(enthalpy, *refs):
    *parts, out = refs
    heat = parts[0][...]
    for part in parts[1:]:
        heat = heat + part[...]
    content = enthalpy[...] + (0.25 / STEPS) * heat
    out[...] = jnp.where(content < 0.0, content / 2.0, jnp.where(content > 1.0, (content - 1.0) / 3.0, 0.0))


def shifted(block, d_col, d_hgt):
    n_col = lax.axis_size("col")
    n_hgt = lax.axis_size("hgt")
    route = [
        (c * n_hgt + h, (c + d_col) * n_hgt + h + d_hgt)
        for c in range(n_col)
        for h in range(n_hgt)
        if 0 <= c + d_col < n_col and 0 <= h + d_hgt < n_hgt
    ]
    return lax.ppermute(block, ("col", "hgt"), route)


def per_device(
    efield_lattice_vector,
    hfield_lattice_vector,
    cell_temp,
    region_tags,
    block_owner,
    block_node,
    node_enthalpy,
):
    nx, nz, ny = cell_temp.shape
    n_col = lax.axis_size("col")
    n_hgt = lax.axis_size("hgt")
    n_dev = n_col * n_hgt
    count = nx * nz * ny // PTS
    cap = 2 * count // n_dev
    node_count = node_enthalpy.shape[0]
    cells = nx * nz * ny
    sem = pltpu.SemaphoreType.DMA

    def kernel(body, outs, ins, args, name, work, aliases=None, scratch=()):
        return pl.pallas_call(
            body,
            out_shape=outs,
            in_specs=ins,
            out_specs=jax.tree.map(lambda out: WHOLE, outs),
            input_output_aliases=aliases or {},
            scratch_shapes=scratch,
            compiler_params=params(VMEM_MIB),
            cost_estimate=cost(work * cells, work * cells),
            name=name,
        )(*args)

    e_start = far(efield_lattice_vector)
    h_start = far(hfield_lattice_vector)
    my_col = lax.axis_index("col").astype(jnp.int32).reshape(1)
    owners = block_owner.reshape(1, count)
    nodes = block_node.reshape(1, count)
    field = vmem(3, nx, nz, ny)
    whole = vmem(nx, nz, ny)
    planes = vmem(2, nz, ny)
    two_rows = vmem(2, nx, ny)
    three_rows = vmem(3, nx, ny)

    to_col, e_low = kernel(
        edge_kernel, (planes, two_rows), [FAR], [e_start], "edge", 4, scratch=[vmem(2, nx, ROWS, ny), sem((2,))]
    )
    col = shifted(to_col, -1, 0)
    hgt = shifted(e_low, 0, -1)
    ca, cb, sigma, e, h, media_rows, e_rows, h_high = kernel(
        load_kernel,
        (whole, whole, whole, field, field, two_rows, three_rows, two_rows),
        [FAR] * 4 + [WHOLE],
        [far(cell_temp), far(region_tags), e_start, h_start, owners + nodes + my_col],
        "load",
        60,
        scratch=[vmem(nx, nz, ny), pltpu.VMEM((nx, nz, ny), jnp.int32), sem((3, 4))],
    )
    begins, heights = starts_of(n_col, n_hgt, cap)
    place, flat = kernel(
        functools.partial(places_kernel, n_col, n_hgt, cap),
        (jax.ShapeDtypeStruct((1, count), jnp.int32), vmem(n_hgt * sum(heights), PTS)),
        [SCALARS, WHOLE, WHOLE],
        [my_col, owners, nodes],
        "places",
        8,
    )
    power = None
    for step in range(STEPS):
        first = step == 0
        h, to_col, h_high = kernel(
            h_edge_kernel,
            (field, planes, two_rows),
            [WHOLE] * 6,
            [e, col, hgt, e_rows, h_high, h],
            f"h_edge_{step}",
            4,
            {5: 0},
        )
        e_hgt = hgt
        col = shifted(to_col, 1, 0)
        hgt = shifted(h_high, 0, 1)
        last = step == STEPS - 1
        outs = (field,) if last else (field, three_rows)
        h, *h_rows = kernel(h_rest_kernel, outs, [WHOLE] * 3, [e, e_hgt, h], f"h_rest_{step}", 40, {2: 0})
        media = [h, ca, cb, sigma]
        if last:
            e, power, h_out = pl.pallas_call(
                functools.partial(e_last_kernel, first),
                out_shape=(field, whole, pltpu.HBM((3, nx, nz, ny), F32)),
                in_specs=[WHOLE] * 8,
                out_specs=(WHOLE, WHOLE, FAR),
                input_output_aliases={6: 0, 7: 1},
                scratch_shapes=[sem],
                compiler_params=params(VMEM_MIB),
                cost_estimate=cost(cells * 50, cells * 50),
                name="e_last",
            )(*media, col, hgt, e, power)
            break
        args = media + [col, hgt, media_rows, *h_rows, e_low, e] + ([] if first else [power])
        e, power, to_col, e_low = kernel(
            functools.partial(e_edge_kernel, first),
            (field, whole, planes, two_rows),
            [WHOLE] * len(args),
            args,
            f"e_edge_{step}",
            5,
            {9: 0} if first else {9: 0, 10: 1},
        )
        h_hgt = hgt
        col = shifted(to_col, -1, 0)
        hgt = shifted(e_low, 0, -1)
        e, power, e_rows = kernel(
            functools.partial(e_rest_kernel, first),
            (field, whole, three_rows),
            [WHOLE] * 7,
            media + [h_hgt, e, power],
            f"e_rest_{step}",
            45,
            {5: 0, 6: 1},
        )

    mine, pair, other, e_out, _ = pl.pallas_call(
        functools.partial(pack_kernel, heights),
        out_shape=(
            pltpu.HBM((n_hgt, 2 * heights[0], PTS), F32),
            pltpu.HBM((n_hgt, heights[1], PTS), F32),
            pltpu.HBM((n_hgt, heights[2], PTS), F32),
            pltpu.HBM((3, nx, nz, ny), F32),
            vmem(n_hgt * sum(heights), PTS),
        ),
        in_specs=[SCALARS] + [WHOLE] * 3,
        out_specs=(FAR,) * 4 + (WHOLE,),
        input_output_aliases={2: 4},
        scratch_shapes=[sem((1 + 3 * n_hgt,))],
        compiler_params=params(VMEM_MIB),
        cost_estimate=cost(cells, cells * 36),
        name="pack",
    )(place.reshape(count), power, flat, e)

    def swap(x, axis):
        return lax.all_to_all(x, axis, split_axis=0, concat_axis=0, tiled=True)

    def across(x, turn):
        return lax.ppermute(x, "col", [(c, c ^ turn) for c in range(n_col)])

    def one_hot_space(sources):
        seats = sources * -(-cap // LANES) * LANES
        return [pltpu.VMEM((node_count, seats), jnp.bfloat16), pltpu.VMEM((seats, 2 * PTS), jnp.bfloat16)]

    node_rows = jax.ShapeDtypeStruct((node_count, PTS), F32)
    from_pair = across(pair, 1)
    other_blocks = swap(other, "hgt")
    sums = kernel(
        functools.partial(collect_kernel, cap),
        (node_rows,) * (n_col - 2),
        [WHOLE],
        [other_blocks],
        "collect_other",
        1,
        scratch=one_hot_space(n_hgt),
    )
    parts = [across(sums[turn - 2], turn) for turn in range(2, n_col)]
    mine = pl.pallas_call(
        merge_kernel,
        out_shape=pltpu.HBM((n_hgt, 2 * heights[0], PTS), F32),
        in_specs=[pl.BlockSpec(memory_space=pl.ANY), FAR],
        out_specs=FAR,
        input_output_aliases={1: 0},
        scratch_shapes=[sem((n_hgt,))],
        compiler_params=params(VMEM_MIB),
        cost_estimate=cost(1, 1),
        name="merge",
    )(from_pair, mine)
    mine_blocks = swap(mine, "hgt")
    own = kernel(
        functools.partial(collect_mine_kernel, cap),
        node_rows,
        [WHOLE],
        [mine_blocks],
        "collect_mine",
        1,
        scratch=one_hot_space(2 * n_hgt),
    )
    node_temp = kernel(
        finish_kernel, node_rows, [WHOLE] * (n_col), [node_enthalpy, own, *parts], "finish", 1
    )
    return e_out, h_out, node_temp


def solution(mesh):
    placed = (
        P(None, "col", "hgt", None),
        P(None, "col", "hgt", None),
        P("col", "hgt", None),
        P("col", "hgt", None),
        P("col", "hgt", None, None, None, None),
        P("col", "hgt", None, None, None),
        P(("col", "hgt"), None),
    )
    return jax.shard_map(
        per_device,
        mesh=mesh,
        in_specs=placed,
        out_specs=(
            P(None, "col", "hgt", None),
            P(None, "col", "hgt", None),
            P(("col", "hgt"), None),
        ),
        check_vma=False,
    )
```

```python
import functools

import jax
import jax.numpy as jnp
from jax import lax
from jax.experimental import pallas as pl
from jax.experimental.pallas import tpu as pltpu
from jax.sharding import PartitionSpec as P

PTS = 128
STEPS = 4
COURANT = 0.55
LANES = 128
ROWS = 8
F32 = jnp.float32
VMEM_MIB = 20

WHOLE = pl.BlockSpec(memory_space=pltpu.VMEM)
SCALARS = pl.BlockSpec(memory_space=pltpu.SMEM)
FAR = pl.BlockSpec(memory_space=pltpu.HBM)


def vmem(*shape):
    return pltpu.VMEM(shape, F32)


def far(x):
    return pltpu.with_memory_space_constraint(x, pltpu.HBM)


def params(mib):
    return pltpu.CompilerParams(vmem_limit_bytes=mib << 20)


def cost(flops, moved):
    return pl.CostEstimate(flops=flops, bytes_accessed=moved, transcendentals=0)


def after_y(f):
    lane = lax.broadcasted_iota(jnp.int32, (ROWS, LANES), 1)
    n = f.shape[1] // LANES
    turned = [pltpu.roll(f[:, k * LANES : (k + 1) * LANES], LANES - 1, 1) for k in range(n)]
    turned.append(jnp.zeros((ROWS, LANES), F32))
    return jnp.concatenate([jnp.where(lane < LANES - 1, turned[k], turned[k + 1]) for k in range(n)], 1)


def before_y(f):
    lane = lax.broadcasted_iota(jnp.int32, (ROWS, LANES), 1)
    n = f.shape[1] // LANES
    turned = [jnp.zeros((ROWS, LANES), F32)]
    turned += [pltpu.roll(f[:, k * LANES : (k + 1) * LANES], 1, 1) for k in range(n)]
    return jnp.concatenate([jnp.where(lane > 0, turned[k + 1], turned[k]) for k in range(n)], 1)


def after_row(f, row):
    place = lax.broadcasted_iota(jnp.int32, f.shape, 0)
    return jnp.where(place < ROWS - 1, pltpu.roll(f, ROWS - 1, 0), jnp.broadcast_to(row, f.shape))


def before_row(f, row):
    place = lax.broadcasted_iota(jnp.int32, f.shape, 0)
    return jnp.where(place > 0, pltpu.roll(f, 1, 0), jnp.broadcast_to(row, f.shape))


def edge_kernel(e, to_col, to_hgt, low, sems):
    nx = e.shape[1]
    col_copy = pltpu.make_async_copy(e.at[pl.ds(1, 2), 0], to_col, sems.at[0])
    low_copy = pltpu.make_async_copy(e.at[pl.ds(0, 2), :, pl.ds(0, ROWS)], low, sems.at[1])
    low_copy.start()
    col_copy.start()
    low_copy.wait()
    for x in range(nx):
        for comp in range(2):
            to_hgt[comp, x : x + 1, :] = low[comp, x, 0:1, :]
    col_copy.wait()


def load_kernel(e_far, h_far, order, e, h, e_rows, h_rows, sems):
    nx, nz = e.shape[1:3]
    e_copy = pltpu.make_async_copy(e_far, e, sems.at[0])
    h_copy = pltpu.make_async_copy(h_far, h, sems.at[1])
    e_copy.start()
    h_copy.start()

    def take(field, rows):
        def body(x, carry):
            for comp in range(rows.shape[0]):
                rows[comp, pl.ds(x, 1), :] = field[comp, x, nz - 1 : nz, :]
            return carry

        lax.fori_loop(0, nx, body, 0)

    e_copy.wait()
    take(e, e_rows)
    h_copy.wait()
    take(h, h_rows)


def coefficients_kernel(temp_far, tags_far, order, ca, cb, sigma_out, media_rows, temp, tags, sems):
    nx, nz, _ = temp.shape
    parts = 8
    size = nx // parts
    copies = []
    for part in range(parts):
        here = pl.ds(part * size, size)
        copies.append(pltpu.make_async_copy(temp_far.at[here], temp.at[here], sems.at[0, part]))
        copies.append(pltpu.make_async_copy(tags_far.at[here], tags.at[here], sems.at[1, part]))
    for copy in copies:
        copy.start()

    def plane(x, carry):
        for z in range(0, nz, ROWS):
            tag = tags[x, z : z + ROWS, :]
            lean = tag == 0
            fat = tag == 1
            frac = 1.0 / (1.0 + jnp.exp(-2.0 * temp[x, z : z + ROWS, :]))
            eps_low = jnp.where(lean, 4.0, jnp.where(fat, 2.5, 5.0))
            eps_rise = jnp.where(lean, 46.0, jnp.where(fat, 3.5, 5.0))
            sig_low = jnp.where(lean, 0.2, jnp.where(fat, 0.05, 0.1))
            sig_rise = jnp.where(lean, 7.8, jnp.where(fat, 0.35, 0.9))
            eps = eps_low + eps_rise * frac
            sigma = sig_low + sig_rise * frac
            half = (0.5 * COURANT) * sigma
            inverse = 1.0 / (eps + half)
            ca[x, z : z + ROWS, :] = (eps - half) * inverse
            cb[x, z : z + ROWS, :] = COURANT * inverse
            sigma_out[x, z : z + ROWS, :] = sigma
        media_rows[0, pl.ds(x, 1), :] = ca[x, 0:1, :]
        media_rows[1, pl.ds(x, 1), :] = cb[x, 0:1, :]
        return carry

    for part in range(parts):
        copies[2 * part].wait()
        copies[2 * part + 1].wait()
        lax.fori_loop(part * size, (part + 1) * size, plane, 0)


def over(first, stop, body):
    if stop - first == 1:
        body(first)
    else:

        def step(x, carry):
            body(x)
            return carry

        lax.fori_loop(first, stop, step, 0)


def h_tile(e, h, col, hgt, x, z):
    nz = e.shape[2]
    here = slice(z, z + ROWS)
    ex, ey, ez = (e[comp, x, here, :] for comp in range(3))
    if z + ROWS < nz:
        row_x, row_y = (e[comp, x, z + ROWS : z + ROWS + 1, :] for comp in range(2))
    else:
        row_x, row_y = (hgt[comp, pl.ds(x, 1), :] for comp in range(2))
    if col is None:
        next_y, next_z = (e[comp, x + 1, here, :] for comp in (1, 2))
    else:
        next_y, next_z = (col[comp, here, :] for comp in range(2))
    h[0, x, here, :] = h[0, x, here, :] - COURANT * ((after_y(ez) - ez) - (after_row(ey, row_y) - ey))
    hy = h[1, x, here, :] - COURANT * ((after_row(ex, row_x) - ex) - (next_z - ez))
    hz = h[2, x, here, :] - COURANT * ((next_y - ey) - (after_y(ex) - ex))
    h[1, x, here, :] = hy
    h[2, x, here, :] = hz
    return hy, hz


def e_tile(first, h, e, power, ca, cb, sigma, col, hgt, x, z):
    here = slice(z, z + ROWS)
    hx, hy, hz = (h[comp, x, here, :] for comp in range(3))
    if z > 0:
        row_x, row_y = (h[comp, x, z - 1 : z, :] for comp in range(2))
    else:
        row_x, row_y = (hgt[comp, pl.ds(x, 1), :] for comp in range(2))
    if col is None:
        past_y, past_z = (h[comp, x - 1, here, :] for comp in (1, 2))
    else:
        past_y, past_z = (col[comp, here, :] for comp in range(2))
    keep = ca[x, here, :]
    drive = cb[x, here, :]
    ex = keep * e[0, x, here, :] + drive * ((hz - before_y(hz)) - (hy - before_row(hy, row_y)))
    ey = keep * e[1, x, here, :] + drive * ((hx - before_row(hx, row_x)) - (hz - past_z))
    ez = keep * e[2, x, here, :] + drive * ((hy - past_y) - (hx - before_y(hx)))
    e[0, x, here, :] = ex
    e[1, x, here, :] = ey
    e[2, x, here, :] = ez
    heat = sigma[x, here, :] * (ex * ex + ey * ey + ez * ez)
    power[x, here, :] = heat if first else power[x, here, :] + heat
    return ey, ez


def h_edge_kernel(e, col, hgt, e_rows, rows_old, h_old, h, to_col, to_hgt):
    nx, nz = e.shape[1:3]
    for z in range(0, nz, ROWS):
        hy, hz = h_tile(e, h, col, hgt, nx - 1, z)
        to_col[0, z : z + ROWS, :] = hy
        to_col[1, z : z + ROWS, :] = hz
    for x in range(0, nx, ROWS):
        here = slice(x, x + ROWS)
        ex, ey, ez = (e_rows[comp, here, :] for comp in range(3))
        row = e_rows[2, x + ROWS : x + ROWS + 1, :] if x + ROWS < nx else col[1, nz - 1 : nz, :]
        to_hgt[0, here, :] = rows_old[0, here, :] - COURANT * ((after_y(ez) - ez) - (hgt[1, here, :] - ey))
        to_hgt[1, here, :] = rows_old[1, here, :] - COURANT * ((hgt[0, here, :] - ex) - (after_row(ez, row) - ez))


def h_rest_kernel(e, hgt, h_old, h, *rows):
    nx, nz = e.shape[1:3]

    def keep(x):
        if rows:
            for comp in range(3):
                rows[0][comp, pl.ds(x, 1), :] = h[comp, x, 0:1, :]

    def plane(x):
        for z in range(0, nz, ROWS):
            h_tile(e, h, None, hgt, x, z)
        keep(x)

    over(0, nx - 1, plane)
    keep(nx - 1)


def e_edge_kernel(first, order, h, ca, cb, sigma, col, hgt, media_rows, h_rows, rows_old, *refs):
    e, power, to_col, to_hgt = refs[-4:]
    nx, nz = e.shape[1:3]
    for z in range(0, nz, ROWS):
        ey, ez = e_tile(first, h, e, power, ca, cb, sigma, col, hgt, 0, z)
        to_col[0, z : z + ROWS, :] = ey
        to_col[1, z : z + ROWS, :] = ez
    for x in range(0, nx, ROWS):
        here = slice(x, x + ROWS)
        hx, hy, hz = (h_rows[comp, here, :] for comp in range(3))
        row = h_rows[2, x - 1 : x, :] if x > 0 else col[1, 0:1, :]
        keep = media_rows[0, here, :]
        drive = media_rows[1, here, :]
        to_hgt[0, here, :] = keep * rows_old[0, here, :] + drive * ((hz - before_y(hz)) - (hy - hgt[1, here, :]))
        to_hgt[1, here, :] = keep * rows_old[1, here, :] + drive * ((hx - hgt[0, here, :]) - (hz - before_row(hz, row)))


def e_rest_kernel(first, h, ca, cb, sigma, hgt, e_old, power_old, e, power, rows):
    nx, nz = e.shape[1:3]

    def keep(x):
        for comp in range(3):
            rows[comp, pl.ds(x, 1), :] = e[comp, x, nz - 1 : nz, :]

    def plane(x):
        for z in range(0, nz, ROWS):
            e_tile(first, h, e, power, ca, cb, sigma, None, hgt, x, z)
        keep(x)

    keep(0)
    over(1, nx, plane)


def e_last_kernel(first, h, ca, cb, sigma, col, hgt, e_old, power_old, e, power, h_out, sem):
    nx, nz = e.shape[1:3]
    copy = pltpu.make_async_copy(h, h_out, sem)
    copy.start()

    def plane(x):
        for z in range(0, nz, ROWS):
            e_tile(first, h, e, power, ca, cb, sigma, col if isinstance(x, int) else None, hgt, x, z)

    plane(0)
    over(1, nx, plane)
    copy.wait()


def places_kernel(n_col, n_hgt, cap, my_col, owner, node, place, flat):
    n_dev = n_col * n_hgt
    count = owner.shape[1]
    width = 256
    rows = lax.broadcasted_iota(jnp.int32, (n_dev, width), 0)
    before = lax.broadcasted_iota(jnp.int32, (width, width), 0)
    after = lax.broadcasted_iota(jnp.int32, (width, width), 1)
    upper = jnp.where(before <= after, 1.0, 0.0).astype(jnp.bfloat16)
    per = -(-cap // LANES)
    room_for = per * LANES
    room = lax.broadcasted_iota(jnp.int32, (room_for, width), 0)
    total = jnp.zeros((n_dev, 1), F32)
    parts_of = jnp.zeros((2 * n_dev, room_for), F32)
    nt = (((1,), (1,)), ((), ()))
    begins, heights = starts_of(n_col, n_hgt, cap)
    for start in range(0, count, width):
        own = owner[:, start : start + width]
        hit = jnp.where(rows == own, 1.0, 0.0)
        running = total + jnp.dot(hit.astype(jnp.bfloat16), upper, preferred_element_type=F32)
        total = running[:, width - 1 : width]
        rank = jnp.sum(hit * running, axis=0, keepdims=True).astype(jnp.int32) - 1
        turn = lax.bitwise_xor(lax.div(own, n_hgt), my_col[0])
        own_hgt = lax.rem(own, n_hgt)
        begin = jnp.where(
            turn == 0,
            begins[0] + own_hgt * heights[0],
            jnp.where(
                turn == 1,
                begins[1] + own_hgt * heights[1],
                begins[2] + own_hgt * heights[2] + (turn - 2) * cap,
            ),
        )
        place[:, start : start + width] = begin + rank
        number = node[:, start : start + width]
        upper_part = lax.div(number, 16)
        lower_part = number - 16 * upper_part
        seat = jnp.where(room == rank, 1.0, 0.0).astype(jnp.bfloat16)
        both = jnp.concatenate([hit * upper_part.astype(F32), hit * lower_part.astype(F32)], 0)
        parts_of = parts_of + lax.dot_general(both.astype(jnp.bfloat16), seat, nt, preferred_element_type=F32)
    taken = lax.broadcasted_iota(jnp.int32, (n_dev, room_for), 1).astype(F32) < total
    table = jnp.where(taken, 16.0 * parts_of[:n_dev] + parts_of[n_dev:], -1.0)
    chunk = 8 * ROWS

    def clear(i, carry):
        flat[pl.ds(pl.multiple_of(i * chunk, chunk), chunk), :] = jnp.zeros((chunk, PTS), F32)
        return carry

    lax.fori_loop(0, flat.shape[0] // chunk, clear, 0)
    for at in range(flat.shape[0] // chunk * chunk, flat.shape[0], ROWS):
        flat[at : at + ROWS, :] = jnp.zeros((ROWS, PTS), F32)
    behind = [cap, cap, (n_col - 2) * cap]
    for begin, height, skip in zip(begins, heights, behind):
        for part in range(n_hgt):
            at = begin + part * height
            flat[at + skip : at + height, :] = jnp.full((height - skip, PTS), -1.0, F32)
    for group in range(n_col):
        turn = lax.bitwise_xor(jnp.int32(group), my_col[0])
        kind = jnp.minimum(turn, 2)
        begin = jnp.where(kind == 0, begins[0], jnp.where(kind == 1, begins[1], begins[2]))
        height = jnp.where(kind == 2, heights[2], heights[0])
        skip = jnp.where(kind == 2, behind[2] + (turn - 2) * per, cap)
        for part in range(n_hgt):
            at = group * n_hgt + part
            for piece in range(per):
                row = table[at : at + 1, piece * LANES : (piece + 1) * LANES]
                flat[pl.ds(begin + part * height + skip + piece, 1), :] = row


def table_rows(parts, cap):
    return -(-parts * -(-cap // LANES) // ROWS) * ROWS


def starts_of(n_col, n_hgt, cap):
    one = cap + table_rows(1, cap)
    heights = [one, one, (n_col - 2) * cap + table_rows(n_col - 2, cap)]
    return [0, n_hgt * heights[0], n_hgt * (heights[0] + heights[1])], heights


def pack_kernel(heights, place, power, flat_old, e, mine, pair, other, e_out, flat, sems):
    nx, nz, ny = power.shape
    e_copy = pltpu.make_async_copy(e, e_out, sems.at[0])
    e_copy.start()
    per_row = ny // PTS

    def plane(x, carry):
        for z in range(nz):
            for k in range(per_row):
                spot = place[x * (nz * per_row) + z * per_row + k]
                flat[pl.ds(spot, 1), :] = power[x, z : z + 1, k * PTS : (k + 1) * PTS]
        return carry

    lax.fori_loop(0, nx, plane, 0)
    copies = []
    first = 0
    for out, rows in zip((mine, pair, other), heights):
        for group in range(out.shape[0]):
            target = out.at[group, pl.ds(0, rows)]
            copies.append(pltpu.make_async_copy(flat.at[pl.ds(first, rows)], target, sems.at[1 + len(copies)]))
            first += rows
    for copy in copies:
        copy.start()
    for copy in copies:
        copy.wait()
    e_copy.wait()


def summed(blocks, first, cap, node_row, chosen, split, node_count):
    ids = lax.broadcasted_iota(jnp.int32, (node_count, LANES), 0).astype(F32)
    n_from, _, pts = blocks.shape
    per = -(-cap // LANES)
    many = len(first)
    for source in range(n_from):
        for i in range(many):
            seat = (source * many + i) * per * LANES
            for piece in range(per):
                row = node_row[i] + piece
                lanes = slice(seat + piece * LANES, seat + (piece + 1) * LANES)
                hit = ids == blocks[source, row : row + 1, :]
                chosen[:, lanes] = jnp.where(hit, 1.0, 0.0).astype(jnp.bfloat16)
            values = blocks[source, first[i] : first[i] + cap, :]
            high = values.astype(jnp.bfloat16)
            split[seat : seat + cap, 0:pts] = high
            split[seat : seat + cap, pts : 2 * pts] = (values - high.astype(F32)).astype(jnp.bfloat16)
    both = jnp.dot(chosen[...], split[...], preferred_element_type=F32)
    return both[:, 0:pts] + both[:, pts : 2 * pts]


def collect_kernel(cap, blocks, *refs):
    *outs, chosen, split = refs
    per = -(-cap // LANES)
    split[...] = jnp.zeros(split.shape, split.dtype)
    for part, out in enumerate(outs):
        out[...] = summed(blocks, [part * cap], cap, [len(outs) * cap + part * per], chosen, split, out.shape[0])


def merge_kernel(pair, mine_old, mine, sems):
    rows = pair.shape[1]
    copies = [
        pltpu.make_async_copy(pair.at[group], mine.at[group, pl.ds(rows, rows)], sems.at[group])
        for group in range(mine.shape[0])
    ]
    for copy in copies:
        copy.start()
    for copy in copies:
        copy.wait()


def collect_mine_kernel(cap, blocks, out, chosen, split):
    half = blocks.shape[1] // 2
    split[...] = jnp.zeros(split.shape, split.dtype)
    out[...] = summed(blocks, [0, half], cap, [cap, half + cap], chosen, split, out.shape[0])


def finish_kernel(enthalpy, *refs):
    *parts, out = refs
    heat = parts[0][...]
    for part in parts[1:]:
        heat = heat + part[...]
    content = enthalpy[...] + (0.25 / STEPS) * heat
    out[...] = jnp.where(content < 0.0, content / 2.0, jnp.where(content > 1.0, (content - 1.0) / 3.0, 0.0))


def shifted(block, d_col, d_hgt):
    n_col = lax.axis_size("col")
    n_hgt = lax.axis_size("hgt")
    route = [
        (c * n_hgt + h, (c + d_col) * n_hgt + h + d_hgt)
        for c in range(n_col)
        for h in range(n_hgt)
        if 0 <= c + d_col < n_col and 0 <= h + d_hgt < n_hgt
    ]
    return lax.ppermute(block, ("col", "hgt"), route)


def per_device(
    efield_lattice_vector,
    hfield_lattice_vector,
    cell_temp,
    region_tags,
    block_owner,
    block_node,
    node_enthalpy,
):
    nx, nz, ny = cell_temp.shape
    n_col = lax.axis_size("col")
    n_hgt = lax.axis_size("hgt")
    n_dev = n_col * n_hgt
    count = nx * nz * ny // PTS
    cap = 2 * count // n_dev
    node_count = node_enthalpy.shape[0]
    cells = nx * nz * ny
    sem = pltpu.SemaphoreType.DMA

    def kernel(body, outs, ins, args, name, work, aliases=None, scratch=()):
        return pl.pallas_call(
            body,
            out_shape=outs,
            in_specs=ins,
            out_specs=jax.tree.map(lambda out: WHOLE, outs),
            input_output_aliases=aliases or {},
            scratch_shapes=scratch,
            compiler_params=params(VMEM_MIB),
            cost_estimate=cost(work * cells, work * cells),
            name=name,
        )(*args)

    e_start = far(efield_lattice_vector)
    h_start = far(hfield_lattice_vector)
    my_col = lax.axis_index("col").astype(jnp.int32).reshape(1)
    owners = block_owner.reshape(1, count)
    nodes = block_node.reshape(1, count)
    field = vmem(3, nx, nz, ny)
    whole = vmem(nx, nz, ny)
    planes = vmem(2, nz, ny)
    two_rows = vmem(2, nx, ny)
    three_rows = vmem(3, nx, ny)

    to_col, e_low = kernel(
        edge_kernel, (planes, two_rows), [FAR], [e_start], "edge", 4, scratch=[vmem(2, nx, ROWS, ny), sem((2,))]
    )
    col = shifted(to_col, -1, 0)
    hgt = shifted(e_low, 0, -1)
    e, h, e_rows, h_high = kernel(
        load_kernel,
        (field, field, three_rows, two_rows),
        [FAR] * 2 + [WHOLE],
        [e_start, h_start, owners + nodes + my_col],
        "load",
        40,
        scratch=[sem((2,))],
    )
    begins, heights = starts_of(n_col, n_hgt, cap)
    place, flat = kernel(
        functools.partial(places_kernel, n_col, n_hgt, cap),
        (jax.ShapeDtypeStruct((1, count), jnp.int32), vmem(n_hgt * sum(heights), PTS)),
        [SCALARS, WHOLE, WHOLE],
        [my_col, owners, nodes],
        "places",
        8,
    )
    power = None
    for step in range(STEPS):
        first = step == 0
        h, to_col, h_high = kernel(
            h_edge_kernel,
            (field, planes, two_rows),
            [WHOLE] * 6,
            [e, col, hgt, e_rows, h_high, h],
            f"h_edge_{step}",
            4,
            {5: 0},
        )
        e_hgt = hgt
        col = shifted(to_col, 1, 0)
        hgt = shifted(h_high, 0, 1)
        if first:
            ca, cb, sigma, media_rows = kernel(
                coefficients_kernel,
                (whole, whole, whole, two_rows),
                [FAR] * 2 + [WHOLE],
                [far(cell_temp), far(region_tags), h_high],
                "coefficients",
                40,
                scratch=[vmem(nx, nz, ny), pltpu.VMEM((nx, nz, ny), jnp.int32), sem((2, 8))],
            )
        last = step == STEPS - 1
        outs = (field,) if last else (field, three_rows)
        h, *h_rows = kernel(h_rest_kernel, outs, [WHOLE] * 3, [e, e_hgt, h], f"h_rest_{step}", 40, {2: 0})
        media = [h, ca, cb, sigma]
        if last:
            e, power, h_out = pl.pallas_call(
                functools.partial(e_last_kernel, first),
                out_shape=(field, whole, pltpu.HBM((3, nx, nz, ny), F32)),
                in_specs=[WHOLE] * 8,
                out_specs=(WHOLE, WHOLE, FAR),
                input_output_aliases={6: 0, 7: 1},
                scratch_shapes=[sem],
                compiler_params=params(VMEM_MIB),
                cost_estimate=cost(cells * 50, cells * 50),
                name="e_last",
            )(*media, col, hgt, e, power)
            break
        order = place if step == 1 else my_col
        args = [order] + media + [col, hgt, media_rows, *h_rows, e_low, e] + ([] if first else [power])
        e, power, to_col, e_low = kernel(
            functools.partial(e_edge_kernel, first),
            (field, whole, planes, two_rows),
            [WHOLE if step == 1 else SCALARS] + [WHOLE] * (len(args) - 1),
            args,
            f"e_edge_{step}",
            5,
            {10: 0} if first else {10: 0, 11: 1},
        )
        h_hgt = hgt
        col = shifted(to_col, -1, 0)
        hgt = shifted(e_low, 0, -1)
        e, power, e_rows = kernel(
            functools.partial(e_rest_kernel, first),
            (field, whole, three_rows),
            [WHOLE] * 7,
            media + [h_hgt, e, power],
            f"e_rest_{step}",
            45,
            {5: 0, 6: 1},
        )

    mine, pair, other, e_out, _ = pl.pallas_call(
        functools.partial(pack_kernel, heights),
        out_shape=(
            pltpu.HBM((n_hgt, 2 * heights[0], PTS), F32),
            pltpu.HBM((n_hgt, heights[1], PTS), F32),
            pltpu.HBM((n_hgt, heights[2], PTS), F32),
            pltpu.HBM((3, nx, nz, ny), F32),
            vmem(n_hgt * sum(heights), PTS),
        ),
        in_specs=[SCALARS] + [WHOLE] * 3,
        out_specs=(FAR,) * 4 + (WHOLE,),
        input_output_aliases={2: 4},
        scratch_shapes=[sem((1 + 3 * n_hgt,))],
        compiler_params=params(VMEM_MIB),
        cost_estimate=cost(cells, cells * 36),
        name="pack",
    )(place.reshape(count), power, flat, e)

    def swap(x, axis):
        return lax.all_to_all(x, axis, split_axis=0, concat_axis=0, tiled=True)

    def across(x, turn):
        return lax.ppermute(x, "col", [(c, c ^ turn) for c in range(n_col)])

    def one_hot_space(sources):
        seats = sources * -(-cap // LANES) * LANES
        return [pltpu.VMEM((node_count, seats), jnp.bfloat16), pltpu.VMEM((seats, 2 * PTS), jnp.bfloat16)]

    node_rows = jax.ShapeDtypeStruct((node_count, PTS), F32)
    from_pair = across(pair, 1)
    other_blocks = swap(other, "hgt")
    sums = kernel(
        functools.partial(collect_kernel, cap),
        (node_rows,) * (n_col - 2),
        [WHOLE],
        [other_blocks],
        "collect_other",
        1,
        scratch=one_hot_space(n_hgt),
    )
    parts = [across(sums[turn - 2], turn) for turn in range(2, n_col)]
    mine = pl.pallas_call(
        merge_kernel,
        out_shape=pltpu.HBM((n_hgt, 2 * heights[0], PTS), F32),
        in_specs=[pl.BlockSpec(memory_space=pl.ANY), FAR],
        out_specs=FAR,
        input_output_aliases={1: 0},
        scratch_shapes=[sem((n_hgt,))],
        compiler_params=params(VMEM_MIB),
        cost_estimate=cost(1, 1),
        name="merge",
    )(from_pair, mine)
    mine_blocks = swap(mine, "hgt")
    own = kernel(
        functools.partial(collect_mine_kernel, cap),
        node_rows,
        [WHOLE],
        [mine_blocks],
        "collect_mine",
        1,
        scratch=one_hot_space(2 * n_hgt),
    )
    node_temp = kernel(
        finish_kernel, node_rows, [WHOLE] * (n_col), [node_enthalpy, own, *parts], "finish", 1
    )
    return e_out, h_out, node_temp


def solution(mesh):
    placed = (
        P(None, "col", "hgt", None),
        P(None, "col", "hgt", None),
        P("col", "hgt", None),
        P("col", "hgt", None),
        P("col", "hgt", None, None, None, None),
        P("col", "hgt", None, None, None),
        P(("col", "hgt"), None),
    )
    return jax.shard_map(
        per_device,
        mesh=mesh,
        in_specs=placed,
        out_specs=(
            P(None, "col", "hgt", None),
            P(None, "col", "hgt", None),
            P(("col", "hgt"), None),
        ),
        check_vma=False,
    )
```

```python
import functools

import jax
import jax.numpy as jnp
from jax import lax
from jax.experimental import pallas as pl
from jax.experimental.pallas import tpu as pltpu
from jax.sharding import PartitionSpec as P

PTS = 128
STEPS = 4
COURANT = 0.55
LANES = 128
ROWS = 8
F32 = jnp.float32
VMEM_MIB = 20

WHOLE = pl.BlockSpec(memory_space=pltpu.VMEM)
SCALARS = pl.BlockSpec(memory_space=pltpu.SMEM)
FAR = pl.BlockSpec(memory_space=pltpu.HBM)


def vmem(*shape):
    return pltpu.VMEM(shape, F32)


def far(x):
    return pltpu.with_memory_space_constraint(x, pltpu.HBM)


def params(mib):
    return pltpu.CompilerParams(vmem_limit_bytes=mib << 20)


def cost(flops, moved):
    return pl.CostEstimate(flops=flops, bytes_accessed=moved, transcendentals=0)


def after_y(f):
    lane = lax.broadcasted_iota(jnp.int32, (ROWS, LANES), 1)
    n = f.shape[1] // LANES
    turned = [pltpu.roll(f[:, k * LANES : (k + 1) * LANES], LANES - 1, 1) for k in range(n)]
    turned.append(jnp.zeros((ROWS, LANES), F32))
    return jnp.concatenate([jnp.where(lane < LANES - 1, turned[k], turned[k + 1]) for k in range(n)], 1)


def before_y(f):
    lane = lax.broadcasted_iota(jnp.int32, (ROWS, LANES), 1)
    n = f.shape[1] // LANES
    turned = [jnp.zeros((ROWS, LANES), F32)]
    turned += [pltpu.roll(f[:, k * LANES : (k + 1) * LANES], 1, 1) for k in range(n)]
    return jnp.concatenate([jnp.where(lane > 0, turned[k + 1], turned[k]) for k in range(n)], 1)


def after_row(f, row):
    place = lax.broadcasted_iota(jnp.int32, f.shape, 0)
    return jnp.where(place < ROWS - 1, pltpu.roll(f, ROWS - 1, 0), jnp.broadcast_to(row, f.shape))


def before_row(f, row):
    place = lax.broadcasted_iota(jnp.int32, f.shape, 0)
    return jnp.where(place > 0, pltpu.roll(f, 1, 0), jnp.broadcast_to(row, f.shape))


def on(predicate, even, odd):
    pl.when(predicate)(even)
    pl.when(jnp.logical_not(predicate))(odd)


def edge_kernel(spot, e, h, order, col_even, col_odd, sems):
    last = e.shape[1] - 1

    def send(fwd, back):
        def run():
            copies = [
                pltpu.make_async_copy(e.at[:, last], fwd.at[pl.ds(0, 3)], sems.at[0]),
                pltpu.make_async_copy(h.at[pl.ds(1, 2), last], fwd.at[pl.ds(3, 2)], sems.at[1]),
                pltpu.make_async_copy(e.at[:, 0], back.at[pl.ds(0, 3)], sems.at[2]),
                pltpu.make_async_copy(e.at[pl.ds(1, 2), 0], back.at[pl.ds(3, 2)], sems.at[3]),
            ]
            for copy in copies:
                copy.start()
            for copy in copies:
                copy.wait()

        return run

    on(lax.rem(spot[0], 2) == 0, send(col_even, col_odd), send(col_odd, col_even))


def load_kernel(
    spot, temp_far, tags_far, e_far, h_far, ca, cb, sigma_out, e, h, own_rows, *refs
):
    hgt_even, hgt_odd, diag_even, diag_odd, temp, tags, sems = refs
    nx, nz, _ = temp.shape
    parts = 4
    size = nx // parts
    copies = []
    for part in range(parts):
        here = pl.ds(part * size, size)
        copies.append(pltpu.make_async_copy(temp_far.at[here], temp.at[here], sems.at[0, part]))
        copies.append(pltpu.make_async_copy(tags_far.at[here], tags.at[here], sems.at[1, part]))
    e_copy = pltpu.make_async_copy(e_far, e, sems.at[2, 0])
    h_copy = pltpu.make_async_copy(h_far, h, sems.at[2, 1])
    for copy in copies:
        copy.start()
    e_copy.start()
    h_copy.start()

    def plane(x, carry):
        for z in range(0, nz, ROWS):
            tag = tags[x, z : z + ROWS, :]
            lean = tag == 0
            fat = tag == 1
            frac = 1.0 / (1.0 + jnp.exp(-2.0 * temp[x, z : z + ROWS, :]))
            eps_low = jnp.where(lean, 4.0, jnp.where(fat, 2.5, 5.0))
            eps_rise = jnp.where(lean, 46.0, jnp.where(fat, 3.5, 5.0))
            sig_low = jnp.where(lean, 0.2, jnp.where(fat, 0.05, 0.1))
            sig_rise = jnp.where(lean, 7.8, jnp.where(fat, 0.35, 0.9))
            eps = eps_low + eps_rise * frac
            sigma = sig_low + sig_rise * frac
            half = (0.5 * COURANT) * sigma
            inverse = 1.0 / (eps + half)
            ca[x, z : z + ROWS, :] = (eps - half) * inverse
            cb[x, z : z + ROWS, :] = COURANT * inverse
            sigma_out[x, z : z + ROWS, :] = sigma
        return carry

    for part in range(parts):
        copies[2 * part].wait()
        copies[2 * part + 1].wait()
        lax.fori_loop(part * size, (part + 1) * size, plane, 0)
    e_copy.wait()
    h_copy.wait()

    pass_on(spot, e, own_rows, hgt_even, hgt_odd, diag_even, diag_odd, h)


def pass_on(spot, e, own_rows, hgt_even, hgt_odd, diag_even, diag_odd, h=None):
    nx, nz = e.shape[1:3]

    def send(fwd, back):
        def run():
            def rows(x, carry):
                for comp in range(3):
                    fwd[comp, pl.ds(x, 1), :] = e[comp, x, nz - 1 : nz, :]
                    low = e[comp, x, 0:1, :]
                    back[comp, pl.ds(x, 1), :] = low
                    if comp < 2:
                        own_rows[comp, pl.ds(x, 1), :] = low
                if h is not None:
                    for comp in range(2):
                        fwd[3 + comp, pl.ds(x, 1), :] = h[comp, x, nz - 1 : nz, :]
                        back[3 + comp, pl.ds(x, 1), :] = e[comp, x, 0:1, :]
                return carry

            lax.fori_loop(0, nx, rows, 0)

        return run

    on(lax.rem(spot[1], 2) == 0, send(hgt_even, hgt_odd), send(hgt_odd, hgt_even))

    def corners(fwd, back):
        def run():
            fwd[...] = e[0, nx - 1, 0:1, :]
            back[...] = e[2, 0, nz - 1 : nz, :]

        return run

    on(lax.rem(spot[0], 2) == 0, corners(diag_even, diag_odd), corners(diag_odd, diag_even))


def over(first, stop, body):
    if stop - first == 1:
        body(first)
    else:

        def step(x, carry):
            body(x)
            return carry

        lax.fori_loop(first, stop, step, 0)


def h_tile(e, h, col, hgt, x, z):
    nz = e.shape[2]
    here = slice(z, z + ROWS)
    ex, ey, ez = (e[comp, x, here, :] for comp in range(3))
    if z + ROWS < nz:
        row_x, row_y = (e[comp, x, z + ROWS : z + ROWS + 1, :] for comp in range(2))
    else:
        row_x, row_y = (hgt[comp, pl.ds(x, 1), :] for comp in range(2))
    if col is None:
        next_y, next_z = (e[comp, x + 1, here, :] for comp in (1, 2))
    else:
        next_y, next_z = (col[comp, here, :] for comp in (1, 2))
    h[0, x, here, :] = h[0, x, here, :] - COURANT * ((after_y(ez) - ez) - (after_row(ey, row_y) - ey))
    hy = h[1, x, here, :] - COURANT * ((after_row(ex, row_x) - ex) - (next_z - ez))
    hz = h[2, x, here, :] - COURANT * ((next_y - ey) - (after_y(ex) - ex))
    h[1, x, here, :] = hy
    h[2, x, here, :] = hz
    return hy, hz


def e_tile(first, h, e, power, ca, cb, sigma, col, hgt, x, z):
    here = slice(z, z + ROWS)
    hx, hy, hz = (h[comp, x, here, :] for comp in range(3))
    if z > 0:
        row_x, row_y = (h[comp, x, z - 1 : z, :] for comp in range(2))
    else:
        row_x, row_y = (hgt[comp, pl.ds(x, 1), :] for comp in range(2))
    if col is None:
        past_y, past_z = (h[comp, x - 1, here, :] for comp in (1, 2))
    else:
        past_y, past_z = (col[comp, here, :] for comp in range(2))
    keep = ca[x, here, :]
    drive = cb[x, here, :]
    ex = keep * e[0, x, here, :] + drive * ((hz - before_y(hz)) - (hy - before_row(hy, row_y)))
    ey = keep * e[1, x, here, :] + drive * ((hx - before_row(hx, row_x)) - (hz - past_z))
    ez = keep * e[2, x, here, :] + drive * ((hy - past_y) - (hx - before_y(hx)))
    e[0, x, here, :] = ex
    e[1, x, here, :] = ey
    e[2, x, here, :] = ez
    heat = sigma[x, here, :] * (ex * ex + ey * ey + ez * ez)
    power[x, here, :] = heat if first else power[x, here, :] + heat
    return ey, ez


def step_kernel(first, last, *refs):
    spot, h_old, e_old, ca, cb, sigma, own_old, col_even, col_odd, hgt_even, hgt_odd, diag_even, diag_odd = refs[:13]
    refs = refs[13:]
    if not first:
        beyond_old, below_old, power_old = refs[:3]
        refs = refs[3:]
    h, e, power, beyond, below = refs[:5]
    refs = refs[5:]
    if last:
        h_out = refs[0]
        refs = refs[1:]
    else:
        own_rows, to_col_even, to_col_odd, to_hgt_even, to_hgt_odd, to_diag_even, to_diag_odd = refs[:7]
        refs = refs[7:]
    col_fwd, col_back, hgt_fwd, hgt_back, corner_x, corner_z = refs[:6]
    nx, nz = e.shape[1:3]
    first_col = lax.rem(spot[0], 2) == 0
    first_hgt = lax.rem(spot[1], 2) == 0

    def take(pairs):
        def run():
            for target, source in pairs:
                target[...] = source[0 : target.shape[0]]

        return run

    on(
        first_col,
        take([(col_fwd, col_odd), (col_back, col_even), (corner_x, diag_odd), (corner_z, diag_even)]),
        take([(col_fwd, col_even), (col_back, col_odd), (corner_x, diag_even), (corner_z, diag_odd)]),
    )
    on(
        first_hgt,
        take([(hgt_fwd, hgt_odd), (hgt_back, hgt_even)]),
        take([(hgt_fwd, hgt_even), (hgt_back, hgt_odd)]),
    )
    inside_x = COURANT * jnp.where(spot[0] > 0, 1.0, 0.0)
    inside_z = COURANT * jnp.where(spot[1] > 0, 1.0, 0.0)

    for z in range(0, nz, ROWS):
        here = slice(z, z + ROWS)
        ex, ey, ez = (col_fwd[comp, here, :] for comp in range(3))
        row = col_fwd[0, z + ROWS : z + ROWS + 1, :] if z + ROWS < nz else corner_x[...]
        hy = col_fwd[3, here, :] if first else beyond_old[0, here, :]
        hz = col_fwd[4, here, :] if first else beyond_old[1, here, :]
        beyond[0, here, :] = hy - inside_x * ((after_row(ex, row) - ex) - (e[2, 0, here, :] - ez))
        beyond[1, here, :] = hz - inside_x * ((e[1, 0, here, :] - ey) - (after_y(ex) - ex))
    for x in range(0, nx, ROWS):
        here = slice(x, x + ROWS)
        ex, ey, ez = (hgt_fwd[comp, here, :] for comp in range(3))
        row = hgt_fwd[2, x + ROWS : x + ROWS + 1, :] if x + ROWS < nx else corner_z[...]
        hx = hgt_fwd[3, here, :] if first else below_old[0, here, :]
        hy = hgt_fwd[4, here, :] if first else below_old[1, here, :]
        below[0, here, :] = hx - inside_z * ((after_y(ez) - ez) - (own_old[1, here, :] - ey))
        below[1, here, :] = hy - inside_z * ((own_old[0, here, :] - ex) - (after_row(ez, row) - ez))

    def h_plane(x):
        for z in range(0, nz, ROWS):
            h_tile(e, h, col_back if isinstance(x, int) else None, hgt_back, x, z)

    over(0, nx - 1, h_plane)
    h_plane(nx - 1)
    if last:
        copy = pltpu.make_async_copy(h, h_out, refs[6])
        copy.start()

    def e_plane(x):
        for z in range(0, nz, ROWS):
            e_tile(first, h, e, power, ca, cb, sigma, beyond if isinstance(x, int) else None, below, x, z)

    e_plane(0)
    over(1, nx, e_plane)
    if last:
        copy.wait()
        return

    def send(fwd, back):
        def run():
            fwd[...] = e[:, nx - 1]
            back[...] = e[:, 0]

        return run

    on(first_col, send(to_col_even, to_col_odd), send(to_col_odd, to_col_even))
    pass_on(spot, e, own_rows, to_hgt_even, to_hgt_odd, to_diag_even, to_diag_odd)


def places_kernel(n_col, n_hgt, cap, my_col, owner, node, place, flat):
    n_dev = n_col * n_hgt
    count = owner.shape[1]
    width = 256
    rows = lax.broadcasted_iota(jnp.int32, (n_dev, width), 0)
    before = lax.broadcasted_iota(jnp.int32, (width, width), 0)
    after = lax.broadcasted_iota(jnp.int32, (width, width), 1)
    upper = jnp.where(before <= after, 1.0, 0.0).astype(jnp.bfloat16)
    per = -(-cap // LANES)
    room_for = per * LANES
    room = lax.broadcasted_iota(jnp.int32, (room_for, width), 0)
    total = jnp.zeros((n_dev, 1), F32)
    parts_of = jnp.zeros((2 * n_dev, room_for), F32)
    nt = (((1,), (1,)), ((), ()))
    begins, heights = starts_of(n_col, n_hgt, cap)
    for start in range(0, count, width):
        own = owner[:, start : start + width]
        hit = jnp.where(rows == own, 1.0, 0.0)
        running = total + jnp.dot(hit.astype(jnp.bfloat16), upper, preferred_element_type=F32)
        total = running[:, width - 1 : width]
        rank = jnp.sum(hit * running, axis=0, keepdims=True).astype(jnp.int32) - 1
        turn = lax.bitwise_xor(lax.div(own, n_hgt), my_col[0])
        own_hgt = lax.rem(own, n_hgt)
        begin = jnp.where(
            turn == 0,
            begins[0] + own_hgt * heights[0],
            jnp.where(
                turn == 1,
                begins[1] + own_hgt * heights[1],
                begins[2] + own_hgt * heights[2] + (turn - 2) * cap,
            ),
        )
        place[:, start : start + width] = begin + rank
        number = node[:, start : start + width]
        upper_part = lax.div(number, 16)
        lower_part = number - 16 * upper_part
        seat = jnp.where(room == rank, 1.0, 0.0).astype(jnp.bfloat16)
        both = jnp.concatenate([hit * upper_part.astype(F32), hit * lower_part.astype(F32)], 0)
        parts_of = parts_of + lax.dot_general(both.astype(jnp.bfloat16), seat, nt, preferred_element_type=F32)
    taken = lax.broadcasted_iota(jnp.int32, (n_dev, room_for), 1).astype(F32) < total
    table = jnp.where(taken, 16.0 * parts_of[:n_dev] + parts_of[n_dev:], -1.0)
    chunk = 8 * ROWS

    def clear(i, carry):
        flat[pl.ds(pl.multiple_of(i * chunk, chunk), chunk), :] = jnp.zeros((chunk, PTS), F32)
        return carry

    lax.fori_loop(0, flat.shape[0] // chunk, clear, 0)
    for at in range(flat.shape[0] // chunk * chunk, flat.shape[0], ROWS):
        flat[at : at + ROWS, :] = jnp.zeros((ROWS, PTS), F32)
    behind = [cap, cap, (n_col - 2) * cap]
    for begin, height, skip in zip(begins, heights, behind):
        for part in range(n_hgt):
            at = begin + part * height
            flat[at + skip : at + height, :] = jnp.full((height - skip, PTS), -1.0, F32)
    for group in range(n_col):
        turn = lax.bitwise_xor(jnp.int32(group), my_col[0])
        kind = jnp.minimum(turn, 2)
        begin = jnp.where(kind == 0, begins[0], jnp.where(kind == 1, begins[1], begins[2]))
        height = jnp.where(kind == 2, heights[2], heights[0])
        skip = jnp.where(kind == 2, behind[2] + (turn - 2) * per, cap)
        for part in range(n_hgt):
            at = group * n_hgt + part
            for piece in range(per):
                row = table[at : at + 1, piece * LANES : (piece + 1) * LANES]
                flat[pl.ds(begin + part * height + skip + piece, 1), :] = row


def table_rows(parts, cap):
    return -(-parts * -(-cap // LANES) // ROWS) * ROWS


def starts_of(n_col, n_hgt, cap):
    one = cap + table_rows(1, cap)
    heights = [one, one, (n_col - 2) * cap + table_rows(n_col - 2, cap)]
    return [0, n_hgt * heights[0], n_hgt * (heights[0] + heights[1])], heights


def pack_kernel(heights, place, power, flat_old, e, mine, pair, other, e_out, flat, sems):
    nx, nz, ny = power.shape
    e_copy = pltpu.make_async_copy(e, e_out, sems.at[0])
    e_copy.start()
    per_row = ny // PTS

    def plane(x, carry):
        for z in range(nz):
            for k in range(per_row):
                spot = place[x * (nz * per_row) + z * per_row + k]
                flat[pl.ds(spot, 1), :] = power[x, z : z + 1, k * PTS : (k + 1) * PTS]
        return carry

    lax.fori_loop(0, nx, plane, 0)
    copies = []
    first = 0
    for out, rows in zip((mine, pair, other), heights):
        for group in range(out.shape[0]):
            target = out.at[group, pl.ds(0, rows)]
            copies.append(pltpu.make_async_copy(flat.at[pl.ds(first, rows)], target, sems.at[1 + len(copies)]))
            first += rows
    for copy in copies:
        copy.start()
    for copy in copies:
        copy.wait()
    e_copy.wait()


def summed(blocks, first, cap, node_row, chosen, split, node_count):
    ids = lax.broadcasted_iota(jnp.int32, (node_count, LANES), 0).astype(F32)
    n_from, _, pts = blocks.shape
    per = -(-cap // LANES)
    many = len(first)
    for source in range(n_from):
        for i in range(many):
            seat = (source * many + i) * per * LANES
            for piece in range(per):
                row = node_row[i] + piece
                lanes = slice(seat + piece * LANES, seat + (piece + 1) * LANES)
                hit = ids == blocks[source, row : row + 1, :]
                chosen[:, lanes] = jnp.where(hit, 1.0, 0.0).astype(jnp.bfloat16)
            values = blocks[source, first[i] : first[i] + cap, :]
            high = values.astype(jnp.bfloat16)
            split[seat : seat + cap, 0:pts] = high
            split[seat : seat + cap, pts : 2 * pts] = (values - high.astype(F32)).astype(jnp.bfloat16)
    both = jnp.dot(chosen[...], split[...], preferred_element_type=F32)
    return both[:, 0:pts] + both[:, pts : 2 * pts]


def collect_kernel(cap, blocks, *refs):
    *outs, chosen, split = refs
    per = -(-cap // LANES)
    split[...] = jnp.zeros(split.shape, split.dtype)
    for part, out in enumerate(outs):
        out[...] = summed(blocks, [part * cap], cap, [len(outs) * cap + part * per], chosen, split, out.shape[0])


def merge_kernel(pair, mine_old, mine, sems):
    rows = pair.shape[1]
    copies = [
        pltpu.make_async_copy(pair.at[group], mine.at[group, pl.ds(rows, rows)], sems.at[group])
        for group in range(mine.shape[0])
    ]
    for copy in copies:
        copy.start()
    for copy in copies:
        copy.wait()


def collect_mine_kernel(cap, blocks, out, chosen, split):
    half = blocks.shape[1] // 2
    split[...] = jnp.zeros(split.shape, split.dtype)
    out[...] = summed(blocks, [0, half], cap, [cap, half + cap], chosen, split, out.shape[0])


def finish_kernel(enthalpy, *refs):
    *parts, out = refs
    heat = parts[0][...]
    for part in parts[1:]:
        heat = heat + part[...]
    content = enthalpy[...] + (0.25 / STEPS) * heat
    out[...] = jnp.where(content < 0.0, content / 2.0, jnp.where(content > 1.0, (content - 1.0) / 3.0, 0.0))


def swapped(block, d_col, d_hgt, odd):
    n_col = lax.axis_size("col")
    n_hgt = lax.axis_size("hgt")
    route = []
    for c in range(n_col):
        for h in range(n_hgt):
            place = c if d_col else h
            if place % 2 == odd and 0 <= c + d_col < n_col and 0 <= h + d_hgt < n_hgt:
                pair = (c * n_hgt + h, (c + d_col) * n_hgt + h + d_hgt)
                route += [pair, pair[::-1]]
    return lax.ppermute(block, ("col", "hgt"), route)


def per_device(
    efield_lattice_vector,
    hfield_lattice_vector,
    cell_temp,
    region_tags,
    block_owner,
    block_node,
    node_enthalpy,
):
    nx, nz, ny = cell_temp.shape
    n_col = lax.axis_size("col")
    n_hgt = lax.axis_size("hgt")
    n_dev = n_col * n_hgt
    count = nx * nz * ny // PTS
    cap = 2 * count // n_dev
    node_count = node_enthalpy.shape[0]
    cells = nx * nz * ny
    sem = pltpu.SemaphoreType.DMA

    def kernel(body, outs, ins, args, name, work, aliases=None, scratch=()):
        return pl.pallas_call(
            body,
            out_shape=outs,
            in_specs=ins,
            out_specs=jax.tree.map(lambda out: WHOLE, outs),
            input_output_aliases=aliases or {},
            scratch_shapes=scratch,
            compiler_params=params(VMEM_MIB),
            cost_estimate=cost(work * cells, work * cells),
            name=name,
        )(*args)

    e_start = far(efield_lattice_vector)
    h_start = far(hfield_lattice_vector)
    spot = jnp.stack([lax.axis_index("col"), lax.axis_index("hgt")]).astype(jnp.int32)
    owners = block_owner.reshape(1, count)
    nodes = block_node.reshape(1, count)
    field = vmem(3, nx, nz, ny)
    whole = vmem(nx, nz, ny)
    pair_planes = vmem(2, nz, ny)
    pair_rows = vmem(2, nx, ny)
    row = vmem(1, ny)

    def exchange(to_col_even, to_col_odd, to_hgt_even, to_hgt_odd, to_diag_even, to_diag_odd):
        return (
            swapped(to_col_even, 1, 0, 0) if to_col_even is not None else None,
            swapped(to_col_odd, 1, 0, 1) if to_col_odd is not None else None,
            swapped(to_hgt_even, 0, 1, 0),
            swapped(to_hgt_odd, 0, 1, 1),
            swapped(to_diag_even, 1, -1, 0),
            swapped(to_diag_odd, 1, -1, 1),
        )

    to_col_even, to_col_odd = kernel(
        edge_kernel,
        (vmem(5, nz, ny), vmem(5, nz, ny)),
        [SCALARS, FAR, FAR, WHOLE],
        [spot, e_start, h_start, owners + nodes],
        "edge",
        4,
        scratch=[sem((4,))],
    )
    col = (swapped(to_col_even, 1, 0, 0), swapped(to_col_odd, 1, 0, 1))
    ca, cb, sigma, e, h, own_rows, *sends = kernel(
        load_kernel,
        (whole, whole, whole, field, field, pair_rows, vmem(5, nx, ny), vmem(5, nx, ny), row, row),
        [SCALARS] + [FAR] * 4,
        [spot, far(cell_temp), far(region_tags), e_start, h_start],
        "load",
        60,
        scratch=[vmem(nx, nz, ny), pltpu.VMEM((nx, nz, ny), jnp.int32), sem((3, 4))],
    )
    others = exchange(None, None, *sends)[2:]
    begins, heights = starts_of(n_col, n_hgt, cap)
    place, flat = kernel(
        functools.partial(places_kernel, n_col, n_hgt, cap),
        (jax.ShapeDtypeStruct((1, count), jnp.int32), vmem(n_hgt * sum(heights), PTS)),
        [SCALARS, WHOLE, WHOLE],
        [spot, owners, nodes],
        "places",
        8,
    )
    beyond = below = power = None
    for step in range(STEPS):
        first = step == 0
        last = step == STEPS - 1
        args = [spot, h, e, ca, cb, sigma, own_rows, *col, *others]
        aliases = {1: 0, 2: 1}
        if not first:
            args += [beyond, below, power]
            aliases[15] = 2
        outs = [field, field, whole, pair_planes, pair_rows]
        if last:
            outs += [pltpu.HBM((3, nx, nz, ny), F32)]
        else:
            outs += [pair_rows] + [vmem(3, nz, ny)] * 2 + [vmem(3, nx, ny)] * 2 + [row] * 2
        deep = 5 if first else 3
        scratch = [vmem(deep, nz, ny), vmem(3, nz, ny), vmem(deep, nx, ny), vmem(2, nx, ny), row, row]
        outs = pl.pallas_call(
            functools.partial(step_kernel, first, last),
            out_shape=tuple(outs),
            in_specs=[SCALARS] + [WHOLE] * (len(args) - 1),
            out_specs=(WHOLE,) * 5 + ((FAR,) if last else (WHOLE,) * 7),
            input_output_aliases=aliases,
            scratch_shapes=scratch + ([sem] if last else []),
            compiler_params=params(VMEM_MIB),
            cost_estimate=cost(cells * 100, cells * 100),
            name=f"step_{step}",
        )(*args)
        h, e, power, beyond, below = outs[:5]
        if last:
            h_out = outs[5]
        else:
            own_rows = outs[5]
            received = exchange(*outs[6:])
            col, others = received[:2], received[2:]

    mine, pair, other, e_out, _ = pl.pallas_call(
        functools.partial(pack_kernel, heights),
        out_shape=(
            pltpu.HBM((n_hgt, 2 * heights[0], PTS), F32),
            pltpu.HBM((n_hgt, heights[1], PTS), F32),
            pltpu.HBM((n_hgt, heights[2], PTS), F32),
            pltpu.HBM((3, nx, nz, ny), F32),
            vmem(n_hgt * sum(heights), PTS),
        ),
        in_specs=[SCALARS] + [WHOLE] * 3,
        out_specs=(FAR,) * 4 + (WHOLE,),
        input_output_aliases={2: 4},
        scratch_shapes=[sem((1 + 3 * n_hgt,))],
        compiler_params=params(VMEM_MIB),
        cost_estimate=cost(cells, cells * 36),
        name="pack",
    )(place.reshape(count), power, flat, e)

    def swap(x, axis):
        return lax.all_to_all(x, axis, split_axis=0, concat_axis=0, tiled=True)

    def across(x, turn):
        return lax.ppermute(x, "col", [(c, c ^ turn) for c in range(n_col)])

    def one_hot_space(sources):
        seats = sources * -(-cap // LANES) * LANES
        return [pltpu.VMEM((node_count, seats), jnp.bfloat16), pltpu.VMEM((seats, 2 * PTS), jnp.bfloat16)]

    node_rows = jax.ShapeDtypeStruct((node_count, PTS), F32)
    from_pair = across(pair, 1)
    other_blocks = swap(other, "hgt")
    sums = kernel(
        functools.partial(collect_kernel, cap),
        (node_rows,) * (n_col - 2),
        [WHOLE],
        [other_blocks],
        "collect_other",
        1,
        scratch=one_hot_space(n_hgt),
    )
    parts = [across(sums[turn - 2], turn) for turn in range(2, n_col)]
    mine = pl.pallas_call(
        merge_kernel,
        out_shape=pltpu.HBM((n_hgt, 2 * heights[0], PTS), F32),
        in_specs=[pl.BlockSpec(memory_space=pl.ANY), FAR],
        out_specs=FAR,
        input_output_aliases={1: 0},
        scratch_shapes=[sem((n_hgt,))],
        compiler_params=params(VMEM_MIB),
        cost_estimate=cost(1, 1),
        name="merge",
    )(from_pair, mine)
    mine_blocks = swap(mine, "hgt")
    own = kernel(
        functools.partial(collect_mine_kernel, cap),
        node_rows,
        [WHOLE],
        [mine_blocks],
        "collect_mine",
        1,
        scratch=one_hot_space(2 * n_hgt),
    )
    node_temp = kernel(
        finish_kernel, node_rows, [WHOLE] * (n_col), [node_enthalpy, own, *parts], "finish", 1
    )
    return e_out, h_out, node_temp


def solution(mesh):
    placed = (
        P(None, "col", "hgt", None),
        P(None, "col", "hgt", None),
        P("col", "hgt", None),
        P("col", "hgt", None),
        P("col", "hgt", None, None, None, None),
        P("col", "hgt", None, None, None),
        P(("col", "hgt"), None),
    )
    return jax.shard_map(
        per_device,
        mesh=mesh,
        in_specs=placed,
        out_specs=(
            P(None, "col", "hgt", None),
            P(None, "col", "hgt", None),
            P(("col", "hgt"), None),
        ),
        check_vma=False,
    )
```

```python
import functools

import jax
import jax.numpy as jnp
from jax import lax
from jax.experimental import pallas as pl
from jax.experimental.pallas import tpu as pltpu
from jax.sharding import PartitionSpec as P

PTS = 128
STEPS = 4
COURANT = 0.55
LANES = 128
ROWS = 8
F32 = jnp.float32
VMEM_MIB = 20

WHOLE = pl.BlockSpec(memory_space=pltpu.VMEM)
SCALARS = pl.BlockSpec(memory_space=pltpu.SMEM)
FAR = pl.BlockSpec(memory_space=pltpu.HBM)


def vmem(*shape):
    return pltpu.VMEM(shape, F32)


def far(x):
    return pltpu.with_memory_space_constraint(x, pltpu.HBM)


def params(mib):
    return pltpu.CompilerParams(vmem_limit_bytes=mib << 20)


def cost(flops, moved):
    return pl.CostEstimate(flops=flops, bytes_accessed=moved, transcendentals=0)


def after_y(f):
    lane = lax.broadcasted_iota(jnp.int32, (ROWS, LANES), 1)
    n = f.shape[1] // LANES
    turned = [pltpu.roll(f[:, k * LANES : (k + 1) * LANES], LANES - 1, 1) for k in range(n)]
    turned.append(jnp.zeros((ROWS, LANES), F32))
    return jnp.concatenate([jnp.where(lane < LANES - 1, turned[k], turned[k + 1]) for k in range(n)], 1)


def before_y(f):
    lane = lax.broadcasted_iota(jnp.int32, (ROWS, LANES), 1)
    n = f.shape[1] // LANES
    turned = [jnp.zeros((ROWS, LANES), F32)]
    turned += [pltpu.roll(f[:, k * LANES : (k + 1) * LANES], 1, 1) for k in range(n)]
    return jnp.concatenate([jnp.where(lane > 0, turned[k + 1], turned[k]) for k in range(n)], 1)


def after_row(f, row):
    place = lax.broadcasted_iota(jnp.int32, f.shape, 0)
    return jnp.where(place < ROWS - 1, pltpu.roll(f, ROWS - 1, 0), jnp.broadcast_to(row, f.shape))


def before_row(f, row):
    place = lax.broadcasted_iota(jnp.int32, f.shape, 0)
    return jnp.where(place > 0, pltpu.roll(f, 1, 0), jnp.broadcast_to(row, f.shape))


def edge_kernel(e, to_col, sem):
    copy = pltpu.make_async_copy(e.at[pl.ds(1, 2), 0], to_col, sem)
    copy.start()
    copy.wait()


def low_kernel(e, order, to_hgt, low, sem):
    nx = e.shape[1]
    copy = pltpu.make_async_copy(e.at[pl.ds(0, 2), :, pl.ds(0, ROWS)], low, sem)
    copy.start()
    copy.wait()
    for x in range(nx):
        for comp in range(2):
            to_hgt[comp, x : x + 1, :] = low[comp, x, 0:1, :]


def load_kernel(
    temp_far, tags_far, e_far, h_far, order, ca, cb, sigma_out, e, h, media_rows, e_rows, h_rows, temp, tags, sems
):
    nx, nz, _ = temp.shape
    parts = 4
    size = nx // parts
    copies = []
    for part in range(parts):
        here = pl.ds(part * size, size)
        copies.append(pltpu.make_async_copy(temp_far.at[here], temp.at[here], sems.at[0, part]))
        copies.append(pltpu.make_async_copy(tags_far.at[here], tags.at[here], sems.at[1, part]))
    fields = []
    for comp in range(3):
        for part in range(parts):
            here = pl.ds(part * size, size)
            fields.append(pltpu.make_async_copy(e_far.at[comp, here], e.at[comp, here], sems.at[2 + comp, part]))
            fields.append(pltpu.make_async_copy(h_far.at[comp, here], h.at[comp, here], sems.at[5 + comp, part]))
    for copy in copies + fields:
        copy.start()

    def plane(x, carry):
        for z in range(0, nz, ROWS):
            tag = tags[x, z : z + ROWS, :]
            lean = tag == 0
            fat = tag == 1
            frac = 1.0 / (1.0 + jnp.exp(-2.0 * temp[x, z : z + ROWS, :]))
            eps_low = jnp.where(lean, 4.0, jnp.where(fat, 2.5, 5.0))
            eps_rise = jnp.where(lean, 46.0, jnp.where(fat, 3.5, 5.0))
            sig_low = jnp.where(lean, 0.2, jnp.where(fat, 0.05, 0.1))
            sig_rise = jnp.where(lean, 7.8, jnp.where(fat, 0.35, 0.9))
            eps = eps_low + eps_rise * frac
            sigma = sig_low + sig_rise * frac
            half = (0.5 * COURANT) * sigma
            inverse = 1.0 / (eps + half)
            ca[x, z : z + ROWS, :] = (eps - half) * inverse
            cb[x, z : z + ROWS, :] = COURANT * inverse
            sigma_out[x, z : z + ROWS, :] = sigma
        media_rows[0, pl.ds(x, 1), :] = ca[x, 0:1, :]
        media_rows[1, pl.ds(x, 1), :] = cb[x, 0:1, :]
        return carry

    for part in range(parts):
        copies[2 * part].wait()
        copies[2 * part + 1].wait()
        lax.fori_loop(part * size, (part + 1) * size, plane, 0)
    for copy in fields:
        copy.wait()

    def rows(x, carry):
        for comp in range(3):
            e_rows[comp, pl.ds(x, 1), :] = e[comp, x, nz - 1 : nz, :]
        for comp in range(2):
            h_rows[comp, pl.ds(x, 1), :] = h[comp, x, nz - 1 : nz, :]
        return carry

    lax.fori_loop(0, nx, rows, 0)


def over(first, stop, body):
    if stop - first == 1:
        body(first)
    else:

        def step(x, carry):
            body(x)
            return carry

        lax.fori_loop(first, stop, step, 0)


def h_tile(e, h, col, hgt, x, z):
    nz = e.shape[2]
    here = slice(z, z + ROWS)
    ex, ey, ez = (e[comp, x, here, :] for comp in range(3))
    if z + ROWS < nz:
        row_x, row_y = (e[comp, x, z + ROWS : z + ROWS + 1, :] for comp in range(2))
    else:
        row_x, row_y = (hgt[comp, pl.ds(x, 1), :] for comp in range(2))
    if col is None:
        next_y, next_z = (e[comp, x + 1, here, :] for comp in (1, 2))
    else:
        next_y, next_z = (col[comp, here, :] for comp in range(2))
    h[0, x, here, :] = h[0, x, here, :] - COURANT * ((after_y(ez) - ez) - (after_row(ey, row_y) - ey))
    hy = h[1, x, here, :] - COURANT * ((after_row(ex, row_x) - ex) - (next_z - ez))
    hz = h[2, x, here, :] - COURANT * ((next_y - ey) - (after_y(ex) - ex))
    h[1, x, here, :] = hy
    h[2, x, here, :] = hz
    return hy, hz


def e_tile(first, h, e, power, ca, cb, sigma, col, hgt, x, z):
    here = slice(z, z + ROWS)
    hx, hy, hz = (h[comp, x, here, :] for comp in range(3))
    if z > 0:
        row_x, row_y = (h[comp, x, z - 1 : z, :] for comp in range(2))
    else:
        row_x, row_y = (hgt[comp, pl.ds(x, 1), :] for comp in range(2))
    if col is None:
        past_y, past_z = (h[comp, x - 1, here, :] for comp in (1, 2))
    else:
        past_y, past_z = (col[comp, here, :] for comp in range(2))
    keep = ca[x, here, :]
    drive = cb[x, here, :]
    ex = keep * e[0, x, here, :] + drive * ((hz - before_y(hz)) - (hy - before_row(hy, row_y)))
    ey = keep * e[1, x, here, :] + drive * ((hx - before_row(hx, row_x)) - (hz - past_z))
    ez = keep * e[2, x, here, :] + drive * ((hy - past_y) - (hx - before_y(hx)))
    e[0, x, here, :] = ex
    e[1, x, here, :] = ey
    e[2, x, here, :] = ez
    heat = sigma[x, here, :] * (ex * ex + ey * ey + ez * ez)
    power[x, here, :] = heat if first else power[x, here, :] + heat
    return ey, ez


def h_edge_kernel(e, col, hgt, e_rows, rows_old, h_old, h, to_col, to_hgt):
    nx, nz = e.shape[1:3]
    for z in range(0, nz, ROWS):
        hy, hz = h_tile(e, h, col, hgt, nx - 1, z)
        to_col[0, z : z + ROWS, :] = hy
        to_col[1, z : z + ROWS, :] = hz
    for x in range(0, nx, ROWS):
        here = slice(x, x + ROWS)
        ex, ey, ez = (e_rows[comp, here, :] for comp in range(3))
        row = e_rows[2, x + ROWS : x + ROWS + 1, :] if x + ROWS < nx else col[1, nz - 1 : nz, :]
        to_hgt[0, here, :] = rows_old[0, here, :] - COURANT * ((after_y(ez) - ez) - (hgt[1, here, :] - ey))
        to_hgt[1, here, :] = rows_old[1, here, :] - COURANT * ((hgt[0, here, :] - ex) - (after_row(ez, row) - ez))


def h_rest_kernel(e, hgt, h_old, h, *rows):
    nx, nz = e.shape[1:3]

    def keep(x):
        if rows:
            for comp in range(3):
                rows[0][comp, pl.ds(x, 1), :] = h[comp, x, 0:1, :]

    def plane(x):
        for z in range(0, nz, ROWS):
            h_tile(e, h, None, hgt, x, z)
        keep(x)

    over(0, nx - 1, plane)
    keep(nx - 1)


def e_edge_kernel(first, h, ca, cb, sigma, col, hgt, media_rows, h_rows, rows_old, *refs):
    e, power, to_col, to_hgt = refs[-4:]
    nx, nz = e.shape[1:3]
    for z in range(0, nz, ROWS):
        ey, ez = e_tile(first, h, e, power, ca, cb, sigma, col, hgt, 0, z)
        to_col[0, z : z + ROWS, :] = ey
        to_col[1, z : z + ROWS, :] = ez
    for x in range(0, nx, ROWS):
        here = slice(x, x + ROWS)
        hx, hy, hz = (h_rows[comp, here, :] for comp in range(3))
        row = h_rows[2, x - 1 : x, :] if x > 0 else col[1, 0:1, :]
        keep = media_rows[0, here, :]
        drive = media_rows[1, here, :]
        to_hgt[0, here, :] = keep * rows_old[0, here, :] + drive * ((hz - before_y(hz)) - (hy - hgt[1, here, :]))
        to_hgt[1, here, :] = keep * rows_old[1, here, :] + drive * ((hx - hgt[0, here, :]) - (hz - before_row(hz, row)))


def e_rest_kernel(first, h, ca, cb, sigma, hgt, e_old, power_old, e, power, rows):
    nx, nz = e.shape[1:3]

    def keep(x):
        for comp in range(3):
            rows[comp, pl.ds(x, 1), :] = e[comp, x, nz - 1 : nz, :]

    def plane(x):
        for z in range(0, nz, ROWS):
            e_tile(first, h, e, power, ca, cb, sigma, None, hgt, x, z)
        keep(x)

    keep(0)
    over(1, nx, plane)


def e_last_kernel(first, h, ca, cb, sigma, col, hgt, e_old, power_old, e, power, h_out, sem):
    nx, nz = e.shape[1:3]
    copy = pltpu.make_async_copy(h, h_out, sem)
    copy.start()

    def plane(x):
        for z in range(0, nz, ROWS):
            e_tile(first, h, e, power, ca, cb, sigma, col if isinstance(x, int) else None, hgt, x, z)

    plane(0)
    over(1, nx, plane)
    copy.wait()


def places_kernel(n_col, n_hgt, cap, my_col, owner, node, place, flat):
    n_dev = n_col * n_hgt
    count = owner.shape[1]
    width = 256
    rows = lax.broadcasted_iota(jnp.int32, (n_dev, width), 0)
    before = lax.broadcasted_iota(jnp.int32, (width, width), 0)
    after = lax.broadcasted_iota(jnp.int32, (width, width), 1)
    upper = jnp.where(before <= after, 1.0, 0.0).astype(jnp.bfloat16)
    per = -(-cap // LANES)
    room_for = per * LANES
    room = lax.broadcasted_iota(jnp.int32, (room_for, width), 0)
    total = jnp.zeros((n_dev, 1), F32)
    parts_of = jnp.zeros((2 * n_dev, room_for), F32)
    nt = (((1,), (1,)), ((), ()))
    begins, heights = starts_of(n_col, n_hgt, cap)
    for start in range(0, count, width):
        own = owner[:, start : start + width]
        hit = jnp.where(rows == own, 1.0, 0.0)
        running = total + jnp.dot(hit.astype(jnp.bfloat16), upper, preferred_element_type=F32)
        total = running[:, width - 1 : width]
        rank = jnp.sum(hit * running, axis=0, keepdims=True).astype(jnp.int32) - 1
        turn = lax.bitwise_xor(lax.div(own, n_hgt), my_col[0])
        own_hgt = lax.rem(own, n_hgt)
        begin = jnp.where(
            turn == 0,
            begins[0] + own_hgt * heights[0],
            jnp.where(
                turn == 1,
                begins[1] + own_hgt * heights[1],
                begins[2] + own_hgt * heights[2] + (turn - 2) * cap,
            ),
        )
        place[:, start : start + width] = begin + rank
        number = node[:, start : start + width]
        upper_part = lax.div(number, 16)
        lower_part = number - 16 * upper_part
        seat = jnp.where(room == rank, 1.0, 0.0).astype(jnp.bfloat16)
        both = jnp.concatenate([hit * upper_part.astype(F32), hit * lower_part.astype(F32)], 0)
        parts_of = parts_of + lax.dot_general(both.astype(jnp.bfloat16), seat, nt, preferred_element_type=F32)
    taken = lax.broadcasted_iota(jnp.int32, (n_dev, room_for), 1).astype(F32) < total
    table = jnp.where(taken, 16.0 * parts_of[:n_dev] + parts_of[n_dev:], -1.0)
    chunk = 8 * ROWS

    def clear(i, carry):
        flat[pl.ds(pl.multiple_of(i * chunk, chunk), chunk), :] = jnp.zeros((chunk, PTS), F32)
        return carry

    lax.fori_loop(0, flat.shape[0] // chunk, clear, 0)
    for at in range(flat.shape[0] // chunk * chunk, flat.shape[0], ROWS):
        flat[at : at + ROWS, :] = jnp.zeros((ROWS, PTS), F32)
    behind = [cap, cap, (n_col - 2) * cap]
    for begin, height, skip in zip(begins, heights, behind):
        for part in range(n_hgt):
            at = begin + part * height
            flat[at + skip : at + height, :] = jnp.full((height - skip, PTS), -1.0, F32)
    for group in range(n_col):
        turn = lax.bitwise_xor(jnp.int32(group), my_col[0])
        kind = jnp.minimum(turn, 2)
        begin = jnp.where(kind == 0, begins[0], jnp.where(kind == 1, begins[1], begins[2]))
        height = jnp.where(kind == 2, heights[2], heights[0])
        skip = jnp.where(kind == 2, behind[2] + (turn - 2) * per, cap)
        for part in range(n_hgt):
            at = group * n_hgt + part
            for piece in range(per):
                row = table[at : at + 1, piece * LANES : (piece + 1) * LANES]
                flat[pl.ds(begin + part * height + skip + piece, 1), :] = row


def table_rows(parts, cap):
    return -(-parts * -(-cap // LANES) // ROWS) * ROWS


def starts_of(n_col, n_hgt, cap):
    one = cap + table_rows(1, cap)
    heights = [one, one, (n_col - 2) * cap + table_rows(n_col - 2, cap)]
    return [0, n_hgt * heights[0], n_hgt * (heights[0] + heights[1])], heights


def pack_kernel(heights, place, power, flat_old, e, mine, pair, other, e_out, flat, sems):
    nx, nz, ny = power.shape
    e_copy = pltpu.make_async_copy(e, e_out, sems.at[0])
    e_copy.start()
    per_row = ny // PTS

    def plane(x, carry):
        for z in range(nz):
            for k in range(per_row):
                spot = place[x * (nz * per_row) + z * per_row + k]
                flat[pl.ds(spot, 1), :] = power[x, z : z + 1, k * PTS : (k + 1) * PTS]
        return carry

    lax.fori_loop(0, nx, plane, 0)
    copies = []
    first = 0
    for out, rows in zip((mine, pair, other), heights):
        for group in range(out.shape[0]):
            target = out.at[group, pl.ds(0, rows)]
            copies.append(pltpu.make_async_copy(flat.at[pl.ds(first, rows)], target, sems.at[1 + len(copies)]))
            first += rows
    for copy in copies:
        copy.start()
    for copy in copies:
        copy.wait()
    e_copy.wait()


def summed(blocks, first, cap, node_row, chosen, split, node_count):
    ids = lax.broadcasted_iota(jnp.int32, (node_count, LANES), 0).astype(F32)
    n_from, _, pts = blocks.shape
    per = -(-cap // LANES)
    many = len(first)
    for source in range(n_from):
        for i in range(many):
            seat = (source * many + i) * per * LANES
            for piece in range(per):
                row = node_row[i] + piece
                lanes = slice(seat + piece * LANES, seat + (piece + 1) * LANES)
                hit = ids == blocks[source, row : row + 1, :]
                chosen[:, lanes] = jnp.where(hit, 1.0, 0.0).astype(jnp.bfloat16)
            values = blocks[source, first[i] : first[i] + cap, :]
            high = values.astype(jnp.bfloat16)
            split[seat : seat + cap, 0:pts] = high
            split[seat : seat + cap, pts : 2 * pts] = (values - high.astype(F32)).astype(jnp.bfloat16)
    both = jnp.dot(chosen[...], split[...], preferred_element_type=F32)
    return both[:, 0:pts] + both[:, pts : 2 * pts]


def collect_kernel(cap, blocks, *refs):
    *outs, chosen, split = refs
    per = -(-cap // LANES)
    split[...] = jnp.zeros(split.shape, split.dtype)
    for part, out in enumerate(outs):
        out[...] = summed(blocks, [part * cap], cap, [len(outs) * cap + part * per], chosen, split, out.shape[0])


def merge_kernel(pair, mine_old, mine, sems):
    rows = pair.shape[1]
    copies = [
        pltpu.make_async_copy(pair.at[group], mine.at[group, pl.ds(rows, rows)], sems.at[group])
        for group in range(mine.shape[0])
    ]
    for copy in copies:
        copy.start()
    for copy in copies:
        copy.wait()


def collect_mine_kernel(cap, blocks, out, chosen, split):
    half = blocks.shape[1] // 2
    split[...] = jnp.zeros(split.shape, split.dtype)
    out[...] = summed(blocks, [0, half], cap, [cap, half + cap], chosen, split, out.shape[0])


def finish_kernel(enthalpy, *refs):
    *parts, out = refs
    heat = parts[0][...]
    for part in parts[1:]:
        heat = heat + part[...]
    content = enthalpy[...] + (0.25 / STEPS) * heat
    out[...] = jnp.where(content < 0.0, content / 2.0, jnp.where(content > 1.0, (content - 1.0) / 3.0, 0.0))


def shifted(block, d_col, d_hgt):
    n_col = lax.axis_size("col")
    n_hgt = lax.axis_size("hgt")
    route = [
        (c * n_hgt + h, (c + d_col) * n_hgt + h + d_hgt)
        for c in range(n_col)
        for h in range(n_hgt)
        if 0 <= c + d_col < n_col and 0 <= h + d_hgt < n_hgt
    ]
    return lax.ppermute(block, ("col", "hgt"), route)


def per_device(
    efield_lattice_vector,
    hfield_lattice_vector,
    cell_temp,
    region_tags,
    block_owner,
    block_node,
    node_enthalpy,
):
    nx, nz, ny = cell_temp.shape
    n_col = lax.axis_size("col")
    n_hgt = lax.axis_size("hgt")
    n_dev = n_col * n_hgt
    count = nx * nz * ny // PTS
    cap = 2 * count // n_dev
    node_count = node_enthalpy.shape[0]
    cells = nx * nz * ny
    sem = pltpu.SemaphoreType.DMA

    def kernel(body, outs, ins, args, name, work, aliases=None, scratch=()):
        return pl.pallas_call(
            body,
            out_shape=outs,
            in_specs=ins,
            out_specs=jax.tree.map(lambda out: WHOLE, outs),
            input_output_aliases=aliases or {},
            scratch_shapes=scratch,
            compiler_params=params(VMEM_MIB),
            cost_estimate=cost(work * cells, work * cells),
            name=name,
        )(*args)

    e_start = far(efield_lattice_vector)
    h_start = far(hfield_lattice_vector)
    my_col = lax.axis_index("col").astype(jnp.int32).reshape(1)
    owners = block_owner.reshape(1, count)
    nodes = block_node.reshape(1, count)
    field = vmem(3, nx, nz, ny)
    whole = vmem(nx, nz, ny)
    planes = vmem(2, nz, ny)
    two_rows = vmem(2, nx, ny)
    three_rows = vmem(3, nx, ny)

    to_col = kernel(edge_kernel, planes, [FAR], [e_start], "edge", 4, scratch=[sem])
    col = shifted(to_col, -1, 0)
    e_low = kernel(
        low_kernel, two_rows, [FAR, WHOLE], [e_start, to_col], "low", 60, scratch=[vmem(2, nx, ROWS, ny), sem]
    )
    hgt = shifted(e_low, 0, -1)
    ca, cb, sigma, e, h, media_rows, e_rows, h_high = kernel(
        load_kernel,
        (whole, whole, whole, field, field, two_rows, three_rows, two_rows),
        [FAR] * 4 + [WHOLE],
        [far(cell_temp), far(region_tags), e_start, h_start, owners + nodes + my_col],
        "load",
        60,
        scratch=[vmem(nx, nz, ny), pltpu.VMEM((nx, nz, ny), jnp.int32), sem((8, 4))],
    )
    begins, heights = starts_of(n_col, n_hgt, cap)
    place, flat = kernel(
        functools.partial(places_kernel, n_col, n_hgt, cap),
        (jax.ShapeDtypeStruct((1, count), jnp.int32), vmem(n_hgt * sum(heights), PTS)),
        [SCALARS, WHOLE, WHOLE],
        [my_col, owners, nodes],
        "places",
        8,
    )
    power = None
    for step in range(STEPS):
        first = step == 0
        h, to_col, h_high = kernel(
            h_edge_kernel,
            (field, planes, two_rows),
            [WHOLE] * 6,
            [e, col, hgt, e_rows, h_high, h],
            f"h_edge_{step}",
            4,
            {5: 0},
        )
        e_hgt = hgt
        col = shifted(to_col, 1, 0)
        hgt = shifted(h_high, 0, 1)
        last = step == STEPS - 1
        outs = (field,) if last else (field, three_rows)
        h, *h_rows = kernel(h_rest_kernel, outs, [WHOLE] * 3, [e, e_hgt, h], f"h_rest_{step}", 40, {2: 0})
        media = [h, ca, cb, sigma]
        if last:
            e, power, h_out = pl.pallas_call(
                functools.partial(e_last_kernel, first),
                out_shape=(field, whole, pltpu.HBM((3, nx, nz, ny), F32)),
                in_specs=[WHOLE] * 8,
                out_specs=(WHOLE, WHOLE, FAR),
                input_output_aliases={6: 0, 7: 1},
                scratch_shapes=[sem],
                compiler_params=params(VMEM_MIB),
                cost_estimate=cost(cells * 50, cells * 50),
                name="e_last",
            )(*media, col, hgt, e, power)
            break
        args = media + [col, hgt, media_rows, *h_rows, e_low, e] + ([] if first else [power])
        e, power, to_col, e_low = kernel(
            functools.partial(e_edge_kernel, first),
            (field, whole, planes, two_rows),
            [WHOLE] * len(args),
            args,
            f"e_edge_{step}",
            5,
            {9: 0} if first else {9: 0, 10: 1},
        )
        h_hgt = hgt
        col = shifted(to_col, -1, 0)
        hgt = shifted(e_low, 0, -1)
        e, power, e_rows = kernel(
            functools.partial(e_rest_kernel, first),
            (field, whole, three_rows),
            [WHOLE] * 7,
            media + [h_hgt, e, power],
            f"e_rest_{step}",
            45,
            {5: 0, 6: 1},
        )

    mine, pair, other, e_out, _ = pl.pallas_call(
        functools.partial(pack_kernel, heights),
        out_shape=(
            pltpu.HBM((n_hgt, 2 * heights[0], PTS), F32),
            pltpu.HBM((n_hgt, heights[1], PTS), F32),
            pltpu.HBM((n_hgt, heights[2], PTS), F32),
            pltpu.HBM((3, nx, nz, ny), F32),
            vmem(n_hgt * sum(heights), PTS),
        ),
        in_specs=[SCALARS] + [WHOLE] * 3,
        out_specs=(FAR,) * 4 + (WHOLE,),
        input_output_aliases={2: 4},
        scratch_shapes=[sem((1 + 3 * n_hgt,))],
        compiler_params=params(VMEM_MIB),
        cost_estimate=cost(cells, cells * 36),
        name="pack",
    )(place.reshape(count), power, flat, e)

    def swap(x, axis):
        return lax.all_to_all(x, axis, split_axis=0, concat_axis=0, tiled=True)

    def across(x, turn):
        return lax.ppermute(x, "col", [(c, c ^ turn) for c in range(n_col)])

    def one_hot_space(sources):
        seats = sources * -(-cap // LANES) * LANES
        return [pltpu.VMEM((node_count, seats), jnp.bfloat16), pltpu.VMEM((seats, 2 * PTS), jnp.bfloat16)]

    node_rows = jax.ShapeDtypeStruct((node_count, PTS), F32)
    from_pair = across(pair, 1)
    other_blocks = swap(other, "hgt")
    sums = kernel(
        functools.partial(collect_kernel, cap),
        (node_rows,) * (n_col - 2),
        [WHOLE],
        [other_blocks],
        "collect_other",
        1,
        scratch=one_hot_space(n_hgt),
    )
    parts = [across(sums[turn - 2], turn) for turn in range(2, n_col)]
    mine = pl.pallas_call(
        merge_kernel,
        out_shape=pltpu.HBM((n_hgt, 2 * heights[0], PTS), F32),
        in_specs=[pl.BlockSpec(memory_space=pl.ANY), FAR],
        out_specs=FAR,
        input_output_aliases={1: 0},
        scratch_shapes=[sem((n_hgt,))],
        compiler_params=params(VMEM_MIB),
        cost_estimate=cost(1, 1),
        name="merge",
    )(from_pair, mine)
    mine_blocks = swap(mine, "hgt")
    own = kernel(
        functools.partial(collect_mine_kernel, cap),
        node_rows,
        [WHOLE],
        [mine_blocks],
        "collect_mine",
        1,
        scratch=one_hot_space(2 * n_hgt),
    )
    node_temp = kernel(
        finish_kernel, node_rows, [WHOLE] * (n_col), [node_enthalpy, own, *parts], "finish", 1
    )
    return e_out, h_out, node_temp


def solution(mesh):
    placed = (
        P(None, "col", "hgt", None),
        P(None, "col", "hgt", None),
        P("col", "hgt", None),
        P("col", "hgt", None),
        P("col", "hgt", None, None, None, None),
        P("col", "hgt", None, None, None),
        P(("col", "hgt"), None),
    )
    return jax.shard_map(
        per_device,
        mesh=mesh,
        in_specs=placed,
        out_specs=(
            P(None, "col", "hgt", None),
            P(None, "col", "hgt", None),
            P(("col", "hgt"), None),
        ),
        check_vma=False,
    )
```

```python
import functools

import jax
import jax.numpy as jnp
from jax import lax
from jax.experimental import pallas as pl
from jax.experimental.pallas import tpu as pltpu
from jax.sharding import PartitionSpec as P

PTS = 128
STEPS = 4
COURANT = 0.55
LANES = 128
ROWS = 8
F32 = jnp.float32
VMEM_MIB = 20

WHOLE = pl.BlockSpec(memory_space=pltpu.VMEM)
SCALARS = pl.BlockSpec(memory_space=pltpu.SMEM)
FAR = pl.BlockSpec(memory_space=pltpu.HBM)


def vmem(*shape):
    return pltpu.VMEM(shape, F32)


def far(x):
    return pltpu.with_memory_space_constraint(x, pltpu.HBM)


def params(mib):
    return pltpu.CompilerParams(vmem_limit_bytes=mib << 20)


def cost(flops, moved):
    return pl.CostEstimate(flops=flops, bytes_accessed=moved, transcendentals=0)


def after_y(f):
    lane = lax.broadcasted_iota(jnp.int32, (ROWS, LANES), 1)
    n = f.shape[1] // LANES
    turned = [pltpu.roll(f[:, k * LANES : (k + 1) * LANES], LANES - 1, 1) for k in range(n)]
    turned.append(jnp.zeros((ROWS, LANES), F32))
    return jnp.concatenate([jnp.where(lane < LANES - 1, turned[k], turned[k + 1]) for k in range(n)], 1)


def before_y(f):
    lane = lax.broadcasted_iota(jnp.int32, (ROWS, LANES), 1)
    n = f.shape[1] // LANES
    turned = [jnp.zeros((ROWS, LANES), F32)]
    turned += [pltpu.roll(f[:, k * LANES : (k + 1) * LANES], 1, 1) for k in range(n)]
    return jnp.concatenate([jnp.where(lane > 0, turned[k + 1], turned[k]) for k in range(n)], 1)


def after_row(f, row):
    place = lax.broadcasted_iota(jnp.int32, f.shape, 0)
    return jnp.where(place < ROWS - 1, pltpu.roll(f, ROWS - 1, 0), jnp.broadcast_to(row, f.shape))


def before_row(f, row):
    place = lax.broadcasted_iota(jnp.int32, f.shape, 0)
    return jnp.where(place > 0, pltpu.roll(f, 1, 0), jnp.broadcast_to(row, f.shape))


def edge_kernel(e, to_col, to_hgt, low, sems):
    nx = e.shape[1]
    col_copy = pltpu.make_async_copy(e.at[pl.ds(1, 2), 0], to_col, sems.at[0])
    low_copy = pltpu.make_async_copy(e.at[pl.ds(0, 2), :, pl.ds(0, ROWS)], low, sems.at[1])
    low_copy.start()
    col_copy.start()
    low_copy.wait()
    for x in range(nx):
        for comp in range(2):
            to_hgt[comp, x : x + 1, :] = low[comp, x, 0:1, :]
    col_copy.wait()


def load_kernel(
    temp_far, tags_far, e_far, h_far, order, ca, cb, sigma_out, e, h, media_rows, e_rows, h_rows, temp, tags, sems
):
    nx, nz, _ = temp.shape
    parts = 4
    size = nx // parts
    copies = []
    for part in range(parts):
        here = pl.ds(part * size, size)
        copies.append(pltpu.make_async_copy(temp_far.at[here], temp.at[here], sems.at[0, part]))
        copies.append(pltpu.make_async_copy(tags_far.at[here], tags.at[here], sems.at[1, part]))
    e_copy = pltpu.make_async_copy(e_far, e, sems.at[2, 0])
    h_copy = pltpu.make_async_copy(h_far, h, sems.at[2, 1])
    for copy in copies:
        copy.start()
    e_copy.start()
    h_copy.start()

    def plane(x, carry):
        for z in range(0, nz, ROWS):
            tag = tags[x, z : z + ROWS, :]
            lean = tag == 0
            fat = tag == 1
            frac = 1.0 / (1.0 + jnp.exp(-2.0 * temp[x, z : z + ROWS, :]))
            eps_low = jnp.where(lean, 4.0, jnp.where(fat, 2.5, 5.0))
            eps_rise = jnp.where(lean, 46.0, jnp.where(fat, 3.5, 5.0))
            sig_low = jnp.where(lean, 0.2, jnp.where(fat, 0.05, 0.1))
            sig_rise = jnp.where(lean, 7.8, jnp.where(fat, 0.35, 0.9))
            eps = eps_low + eps_rise * frac
            sigma = sig_low + sig_rise * frac
            half = (0.5 * COURANT) * sigma
            inverse = 1.0 / (eps + half)
            ca[x, z : z + ROWS, :] = (eps - half) * inverse
            cb[x, z : z + ROWS, :] = COURANT * inverse
            sigma_out[x, z : z + ROWS, :] = sigma
        media_rows[0, pl.ds(x, 1), :] = ca[x, 0:1, :]
        media_rows[1, pl.ds(x, 1), :] = cb[x, 0:1, :]
        return carry

    for part in range(parts):
        copies[2 * part].wait()
        copies[2 * part + 1].wait()
        lax.fori_loop(part * size, (part + 1) * size, plane, 0)
    e_copy.wait()
    h_copy.wait()

    def rows(x, carry):
        for comp in range(3):
            e_rows[comp, pl.ds(x, 1), :] = e[comp, x, nz - 1 : nz, :]
        for comp in range(2):
            h_rows[comp, pl.ds(x, 1), :] = h[comp, x, nz - 1 : nz, :]
        return carry

    lax.fori_loop(0, nx, rows, 0)


def over(first, stop, body):
    if stop - first == 1:
        body(first)
    else:

        def step(x, carry):
            body(x)
            return carry

        lax.fori_loop(first, stop, step, 0)


def h_tile(e, h, col, hgt, x, z):
    nz = e.shape[2]
    here = slice(z, z + ROWS)
    ex, ey, ez = (e[comp, x, here, :] for comp in range(3))
    if z + ROWS < nz:
        row_x, row_y = (e[comp, x, z + ROWS : z + ROWS + 1, :] for comp in range(2))
    else:
        row_x, row_y = (hgt[comp, pl.ds(x, 1), :] for comp in range(2))
    if col is None:
        next_y, next_z = (e[comp, x + 1, here, :] for comp in (1, 2))
    else:
        next_y, next_z = (col[comp, here, :] for comp in range(2))
    h[0, x, here, :] = h[0, x, here, :] - COURANT * ((after_y(ez) - ez) - (after_row(ey, row_y) - ey))
    hy = h[1, x, here, :] - COURANT * ((after_row(ex, row_x) - ex) - (next_z - ez))
    hz = h[2, x, here, :] - COURANT * ((next_y - ey) - (after_y(ex) - ex))
    h[1, x, here, :] = hy
    h[2, x, here, :] = hz
    return hy, hz


def e_tile(first, h, e, power, ca, cb, sigma, col, hgt, x, z):
    here = slice(z, z + ROWS)
    hx, hy, hz = (h[comp, x, here, :] for comp in range(3))
    if z > 0:
        row_x, row_y = (h[comp, x, z - 1 : z, :] for comp in range(2))
    else:
        row_x, row_y = (hgt[comp, pl.ds(x, 1), :] for comp in range(2))
    if col is None:
        past_y, past_z = (h[comp, x - 1, here, :] for comp in (1, 2))
    else:
        past_y, past_z = (col[comp, here, :] for comp in range(2))
    keep = ca[x, here, :]
    drive = cb[x, here, :]
    ex = keep * e[0, x, here, :] + drive * ((hz - before_y(hz)) - (hy - before_row(hy, row_y)))
    ey = keep * e[1, x, here, :] + drive * ((hx - before_row(hx, row_x)) - (hz - past_z))
    ez = keep * e[2, x, here, :] + drive * ((hy - past_y) - (hx - before_y(hx)))
    e[0, x, here, :] = ex
    e[1, x, here, :] = ey
    e[2, x, here, :] = ez
    heat = sigma[x, here, :] * (ex * ex + ey * ey + ez * ez)
    power[x, here, :] = heat if first else power[x, here, :] + heat
    return ey, ez


def h_edge_kernel(e, col, hgt, e_rows, rows_old, h_old, h, to_col, to_hgt):
    nx, nz = e.shape[1:3]
    for z in range(0, nz, ROWS):
        hy, hz = h_tile(e, h, col, hgt, nx - 1, z)
        to_col[0, z : z + ROWS, :] = hy
        to_col[1, z : z + ROWS, :] = hz
    for x in range(0, nx, ROWS):
        here = slice(x, x + ROWS)
        ex, ey, ez = (e_rows[comp, here, :] for comp in range(3))
        row = e_rows[2, x + ROWS : x + ROWS + 1, :] if x + ROWS < nx else col[1, nz - 1 : nz, :]
        to_hgt[0, here, :] = rows_old[0, here, :] - COURANT * ((after_y(ez) - ez) - (hgt[1, here, :] - ey))
        to_hgt[1, here, :] = rows_old[1, here, :] - COURANT * ((hgt[0, here, :] - ex) - (after_row(ez, row) - ez))


def h_rest_kernel(e, hgt, h_old, h, *rows):
    nx, nz = e.shape[1:3]

    def keep(x):
        if rows:
            for comp in range(3):
                rows[0][comp, pl.ds(x, 1), :] = h[comp, x, 0:1, :]

    def plane(x):
        for z in range(0, nz, ROWS):
            h_tile(e, h, None, hgt, x, z)
        keep(x)

    over(0, nx - 1, plane)
    keep(nx - 1)


def e_edge_kernel(first, h, ca, cb, sigma, col, hgt, media_rows, h_rows, rows_old, *refs):
    e, power, to_col, to_hgt = refs[-4:]
    nx, nz = e.shape[1:3]
    for z in range(0, nz, ROWS):
        ey, ez = e_tile(first, h, e, power, ca, cb, sigma, col, hgt, 0, z)
        to_col[0, z : z + ROWS, :] = ey
        to_col[1, z : z + ROWS, :] = ez
    for x in range(0, nx, ROWS):
        here = slice(x, x + ROWS)
        hx, hy, hz = (h_rows[comp, here, :] for comp in range(3))
        row = h_rows[2, x - 1 : x, :] if x > 0 else col[1, 0:1, :]
        keep = media_rows[0, here, :]
        drive = media_rows[1, here, :]
        to_hgt[0, here, :] = keep * rows_old[0, here, :] + drive * ((hz - before_y(hz)) - (hy - hgt[1, here, :]))
        to_hgt[1, here, :] = keep * rows_old[1, here, :] + drive * ((hx - hgt[0, here, :]) - (hz - before_row(hz, row)))


def e_rest_kernel(first, h, ca, cb, sigma, hgt, e_old, power_old, e, power, rows):
    nx, nz = e.shape[1:3]

    def keep(x):
        for comp in range(3):
            rows[comp, pl.ds(x, 1), :] = e[comp, x, nz - 1 : nz, :]

    def plane(x):
        for z in range(0, nz, ROWS):
            e_tile(first, h, e, power, ca, cb, sigma, None, hgt, x, z)
        keep(x)

    keep(0)
    over(1, nx, plane)


def e_last_kernel(
    heights, place, h, ca, cb, sigma, col, hgt, e_old, power_old, flat_old, e, power, flat, h_out, e_out, *refs
):
    mine, pair, other, sems = refs
    nx, nz, ny = power.shape
    per_row = ny // PTS
    h_copy = pltpu.make_async_copy(h, h_out, sems.at[0])
    h_copy.start()

    def e_copy(x):
        return pltpu.make_async_copy(e.at[:, x], e_out.at[:, x], sems.at[1])

    def scatter(x, z):
        for row in range(z, z + ROWS):
            for k in range(per_row):
                spot = place[x * (nz * per_row) + row * per_row + k]
                flat[pl.ds(spot, 1), :] = power[x, row : row + 1, k * PTS : (k + 1) * PTS]

    for z in range(0, nz, ROWS):
        e_tile(False, h, e, power, ca, cb, sigma, col, hgt, 0, z)

    def plane(x, carry):
        e_copy(x - 1).start()
        for z in range(0, nz, ROWS):
            e_tile(False, h, e, power, ca, cb, sigma, None, hgt, x, z)
            scatter(x - 1, z)
        return carry

    lax.fori_loop(1, nx, plane, 0)
    e_copy(nx - 1).start()
    for z in range(0, nz, ROWS):
        scatter(nx - 1, z)
    copies = []
    first = 0
    for out, rows in zip((mine, pair, other), heights):
        for group in range(out.shape[0]):
            target = out.at[group, pl.ds(0, rows)]
            copies.append(pltpu.make_async_copy(flat.at[pl.ds(first, rows)], target, sems.at[2 + len(copies)]))
            first += rows
    for copy in copies:
        copy.start()
    for copy in copies:
        copy.wait()
    h_copy.wait()

    def finish(x, carry):
        e_copy(x).wait()
        return carry

    lax.fori_loop(0, nx, finish, 0)


def places_kernel(n_col, n_hgt, cap, my_col, owner, node, place, flat):
    n_dev = n_col * n_hgt
    count = owner.shape[1]
    width = 256
    rows = lax.broadcasted_iota(jnp.int32, (n_dev, width), 0)
    before = lax.broadcasted_iota(jnp.int32, (width, width), 0)
    after = lax.broadcasted_iota(jnp.int32, (width, width), 1)
    upper = jnp.where(before <= after, 1.0, 0.0).astype(jnp.bfloat16)
    per = -(-cap // LANES)
    room_for = per * LANES
    room = lax.broadcasted_iota(jnp.int32, (room_for, width), 0)
    total = jnp.zeros((n_dev, 1), F32)
    parts_of = jnp.zeros((2 * n_dev, room_for), F32)
    nt = (((1,), (1,)), ((), ()))
    begins, heights = starts_of(n_col, n_hgt, cap)
    for start in range(0, count, width):
        own = owner[:, start : start + width]
        hit = jnp.where(rows == own, 1.0, 0.0)
        running = total + jnp.dot(hit.astype(jnp.bfloat16), upper, preferred_element_type=F32)
        total = running[:, width - 1 : width]
        rank = jnp.sum(hit * running, axis=0, keepdims=True).astype(jnp.int32) - 1
        turn = lax.bitwise_xor(lax.div(own, n_hgt), my_col[0])
        own_hgt = lax.rem(own, n_hgt)
        begin = jnp.where(
            turn == 0,
            begins[0] + own_hgt * heights[0],
            jnp.where(
                turn == 1,
                begins[1] + own_hgt * heights[1],
                begins[2] + own_hgt * heights[2] + (turn - 2) * cap,
            ),
        )
        place[:, start : start + width] = begin + rank
        number = node[:, start : start + width]
        upper_part = lax.div(number, 16)
        lower_part = number - 16 * upper_part
        seat = jnp.where(room == rank, 1.0, 0.0).astype(jnp.bfloat16)
        both = jnp.concatenate([hit * upper_part.astype(F32), hit * lower_part.astype(F32)], 0)
        parts_of = parts_of + lax.dot_general(both.astype(jnp.bfloat16), seat, nt, preferred_element_type=F32)
    taken = lax.broadcasted_iota(jnp.int32, (n_dev, room_for), 1).astype(F32) < total
    table = jnp.where(taken, 16.0 * parts_of[:n_dev] + parts_of[n_dev:], -1.0)
    chunk = 8 * ROWS

    def clear(i, carry):
        flat[pl.ds(pl.multiple_of(i * chunk, chunk), chunk), :] = jnp.zeros((chunk, PTS), F32)
        return carry

    lax.fori_loop(0, flat.shape[0] // chunk, clear, 0)
    for at in range(flat.shape[0] // chunk * chunk, flat.shape[0], ROWS):
        flat[at : at + ROWS, :] = jnp.zeros((ROWS, PTS), F32)
    behind = [cap, cap, (n_col - 2) * cap]
    for begin, height, skip in zip(begins, heights, behind):
        for part in range(n_hgt):
            at = begin + part * height
            flat[at + skip : at + height, :] = jnp.full((height - skip, PTS), -1.0, F32)
    for group in range(n_col):
        turn = lax.bitwise_xor(jnp.int32(group), my_col[0])
        kind = jnp.minimum(turn, 2)
        begin = jnp.where(kind == 0, begins[0], jnp.where(kind == 1, begins[1], begins[2]))
        height = jnp.where(kind == 2, heights[2], heights[0])
        skip = jnp.where(kind == 2, behind[2] + (turn - 2) * per, cap)
        for part in range(n_hgt):
            at = group * n_hgt + part
            for piece in range(per):
                row = table[at : at + 1, piece * LANES : (piece + 1) * LANES]
                flat[pl.ds(begin + part * height + skip + piece, 1), :] = row


def table_rows(parts, cap):
    return -(-parts * -(-cap // LANES) // ROWS) * ROWS


def starts_of(n_col, n_hgt, cap):
    one = cap + table_rows(1, cap)
    heights = [one, one, (n_col - 2) * cap + table_rows(n_col - 2, cap)]
    return [0, n_hgt * heights[0], n_hgt * (heights[0] + heights[1])], heights


def summed(blocks, first, cap, node_row, chosen, split, node_count):
    ids = lax.broadcasted_iota(jnp.int32, (node_count, LANES), 0).astype(F32)
    n_from, _, pts = blocks.shape
    per = -(-cap // LANES)
    many = len(first)
    for source in range(n_from):
        for i in range(many):
            seat = (source * many + i) * per * LANES
            for piece in range(per):
                row = node_row[i] + piece
                lanes = slice(seat + piece * LANES, seat + (piece + 1) * LANES)
                hit = ids == blocks[source, row : row + 1, :]
                chosen[:, lanes] = jnp.where(hit, 1.0, 0.0).astype(jnp.bfloat16)
            values = blocks[source, first[i] : first[i] + cap, :]
            high = values.astype(jnp.bfloat16)
            split[seat : seat + cap, 0:pts] = high
            split[seat : seat + cap, pts : 2 * pts] = (values - high.astype(F32)).astype(jnp.bfloat16)
    both = jnp.dot(chosen[...], split[...], preferred_element_type=F32)
    return both[:, 0:pts] + both[:, pts : 2 * pts]


def collect_kernel(cap, blocks, *refs):
    *outs, chosen, split = refs
    per = -(-cap // LANES)
    split[...] = jnp.zeros(split.shape, split.dtype)
    for part, out in enumerate(outs):
        out[...] = summed(blocks, [part * cap], cap, [len(outs) * cap + part * per], chosen, split, out.shape[0])


def merge_kernel(pair, mine_old, mine, sems):
    rows = pair.shape[1]
    copies = [
        pltpu.make_async_copy(pair.at[group], mine.at[group, pl.ds(rows, rows)], sems.at[group])
        for group in range(mine.shape[0])
    ]
    for copy in copies:
        copy.start()
    for copy in copies:
        copy.wait()


def collect_mine_kernel(cap, blocks, out, chosen, split):
    half = blocks.shape[1] // 2
    split[...] = jnp.zeros(split.shape, split.dtype)
    out[...] = summed(blocks, [0, half], cap, [cap, half + cap], chosen, split, out.shape[0])


def finish_kernel(enthalpy, *refs):
    *parts, out = refs
    heat = parts[0][...]
    for part in parts[1:]:
        heat = heat + part[...]
    content = enthalpy[...] + (0.25 / STEPS) * heat
    out[...] = jnp.where(content < 0.0, content / 2.0, jnp.where(content > 1.0, (content - 1.0) / 3.0, 0.0))


def shifted(block, d_col, d_hgt):
    n_col = lax.axis_size("col")
    n_hgt = lax.axis_size("hgt")
    route = [
        (c * n_hgt + h, (c + d_col) * n_hgt + h + d_hgt)
        for c in range(n_col)
        for h in range(n_hgt)
        if 0 <= c + d_col < n_col and 0 <= h + d_hgt < n_hgt
    ]
    return lax.ppermute(block, ("col", "hgt"), route)


def per_device(
    efield_lattice_vector,
    hfield_lattice_vector,
    cell_temp,
    region_tags,
    block_owner,
    block_node,
    node_enthalpy,
):
    nx, nz, ny = cell_temp.shape
    n_col = lax.axis_size("col")
    n_hgt = lax.axis_size("hgt")
    n_dev = n_col * n_hgt
    count = nx * nz * ny // PTS
    cap = 2 * count // n_dev
    node_count = node_enthalpy.shape[0]
    cells = nx * nz * ny
    sem = pltpu.SemaphoreType.DMA

    def kernel(body, outs, ins, args, name, work, aliases=None, scratch=()):
        return pl.pallas_call(
            body,
            out_shape=outs,
            in_specs=ins,
            out_specs=jax.tree.map(lambda out: WHOLE, outs),
            input_output_aliases=aliases or {},
            scratch_shapes=scratch,
            compiler_params=params(VMEM_MIB),
            cost_estimate=cost(work * cells, work * cells),
            name=name,
        )(*args)

    e_start = far(efield_lattice_vector)
    h_start = far(hfield_lattice_vector)
    my_col = lax.axis_index("col").astype(jnp.int32).reshape(1)
    owners = block_owner.reshape(1, count)
    nodes = block_node.reshape(1, count)
    field = vmem(3, nx, nz, ny)
    whole = vmem(nx, nz, ny)
    planes = vmem(2, nz, ny)
    two_rows = vmem(2, nx, ny)
    three_rows = vmem(3, nx, ny)

    to_col, e_low = kernel(
        edge_kernel, (planes, two_rows), [FAR], [e_start], "edge", 4, scratch=[vmem(2, nx, ROWS, ny), sem((2,))]
    )
    col = shifted(to_col, -1, 0)
    hgt = shifted(e_low, 0, -1)
    ca, cb, sigma, e, h, media_rows, e_rows, h_high = kernel(
        load_kernel,
        (whole, whole, whole, field, field, two_rows, three_rows, two_rows),
        [FAR] * 4 + [WHOLE],
        [far(cell_temp), far(region_tags), e_start, h_start, owners + nodes + my_col],
        "load",
        60,
        scratch=[vmem(nx, nz, ny), pltpu.VMEM((nx, nz, ny), jnp.int32), sem((3, 4))],
    )
    begins, heights = starts_of(n_col, n_hgt, cap)
    place, flat = kernel(
        functools.partial(places_kernel, n_col, n_hgt, cap),
        (jax.ShapeDtypeStruct((1, count), jnp.int32), vmem(n_hgt * sum(heights), PTS)),
        [SCALARS, WHOLE, WHOLE],
        [my_col, owners, nodes],
        "places",
        8,
    )
    power = None
    for step in range(STEPS):
        first = step == 0
        h, to_col, h_high = kernel(
            h_edge_kernel,
            (field, planes, two_rows),
            [WHOLE] * 6,
            [e, col, hgt, e_rows, h_high, h],
            f"h_edge_{step}",
            4,
            {5: 0},
        )
        e_hgt = hgt
        col = shifted(to_col, 1, 0)
        hgt = shifted(h_high, 0, 1)
        last = step == STEPS - 1
        outs = (field,) if last else (field, three_rows)
        h, *h_rows = kernel(h_rest_kernel, outs, [WHOLE] * 3, [e, e_hgt, h], f"h_rest_{step}", 40, {2: 0})
        media = [h, ca, cb, sigma]
        if last:
            flat_rows = n_hgt * sum(heights)
            _, _, _, h_out, e_out, mine, pair, other = pl.pallas_call(
                functools.partial(e_last_kernel, heights),
                out_shape=(
                    field,
                    whole,
                    vmem(flat_rows, PTS),
                    pltpu.HBM((3, nx, nz, ny), F32),
                    pltpu.HBM((3, nx, nz, ny), F32),
                    pltpu.HBM((n_hgt, 2 * heights[0], PTS), F32),
                    pltpu.HBM((n_hgt, heights[1], PTS), F32),
                    pltpu.HBM((n_hgt, heights[2], PTS), F32),
                ),
                in_specs=[SCALARS] + [WHOLE] * 9,
                out_specs=(WHOLE,) * 3 + (FAR,) * 5,
                input_output_aliases={7: 0, 8: 1, 9: 2},
                scratch_shapes=[sem((2 + 3 * n_hgt,))],
                compiler_params=params(VMEM_MIB),
                cost_estimate=cost(cells * 50, cells * 50),
                name="e_last",
            )(place.reshape(count), *media, col, hgt, e, power, flat)
            break
        args = media + [col, hgt, media_rows, *h_rows, e_low, e] + ([] if first else [power])
        e, power, to_col, e_low = kernel(
            functools.partial(e_edge_kernel, first),
            (field, whole, planes, two_rows),
            [WHOLE] * len(args),
            args,
            f"e_edge_{step}",
            5,
            {9: 0} if first else {9: 0, 10: 1},
        )
        h_hgt = hgt
        col = shifted(to_col, -1, 0)
        hgt = shifted(e_low, 0, -1)
        e, power, e_rows = kernel(
            functools.partial(e_rest_kernel, first),
            (field, whole, three_rows),
            [WHOLE] * 7,
            media + [h_hgt, e, power],
            f"e_rest_{step}",
            45,
            {5: 0, 6: 1},
        )

    def swap(x, axis):
        return lax.all_to_all(x, axis, split_axis=0, concat_axis=0, tiled=True)

    def across(x, turn):
        return lax.ppermute(x, "col", [(c, c ^ turn) for c in range(n_col)])

    def one_hot_space(sources):
        seats = sources * -(-cap // LANES) * LANES
        return [pltpu.VMEM((node_count, seats), jnp.bfloat16), pltpu.VMEM((seats, 2 * PTS), jnp.bfloat16)]

    node_rows = jax.ShapeDtypeStruct((node_count, PTS), F32)
    from_pair = across(pair, 1)
    other_blocks = swap(other, "hgt")
    sums = kernel(
        functools.partial(collect_kernel, cap),
        (node_rows,) * (n_col - 2),
        [WHOLE],
        [other_blocks],
        "collect_other",
        1,
        scratch=one_hot_space(n_hgt),
    )
    parts = [across(sums[turn - 2], turn) for turn in range(2, n_col)]
    mine = pl.pallas_call(
        merge_kernel,
        out_shape=pltpu.HBM((n_hgt, 2 * heights[0], PTS), F32),
        in_specs=[pl.BlockSpec(memory_space=pl.ANY), FAR],
        out_specs=FAR,
        input_output_aliases={1: 0},
        scratch_shapes=[sem((n_hgt,))],
        compiler_params=params(VMEM_MIB),
        cost_estimate=cost(1, 1),
        name="merge",
    )(from_pair, mine)
    mine_blocks = swap(mine, "hgt")
    own = kernel(
        functools.partial(collect_mine_kernel, cap),
        node_rows,
        [WHOLE],
        [mine_blocks],
        "collect_mine",
        1,
        scratch=one_hot_space(2 * n_hgt),
    )
    node_temp = kernel(
        finish_kernel, node_rows, [WHOLE] * (n_col), [node_enthalpy, own, *parts], "finish", 1
    )
    return e_out, h_out, node_temp


def solution(mesh):
    placed = (
        P(None, "col", "hgt", None),
        P(None, "col", "hgt", None),
        P("col", "hgt", None),
        P("col", "hgt", None),
        P("col", "hgt", None, None, None, None),
        P("col", "hgt", None, None, None),
        P(("col", "hgt"), None),
    )
    return jax.shard_map(
        per_device,
        mesh=mesh,
        in_specs=placed,
        out_specs=(
            P(None, "col", "hgt", None),
            P(None, "col", "hgt", None),
            P(("col", "hgt"), None),
        ),
        check_vma=False,
    )
```

```python
import functools

import jax
import jax.numpy as jnp
from jax import lax
from jax.experimental import pallas as pl
from jax.experimental.pallas import tpu as pltpu
from jax.sharding import PartitionSpec as P

PTS = 128
STEPS = 4
COURANT = 0.55
LANES = 128
ROWS = 8
F32 = jnp.float32
VMEM_MIB = 20

WHOLE = pl.BlockSpec(memory_space=pltpu.VMEM)
SCALARS = pl.BlockSpec(memory_space=pltpu.SMEM)
FAR = pl.BlockSpec(memory_space=pltpu.HBM)


def vmem(*shape):
    return pltpu.VMEM(shape, F32)


def far(x):
    return pltpu.with_memory_space_constraint(x, pltpu.HBM)


def params(mib):
    return pltpu.CompilerParams(vmem_limit_bytes=mib << 20)


def cost(flops, moved):
    return pl.CostEstimate(flops=flops, bytes_accessed=moved, transcendentals=0)


def after_y(f):
    lane = lax.broadcasted_iota(jnp.int32, (ROWS, LANES), 1)
    n = f.shape[1] // LANES
    turned = [pltpu.roll(f[:, k * LANES : (k + 1) * LANES], LANES - 1, 1) for k in range(n)]
    turned.append(jnp.zeros((ROWS, LANES), F32))
    return jnp.concatenate([jnp.where(lane < LANES - 1, turned[k], turned[k + 1]) for k in range(n)], 1)


def before_y(f):
    lane = lax.broadcasted_iota(jnp.int32, (ROWS, LANES), 1)
    n = f.shape[1] // LANES
    turned = [jnp.zeros((ROWS, LANES), F32)]
    turned += [pltpu.roll(f[:, k * LANES : (k + 1) * LANES], 1, 1) for k in range(n)]
    return jnp.concatenate([jnp.where(lane > 0, turned[k + 1], turned[k]) for k in range(n)], 1)


def after_row(f, row):
    place = lax.broadcasted_iota(jnp.int32, f.shape, 0)
    return jnp.where(place < ROWS - 1, pltpu.roll(f, ROWS - 1, 0), jnp.broadcast_to(row, f.shape))


def before_row(f, row):
    place = lax.broadcasted_iota(jnp.int32, f.shape, 0)
    return jnp.where(place > 0, pltpu.roll(f, 1, 0), jnp.broadcast_to(row, f.shape))


def edge_kernel(e, to_col, to_hgt, low, sems):
    nx = e.shape[1]
    col_copy = pltpu.make_async_copy(e.at[pl.ds(1, 2), 0], to_col, sems.at[0])
    low_copy = pltpu.make_async_copy(e.at[pl.ds(0, 2), :, pl.ds(0, ROWS)], low, sems.at[1])
    low_copy.start()
    col_copy.start()
    low_copy.wait()
    for x in range(nx):
        for comp in range(2):
            to_hgt[comp, x : x + 1, :] = low[comp, x, 0:1, :]
    col_copy.wait()


def load_kernel(
    temp_far, tags_far, e_far, h_far, order, ca, cb, sigma_out, e, h, media_rows, e_rows, h_rows, temp, tags, sems
):
    nx, nz, _ = temp.shape
    parts = 4
    size = nx // parts
    copies = []
    for part in range(parts):
        here = pl.ds(part * size, size)
        copies.append(pltpu.make_async_copy(temp_far.at[here], temp.at[here], sems.at[0, part]))
        copies.append(pltpu.make_async_copy(tags_far.at[here], tags.at[here], sems.at[1, part]))
    e_copy = pltpu.make_async_copy(e_far, e, sems.at[2, 0])
    h_copy = pltpu.make_async_copy(h_far, h, sems.at[2, 1])
    for copy in copies:
        copy.start()
    e_copy.start()
    h_copy.start()

    def plane(x, carry):
        for z in range(0, nz, ROWS):
            tag = tags[x, z : z + ROWS, :]
            lean = tag == 0
            fat = tag == 1
            frac = 1.0 / (1.0 + jnp.exp(-2.0 * temp[x, z : z + ROWS, :]))
            eps_low = jnp.where(lean, 4.0, jnp.where(fat, 2.5, 5.0))
            eps_rise = jnp.where(lean, 46.0, jnp.where(fat, 3.5, 5.0))
            sig_low = jnp.where(lean, 0.2, jnp.where(fat, 0.05, 0.1))
            sig_rise = jnp.where(lean, 7.8, jnp.where(fat, 0.35, 0.9))
            eps = eps_low + eps_rise * frac
            sigma = sig_low + sig_rise * frac
            half = (0.5 * COURANT) * sigma
            inverse = 1.0 / (eps + half)
            ca[x, z : z + ROWS, :] = (eps - half) * inverse
            cb[x, z : z + ROWS, :] = COURANT * inverse
            sigma_out[x, z : z + ROWS, :] = sigma
        media_rows[0, pl.ds(x, 1), :] = ca[x, 0:1, :]
        media_rows[1, pl.ds(x, 1), :] = cb[x, 0:1, :]
        return carry

    for part in range(parts):
        copies[2 * part].wait()
        copies[2 * part + 1].wait()
        lax.fori_loop(part * size, (part + 1) * size, plane, 0)
    e_copy.wait()
    h_copy.wait()

    def rows(x, carry):
        for comp in range(3):
            e_rows[comp, pl.ds(x, 1), :] = e[comp, x, nz - 1 : nz, :]
        for comp in range(2):
            h_rows[comp, pl.ds(x, 1), :] = h[comp, x, nz - 1 : nz, :]
        return carry

    lax.fori_loop(0, nx, rows, 0)


def over(first, stop, body):
    if stop - first == 1:
        body(first)
    else:

        def step(x, carry):
            body(x)
            return carry

        lax.fori_loop(first, stop, step, 0)


def h_tile(e, h, col, hgt, x, z):
    nz = e.shape[2]
    here = slice(z, z + ROWS)
    ex, ey, ez = (e[comp, x, here, :] for comp in range(3))
    if z + ROWS < nz:
        row_x, row_y = (e[comp, x, z + ROWS : z + ROWS + 1, :] for comp in range(2))
    else:
        row_x, row_y = (hgt[comp, pl.ds(x, 1), :] for comp in range(2))
    if col is None:
        next_y, next_z = (e[comp, x + 1, here, :] for comp in (1, 2))
    else:
        next_y, next_z = (col[comp, here, :] for comp in range(2))
    h[0, x, here, :] = h[0, x, here, :] - COURANT * ((after_y(ez) - ez) - (after_row(ey, row_y) - ey))
    hy = h[1, x, here, :] - COURANT * ((after_row(ex, row_x) - ex) - (next_z - ez))
    hz = h[2, x, here, :] - COURANT * ((next_y - ey) - (after_y(ex) - ex))
    h[1, x, here, :] = hy
    h[2, x, here, :] = hz
    return hy, hz


def e_tile(first, h, e, power, ca, cb, sigma, col, hgt, x, z):
    here = slice(z, z + ROWS)
    hx, hy, hz = (h[comp, x, here, :] for comp in range(3))
    if z > 0:
        row_x, row_y = (h[comp, x, z - 1 : z, :] for comp in range(2))
    else:
        row_x, row_y = (hgt[comp, pl.ds(x, 1), :] for comp in range(2))
    if col is None:
        past_y, past_z = (h[comp, x - 1, here, :] for comp in (1, 2))
    else:
        past_y, past_z = (col[comp, here, :] for comp in range(2))
    keep = ca[x, here, :]
    drive = cb[x, here, :]
    ex = keep * e[0, x, here, :] + drive * ((hz - before_y(hz)) - (hy - before_row(hy, row_y)))
    ey = keep * e[1, x, here, :] + drive * ((hx - before_row(hx, row_x)) - (hz - past_z))
    ez = keep * e[2, x, here, :] + drive * ((hy - past_y) - (hx - before_y(hx)))
    e[0, x, here, :] = ex
    e[1, x, here, :] = ey
    e[2, x, here, :] = ez
    heat = sigma[x, here, :] * (ex * ex + ey * ey + ez * ez)
    power[x, here, :] = heat if first else power[x, here, :] + heat
    return ey, ez


def h_edge_kernel(e, col, hgt, e_rows, rows_old, h_old, h, to_col, to_hgt):
    nx, nz = e.shape[1:3]
    for z in range(0, nz, ROWS):
        hy, hz = h_tile(e, h, col, hgt, nx - 1, z)
        to_col[0, z : z + ROWS, :] = hy
        to_col[1, z : z + ROWS, :] = hz
    for x in range(0, nx, ROWS):
        here = slice(x, x + ROWS)
        ex, ey, ez = (e_rows[comp, here, :] for comp in range(3))
        row = e_rows[2, x + ROWS : x + ROWS + 1, :] if x + ROWS < nx else col[1, nz - 1 : nz, :]
        to_hgt[0, here, :] = rows_old[0, here, :] - COURANT * ((after_y(ez) - ez) - (hgt[1, here, :] - ey))
        to_hgt[1, here, :] = rows_old[1, here, :] - COURANT * ((hgt[0, here, :] - ex) - (after_row(ez, row) - ez))


def h_rest_kernel(e, hgt, h_old, h, *rows):
    nx, nz = e.shape[1:3]

    def keep(x):
        if rows:
            for comp in range(3):
                rows[0][comp, pl.ds(x, 1), :] = h[comp, x, 0:1, :]

    def plane(x):
        for z in range(0, nz, ROWS):
            h_tile(e, h, None, hgt, x, z)
        keep(x)

    over(0, nx - 1, plane)
    keep(nx - 1)


def e_edge_kernel(first, h, ca, cb, sigma, col, hgt, media_rows, h_rows, rows_old, *refs):
    e, power, to_col, to_hgt = refs[-4:]
    nx, nz = e.shape[1:3]
    for z in range(0, nz, ROWS):
        ey, ez = e_tile(first, h, e, power, ca, cb, sigma, col, hgt, 0, z)
        to_col[0, z : z + ROWS, :] = ey
        to_col[1, z : z + ROWS, :] = ez
    for x in range(0, nx, ROWS):
        here = slice(x, x + ROWS)
        hx, hy, hz = (h_rows[comp, here, :] for comp in range(3))
        row = h_rows[2, x - 1 : x, :] if x > 0 else col[1, 0:1, :]
        keep = media_rows[0, here, :]
        drive = media_rows[1, here, :]
        to_hgt[0, here, :] = keep * rows_old[0, here, :] + drive * ((hz - before_y(hz)) - (hy - hgt[1, here, :]))
        to_hgt[1, here, :] = keep * rows_old[1, here, :] + drive * ((hx - hgt[0, here, :]) - (hz - before_row(hz, row)))


def e_rest_kernel(first, h, ca, cb, sigma, hgt, e_old, power_old, e, power, rows):
    nx, nz = e.shape[1:3]

    def keep(x):
        for comp in range(3):
            rows[comp, pl.ds(x, 1), :] = e[comp, x, nz - 1 : nz, :]

    def plane(x):
        for z in range(0, nz, ROWS):
            e_tile(first, h, e, power, ca, cb, sigma, None, hgt, x, z)
        keep(x)

    keep(0)
    over(1, nx, plane)


def e_last_kernel(first, h, ca, cb, sigma, col, hgt, e_old, power_old, e, power, h_out, sem):
    nx, nz = e.shape[1:3]
    copy = pltpu.make_async_copy(h, h_out, sem)
    copy.start()

    def plane(x):
        for z in range(0, nz, ROWS):
            e_tile(first, h, e, power, ca, cb, sigma, col if isinstance(x, int) else None, hgt, x, z)

    plane(0)
    over(1, nx, plane)
    copy.wait()


def places_kernel(n_col, n_hgt, cap, my_col, owner, node, place, flat):
    n_dev = n_col * n_hgt
    count = owner.shape[1]
    width = 256
    rows = lax.broadcasted_iota(jnp.int32, (n_dev, width), 0)
    before = lax.broadcasted_iota(jnp.int32, (width, width), 0)
    after = lax.broadcasted_iota(jnp.int32, (width, width), 1)
    upper = jnp.where(before <= after, 1.0, 0.0).astype(jnp.bfloat16)
    per = -(-cap // LANES)
    room_for = per * LANES
    room = lax.broadcasted_iota(jnp.int32, (room_for, width), 0)
    total = jnp.zeros((n_dev, 1), F32)
    parts_of = jnp.zeros((2 * n_dev, room_for), F32)
    nt = (((1,), (1,)), ((), ()))
    begins, heights = starts_of(n_col, n_hgt, cap)
    for start in range(0, count, width):
        own = owner[:, start : start + width]
        hit = jnp.where(rows == own, 1.0, 0.0)
        running = total + jnp.dot(hit.astype(jnp.bfloat16), upper, preferred_element_type=F32)
        total = running[:, width - 1 : width]
        rank = jnp.sum(hit * running, axis=0, keepdims=True).astype(jnp.int32) - 1
        turn = lax.bitwise_xor(lax.div(own, n_hgt), my_col[0])
        own_hgt = lax.rem(own, n_hgt)
        begin = jnp.where(
            turn == 0,
            begins[0] + own_hgt * heights[0],
            jnp.where(
                turn == 1,
                begins[1] + own_hgt * heights[1],
                begins[2] + own_hgt * heights[2] + (turn - 2) * cap,
            ),
        )
        place[:, start : start + width] = begin + rank
        number = node[:, start : start + width]
        upper_part = lax.div(number, 16)
        lower_part = number - 16 * upper_part
        seat = jnp.where(room == rank, 1.0, 0.0).astype(jnp.bfloat16)
        both = jnp.concatenate([hit * upper_part.astype(F32), hit * lower_part.astype(F32)], 0)
        parts_of = parts_of + lax.dot_general(both.astype(jnp.bfloat16), seat, nt, preferred_element_type=F32)
    taken = lax.broadcasted_iota(jnp.int32, (n_dev, room_for), 1).astype(F32) < total
    table = jnp.where(taken, 16.0 * parts_of[:n_dev] + parts_of[n_dev:], -1.0)
    chunk = 8 * ROWS

    def clear(i, carry):
        flat[pl.ds(pl.multiple_of(i * chunk, chunk), chunk), :] = jnp.zeros((chunk, PTS), F32)
        return carry

    lax.fori_loop(0, flat.shape[0] // chunk, clear, 0)
    for at in range(flat.shape[0] // chunk * chunk, flat.shape[0], ROWS):
        flat[at : at + ROWS, :] = jnp.zeros((ROWS, PTS), F32)
    behind = [cap, cap, (n_col - 2) * cap]
    for begin, height, skip in zip(begins, heights, behind):
        for part in range(n_hgt):
            at = begin + part * height
            flat[at + skip : at + height, :] = jnp.full((height - skip, PTS), -1.0, F32)
    for group in range(n_col):
        turn = lax.bitwise_xor(jnp.int32(group), my_col[0])
        kind = jnp.minimum(turn, 2)
        begin = jnp.where(kind == 0, begins[0], jnp.where(kind == 1, begins[1], begins[2]))
        height = jnp.where(kind == 2, heights[2], heights[0])
        skip = jnp.where(kind == 2, behind[2] + (turn - 2) * per, cap)
        for part in range(n_hgt):
            at = group * n_hgt + part
            for piece in range(per):
                row = table[at : at + 1, piece * LANES : (piece + 1) * LANES]
                flat[pl.ds(begin + part * height + skip + piece, 1), :] = row


def table_rows(parts, cap):
    return -(-parts * -(-cap // LANES) // ROWS) * ROWS


def starts_of(n_col, n_hgt, cap):
    one = cap + table_rows(1, cap)
    heights = [one, one, (n_col - 2) * cap + table_rows(n_col - 2, cap)]
    return [0, n_hgt * heights[0], n_hgt * (heights[0] + heights[1])], heights


def pack_kernel(heights, place, power, flat_old, e, pair, other, e_out, flat, sems):
    nx, nz, ny = power.shape
    e_copy = pltpu.make_async_copy(e, e_out, sems.at[0])
    e_copy.start()
    per_row = ny // PTS

    def plane(x, carry):
        for z in range(nz):
            for k in range(per_row):
                spot = place[x * (nz * per_row) + z * per_row + k]
                flat[pl.ds(spot, 1), :] = power[x, z : z + 1, k * PTS : (k + 1) * PTS]
        return carry

    lax.fori_loop(0, nx, plane, 0)
    copies = []
    first = pair.shape[0] * heights[0]
    for out, rows in zip((pair, other), heights[1:]):
        for group in range(out.shape[0]):
            target = out.at[group, pl.ds(0, rows)]
            copies.append(pltpu.make_async_copy(flat.at[pl.ds(first, rows)], target, sems.at[1 + len(copies)]))
            first += rows
    for copy in copies:
        copy.start()
    for copy in copies:
        copy.wait()
    e_copy.wait()


def summed(blocks, first, cap, node_row, chosen, split, node_count):
    ids = lax.broadcasted_iota(jnp.int32, (node_count, LANES), 0).astype(F32)
    n_from, _, pts = blocks.shape
    per = -(-cap // LANES)
    many = len(first)
    for source in range(n_from):
        for i in range(many):
            seat = (source * many + i) * per * LANES
            for piece in range(per):
                row = node_row[i] + piece
                lanes = slice(seat + piece * LANES, seat + (piece + 1) * LANES)
                hit = ids == blocks[source, row : row + 1, :]
                chosen[:, lanes] = jnp.where(hit, 1.0, 0.0).astype(jnp.bfloat16)
            values = blocks[source, first[i] : first[i] + cap, :]
            high = values.astype(jnp.bfloat16)
            split[seat : seat + cap, 0:pts] = high
            split[seat : seat + cap, pts : 2 * pts] = (values - high.astype(F32)).astype(jnp.bfloat16)
    both = jnp.dot(chosen[...], split[...], preferred_element_type=F32)
    return both[:, 0:pts] + both[:, pts : 2 * pts]


def collect_kernel(part, cap, blocks, out, chosen, split, mine, sems):
    n_from = blocks.shape[0]
    rest = mine.shape[1] - cap
    begin = blocks.shape[1] - rest
    per = -(-cap // LANES)
    copies = []
    for source in range(n_from):
        rows = blocks.at[source, pl.ds(part * cap, cap)]
        nodes = blocks.at[source, pl.ds(begin, rest)]
        copies.append(pltpu.make_async_copy(rows, mine.at[source, pl.ds(0, cap)], sems.at[0, source]))
        copies.append(pltpu.make_async_copy(nodes, mine.at[source, pl.ds(cap, rest)], sems.at[1, source]))
    for copy in copies:
        copy.start()
    split[...] = jnp.zeros(split.shape, split.dtype)
    for copy in copies:
        copy.wait()
    out[...] = summed(mine, [0], cap, [cap + part * per], chosen, split, out.shape[0])


def own_kernel(cap, height, flat, mine, sems):
    copies = [
        pltpu.make_async_copy(flat.at[pl.ds(group * height, cap)], mine.at[group, pl.ds(0, cap)], sems.at[group])
        for group in range(mine.shape[0])
    ]
    for copy in copies:
        copy.start()
    for copy in copies:
        copy.wait()


def merge_kernel(cap, height, flat, pair, mine_old, mine, tile, sems):
    per = -(-cap // LANES)
    groups = mine.shape[0]
    copies = []
    for group in range(groups):
        target = mine.at[group, pl.ds(cap, cap)]
        copies.append(pltpu.make_async_copy(pair.at[group, pl.ds(0, cap)], target, sems.at[0, group]))
    for copy in copies:
        copy.start()
    rest = tile.shape[1]
    tile[...] = jnp.full(tile.shape, -1.0, F32)
    for group in range(groups):
        tile[group, 0:per, :] = pair[group, cap : cap + per, :]
        tile[group, per : 2 * per, :] = flat[group * height + cap : group * height + cap + per, :]
        target = mine.at[group, pl.ds(2 * cap, rest)]
        copies.append(pltpu.make_async_copy(tile.at[group], target, sems.at[1, group]))
        copies[-1].start()
    for copy in copies:
        copy.wait()


def collect_mine_kernel(cap, blocks, out, chosen, split):
    per = -(-cap // LANES)
    split[...] = jnp.zeros(split.shape, split.dtype)
    out[...] = summed(blocks, [0, cap], cap, [2 * cap + per, 2 * cap], chosen, split, out.shape[0])


def finish_kernel(enthalpy, *refs):
    *parts, out = refs
    heat = parts[0][...]
    for part in parts[1:]:
        heat = heat + part[...]
    content = enthalpy[...] + (0.25 / STEPS) * heat
    out[...] = jnp.where(content < 0.0, content / 2.0, jnp.where(content > 1.0, (content - 1.0) / 3.0, 0.0))


def shifted(block, d_col, d_hgt):
    n_col = lax.axis_size("col")
    n_hgt = lax.axis_size("hgt")
    route = [
        (c * n_hgt + h, (c + d_col) * n_hgt + h + d_hgt)
        for c in range(n_col)
        for h in range(n_hgt)
        if 0 <= c + d_col < n_col and 0 <= h + d_hgt < n_hgt
    ]
    return lax.ppermute(block, ("col", "hgt"), route)


def per_device(
    efield_lattice_vector,
    hfield_lattice_vector,
    cell_temp,
    region_tags,
    block_owner,
    block_node,
    node_enthalpy,
):
    nx, nz, ny = cell_temp.shape
    n_col = lax.axis_size("col")
    n_hgt = lax.axis_size("hgt")
    n_dev = n_col * n_hgt
    count = nx * nz * ny // PTS
    cap = 2 * count // n_dev
    node_count = node_enthalpy.shape[0]
    cells = nx * nz * ny
    sem = pltpu.SemaphoreType.DMA

    def kernel(body, outs, ins, args, name, work, aliases=None, scratch=()):
        return pl.pallas_call(
            body,
            out_shape=outs,
            in_specs=ins,
            out_specs=jax.tree.map(lambda out: WHOLE, outs),
            input_output_aliases=aliases or {},
            scratch_shapes=scratch,
            compiler_params=params(VMEM_MIB),
            cost_estimate=cost(work * cells, work * cells),
            name=name,
        )(*args)

    e_start = far(efield_lattice_vector)
    h_start = far(hfield_lattice_vector)
    my_col = lax.axis_index("col").astype(jnp.int32).reshape(1)
    owners = block_owner.reshape(1, count)
    nodes = block_node.reshape(1, count)
    field = vmem(3, nx, nz, ny)
    whole = vmem(nx, nz, ny)
    planes = vmem(2, nz, ny)
    two_rows = vmem(2, nx, ny)
    three_rows = vmem(3, nx, ny)

    to_col, e_low = kernel(
        edge_kernel, (planes, two_rows), [FAR], [e_start], "edge", 4, scratch=[vmem(2, nx, ROWS, ny), sem((2,))]
    )
    col = shifted(to_col, -1, 0)
    hgt = shifted(e_low, 0, -1)
    ca, cb, sigma, e, h, media_rows, e_rows, h_high = kernel(
        load_kernel,
        (whole, whole, whole, field, field, two_rows, three_rows, two_rows),
        [FAR] * 4 + [WHOLE],
        [far(cell_temp), far(region_tags), e_start, h_start, owners + nodes + my_col],
        "load",
        60,
        scratch=[vmem(nx, nz, ny), pltpu.VMEM((nx, nz, ny), jnp.int32), sem((3, 4))],
    )
    begins, heights = starts_of(n_col, n_hgt, cap)
    place, flat = kernel(
        functools.partial(places_kernel, n_col, n_hgt, cap),
        (jax.ShapeDtypeStruct((1, count), jnp.int32), vmem(n_hgt * sum(heights), PTS)),
        [SCALARS, WHOLE, WHOLE],
        [my_col, owners, nodes],
        "places",
        8,
    )
    power = None
    for step in range(STEPS):
        first = step == 0
        h, to_col, h_high = kernel(
            h_edge_kernel,
            (field, planes, two_rows),
            [WHOLE] * 6,
            [e, col, hgt, e_rows, h_high, h],
            f"h_edge_{step}",
            4,
            {5: 0},
        )
        e_hgt = hgt
        col = shifted(to_col, 1, 0)
        hgt = shifted(h_high, 0, 1)
        last = step == STEPS - 1
        outs = (field,) if last else (field, three_rows)
        h, *h_rows = kernel(h_rest_kernel, outs, [WHOLE] * 3, [e, e_hgt, h], f"h_rest_{step}", 40, {2: 0})
        media = [h, ca, cb, sigma]
        if last:
            e, power, h_out = pl.pallas_call(
                functools.partial(e_last_kernel, first),
                out_shape=(field, whole, pltpu.HBM((3, nx, nz, ny), F32)),
                in_specs=[WHOLE] * 8,
                out_specs=(WHOLE, WHOLE, FAR),
                input_output_aliases={6: 0, 7: 1},
                scratch_shapes=[sem],
                compiler_params=params(VMEM_MIB),
                cost_estimate=cost(cells * 50, cells * 50),
                name="e_last",
            )(*media, col, hgt, e, power)
            break
        args = media + [col, hgt, media_rows, *h_rows, e_low, e] + ([] if first else [power])
        e, power, to_col, e_low = kernel(
            functools.partial(e_edge_kernel, first),
            (field, whole, planes, two_rows),
            [WHOLE] * len(args),
            args,
            f"e_edge_{step}",
            5,
            {9: 0} if first else {9: 0, 10: 1},
        )
        h_hgt = hgt
        col = shifted(to_col, -1, 0)
        hgt = shifted(e_low, 0, -1)
        e, power, e_rows = kernel(
            functools.partial(e_rest_kernel, first),
            (field, whole, three_rows),
            [WHOLE] * 7,
            media + [h_hgt, e, power],
            f"e_rest_{step}",
            45,
            {5: 0, 6: 1},
        )

    pair, other, e_out, flat = pl.pallas_call(
        functools.partial(pack_kernel, heights),
        out_shape=(
            pltpu.HBM((n_hgt, heights[1], PTS), F32),
            pltpu.HBM((n_hgt, heights[2], PTS), F32),
            pltpu.HBM((3, nx, nz, ny), F32),
            vmem(n_hgt * sum(heights), PTS),
        ),
        in_specs=[SCALARS] + [WHOLE] * 3,
        out_specs=(FAR,) * 3 + (WHOLE,),
        input_output_aliases={2: 3},
        scratch_shapes=[sem((1 + 2 * n_hgt,))],
        compiler_params=params(VMEM_MIB),
        cost_estimate=cost(cells, cells * 36),
        name="pack",
    )(place.reshape(count), power, flat, e)

    def swap(x, axis):
        return lax.all_to_all(x, axis, split_axis=0, concat_axis=0, tiled=True)

    def across(x, turn):
        return lax.ppermute(x, "col", [(c, c ^ turn) for c in range(n_col)])

    def one_hot_space(sources):
        seats = sources * -(-cap // LANES) * LANES
        return [pltpu.VMEM((node_count, seats), jnp.bfloat16), pltpu.VMEM((seats, 2 * PTS), jnp.bfloat16)]

    node_rows = jax.ShapeDtypeStruct((node_count, PTS), F32)
    from_pair = across(pair, 1)
    other_blocks = swap(other, "hgt")
    sums = [
        kernel(
            functools.partial(collect_kernel, part, cap),
            node_rows,
            [pl.BlockSpec(memory_space=pl.ANY)],
            [other_blocks],
            f"collect_other_{part}",
            1,
            scratch=one_hot_space(n_hgt) + [vmem(n_hgt, cap + table_rows(n_col - 2, cap), PTS), sem((2, n_hgt))],
        )
        for part in range(n_col - 2)
    ]
    parts = [across(sums[turn - 2], turn) for turn in range(2, n_col)]
    both = pltpu.HBM((n_hgt, 2 * cap + table_rows(2, cap), PTS), F32)
    mine = pl.pallas_call(
        functools.partial(own_kernel, cap, heights[0]),
        out_shape=both,
        in_specs=[WHOLE],
        out_specs=FAR,
        scratch_shapes=[sem((n_hgt,))],
        compiler_params=params(VMEM_MIB),
        cost_estimate=cost(cells, cells * 20),
        name="own",
    )(flat)
    mine = pl.pallas_call(
        functools.partial(merge_kernel, cap, heights[0]),
        out_shape=both,
        in_specs=[WHOLE, WHOLE, FAR],
        out_specs=FAR,
        input_output_aliases={2: 0},
        scratch_shapes=[vmem(n_hgt, table_rows(2, cap), PTS), sem((2, n_hgt))],
        compiler_params=params(VMEM_MIB),
        cost_estimate=cost(1, 1),
        name="merge",
    )(flat, from_pair, mine)
    mine_blocks = swap(mine, "hgt")
    own = kernel(
        functools.partial(collect_mine_kernel, cap),
        node_rows,
        [WHOLE],
        [mine_blocks],
        "collect_mine",
        1,
        scratch=one_hot_space(2 * n_hgt),
    )
    node_temp = kernel(
        finish_kernel, node_rows, [WHOLE] * (n_col), [node_enthalpy, own, *parts], "finish", 1
    )
    return e_out, h_out, node_temp


def solution(mesh):
    placed = (
        P(None, "col", "hgt", None),
        P(None, "col", "hgt", None),
        P("col", "hgt", None),
        P("col", "hgt", None),
        P("col", "hgt", None, None, None, None),
        P("col", "hgt", None, None, None),
        P(("col", "hgt"), None),
    )
    return jax.shard_map(
        per_device,
        mesh=mesh,
        in_specs=placed,
        out_specs=(
            P(None, "col", "hgt", None),
            P(None, "col", "hgt", None),
            P(("col", "hgt"), None),
        ),
        check_vma=False,
    )
```

```python
import functools

import jax
import jax.numpy as jnp
from jax import lax
from jax.experimental import pallas as pl
from jax.experimental.pallas import tpu as pltpu
from jax.sharding import PartitionSpec as P

PTS = 128
STEPS = 4
COURANT = 0.55
LANES = 128
ROWS = 8
F32 = jnp.float32
VMEM_MIB = 20

WHOLE = pl.BlockSpec(memory_space=pltpu.VMEM)
SCALARS = pl.BlockSpec(memory_space=pltpu.SMEM)
FAR = pl.BlockSpec(memory_space=pltpu.HBM)


def vmem(*shape):
    return pltpu.VMEM(shape, F32)


def far(x):
    return pltpu.with_memory_space_constraint(x, pltpu.HBM)


def params(mib):
    return pltpu.CompilerParams(vmem_limit_bytes=mib << 20)


def cost(flops, moved):
    return pl.CostEstimate(flops=flops, bytes_accessed=moved, transcendentals=0)


def after_y(f):
    lane = lax.broadcasted_iota(jnp.int32, (ROWS, LANES), 1)
    n = f.shape[1] // LANES
    turned = [pltpu.roll(f[:, k * LANES : (k + 1) * LANES], LANES - 1, 1) for k in range(n)]
    turned.append(jnp.zeros((ROWS, LANES), F32))
    return jnp.concatenate([jnp.where(lane < LANES - 1, turned[k], turned[k + 1]) for k in range(n)], 1)


def before_y(f):
    lane = lax.broadcasted_iota(jnp.int32, (ROWS, LANES), 1)
    n = f.shape[1] // LANES
    turned = [jnp.zeros((ROWS, LANES), F32)]
    turned += [pltpu.roll(f[:, k * LANES : (k + 1) * LANES], 1, 1) for k in range(n)]
    return jnp.concatenate([jnp.where(lane > 0, turned[k + 1], turned[k]) for k in range(n)], 1)


def after_row(f, row):
    place = lax.broadcasted_iota(jnp.int32, f.shape, 0)
    return jnp.where(place < ROWS - 1, pltpu.roll(f, ROWS - 1, 0), jnp.broadcast_to(row, f.shape))


def before_row(f, row):
    place = lax.broadcasted_iota(jnp.int32, f.shape, 0)
    return jnp.where(place > 0, pltpu.roll(f, 1, 0), jnp.broadcast_to(row, f.shape))


def edge_kernel(e, to_col, to_hgt, low, sems):
    nx = e.shape[1]
    col_copy = pltpu.make_async_copy(e.at[pl.ds(1, 2), 0], to_col, sems.at[0])
    low_copy = pltpu.make_async_copy(e.at[pl.ds(0, 2), :, pl.ds(0, ROWS)], low, sems.at[1])
    low_copy.start()
    col_copy.start()
    low_copy.wait()
    for x in range(nx):
        for comp in range(2):
            to_hgt[comp, x : x + 1, :] = low[comp, x, 0:1, :]
    col_copy.wait()


def load_kernel(
    temp_far, tags_far, e_far, h_far, order, ca, cb, sigma_out, e, h, media_rows, e_rows, h_rows, temp, tags, sems
):
    nx, nz, _ = temp.shape
    parts = 4
    size = nx // parts
    copies = []
    for part in range(parts):
        here = pl.ds(part * size, size)
        copies.append(pltpu.make_async_copy(temp_far.at[here], temp.at[here], sems.at[0, part]))
        copies.append(pltpu.make_async_copy(tags_far.at[here], tags.at[here], sems.at[1, part]))
    e_copy = pltpu.make_async_copy(e_far, e, sems.at[2, 0])
    h_copy = pltpu.make_async_copy(h_far, h, sems.at[2, 1])
    for copy in copies:
        copy.start()
    e_copy.start()
    h_copy.start()

    def plane(x, carry):
        for z in range(0, nz, ROWS):
            tag = tags[x, z : z + ROWS, :]
            lean = tag == 0
            fat = tag == 1
            frac = 1.0 / (1.0 + jnp.exp(-2.0 * temp[x, z : z + ROWS, :]))
            eps_low = jnp.where(lean, 4.0, jnp.where(fat, 2.5, 5.0))
            eps_rise = jnp.where(lean, 46.0, jnp.where(fat, 3.5, 5.0))
            sig_low = jnp.where(lean, 0.2, jnp.where(fat, 0.05, 0.1))
            sig_rise = jnp.where(lean, 7.8, jnp.where(fat, 0.35, 0.9))
            eps = eps_low + eps_rise * frac
            sigma = sig_low + sig_rise * frac
            half = (0.5 * COURANT) * sigma
            inverse = 1.0 / (eps + half)
            ca[x, z : z + ROWS, :] = (eps - half) * inverse
            cb[x, z : z + ROWS, :] = COURANT * inverse
            sigma_out[x, z : z + ROWS, :] = sigma
        media_rows[0, pl.ds(x, 1), :] = ca[x, 0:1, :]
        media_rows[1, pl.ds(x, 1), :] = cb[x, 0:1, :]
        return carry

    for part in range(parts):
        copies[2 * part].wait()
        copies[2 * part + 1].wait()
        lax.fori_loop(part * size, (part + 1) * size, plane, 0)
    e_copy.wait()
    h_copy.wait()

    def rows(x, carry):
        for comp in range(3):
            e_rows[comp, pl.ds(x, 1), :] = e[comp, x, nz - 1 : nz, :]
        for comp in range(2):
            h_rows[comp, pl.ds(x, 1), :] = h[comp, x, nz - 1 : nz, :]
        return carry

    lax.fori_loop(0, nx, rows, 0)


def over(first, stop, body):
    if stop - first == 1:
        body(first)
    else:

        def step(x, carry):
            body(x)
            return carry

        lax.fori_loop(first, stop, step, 0)


def h_tile(e, h, col, hgt, x, z):
    nz = e.shape[2]
    here = slice(z, z + ROWS)
    ex, ey, ez = (e[comp, x, here, :] for comp in range(3))
    if z + ROWS < nz:
        row_x, row_y = (e[comp, x, z + ROWS : z + ROWS + 1, :] for comp in range(2))
    else:
        row_x, row_y = (hgt[comp, pl.ds(x, 1), :] for comp in range(2))
    if col is None:
        next_y, next_z = (e[comp, x + 1, here, :] for comp in (1, 2))
    else:
        next_y, next_z = (col[comp, here, :] for comp in range(2))
    h[0, x, here, :] = h[0, x, here, :] - COURANT * ((after_y(ez) - ez) - (after_row(ey, row_y) - ey))
    hy = h[1, x, here, :] - COURANT * ((after_row(ex, row_x) - ex) - (next_z - ez))
    hz = h[2, x, here, :] - COURANT * ((next_y - ey) - (after_y(ex) - ex))
    h[1, x, here, :] = hy
    h[2, x, here, :] = hz
    return hy, hz


def e_tile(first, h, e, power, ca, cb, sigma, col, hgt, x, z):
    here = slice(z, z + ROWS)
    hx, hy, hz = (h[comp, x, here, :] for comp in range(3))
    if z > 0:
        row_x, row_y = (h[comp, x, z - 1 : z, :] for comp in range(2))
    else:
        row_x, row_y = (hgt[comp, pl.ds(x, 1), :] for comp in range(2))
    if col is None:
        past_y, past_z = (h[comp, x - 1, here, :] for comp in (1, 2))
    else:
        past_y, past_z = (col[comp, here, :] for comp in range(2))
    keep = ca[x, here, :]
    drive = cb[x, here, :]
    ex = keep * e[0, x, here, :] + drive * ((hz - before_y(hz)) - (hy - before_row(hy, row_y)))
    ey = keep * e[1, x, here, :] + drive * ((hx - before_row(hx, row_x)) - (hz - past_z))
    ez = keep * e[2, x, here, :] + drive * ((hy - past_y) - (hx - before_y(hx)))
    e[0, x, here, :] = ex
    e[1, x, here, :] = ey
    e[2, x, here, :] = ez
    heat = sigma[x, here, :] * (ex * ex + ey * ey + ez * ez)
    power[x, here, :] = heat if first else power[x, here, :] + heat
    return ey, ez


def h_edge_kernel(e, col, hgt, e_rows, rows_old, h_old, h, to_col, to_hgt):
    nx, nz = e.shape[1:3]
    for z in range(0, nz, ROWS):
        hy, hz = h_tile(e, h, col, hgt, nx - 1, z)
        to_col[0, z : z + ROWS, :] = hy
        to_col[1, z : z + ROWS, :] = hz
    for x in range(0, nx, ROWS):
        here = slice(x, x + ROWS)
        ex, ey, ez = (e_rows[comp, here, :] for comp in range(3))
        row = e_rows[2, x + ROWS : x + ROWS + 1, :] if x + ROWS < nx else col[1, nz - 1 : nz, :]
        to_hgt[0, here, :] = rows_old[0, here, :] - COURANT * ((after_y(ez) - ez) - (hgt[1, here, :] - ey))
        to_hgt[1, here, :] = rows_old[1, here, :] - COURANT * ((hgt[0, here, :] - ex) - (after_row(ez, row) - ez))


def h_rest_kernel(e, hgt, h_old, h, *rows):
    nx, nz = e.shape[1:3]

    def keep(x):
        if rows:
            for comp in range(3):
                rows[0][comp, pl.ds(x, 1), :] = h[comp, x, 0:1, :]

    def plane(x):
        for z in range(0, nz, ROWS):
            h_tile(e, h, None, hgt, x, z)
        keep(x)

    over(0, nx - 1, plane)
    keep(nx - 1)


def e_edge_kernel(first, h, ca, cb, sigma, col, hgt, media_rows, h_rows, rows_old, *refs):
    e, power, to_col, to_hgt = refs[-4:]
    nx, nz = e.shape[1:3]
    for z in range(0, nz, ROWS):
        ey, ez = e_tile(first, h, e, power, ca, cb, sigma, col, hgt, 0, z)
        to_col[0, z : z + ROWS, :] = ey
        to_col[1, z : z + ROWS, :] = ez
    for x in range(0, nx, ROWS):
        here = slice(x, x + ROWS)
        hx, hy, hz = (h_rows[comp, here, :] for comp in range(3))
        row = h_rows[2, x - 1 : x, :] if x > 0 else col[1, 0:1, :]
        keep = media_rows[0, here, :]
        drive = media_rows[1, here, :]
        to_hgt[0, here, :] = keep * rows_old[0, here, :] + drive * ((hz - before_y(hz)) - (hy - hgt[1, here, :]))
        to_hgt[1, here, :] = keep * rows_old[1, here, :] + drive * ((hx - hgt[0, here, :]) - (hz - before_row(hz, row)))


def e_rest_kernel(first, h, ca, cb, sigma, hgt, e_old, power_old, e, power, rows):
    nx, nz = e.shape[1:3]

    def keep(x):
        for comp in range(3):
            rows[comp, pl.ds(x, 1), :] = e[comp, x, nz - 1 : nz, :]

    def plane(x):
        for z in range(0, nz, ROWS):
            e_tile(first, h, e, power, ca, cb, sigma, None, hgt, x, z)
        keep(x)

    keep(0)
    over(1, nx, plane)


def e_last_kernel(first, h, ca, cb, sigma, col, hgt, e_old, power_old, e, power, h_out, sem):
    nx, nz = e.shape[1:3]
    copy = pltpu.make_async_copy(h, h_out, sem)
    copy.start()

    def plane(x):
        for z in range(0, nz, ROWS):
            e_tile(first, h, e, power, ca, cb, sigma, col if isinstance(x, int) else None, hgt, x, z)

    plane(0)
    over(1, nx, plane)
    copy.wait()


def places_kernel(n_col, n_hgt, cap, my_col, owner, node, place, flat):
    n_dev = n_col * n_hgt
    count = owner.shape[1]
    width = 256
    rows = lax.broadcasted_iota(jnp.int32, (n_dev, width), 0)
    before = lax.broadcasted_iota(jnp.int32, (width, width), 0)
    after = lax.broadcasted_iota(jnp.int32, (width, width), 1)
    upper = jnp.where(before <= after, 1.0, 0.0).astype(jnp.bfloat16)
    per = -(-cap // LANES)
    room_for = per * LANES
    room = lax.broadcasted_iota(jnp.int32, (room_for, width), 0)
    total = jnp.zeros((n_dev, 1), F32)
    parts_of = jnp.zeros((2 * n_dev, room_for), F32)
    nt = (((1,), (1,)), ((), ()))
    begins, heights = starts_of(n_col, n_hgt, cap)
    for start in range(0, count, width):
        own = owner[:, start : start + width]
        hit = jnp.where(rows == own, 1.0, 0.0)
        running = total + jnp.dot(hit.astype(jnp.bfloat16), upper, preferred_element_type=F32)
        total = running[:, width - 1 : width]
        rank = jnp.sum(hit * running, axis=0, keepdims=True).astype(jnp.int32) - 1
        turn = lax.bitwise_xor(lax.div(own, n_hgt), my_col[0])
        own_hgt = lax.rem(own, n_hgt)
        begin = jnp.where(
            turn == 0,
            begins[0] + own_hgt * heights[0],
            jnp.where(
                turn == 1,
                begins[1] + own_hgt * heights[1],
                begins[2] + own_hgt * heights[2] + (turn - 2) * cap,
            ),
        )
        place[:, start : start + width] = begin + rank
        number = node[:, start : start + width]
        upper_part = lax.div(number, 16)
        lower_part = number - 16 * upper_part
        seat = jnp.where(room == rank, 1.0, 0.0).astype(jnp.bfloat16)
        both = jnp.concatenate([hit * upper_part.astype(F32), hit * lower_part.astype(F32)], 0)
        parts_of = parts_of + lax.dot_general(both.astype(jnp.bfloat16), seat, nt, preferred_element_type=F32)
    taken = lax.broadcasted_iota(jnp.int32, (n_dev, room_for), 1).astype(F32) < total
    table = jnp.where(taken, 16.0 * parts_of[:n_dev] + parts_of[n_dev:], -1.0)
    chunk = 8 * ROWS

    def clear(i, carry):
        flat[pl.ds(pl.multiple_of(i * chunk, chunk), chunk), :] = jnp.zeros((chunk, PTS), F32)
        return carry

    lax.fori_loop(0, flat.shape[0] // chunk, clear, 0)
    for at in range(flat.shape[0] // chunk * chunk, flat.shape[0], ROWS):
        flat[at : at + ROWS, :] = jnp.zeros((ROWS, PTS), F32)
    behind = [cap, cap, (n_col - 2) * cap]
    for begin, height, skip in zip(begins, heights, behind):
        for part in range(n_hgt):
            at = begin + part * height
            flat[at + skip : at + height, :] = jnp.full((height - skip, PTS), -1.0, F32)
    for group in range(n_col):
        turn = lax.bitwise_xor(jnp.int32(group), my_col[0])
        kind = jnp.minimum(turn, 2)
        begin = jnp.where(kind == 0, begins[0], jnp.where(kind == 1, begins[1], begins[2]))
        height = jnp.where(kind == 2, heights[2], heights[0])
        skip = jnp.where(kind == 2, behind[2] + (turn - 2) * per, cap)
        for part in range(n_hgt):
            at = group * n_hgt + part
            for piece in range(per):
                row = table[at : at + 1, piece * LANES : (piece + 1) * LANES]
                flat[pl.ds(begin + part * height + skip + piece, 1), :] = row


def table_rows(parts, cap):
    return -(-parts * -(-cap // LANES) // ROWS) * ROWS


def starts_of(n_col, n_hgt, cap):
    one = cap + table_rows(1, cap)
    heights = [one, one, (n_col - 2) * cap + table_rows(n_col - 2, cap)]
    return [0, n_hgt * heights[0], n_hgt * (heights[0] + heights[1])], heights


def pack_kernel(heights, place, power, flat_old, e, pair, other, e_out, flat, sems):
    nx, nz, ny = power.shape
    e_copy = pltpu.make_async_copy(e, e_out, sems.at[0])
    e_copy.start()
    per_row = ny // PTS

    def plane(x, carry):
        for z in range(nz):
            for k in range(per_row):
                spot = place[x * (nz * per_row) + z * per_row + k]
                flat[pl.ds(spot, 1), :] = power[x, z : z + 1, k * PTS : (k + 1) * PTS]
        return carry

    lax.fori_loop(0, nx, plane, 0)
    copies = []
    first = pair.shape[0] * heights[0]
    for out, rows in zip((pair, other), heights[1:]):
        for group in range(out.shape[0]):
            target = out.at[group, pl.ds(0, rows)]
            copies.append(pltpu.make_async_copy(flat.at[pl.ds(first, rows)], target, sems.at[1 + len(copies)]))
            first += rows
    for copy in copies:
        copy.start()
    for copy in copies:
        copy.wait()
    e_copy.wait()


def summed(blocks, first, cap, node_row, chosen, split, node_count):
    ids = lax.broadcasted_iota(jnp.int32, (node_count, LANES), 0).astype(F32)
    n_from, _, pts = blocks.shape
    per = -(-cap // LANES)
    many = len(first)
    for source in range(n_from):
        for i in range(many):
            seat = (source * many + i) * per * LANES
            for piece in range(per):
                row = node_row[i] + piece
                lanes = slice(seat + piece * LANES, seat + (piece + 1) * LANES)
                hit = ids == blocks[source, row : row + 1, :]
                chosen[:, lanes] = jnp.where(hit, 1.0, 0.0).astype(jnp.bfloat16)
            values = blocks[source, first[i] : first[i] + cap, :]
            high = values.astype(jnp.bfloat16)
            split[seat : seat + cap, 0:pts] = high
            split[seat : seat + cap, pts : 2 * pts] = (values - high.astype(F32)).astype(jnp.bfloat16)
    both = jnp.dot(chosen[...], split[...], preferred_element_type=F32)
    return both[:, 0:pts] + both[:, pts : 2 * pts]


def collect_kernel(cap, blocks, *refs):
    *outs, chosen, split, near, sems = refs
    n_from, rows, _ = blocks.shape
    per = -(-cap // LANES)
    after = len(outs) * cap
    pieces = [(after, rows - after)] + [(part * cap, cap) for part in range(len(outs))]
    copies = []
    for i, (begin, size) in enumerate(pieces):
        here = pl.ds(begin, size)
        copies.append(pltpu.make_async_copy(blocks.at[:, here], near.at[:, here], sems.at[i]))
        copies[i].start()
    split[...] = jnp.zeros(split.shape, split.dtype)
    copies[0].wait()
    for part, out in enumerate(outs):
        copies[1 + part].wait()
        out[...] = summed(near, [part * cap], cap, [after + part * per], chosen, split, out.shape[0])


def own_kernel(cap, height, flat, mine, sems):
    copies = [
        pltpu.make_async_copy(flat.at[pl.ds(group * height, cap)], mine.at[group, pl.ds(0, cap)], sems.at[group])
        for group in range(mine.shape[0])
    ]
    for copy in copies:
        copy.start()
    for copy in copies:
        copy.wait()


def merge_kernel(cap, height, flat, pair, mine_old, mine, tile, sems):
    per = -(-cap // LANES)
    groups = mine.shape[0]
    copies = []
    for group in range(groups):
        target = mine.at[group, pl.ds(cap, cap)]
        copies.append(pltpu.make_async_copy(pair.at[group, pl.ds(0, cap)], target, sems.at[0, group]))
    for copy in copies:
        copy.start()
    rest = tile.shape[1]
    tile[...] = jnp.full(tile.shape, -1.0, F32)
    for group in range(groups):
        tile[group, 0:per, :] = pair[group, cap : cap + per, :]
        tile[group, per : 2 * per, :] = flat[group * height + cap : group * height + cap + per, :]
        target = mine.at[group, pl.ds(2 * cap, rest)]
        copies.append(pltpu.make_async_copy(tile.at[group], target, sems.at[1, group]))
        copies[-1].start()
    for copy in copies:
        copy.wait()


def collect_mine_kernel(cap, blocks, out, chosen, split):
    per = -(-cap // LANES)
    split[...] = jnp.zeros(split.shape, split.dtype)
    out[...] = summed(blocks, [0, cap], cap, [2 * cap + per, 2 * cap], chosen, split, out.shape[0])


def finish_kernel(enthalpy, *refs):
    *parts, out = refs
    heat = parts[0][...]
    for part in parts[1:]:
        heat = heat + part[...]
    content = enthalpy[...] + (0.25 / STEPS) * heat
    out[...] = jnp.where(content < 0.0, content / 2.0, jnp.where(content > 1.0, (content - 1.0) / 3.0, 0.0))


def shifted(block, d_col, d_hgt):
    n_col = lax.axis_size("col")
    n_hgt = lax.axis_size("hgt")
    route = [
        (c * n_hgt + h, (c + d_col) * n_hgt + h + d_hgt)
        for c in range(n_col)
        for h in range(n_hgt)
        if 0 <= c + d_col < n_col and 0 <= h + d_hgt < n_hgt
    ]
    return lax.ppermute(block, ("col", "hgt"), route)


def per_device(
    efield_lattice_vector,
    hfield_lattice_vector,
    cell_temp,
    region_tags,
    block_owner,
    block_node,
    node_enthalpy,
):
    nx, nz, ny = cell_temp.shape
    n_col = lax.axis_size("col")
    n_hgt = lax.axis_size("hgt")
    n_dev = n_col * n_hgt
    count = nx * nz * ny // PTS
    cap = 2 * count // n_dev
    node_count = node_enthalpy.shape[0]
    cells = nx * nz * ny
    sem = pltpu.SemaphoreType.DMA

    def kernel(body, outs, ins, args, name, work, aliases=None, scratch=()):
        return pl.pallas_call(
            body,
            out_shape=outs,
            in_specs=ins,
            out_specs=jax.tree.map(lambda out: WHOLE, outs),
            input_output_aliases=aliases or {},
            scratch_shapes=scratch,
            compiler_params=params(VMEM_MIB),
            cost_estimate=cost(work * cells, work * cells),
            name=name,
        )(*args)

    e_start = far(efield_lattice_vector)
    h_start = far(hfield_lattice_vector)
    my_col = lax.axis_index("col").astype(jnp.int32).reshape(1)
    owners = block_owner.reshape(1, count)
    nodes = block_node.reshape(1, count)
    field = vmem(3, nx, nz, ny)
    whole = vmem(nx, nz, ny)
    planes = vmem(2, nz, ny)
    two_rows = vmem(2, nx, ny)
    three_rows = vmem(3, nx, ny)

    to_col, e_low = kernel(
        edge_kernel, (planes, two_rows), [FAR], [e_start], "edge", 4, scratch=[vmem(2, nx, ROWS, ny), sem((2,))]
    )
    col = shifted(to_col, -1, 0)
    hgt = shifted(e_low, 0, -1)
    ca, cb, sigma, e, h, media_rows, e_rows, h_high = kernel(
        load_kernel,
        (whole, whole, whole, field, field, two_rows, three_rows, two_rows),
        [FAR] * 4 + [WHOLE],
        [far(cell_temp), far(region_tags), e_start, h_start, owners + nodes + my_col],
        "load",
        60,
        scratch=[vmem(nx, nz, ny), pltpu.VMEM((nx, nz, ny), jnp.int32), sem((3, 4))],
    )
    begins, heights = starts_of(n_col, n_hgt, cap)
    place, flat = kernel(
        functools.partial(places_kernel, n_col, n_hgt, cap),
        (jax.ShapeDtypeStruct((1, count), jnp.int32), vmem(n_hgt * sum(heights), PTS)),
        [SCALARS, WHOLE, WHOLE],
        [my_col, owners, nodes],
        "places",
        8,
    )
    power = None
    for step in range(STEPS):
        first = step == 0
        h, to_col, h_high = kernel(
            h_edge_kernel,
            (field, planes, two_rows),
            [WHOLE] * 6,
            [e, col, hgt, e_rows, h_high, h],
            f"h_edge_{step}",
            4,
            {5: 0},
        )
        e_hgt = hgt
        col = shifted(to_col, 1, 0)
        hgt = shifted(h_high, 0, 1)
        last = step == STEPS - 1
        outs = (field,) if last else (field, three_rows)
        h, *h_rows = kernel(h_rest_kernel, outs, [WHOLE] * 3, [e, e_hgt, h], f"h_rest_{step}", 40, {2: 0})
        media = [h, ca, cb, sigma]
        if last:
            e, power, h_out = pl.pallas_call(
                functools.partial(e_last_kernel, first),
                out_shape=(field, whole, pltpu.HBM((3, nx, nz, ny), F32)),
                in_specs=[WHOLE] * 8,
                out_specs=(WHOLE, WHOLE, FAR),
                input_output_aliases={6: 0, 7: 1},
                scratch_shapes=[sem],
                compiler_params=params(VMEM_MIB),
                cost_estimate=cost(cells * 50, cells * 50),
                name="e_last",
            )(*media, col, hgt, e, power)
            break
        args = media + [col, hgt, media_rows, *h_rows, e_low, e] + ([] if first else [power])
        e, power, to_col, e_low = kernel(
            functools.partial(e_edge_kernel, first),
            (field, whole, planes, two_rows),
            [WHOLE] * len(args),
            args,
            f"e_edge_{step}",
            5,
            {9: 0} if first else {9: 0, 10: 1},
        )
        h_hgt = hgt
        col = shifted(to_col, -1, 0)
        hgt = shifted(e_low, 0, -1)
        e, power, e_rows = kernel(
            functools.partial(e_rest_kernel, first),
            (field, whole, three_rows),
            [WHOLE] * 7,
            media + [h_hgt, e, power],
            f"e_rest_{step}",
            45,
            {5: 0, 6: 1},
        )

    pair, other, e_out, flat = pl.pallas_call(
        functools.partial(pack_kernel, heights),
        out_shape=(
            pltpu.HBM((n_hgt, heights[1], PTS), F32),
            pltpu.HBM((n_hgt, heights[2], PTS), F32),
            pltpu.HBM((3, nx, nz, ny), F32),
            vmem(n_hgt * sum(heights), PTS),
        ),
        in_specs=[SCALARS] + [WHOLE] * 3,
        out_specs=(FAR,) * 3 + (WHOLE,),
        input_output_aliases={2: 3},
        scratch_shapes=[sem((1 + 2 * n_hgt,))],
        compiler_params=params(VMEM_MIB),
        cost_estimate=cost(cells, cells * 36),
        name="pack",
    )(place.reshape(count), power, flat, e)

    def swap(x, axis):
        return lax.all_to_all(x, axis, split_axis=0, concat_axis=0, tiled=True)

    def across(x, turn):
        return lax.ppermute(x, "col", [(c, c ^ turn) for c in range(n_col)])

    def one_hot_space(sources):
        seats = sources * -(-cap // LANES) * LANES
        return [pltpu.VMEM((node_count, seats), jnp.bfloat16), pltpu.VMEM((seats, 2 * PTS), jnp.bfloat16)]

    node_rows = jax.ShapeDtypeStruct((node_count, PTS), F32)
    from_pair = across(pair, 1)
    other_blocks = swap(other, "hgt")
    sums = kernel(
        functools.partial(collect_kernel, cap),
        (node_rows,) * (n_col - 2),
        [pl.BlockSpec(memory_space=pl.ANY)],
        [other_blocks],
        "collect_other",
        1,
        scratch=one_hot_space(n_hgt) + [vmem(n_hgt, heights[2], PTS), sem((n_col - 1,))],
    )
    parts = [across(sums[turn - 2], turn) for turn in range(2, n_col)]
    both = pltpu.HBM((n_hgt, 2 * cap + table_rows(2, cap), PTS), F32)
    mine = pl.pallas_call(
        functools.partial(own_kernel, cap, heights[0]),
        out_shape=both,
        in_specs=[WHOLE],
        out_specs=FAR,
        scratch_shapes=[sem((n_hgt,))],
        compiler_params=params(VMEM_MIB),
        cost_estimate=cost(cells, cells * 20),
        name="own",
    )(flat)
    mine = pl.pallas_call(
        functools.partial(merge_kernel, cap, heights[0]),
        out_shape=both,
        in_specs=[WHOLE, WHOLE, FAR],
        out_specs=FAR,
        input_output_aliases={2: 0},
        scratch_shapes=[vmem(n_hgt, table_rows(2, cap), PTS), sem((2, n_hgt))],
        compiler_params=params(VMEM_MIB),
        cost_estimate=cost(1, 1),
        name="merge",
    )(flat, from_pair, mine)
    mine_blocks = swap(mine, "hgt")
    own = kernel(
        functools.partial(collect_mine_kernel, cap),
        node_rows,
        [WHOLE],
        [mine_blocks],
        "collect_mine",
        1,
        scratch=one_hot_space(2 * n_hgt),
    )
    node_temp = kernel(
        finish_kernel, node_rows, [WHOLE] * (n_col), [node_enthalpy, own, *parts], "finish", 1
    )
    return e_out, h_out, node_temp


def solution(mesh):
    placed = (
        P(None, "col", "hgt", None),
        P(None, "col", "hgt", None),
        P("col", "hgt", None),
        P("col", "hgt", None),
        P("col", "hgt", None, None, None, None),
        P("col", "hgt", None, None, None),
        P(("col", "hgt"), None),
    )
    return jax.shard_map(
        per_device,
        mesh=mesh,
        in_specs=placed,
        out_specs=(
            P(None, "col", "hgt", None),
            P(None, "col", "hgt", None),
            P(("col", "hgt"), None),
        ),
        check_vma=False,
    )
```

```python
import functools

import jax
import jax.numpy as jnp
from jax import lax
from jax.experimental import pallas as pl
from jax.experimental.pallas import tpu as pltpu
from jax.sharding import PartitionSpec as P

PTS = 128
STEPS = 4
COURANT = 0.55
LANES = 128
ROWS = 8
F32 = jnp.float32
VMEM_MIB = 20

WHOLE = pl.BlockSpec(memory_space=pltpu.VMEM)
SCALARS = pl.BlockSpec(memory_space=pltpu.SMEM)
FAR = pl.BlockSpec(memory_space=pltpu.HBM)


def vmem(*shape):
    return pltpu.VMEM(shape, F32)


def far(x):
    return pltpu.with_memory_space_constraint(x, pltpu.HBM)


def params(mib):
    return pltpu.CompilerParams(vmem_limit_bytes=mib << 20)


def cost(flops, moved):
    return pl.CostEstimate(flops=flops, bytes_accessed=moved, transcendentals=0)


def after_y(f):
    lane = lax.broadcasted_iota(jnp.int32, (ROWS, LANES), 1)
    n = f.shape[1] // LANES
    turned = [pltpu.roll(f[:, k * LANES : (k + 1) * LANES], LANES - 1, 1) for k in range(n)]
    turned.append(jnp.zeros((ROWS, LANES), F32))
    return jnp.concatenate([jnp.where(lane < LANES - 1, turned[k], turned[k + 1]) for k in range(n)], 1)


def before_y(f):
    lane = lax.broadcasted_iota(jnp.int32, (ROWS, LANES), 1)
    n = f.shape[1] // LANES
    turned = [jnp.zeros((ROWS, LANES), F32)]
    turned += [pltpu.roll(f[:, k * LANES : (k + 1) * LANES], 1, 1) for k in range(n)]
    return jnp.concatenate([jnp.where(lane > 0, turned[k + 1], turned[k]) for k in range(n)], 1)


def after_row(f, row):
    place = lax.broadcasted_iota(jnp.int32, f.shape, 0)
    return jnp.where(place < ROWS - 1, pltpu.roll(f, ROWS - 1, 0), jnp.broadcast_to(row, f.shape))


def before_row(f, row):
    place = lax.broadcasted_iota(jnp.int32, f.shape, 0)
    return jnp.where(place > 0, pltpu.roll(f, 1, 0), jnp.broadcast_to(row, f.shape))


def edge_kernel(e, to_col, to_hgt, low, sems):
    nx = e.shape[1]
    col_copy = pltpu.make_async_copy(e.at[pl.ds(1, 2), 0], to_col, sems.at[0])
    low_copy = pltpu.make_async_copy(e.at[pl.ds(0, 2), :, pl.ds(0, ROWS)], low, sems.at[1])
    low_copy.start()
    col_copy.start()
    low_copy.wait()
    for x in range(nx):
        for comp in range(2):
            to_hgt[comp, x : x + 1, :] = low[comp, x, 0:1, :]
    col_copy.wait()


def load_kernel(
    temp_far, tags_far, e_far, h_far, order, ca, cb, sigma_out, e, h, media_rows, e_rows, h_rows, temp, tags, sems
):
    nx, nz, _ = temp.shape
    parts = 4
    size = nx // parts
    copies = []
    for part in range(parts):
        here = pl.ds(part * size, size)
        copies.append(pltpu.make_async_copy(temp_far.at[here], temp.at[here], sems.at[0, part]))
        copies.append(pltpu.make_async_copy(tags_far.at[here], tags.at[here], sems.at[1, part]))
    e_copy = pltpu.make_async_copy(e_far, e, sems.at[2, 0])
    h_copy = pltpu.make_async_copy(h_far, h, sems.at[2, 1])
    for copy in copies:
        copy.start()
    e_copy.start()
    h_copy.start()

    def plane(x, carry):
        for z in range(0, nz, ROWS):
            tag = tags[x, z : z + ROWS, :]
            lean = tag == 0
            fat = tag == 1
            frac = 1.0 / (1.0 + jnp.exp(-2.0 * temp[x, z : z + ROWS, :]))
            eps_low = jnp.where(lean, 4.0, jnp.where(fat, 2.5, 5.0))
            eps_rise = jnp.where(lean, 46.0, jnp.where(fat, 3.5, 5.0))
            sig_low = jnp.where(lean, 0.2, jnp.where(fat, 0.05, 0.1))
            sig_rise = jnp.where(lean, 7.8, jnp.where(fat, 0.35, 0.9))
            eps = eps_low + eps_rise * frac
            sigma = sig_low + sig_rise * frac
            half = (0.5 * COURANT) * sigma
            inverse = 1.0 / (eps + half)
            ca[x, z : z + ROWS, :] = (eps - half) * inverse
            cb[x, z : z + ROWS, :] = COURANT * inverse
            sigma_out[x, z : z + ROWS, :] = sigma
        media_rows[0, pl.ds(x, 1), :] = ca[x, 0:1, :]
        media_rows[1, pl.ds(x, 1), :] = cb[x, 0:1, :]
        return carry

    for part in range(parts):
        copies[2 * part].wait()
        copies[2 * part + 1].wait()
        lax.fori_loop(part * size, (part + 1) * size, plane, 0)
    e_copy.wait()
    h_copy.wait()

    def rows(x, carry):
        for comp in range(3):
            e_rows[comp, pl.ds(x, 1), :] = e[comp, x, nz - 1 : nz, :]
        for comp in range(2):
            h_rows[comp, pl.ds(x, 1), :] = h[comp, x, nz - 1 : nz, :]
        return carry

    lax.fori_loop(0, nx, rows, 0)


def over(first, stop, body):
    if stop - first == 1:
        body(first)
    else:

        def step(x, carry):
            body(x)
            return carry

        lax.fori_loop(first, stop, step, 0)


def h_tile(e, h, col, hgt, x, z):
    nz = e.shape[2]
    here = slice(z, z + ROWS)
    ex, ey, ez = (e[comp, x, here, :] for comp in range(3))
    if z + ROWS < nz:
        row_x, row_y = (e[comp, x, z + ROWS : z + ROWS + 1, :] for comp in range(2))
    else:
        row_x, row_y = (hgt[comp, pl.ds(x, 1), :] for comp in range(2))
    if col is None:
        next_y, next_z = (e[comp, x + 1, here, :] for comp in (1, 2))
    else:
        next_y, next_z = (col[comp, here, :] for comp in range(2))
    h[0, x, here, :] = h[0, x, here, :] - COURANT * ((after_y(ez) - ez) - (after_row(ey, row_y) - ey))
    hy = h[1, x, here, :] - COURANT * ((after_row(ex, row_x) - ex) - (next_z - ez))
    hz = h[2, x, here, :] - COURANT * ((next_y - ey) - (after_y(ex) - ex))
    h[1, x, here, :] = hy
    h[2, x, here, :] = hz
    return hy, hz


def e_tile(first, h, e, power, ca, cb, sigma, col, hgt, x, z):
    here = slice(z, z + ROWS)
    hx, hy, hz = (h[comp, x, here, :] for comp in range(3))
    if z > 0:
        row_x, row_y = (h[comp, x, z - 1 : z, :] for comp in range(2))
    else:
        row_x, row_y = (hgt[comp, pl.ds(x, 1), :] for comp in range(2))
    if col is None:
        past_y, past_z = (h[comp, x - 1, here, :] for comp in (1, 2))
    else:
        past_y, past_z = (col[comp, here, :] for comp in range(2))
    keep = ca[x, here, :]
    drive = cb[x, here, :]
    ex = keep * e[0, x, here, :] + drive * ((hz - before_y(hz)) - (hy - before_row(hy, row_y)))
    ey = keep * e[1, x, here, :] + drive * ((hx - before_row(hx, row_x)) - (hz - past_z))
    ez = keep * e[2, x, here, :] + drive * ((hy - past_y) - (hx - before_y(hx)))
    e[0, x, here, :] = ex
    e[1, x, here, :] = ey
    e[2, x, here, :] = ez
    heat = sigma[x, here, :] * (ex * ex + ey * ey + ez * ez)
    power[x, here, :] = heat if first else power[x, here, :] + heat
    return ey, ez


def h_edge_kernel(e, col, hgt, e_rows, rows_old, h_old, h, to_col, to_hgt):
    nx, nz = e.shape[1:3]
    for z in range(0, nz, ROWS):
        hy, hz = h_tile(e, h, col, hgt, nx - 1, z)
        to_col[0, z : z + ROWS, :] = hy
        to_col[1, z : z + ROWS, :] = hz
    for x in range(0, nx, ROWS):
        here = slice(x, x + ROWS)
        ex, ey, ez = (e_rows[comp, here, :] for comp in range(3))
        row = e_rows[2, x + ROWS : x + ROWS + 1, :] if x + ROWS < nx else col[1, nz - 1 : nz, :]
        to_hgt[0, here, :] = rows_old[0, here, :] - COURANT * ((after_y(ez) - ez) - (hgt[1, here, :] - ey))
        to_hgt[1, here, :] = rows_old[1, here, :] - COURANT * ((hgt[0, here, :] - ex) - (after_row(ez, row) - ez))


def h_rest_kernel(e, hgt, h_old, h, *rows):
    nx, nz = e.shape[1:3]

    def keep(x):
        if rows:
            for comp in range(3):
                rows[0][comp, pl.ds(x, 1), :] = h[comp, x, 0:1, :]

    def plane(x):
        for z in range(0, nz, ROWS):
            h_tile(e, h, None, hgt, x, z)
        keep(x)

    over(0, nx - 1, plane)
    keep(nx - 1)


def e_edge_kernel(first, h, ca, cb, sigma, col, hgt, media_rows, h_rows, rows_old, *refs):
    e, power, to_col, to_hgt = refs[-4:]
    nx, nz = e.shape[1:3]
    for z in range(0, nz, ROWS):
        ey, ez = e_tile(first, h, e, power, ca, cb, sigma, col, hgt, 0, z)
        to_col[0, z : z + ROWS, :] = ey
        to_col[1, z : z + ROWS, :] = ez
    for x in range(0, nx, ROWS):
        here = slice(x, x + ROWS)
        hx, hy, hz = (h_rows[comp, here, :] for comp in range(3))
        row = h_rows[2, x - 1 : x, :] if x > 0 else col[1, 0:1, :]
        keep = media_rows[0, here, :]
        drive = media_rows[1, here, :]
        to_hgt[0, here, :] = keep * rows_old[0, here, :] + drive * ((hz - before_y(hz)) - (hy - hgt[1, here, :]))
        to_hgt[1, here, :] = keep * rows_old[1, here, :] + drive * ((hx - hgt[0, here, :]) - (hz - before_row(hz, row)))


def e_rest_kernel(first, h, ca, cb, sigma, hgt, e_old, power_old, e, power, rows):
    nx, nz = e.shape[1:3]

    def keep(x):
        for comp in range(3):
            rows[comp, pl.ds(x, 1), :] = e[comp, x, nz - 1 : nz, :]

    def plane(x):
        for z in range(0, nz, ROWS):
            e_tile(first, h, e, power, ca, cb, sigma, None, hgt, x, z)
        keep(x)

    keep(0)
    over(1, nx, plane)


def e_last_kernel(first, h, ca, cb, sigma, col, hgt, e_old, power_old, e, power, h_out, sem):
    nx, nz = e.shape[1:3]
    copy = pltpu.make_async_copy(h, h_out, sem)
    copy.start()

    def plane(x):
        for z in range(0, nz, ROWS):
            e_tile(first, h, e, power, ca, cb, sigma, col if isinstance(x, int) else None, hgt, x, z)

    plane(0)
    over(1, nx, plane)
    copy.wait()


def places_kernel(n_col, n_hgt, cap, my_col, owner, node, place, flat):
    n_dev = n_col * n_hgt
    count = owner.shape[1]
    width = 256
    rows = lax.broadcasted_iota(jnp.int32, (n_dev, width), 0)
    before = lax.broadcasted_iota(jnp.int32, (width, width), 0)
    after = lax.broadcasted_iota(jnp.int32, (width, width), 1)
    upper = jnp.where(before <= after, 1.0, 0.0).astype(jnp.bfloat16)
    per = -(-cap // LANES)
    room_for = per * LANES
    room = lax.broadcasted_iota(jnp.int32, (room_for, width), 0)
    total = jnp.zeros((n_dev, 1), F32)
    parts_of = jnp.zeros((2 * n_dev, room_for), F32)
    nt = (((1,), (1,)), ((), ()))
    begins, heights = starts_of(n_col, n_hgt, cap)
    for start in range(0, count, width):
        own = owner[:, start : start + width]
        hit = jnp.where(rows == own, 1.0, 0.0)
        running = total + jnp.dot(hit.astype(jnp.bfloat16), upper, preferred_element_type=F32)
        total = running[:, width - 1 : width]
        rank = jnp.sum(hit * running, axis=0, keepdims=True).astype(jnp.int32) - 1
        turn = lax.bitwise_xor(lax.div(own, n_hgt), my_col[0])
        own_hgt = lax.rem(own, n_hgt)
        begin = jnp.where(
            turn == 0,
            begins[0] + own_hgt * heights[0],
            jnp.where(
                turn == 1,
                begins[1] + own_hgt * heights[1],
                begins[2] + own_hgt * heights[2] + (turn - 2) * cap,
            ),
        )
        place[:, start : start + width] = begin + rank
        number = node[:, start : start + width]
        upper_part = lax.div(number, 16)
        lower_part = number - 16 * upper_part
        seat = jnp.where(room == rank, 1.0, 0.0).astype(jnp.bfloat16)
        both = jnp.concatenate([hit * upper_part.astype(F32), hit * lower_part.astype(F32)], 0)
        parts_of = parts_of + lax.dot_general(both.astype(jnp.bfloat16), seat, nt, preferred_element_type=F32)
    taken = lax.broadcasted_iota(jnp.int32, (n_dev, room_for), 1).astype(F32) < total
    table = jnp.where(taken, 16.0 * parts_of[:n_dev] + parts_of[n_dev:], -1.0)
    chunk = 8 * ROWS

    def clear(i, carry):
        flat[pl.ds(pl.multiple_of(i * chunk, chunk), chunk), :] = jnp.zeros((chunk, PTS), F32)
        return carry

    lax.fori_loop(0, flat.shape[0] // chunk, clear, 0)
    for at in range(flat.shape[0] // chunk * chunk, flat.shape[0], ROWS):
        flat[at : at + ROWS, :] = jnp.zeros((ROWS, PTS), F32)
    behind = [cap, cap, (n_col - 2) * cap]
    for begin, height, skip in zip(begins, heights, behind):
        for part in range(n_hgt):
            at = begin + part * height
            flat[at + skip : at + height, :] = jnp.full((height - skip, PTS), -1.0, F32)
    for group in range(n_col):
        turn = lax.bitwise_xor(jnp.int32(group), my_col[0])
        kind = jnp.minimum(turn, 2)
        begin = jnp.where(kind == 0, begins[0], jnp.where(kind == 1, begins[1], begins[2]))
        height = jnp.where(kind == 2, heights[2], heights[0])
        skip = jnp.where(kind == 2, behind[2] + (turn - 2) * per, cap)
        for part in range(n_hgt):
            at = group * n_hgt + part
            for piece in range(per):
                row = table[at : at + 1, piece * LANES : (piece + 1) * LANES]
                flat[pl.ds(begin + part * height + skip + piece, 1), :] = row


def table_rows(parts, cap):
    return -(-parts * -(-cap // LANES) // ROWS) * ROWS


def starts_of(n_col, n_hgt, cap):
    one = cap + table_rows(1, cap)
    heights = [one, one, (n_col - 2) * cap + table_rows(n_col - 2, cap)]
    return [0, n_hgt * heights[0], n_hgt * (heights[0] + heights[1])], heights


def pack_kernel(heights, place, power, flat_old, e, pair, other, e_out, flat, sems):
    nx, nz, ny = power.shape
    e_copy = pltpu.make_async_copy(e, e_out, sems.at[0])
    e_copy.start()
    per_row = ny // PTS

    def plane(x, carry):
        for z in range(nz):
            for k in range(per_row):
                spot = place[x * (nz * per_row) + z * per_row + k]
                flat[pl.ds(spot, 1), :] = power[x, z : z + 1, k * PTS : (k + 1) * PTS]
        return carry

    lax.fori_loop(0, nx, plane, 0)
    copies = []
    first = pair.shape[0] * heights[0]
    for out, rows in zip((pair, other), heights[1:]):
        for group in range(out.shape[0]):
            target = out.at[group, pl.ds(0, rows)]
            copies.append(pltpu.make_async_copy(flat.at[pl.ds(first, rows)], target, sems.at[1 + len(copies)]))
            first += rows
    for copy in copies:
        copy.start()
    for copy in copies:
        copy.wait()
    e_copy.wait()


def summed(blocks, first, cap, node_row, chosen, split, node_count):
    ids = lax.broadcasted_iota(jnp.int32, (node_count, LANES), 0).astype(F32)
    n_from, _, pts = blocks.shape
    per = -(-cap // LANES)
    many = len(first)
    for source in range(n_from):
        for i in range(many):
            seat = (source * many + i) * per * LANES
            for piece in range(per):
                row = node_row[i] + piece
                lanes = slice(seat + piece * LANES, seat + (piece + 1) * LANES)
                hit = ids == blocks[source, row : row + 1, :]
                chosen[:, lanes] = jnp.where(hit, 1.0, 0.0).astype(jnp.bfloat16)
            values = blocks[source, first[i] : first[i] + cap, :]
            high = values.astype(jnp.bfloat16)
            split[seat : seat + cap, 0:pts] = high
            split[seat : seat + cap, pts : 2 * pts] = (values - high.astype(F32)).astype(jnp.bfloat16)
    both = jnp.dot(chosen[...], split[...], preferred_element_type=F32)
    return both[:, 0:pts] + both[:, pts : 2 * pts]


def collect_kernel(cap, parts, n_part, blocks, *refs):
    *outs, chosen, split, near, sems = refs
    rows = blocks.shape[1]
    per = -(-cap // LANES)
    after = n_part * cap
    pieces = [(after, rows - after)] + [(part * cap, cap) for part in parts]
    copies = []
    for i, (begin, size) in enumerate(pieces):
        here = pl.ds(begin, size)
        copies.append(pltpu.make_async_copy(blocks.at[:, here], near.at[:, here], sems.at[i]))
        copies[i].start()
    split[...] = jnp.zeros(split.shape, split.dtype)
    copies[0].wait()
    for i, (part, out) in enumerate(zip(parts, outs)):
        copies[1 + i].wait()
        out[...] = summed(near, [part * cap], cap, [after + part * per], chosen, split, out.shape[0])


def add_kernel(*refs):
    n = len(refs) // 3
    for own, other, out in zip(refs[:n], refs[n : 2 * n], refs[2 * n :]):
        out[...] = own[...] + other[...]


def own_kernel(cap, height, flat, mine, sems):
    copies = [
        pltpu.make_async_copy(flat.at[pl.ds(group * height, cap)], mine.at[group, pl.ds(0, cap)], sems.at[group])
        for group in range(mine.shape[0])
    ]
    for copy in copies:
        copy.start()
    for copy in copies:
        copy.wait()


def merge_kernel(cap, height, flat, pair, mine_old, mine, tile, sems):
    per = -(-cap // LANES)
    groups = mine.shape[0]
    copies = []
    for group in range(groups):
        target = mine.at[group, pl.ds(cap, cap)]
        copies.append(pltpu.make_async_copy(pair.at[group, pl.ds(0, cap)], target, sems.at[0, group]))
    for copy in copies:
        copy.start()
    rest = tile.shape[1]
    tile[...] = jnp.full(tile.shape, -1.0, F32)
    for group in range(groups):
        tile[group, 0:per, :] = pair[group, cap : cap + per, :]
        tile[group, per : 2 * per, :] = flat[group * height + cap : group * height + cap + per, :]
        target = mine.at[group, pl.ds(2 * cap, rest)]
        copies.append(pltpu.make_async_copy(tile.at[group], target, sems.at[1, group]))
        copies[-1].start()
    for copy in copies:
        copy.wait()


def collect_mine_kernel(cap, blocks, out, chosen, split):
    per = -(-cap // LANES)
    split[...] = jnp.zeros(split.shape, split.dtype)
    out[...] = summed(blocks, [0, cap], cap, [2 * cap + per, 2 * cap], chosen, split, out.shape[0])


def finish_kernel(enthalpy, *refs):
    *parts, out = refs
    heat = parts[0][...]
    for part in parts[1:]:
        heat = heat + part[...]
    content = enthalpy[...] + (0.25 / STEPS) * heat
    out[...] = jnp.where(content < 0.0, content / 2.0, jnp.where(content > 1.0, (content - 1.0) / 3.0, 0.0))


def shifted(block, d_col, d_hgt):
    n_col = lax.axis_size("col")
    n_hgt = lax.axis_size("hgt")
    route = [
        (c * n_hgt + h, (c + d_col) * n_hgt + h + d_hgt)
        for c in range(n_col)
        for h in range(n_hgt)
        if 0 <= c + d_col < n_col and 0 <= h + d_hgt < n_hgt
    ]
    return lax.ppermute(block, ("col", "hgt"), route)


def per_device(
    efield_lattice_vector,
    hfield_lattice_vector,
    cell_temp,
    region_tags,
    block_owner,
    block_node,
    node_enthalpy,
):
    nx, nz, ny = cell_temp.shape
    n_col = lax.axis_size("col")
    n_hgt = lax.axis_size("hgt")
    n_dev = n_col * n_hgt
    count = nx * nz * ny // PTS
    cap = 2 * count // n_dev
    node_count = node_enthalpy.shape[0]
    cells = nx * nz * ny
    sem = pltpu.SemaphoreType.DMA

    def kernel(body, outs, ins, args, name, work, aliases=None, scratch=()):
        return pl.pallas_call(
            body,
            out_shape=outs,
            in_specs=ins,
            out_specs=jax.tree.map(lambda out: WHOLE, outs),
            input_output_aliases=aliases or {},
            scratch_shapes=scratch,
            compiler_params=params(VMEM_MIB),
            cost_estimate=cost(work * cells, work * cells),
            name=name,
        )(*args)

    e_start = far(efield_lattice_vector)
    h_start = far(hfield_lattice_vector)
    my_col = lax.axis_index("col").astype(jnp.int32).reshape(1)
    owners = block_owner.reshape(1, count)
    nodes = block_node.reshape(1, count)
    field = vmem(3, nx, nz, ny)
    whole = vmem(nx, nz, ny)
    planes = vmem(2, nz, ny)
    two_rows = vmem(2, nx, ny)
    three_rows = vmem(3, nx, ny)

    to_col, e_low = kernel(
        edge_kernel, (planes, two_rows), [FAR], [e_start], "edge", 4, scratch=[vmem(2, nx, ROWS, ny), sem((2,))]
    )
    col = shifted(to_col, -1, 0)
    hgt = shifted(e_low, 0, -1)
    ca, cb, sigma, e, h, media_rows, e_rows, h_high = kernel(
        load_kernel,
        (whole, whole, whole, field, field, two_rows, three_rows, two_rows),
        [FAR] * 4 + [WHOLE],
        [far(cell_temp), far(region_tags), e_start, h_start, owners + nodes + my_col],
        "load",
        60,
        scratch=[vmem(nx, nz, ny), pltpu.VMEM((nx, nz, ny), jnp.int32), sem((3, 4))],
    )
    begins, heights = starts_of(n_col, n_hgt, cap)
    place, flat = kernel(
        functools.partial(places_kernel, n_col, n_hgt, cap),
        (jax.ShapeDtypeStruct((1, count), jnp.int32), vmem(n_hgt * sum(heights), PTS)),
        [SCALARS, WHOLE, WHOLE],
        [my_col, owners, nodes],
        "places",
        8,
    )
    power = None
    for step in range(STEPS):
        first = step == 0
        h, to_col, h_high = kernel(
            h_edge_kernel,
            (field, planes, two_rows),
            [WHOLE] * 6,
            [e, col, hgt, e_rows, h_high, h],
            f"h_edge_{step}",
            4,
            {5: 0},
        )
        e_hgt = hgt
        col = shifted(to_col, 1, 0)
        hgt = shifted(h_high, 0, 1)
        last = step == STEPS - 1
        outs = (field,) if last else (field, three_rows)
        h, *h_rows = kernel(h_rest_kernel, outs, [WHOLE] * 3, [e, e_hgt, h], f"h_rest_{step}", 40, {2: 0})
        media = [h, ca, cb, sigma]
        if last:
            e, power, h_out = pl.pallas_call(
                functools.partial(e_last_kernel, first),
                out_shape=(field, whole, pltpu.HBM((3, nx, nz, ny), F32)),
                in_specs=[WHOLE] * 8,
                out_specs=(WHOLE, WHOLE, FAR),
                input_output_aliases={6: 0, 7: 1},
                scratch_shapes=[sem],
                compiler_params=params(VMEM_MIB),
                cost_estimate=cost(cells * 50, cells * 50),
                name="e_last",
            )(*media, col, hgt, e, power)
            break
        args = media + [col, hgt, media_rows, *h_rows, e_low, e] + ([] if first else [power])
        e, power, to_col, e_low = kernel(
            functools.partial(e_edge_kernel, first),
            (field, whole, planes, two_rows),
            [WHOLE] * len(args),
            args,
            f"e_edge_{step}",
            5,
            {9: 0} if first else {9: 0, 10: 1},
        )
        h_hgt = hgt
        col = shifted(to_col, -1, 0)
        hgt = shifted(e_low, 0, -1)
        e, power, e_rows = kernel(
            functools.partial(e_rest_kernel, first),
            (field, whole, three_rows),
            [WHOLE] * 7,
            media + [h_hgt, e, power],
            f"e_rest_{step}",
            45,
            {5: 0, 6: 1},
        )

    pair, other, e_out, flat = pl.pallas_call(
        functools.partial(pack_kernel, heights),
        out_shape=(
            pltpu.HBM((n_hgt, heights[1], PTS), F32),
            pltpu.HBM((n_hgt, heights[2], PTS), F32),
            pltpu.HBM((3, nx, nz, ny), F32),
            vmem(n_hgt * sum(heights), PTS),
        ),
        in_specs=[SCALARS] + [WHOLE] * 3,
        out_specs=(FAR,) * 3 + (WHOLE,),
        input_output_aliases={2: 3},
        scratch_shapes=[sem((1 + 2 * n_hgt,))],
        compiler_params=params(VMEM_MIB),
        cost_estimate=cost(cells, cells * 36),
        name="pack",
    )(place.reshape(count), power, flat, e)

    def swap(x, axis):
        return lax.all_to_all(x, axis, split_axis=0, concat_axis=0, tiled=True)

    def across(x, turn):
        return lax.ppermute(x, "col", [(c, c ^ turn) for c in range(n_col)])

    def one_hot_space(sources):
        seats = sources * -(-cap // LANES) * LANES
        return [pltpu.VMEM((node_count, seats), jnp.bfloat16), pltpu.VMEM((seats, 2 * PTS), jnp.bfloat16)]

    node_rows = jax.ShapeDtypeStruct((node_count, PTS), F32)
    from_pair = across(pair, 1)
    other_blocks = swap(other, "hgt")
    def collect(turns, name):
        return kernel(
            functools.partial(collect_kernel, cap, [turn - 2 for turn in turns], n_col - 2),
            (node_rows,) * len(turns),
            [pl.BlockSpec(memory_space=pl.ANY)],
            [other_blocks],
            name,
            8,
            scratch=one_hot_space(n_hgt) + [vmem(n_hgt, heights[2], PTS), sem((1 + len(turns),))],
        )

    turns = list(range(2, n_col, 2))
    swapped = [across(part, 1) for part in collect([turn + 1 for turn in turns], "collect_odd")]
    kept = collect(turns, "collect_even")
    sums = kernel(
        add_kernel, (node_rows,) * len(turns), [WHOLE] * (2 * len(turns)), [*kept, *swapped], "add", 1
    )
    parts = [across(part, turn) for part, turn in zip(sums, turns)]
    both = pltpu.HBM((n_hgt, 2 * cap + table_rows(2, cap), PTS), F32)
    mine = pl.pallas_call(
        functools.partial(own_kernel, cap, heights[0]),
        out_shape=both,
        in_specs=[WHOLE],
        out_specs=FAR,
        scratch_shapes=[sem((n_hgt,))],
        compiler_params=params(VMEM_MIB),
        cost_estimate=cost(cells, cells * 20),
        name="own",
    )(flat)
    mine = pl.pallas_call(
        functools.partial(merge_kernel, cap, heights[0]),
        out_shape=both,
        in_specs=[WHOLE, WHOLE, FAR],
        out_specs=FAR,
        input_output_aliases={2: 0},
        scratch_shapes=[vmem(n_hgt, table_rows(2, cap), PTS), sem((2, n_hgt))],
        compiler_params=params(VMEM_MIB),
        cost_estimate=cost(1, 1),
        name="merge",
    )(flat, from_pair, mine)
    mine_blocks = swap(mine, "hgt")
    own = kernel(
        functools.partial(collect_mine_kernel, cap),
        node_rows,
        [WHOLE],
        [mine_blocks],
        "collect_mine",
        1,
        scratch=one_hot_space(2 * n_hgt),
    )
    node_temp = kernel(
        finish_kernel, node_rows, [WHOLE] * (2 + len(parts)), [node_enthalpy, own, *parts], "finish", 1
    )
    return e_out, h_out, node_temp


def solution(mesh):
    placed = (
        P(None, "col", "hgt", None),
        P(None, "col", "hgt", None),
        P("col", "hgt", None),
        P("col", "hgt", None),
        P("col", "hgt", None, None, None, None),
        P("col", "hgt", None, None, None),
        P(("col", "hgt"), None),
    )
    return jax.shard_map(
        per_device,
        mesh=mesh,
        in_specs=placed,
        out_specs=(
            P(None, "col", "hgt", None),
            P(None, "col", "hgt", None),
            P(("col", "hgt"), None),
        ),
        check_vma=False,
    )
```

```python
import functools

import jax
import jax.numpy as jnp
from jax import lax
from jax.experimental import pallas as pl
from jax.experimental.pallas import tpu as pltpu
from jax.sharding import PartitionSpec as P

PTS = 128
STEPS = 4
COURANT = 0.55
LANES = 128
ROWS = 8
F32 = jnp.float32
VMEM_MIB = 20

WHOLE = pl.BlockSpec(memory_space=pltpu.VMEM)
SCALARS = pl.BlockSpec(memory_space=pltpu.SMEM)
FAR = pl.BlockSpec(memory_space=pltpu.HBM)


def vmem(*shape):
    return pltpu.VMEM(shape, F32)


def far(x):
    return pltpu.with_memory_space_constraint(x, pltpu.HBM)


def params(mib):
    return pltpu.CompilerParams(vmem_limit_bytes=mib << 20)


def cost(flops, moved):
    return pl.CostEstimate(flops=flops, bytes_accessed=moved, transcendentals=0)


def after_y(f):
    lane = lax.broadcasted_iota(jnp.int32, (ROWS, LANES), 1)
    n = f.shape[1] // LANES
    turned = [pltpu.roll(f[:, k * LANES : (k + 1) * LANES], LANES - 1, 1) for k in range(n)]
    turned.append(jnp.zeros((ROWS, LANES), F32))
    return jnp.concatenate([jnp.where(lane < LANES - 1, turned[k], turned[k + 1]) for k in range(n)], 1)


def before_y(f):
    lane = lax.broadcasted_iota(jnp.int32, (ROWS, LANES), 1)
    n = f.shape[1] // LANES
    turned = [jnp.zeros((ROWS, LANES), F32)]
    turned += [pltpu.roll(f[:, k * LANES : (k + 1) * LANES], 1, 1) for k in range(n)]
    return jnp.concatenate([jnp.where(lane > 0, turned[k + 1], turned[k]) for k in range(n)], 1)


def after_row(f, row):
    place = lax.broadcasted_iota(jnp.int32, f.shape, 0)
    return jnp.where(place < ROWS - 1, pltpu.roll(f, ROWS - 1, 0), jnp.broadcast_to(row, f.shape))


def before_row(f, row):
    place = lax.broadcasted_iota(jnp.int32, f.shape, 0)
    return jnp.where(place > 0, pltpu.roll(f, 1, 0), jnp.broadcast_to(row, f.shape))


def edge_kernel(e, to_col, to_hgt, low, sems):
    nx = e.shape[1]
    col_copy = pltpu.make_async_copy(e.at[pl.ds(1, 2), 0], to_col, sems.at[0])
    low_copy = pltpu.make_async_copy(e.at[pl.ds(0, 2), :, pl.ds(0, ROWS)], low, sems.at[1])
    low_copy.start()
    col_copy.start()
    low_copy.wait()
    for x in range(nx):
        for comp in range(2):
            to_hgt[comp, x : x + 1, :] = low[comp, x, 0:1, :]
    col_copy.wait()


def load_kernel(
    temp_far, tags_far, e_far, h_far, order, ca, cb, sigma_out, e, h, media_rows, e_rows, h_rows, temp, tags, sems
):
    nx, nz, _ = temp.shape
    parts = 4
    size = nx // parts
    copies = []
    for part in range(parts):
        here = pl.ds(part * size, size)
        copies.append(pltpu.make_async_copy(temp_far.at[here], temp.at[here], sems.at[0, part]))
        copies.append(pltpu.make_async_copy(tags_far.at[here], tags.at[here], sems.at[1, part]))
    e_copy = pltpu.make_async_copy(e_far, e, sems.at[2, 0])
    h_copy = pltpu.make_async_copy(h_far, h, sems.at[2, 1])
    for copy in copies:
        copy.start()
    e_copy.start()
    h_copy.start()

    def plane(x, carry):
        for z in range(0, nz, ROWS):
            tag = tags[x, z : z + ROWS, :]
            lean = tag == 0
            fat = tag == 1
            frac = 1.0 / (1.0 + jnp.exp(-2.0 * temp[x, z : z + ROWS, :]))
            eps_low = jnp.where(lean, 4.0, jnp.where(fat, 2.5, 5.0))
            eps_rise = jnp.where(lean, 46.0, jnp.where(fat, 3.5, 5.0))
            sig_low = jnp.where(lean, 0.2, jnp.where(fat, 0.05, 0.1))
            sig_rise = jnp.where(lean, 7.8, jnp.where(fat, 0.35, 0.9))
            eps = eps_low + eps_rise * frac
            sigma = sig_low + sig_rise * frac
            half = (0.5 * COURANT) * sigma
            inverse = 1.0 / (eps + half)
            ca[x, z : z + ROWS, :] = (eps - half) * inverse
            cb[x, z : z + ROWS, :] = COURANT * inverse
            sigma_out[x, z : z + ROWS, :] = sigma
        media_rows[0, pl.ds(x, 1), :] = ca[x, 0:1, :]
        media_rows[1, pl.ds(x, 1), :] = cb[x, 0:1, :]
        return carry

    for part in range(parts):
        copies[2 * part].wait()
        copies[2 * part + 1].wait()
        lax.fori_loop(part * size, (part + 1) * size, plane, 0)
    e_copy.wait()
    h_copy.wait()

    def rows(x, carry):
        for comp in range(3):
            e_rows[comp, pl.ds(x, 1), :] = e[comp, x, nz - 1 : nz, :]
        for comp in range(2):
            h_rows[comp, pl.ds(x, 1), :] = h[comp, x, nz - 1 : nz, :]
        return carry

    lax.fori_loop(0, nx, rows, 0)


def over(first, stop, body):
    if stop - first == 1:
        body(first)
    else:

        def step(x, carry):
            body(x)
            return carry

        lax.fori_loop(first, stop, step, 0)


def h_tile(e, h, col, hgt, x, z):
    nz = e.shape[2]
    here = slice(z, z + ROWS)
    ex, ey, ez = (e[comp, x, here, :] for comp in range(3))
    if z + ROWS < nz:
        row_x, row_y = (e[comp, x, z + ROWS : z + ROWS + 1, :] for comp in range(2))
    else:
        row_x, row_y = (hgt[comp, pl.ds(x, 1), :] for comp in range(2))
    if col is None:
        next_y, next_z = (e[comp, x + 1, here, :] for comp in (1, 2))
    else:
        next_y, next_z = (col[comp, here, :] for comp in range(2))
    h[0, x, here, :] = h[0, x, here, :] - COURANT * ((after_y(ez) - ez) - (after_row(ey, row_y) - ey))
    hy = h[1, x, here, :] - COURANT * ((after_row(ex, row_x) - ex) - (next_z - ez))
    hz = h[2, x, here, :] - COURANT * ((next_y - ey) - (after_y(ex) - ex))
    h[1, x, here, :] = hy
    h[2, x, here, :] = hz
    return hy, hz


def e_tile(first, h, e, power, ca, cb, sigma, col, hgt, x, z):
    here = slice(z, z + ROWS)
    hx, hy, hz = (h[comp, x, here, :] for comp in range(3))
    if z > 0:
        row_x, row_y = (h[comp, x, z - 1 : z, :] for comp in range(2))
    else:
        row_x, row_y = (hgt[comp, pl.ds(x, 1), :] for comp in range(2))
    if col is None:
        past_y, past_z = (h[comp, x - 1, here, :] for comp in (1, 2))
    else:
        past_y, past_z = (col[comp, here, :] for comp in range(2))
    keep = ca[x, here, :]
    drive = cb[x, here, :]
    ex = keep * e[0, x, here, :] + drive * ((hz - before_y(hz)) - (hy - before_row(hy, row_y)))
    ey = keep * e[1, x, here, :] + drive * ((hx - before_row(hx, row_x)) - (hz - past_z))
    ez = keep * e[2, x, here, :] + drive * ((hy - past_y) - (hx - before_y(hx)))
    e[0, x, here, :] = ex
    e[1, x, here, :] = ey
    e[2, x, here, :] = ez
    heat = sigma[x, here, :] * (ex * ex + ey * ey + ez * ez)
    power[x, here, :] = heat if first else power[x, here, :] + heat
    return ey, ez


def h_edge_kernel(e, col, hgt, e_rows, rows_old, h_old, h, to_col, to_hgt):
    nx, nz = e.shape[1:3]
    for z in range(0, nz, ROWS):
        hy, hz = h_tile(e, h, col, hgt, nx - 1, z)
        to_col[0, z : z + ROWS, :] = hy
        to_col[1, z : z + ROWS, :] = hz
    for x in range(0, nx, ROWS):
        here = slice(x, x + ROWS)
        ex, ey, ez = (e_rows[comp, here, :] for comp in range(3))
        row = e_rows[2, x + ROWS : x + ROWS + 1, :] if x + ROWS < nx else col[1, nz - 1 : nz, :]
        to_hgt[0, here, :] = rows_old[0, here, :] - COURANT * ((after_y(ez) - ez) - (hgt[1, here, :] - ey))
        to_hgt[1, here, :] = rows_old[1, here, :] - COURANT * ((hgt[0, here, :] - ex) - (after_row(ez, row) - ez))


def h_rest_kernel(e, hgt, h_old, h, *rows):
    nx, nz = e.shape[1:3]

    def keep(x):
        if rows:
            for comp in range(3):
                rows[0][comp, pl.ds(x, 1), :] = h[comp, x, 0:1, :]

    def plane(x):
        for z in range(0, nz, ROWS):
            h_tile(e, h, None, hgt, x, z)
        keep(x)

    over(0, nx - 1, plane)
    keep(nx - 1)


def e_edge_kernel(first, h, ca, cb, sigma, col, hgt, media_rows, h_rows, rows_old, *refs):
    e, power, to_col, to_hgt = refs[-4:]
    nx, nz = e.shape[1:3]
    for z in range(0, nz, ROWS):
        ey, ez = e_tile(first, h, e, power, ca, cb, sigma, col, hgt, 0, z)
        to_col[0, z : z + ROWS, :] = ey
        to_col[1, z : z + ROWS, :] = ez
    for x in range(0, nx, ROWS):
        here = slice(x, x + ROWS)
        hx, hy, hz = (h_rows[comp, here, :] for comp in range(3))
        row = h_rows[2, x - 1 : x, :] if x > 0 else col[1, 0:1, :]
        keep = media_rows[0, here, :]
        drive = media_rows[1, here, :]
        to_hgt[0, here, :] = keep * rows_old[0, here, :] + drive * ((hz - before_y(hz)) - (hy - hgt[1, here, :]))
        to_hgt[1, here, :] = keep * rows_old[1, here, :] + drive * ((hx - hgt[0, here, :]) - (hz - before_row(hz, row)))


def e_rest_kernel(first, h, ca, cb, sigma, hgt, e_old, power_old, e, power, rows):
    nx, nz = e.shape[1:3]

    def keep(x):
        for comp in range(3):
            rows[comp, pl.ds(x, 1), :] = e[comp, x, nz - 1 : nz, :]

    def plane(x):
        for z in range(0, nz, ROWS):
            e_tile(first, h, e, power, ca, cb, sigma, None, hgt, x, z)
        keep(x)

    keep(0)
    over(1, nx, plane)


def e_last_kernel(first, h, ca, cb, sigma, col, hgt, e_old, power_old, e, power, h_out, sem):
    nx, nz = e.shape[1:3]
    copy = pltpu.make_async_copy(h, h_out, sem)
    copy.start()

    def plane(x):
        for z in range(0, nz, ROWS):
            e_tile(first, h, e, power, ca, cb, sigma, col if isinstance(x, int) else None, hgt, x, z)

    plane(0)
    over(1, nx, plane)
    copy.wait()


def places_kernel(n_col, n_hgt, cap, my_col, owner, node, place, flat):
    n_dev = n_col * n_hgt
    count = owner.shape[1]
    width = 256
    rows = lax.broadcasted_iota(jnp.int32, (n_dev, width), 0)
    before = lax.broadcasted_iota(jnp.int32, (width, width), 0)
    after = lax.broadcasted_iota(jnp.int32, (width, width), 1)
    upper = jnp.where(before <= after, 1.0, 0.0).astype(jnp.bfloat16)
    per = -(-cap // LANES)
    room_for = per * LANES
    room = lax.broadcasted_iota(jnp.int32, (room_for, width), 0)
    total = jnp.zeros((n_dev, 1), F32)
    parts_of = jnp.zeros((2 * n_dev, room_for), F32)
    nt = (((1,), (1,)), ((), ()))
    begins, heights = starts_of(n_col, n_hgt, cap)
    cut = cut_of(cap)
    behind = [cut, cap, (n_col - 2) * cap + cap - cut]
    for start in range(0, count, width):
        own = owner[:, start : start + width]
        hit = jnp.where(rows == own, 1.0, 0.0)
        running = total + jnp.dot(hit.astype(jnp.bfloat16), upper, preferred_element_type=F32)
        total = running[:, width - 1 : width]
        rank = jnp.sum(hit * running, axis=0, keepdims=True).astype(jnp.int32) - 1
        turn = lax.bitwise_xor(lax.div(own, n_hgt), my_col[0])
        own_hgt = lax.rem(own, n_hgt)
        begin = jnp.where(
            turn == 0,
            jnp.where(rank < cut, begins[0] + own_hgt * heights[0], begins[2] + own_hgt * heights[2] + behind[2] - cap),
            jnp.where(
                turn == 1,
                begins[1] + own_hgt * heights[1],
                begins[2] + own_hgt * heights[2] + (turn - 2) * cap,
            ),
        )
        place[:, start : start + width] = begin + rank
        number = node[:, start : start + width]
        upper_part = lax.div(number, 16)
        lower_part = number - 16 * upper_part
        seat = jnp.where(room == rank, 1.0, 0.0).astype(jnp.bfloat16)
        both = jnp.concatenate([hit * upper_part.astype(F32), hit * lower_part.astype(F32)], 0)
        parts_of = parts_of + lax.dot_general(both.astype(jnp.bfloat16), seat, nt, preferred_element_type=F32)
    taken = lax.broadcasted_iota(jnp.int32, (n_dev, room_for), 1).astype(F32) < total
    table = jnp.where(taken, 16.0 * parts_of[:n_dev] + parts_of[n_dev:], -1.0)
    chunk = 8 * ROWS

    def clear(i, carry):
        flat[pl.ds(pl.multiple_of(i * chunk, chunk), chunk), :] = jnp.zeros((chunk, PTS), F32)
        return carry

    lax.fori_loop(0, flat.shape[0] // chunk, clear, 0)
    for at in range(flat.shape[0] // chunk * chunk, flat.shape[0], ROWS):
        flat[at : at + ROWS, :] = jnp.zeros((ROWS, PTS), F32)
    for begin, height, skip in zip(begins, heights, behind):
        for part in range(n_hgt):
            at = begin + part * height
            flat[at + skip : at + height, :] = jnp.full((height - skip, PTS), -1.0, F32)
    for group in range(n_col):
        turn = lax.bitwise_xor(jnp.int32(group), my_col[0])
        kind = jnp.minimum(turn, 2)
        begin = jnp.where(kind == 0, begins[0], jnp.where(kind == 1, begins[1], begins[2]))
        height = jnp.where(kind == 0, heights[0], jnp.where(kind == 1, heights[1], heights[2]))
        skip = jnp.where(kind == 0, cut, jnp.where(kind == 1, cap, behind[2] + (turn - 2) * per))
        for part in range(n_hgt):
            at = group * n_hgt + part
            for piece in range(per):
                row = table[at : at + 1, piece * LANES : (piece + 1) * LANES]
                flat[pl.ds(begin + part * height + skip + piece, 1), :] = row

        @pl.when(turn == 0)
        def _():
            piece = cut // LANES
            for part in range(n_hgt):
                row = begins[2] + part * heights[2] + behind[2] + (n_col - 2) * per
                at = group * n_hgt + part
                flat[row : row + 1, :] = table[at : at + 1, piece * LANES : (piece + 1) * LANES]


def cut_of(cap):
    return cap - cap // 6 // ROWS * ROWS


def table_rows(parts, cap):
    return -(-parts * -(-cap // LANES) // ROWS) * ROWS


def starts_of(n_col, n_hgt, cap):
    cut = cut_of(cap)
    others = (n_col - 2) * cap + cap - cut + table_rows(n_col - 1, cap)
    heights = [cut + table_rows(1, cap), cap + table_rows(1, cap), others]
    return [0, n_hgt * heights[0], n_hgt * (heights[0] + heights[1])], heights


def pack_kernel(heights, place, power, flat_old, e, pair, other, e_out, flat, sems):
    nx, nz, ny = power.shape
    e_copy = pltpu.make_async_copy(e, e_out, sems.at[0])
    e_copy.start()
    per_row = ny // PTS

    def plane(x, carry):
        for z in range(nz):
            for k in range(per_row):
                spot = place[x * (nz * per_row) + z * per_row + k]
                flat[pl.ds(spot, 1), :] = power[x, z : z + 1, k * PTS : (k + 1) * PTS]
        return carry

    lax.fori_loop(0, nx, plane, 0)
    copies = []
    first = pair.shape[0] * heights[0]
    for out, rows in zip((pair, other), heights[1:]):
        for group in range(out.shape[0]):
            target = out.at[group, pl.ds(0, rows)]
            copies.append(pltpu.make_async_copy(flat.at[pl.ds(first, rows)], target, sems.at[1 + len(copies)]))
            first += rows
    for copy in copies:
        copy.start()
    for copy in copies:
        copy.wait()
    e_copy.wait()


def summed(blocks, first, caps, node_row, chosen, split, node_count):
    ids = lax.broadcasted_iota(jnp.int32, (node_count, LANES), 0).astype(F32)
    n_from, _, pts = blocks.shape
    per = -(-max(caps) // LANES)
    many = len(first)
    for source in range(n_from):
        for i in range(many):
            seat = (source * many + i) * per * LANES
            for piece in range(per):
                row = node_row[i] + piece
                lanes = slice(seat + piece * LANES, seat + (piece + 1) * LANES)
                hit = ids == blocks[source, row : row + 1, :]
                chosen[:, lanes] = jnp.where(hit, 1.0, 0.0).astype(jnp.bfloat16)
            cap = caps[i]
            values = blocks[source, first[i] : first[i] + cap, :]
            high = values.astype(jnp.bfloat16)
            split[seat : seat + cap, 0:pts] = high
            split[seat : seat + cap, pts : 2 * pts] = (values - high.astype(F32)).astype(jnp.bfloat16)
    both = jnp.dot(chosen[...], split[...], preferred_element_type=F32)
    return both[:, 0:pts] + both[:, pts : 2 * pts]


def collect_kernel(cap, parts, n_part, blocks, *refs):
    *outs, chosen, split, near, sems = refs
    rows = blocks.shape[1]
    per = -(-cap // LANES)
    after = n_part * cap
    table = after + cap - cut_of(cap)
    pieces = [(after, rows - after)] + [(part * cap, cap) for part in parts]
    copies = []
    for i, (begin, size) in enumerate(pieces):
        here = pl.ds(begin, size)
        copies.append(pltpu.make_async_copy(blocks.at[:, here], near.at[:, here], sems.at[i]))
        copies[i].start()
    split[...] = jnp.zeros(split.shape, split.dtype)
    copies[0].wait()
    for i, (part, out) in enumerate(zip(parts, outs)):
        copies[1 + i].wait()
        out[...] = summed(near, [part * cap], [cap], [table + part * per], chosen, split, out.shape[0])


def collect_tail_kernel(cap, n_part, blocks, out, chosen, split, near, sem):
    n_from, rows, pts = blocks.shape
    cut = cut_of(cap)
    begin = n_part * cap
    copy = pltpu.make_async_copy(blocks.at[:, pl.ds(begin, rows - begin)], near, sem)
    copy.start()
    split[...] = jnp.zeros(split.shape, split.dtype)
    copy.wait()
    ids = lax.broadcasted_iota(jnp.int32, (out.shape[0], LANES), 0).astype(F32)
    row = cap - cut + n_part * -(-cap // LANES)
    for source in range(n_from):
        hit = ids == near[source, row : row + 1, :]
        chosen[:, source * LANES : (source + 1) * LANES] = jnp.where(hit, 1.0, 0.0).astype(jnp.bfloat16)
        values = near[source, 0 : cap - cut, :]
        high = values.astype(jnp.bfloat16)
        here = slice(source * LANES + cut % LANES, source * LANES + cut % LANES + cap - cut)
        split[here, 0:pts] = high
        split[here, pts : 2 * pts] = (values - high.astype(F32)).astype(jnp.bfloat16)
    both = jnp.dot(chosen[...], split[...], preferred_element_type=F32)
    out[...] = both[:, 0:pts] + both[:, pts : 2 * pts]


def add_kernel(*refs):
    n = len(refs) // 3
    for own, other, out in zip(refs[:n], refs[n : 2 * n], refs[2 * n :]):
        out[...] = own[...] + other[...]


def own_kernel(cap, height, flat, mine, sems):
    cap = cut_of(cap)
    copies = [
        pltpu.make_async_copy(flat.at[pl.ds(group * height, cap)], mine.at[group, pl.ds(0, cap)], sems.at[group])
        for group in range(mine.shape[0])
    ]
    for copy in copies:
        copy.start()
    for copy in copies:
        copy.wait()


def merge_kernel(cap, height, flat, pair, mine_old, mine, tile, sems):
    per = -(-cap // LANES)
    cut = cut_of(cap)
    groups = mine.shape[0]
    copies = []
    for group in range(groups):
        target = mine.at[group, pl.ds(cut, cap)]
        copies.append(pltpu.make_async_copy(pair.at[group, pl.ds(0, cap)], target, sems.at[0, group]))
    for copy in copies:
        copy.start()
    rest = tile.shape[1]
    tile[...] = jnp.full(tile.shape, -1.0, F32)
    for group in range(groups):
        tile[group, 0:per, :] = pair[group, cap : cap + per, :]
        tile[group, per : 2 * per, :] = flat[group * height + cut : group * height + cut + per, :]
        target = mine.at[group, pl.ds(cut + cap, rest)]
        copies.append(pltpu.make_async_copy(tile.at[group], target, sems.at[1, group]))
        copies[-1].start()
    for copy in copies:
        copy.wait()


def collect_mine_kernel(cap, blocks, out, chosen, split):
    per = -(-cap // LANES)
    split[...] = jnp.zeros(split.shape, split.dtype)
    cut = cut_of(cap)
    nodes = [cut + cap + per, cut + cap]
    out[...] = summed(blocks, [0, cut], [cut, cap], nodes, chosen, split, out.shape[0])


def finish_kernel(enthalpy, *refs):
    *parts, out = refs
    heat = parts[0][...]
    for part in parts[1:]:
        heat = heat + part[...]
    content = enthalpy[...] + (0.25 / STEPS) * heat
    out[...] = jnp.where(content < 0.0, content / 2.0, jnp.where(content > 1.0, (content - 1.0) / 3.0, 0.0))


def shifted(block, d_col, d_hgt):
    n_col = lax.axis_size("col")
    n_hgt = lax.axis_size("hgt")
    route = [
        (c * n_hgt + h, (c + d_col) * n_hgt + h + d_hgt)
        for c in range(n_col)
        for h in range(n_hgt)
        if 0 <= c + d_col < n_col and 0 <= h + d_hgt < n_hgt
    ]
    return lax.ppermute(block, ("col", "hgt"), route)


def per_device(
    efield_lattice_vector,
    hfield_lattice_vector,
    cell_temp,
    region_tags,
    block_owner,
    block_node,
    node_enthalpy,
):
    nx, nz, ny = cell_temp.shape
    n_col = lax.axis_size("col")
    n_hgt = lax.axis_size("hgt")
    n_dev = n_col * n_hgt
    count = nx * nz * ny // PTS
    cap = 2 * count // n_dev
    node_count = node_enthalpy.shape[0]
    cells = nx * nz * ny
    sem = pltpu.SemaphoreType.DMA

    def kernel(body, outs, ins, args, name, work, aliases=None, scratch=()):
        return pl.pallas_call(
            body,
            out_shape=outs,
            in_specs=ins,
            out_specs=jax.tree.map(lambda out: WHOLE, outs),
            input_output_aliases=aliases or {},
            scratch_shapes=scratch,
            compiler_params=params(VMEM_MIB),
            cost_estimate=cost(work * cells, work * cells),
            name=name,
        )(*args)

    e_start = far(efield_lattice_vector)
    h_start = far(hfield_lattice_vector)
    my_col = lax.axis_index("col").astype(jnp.int32).reshape(1)
    owners = block_owner.reshape(1, count)
    nodes = block_node.reshape(1, count)
    field = vmem(3, nx, nz, ny)
    whole = vmem(nx, nz, ny)
    planes = vmem(2, nz, ny)
    two_rows = vmem(2, nx, ny)
    three_rows = vmem(3, nx, ny)

    to_col, e_low = kernel(
        edge_kernel, (planes, two_rows), [FAR], [e_start], "edge", 4, scratch=[vmem(2, nx, ROWS, ny), sem((2,))]
    )
    col = shifted(to_col, -1, 0)
    hgt = shifted(e_low, 0, -1)
    ca, cb, sigma, e, h, media_rows, e_rows, h_high = kernel(
        load_kernel,
        (whole, whole, whole, field, field, two_rows, three_rows, two_rows),
        [FAR] * 4 + [WHOLE],
        [far(cell_temp), far(region_tags), e_start, h_start, owners + nodes + my_col],
        "load",
        60,
        scratch=[vmem(nx, nz, ny), pltpu.VMEM((nx, nz, ny), jnp.int32), sem((3, 4))],
    )
    begins, heights = starts_of(n_col, n_hgt, cap)
    place, flat = kernel(
        functools.partial(places_kernel, n_col, n_hgt, cap),
        (jax.ShapeDtypeStruct((1, count), jnp.int32), vmem(n_hgt * sum(heights), PTS)),
        [SCALARS, WHOLE, WHOLE],
        [my_col, owners, nodes],
        "places",
        8,
    )
    power = None
    for step in range(STEPS):
        first = step == 0
        h, to_col, h_high = kernel(
            h_edge_kernel,
            (field, planes, two_rows),
            [WHOLE] * 6,
            [e, col, hgt, e_rows, h_high, h],
            f"h_edge_{step}",
            4,
            {5: 0},
        )
        e_hgt = hgt
        col = shifted(to_col, 1, 0)
        hgt = shifted(h_high, 0, 1)
        last = step == STEPS - 1
        outs = (field,) if last else (field, three_rows)
        h, *h_rows = kernel(h_rest_kernel, outs, [WHOLE] * 3, [e, e_hgt, h], f"h_rest_{step}", 40, {2: 0})
        media = [h, ca, cb, sigma]
        if last:
            e, power, h_out = pl.pallas_call(
                functools.partial(e_last_kernel, first),
                out_shape=(field, whole, pltpu.HBM((3, nx, nz, ny), F32)),
                in_specs=[WHOLE] * 8,
                out_specs=(WHOLE, WHOLE, FAR),
                input_output_aliases={6: 0, 7: 1},
                scratch_shapes=[sem],
                compiler_params=params(VMEM_MIB),
                cost_estimate=cost(cells * 50, cells * 50),
                name="e_last",
            )(*media, col, hgt, e, power)
            break
        args = media + [col, hgt, media_rows, *h_rows, e_low, e] + ([] if first else [power])
        e, power, to_col, e_low = kernel(
            functools.partial(e_edge_kernel, first),
            (field, whole, planes, two_rows),
            [WHOLE] * len(args),
            args,
            f"e_edge_{step}",
            5,
            {9: 0} if first else {9: 0, 10: 1},
        )
        h_hgt = hgt
        col = shifted(to_col, -1, 0)
        hgt = shifted(e_low, 0, -1)
        e, power, e_rows = kernel(
            functools.partial(e_rest_kernel, first),
            (field, whole, three_rows),
            [WHOLE] * 7,
            media + [h_hgt, e, power],
            f"e_rest_{step}",
            45,
            {5: 0, 6: 1},
        )

    pair, other, e_out, flat = pl.pallas_call(
        functools.partial(pack_kernel, heights),
        out_shape=(
            pltpu.HBM((n_hgt, heights[1], PTS), F32),
            pltpu.HBM((n_hgt, heights[2], PTS), F32),
            pltpu.HBM((3, nx, nz, ny), F32),
            vmem(n_hgt * sum(heights), PTS),
        ),
        in_specs=[SCALARS] + [WHOLE] * 3,
        out_specs=(FAR,) * 3 + (WHOLE,),
        input_output_aliases={2: 3},
        scratch_shapes=[sem((1 + 2 * n_hgt,))],
        compiler_params=params(VMEM_MIB),
        cost_estimate=cost(cells, cells * 36),
        name="pack",
    )(place.reshape(count), power, flat, e)

    def swap(x, axis):
        return lax.all_to_all(x, axis, split_axis=0, concat_axis=0, tiled=True)

    def across(x, turn):
        return lax.ppermute(x, "col", [(c, c ^ turn) for c in range(n_col)])

    def one_hot_space(sources):
        seats = sources * -(-cap // LANES) * LANES
        return [pltpu.VMEM((node_count, seats), jnp.bfloat16), pltpu.VMEM((seats, 2 * PTS), jnp.bfloat16)]

    node_rows = jax.ShapeDtypeStruct((node_count, PTS), F32)
    from_pair = across(pair, 1)
    other_blocks = swap(other, "hgt")
    def collect(turns, name):
        return kernel(
            functools.partial(collect_kernel, cap, [turn - 2 for turn in turns], n_col - 2),
            (node_rows,) * len(turns),
            [pl.BlockSpec(memory_space=pl.ANY)],
            [other_blocks],
            name,
            8,
            scratch=one_hot_space(n_hgt) + [vmem(n_hgt, heights[2], PTS), sem((1 + len(turns),))],
        )

    turns = list(range(2, n_col, 2))
    swapped = [across(part, 1) for part in collect([turn + 1 for turn in turns], "collect_odd")]
    kept = collect(turns, "collect_even")
    sums = kernel(
        add_kernel, (node_rows,) * len(turns), [WHOLE] * (2 * len(turns)), [*kept, *swapped], "add", 1
    )
    parts = [across(part, turn) for part, turn in zip(sums, turns)]
    tail = kernel(
        functools.partial(collect_tail_kernel, cap, n_col - 2),
        node_rows,
        [pl.BlockSpec(memory_space=pl.ANY)],
        [other_blocks],
        "collect_tail",
        8,
        scratch=[
            pltpu.VMEM((node_count, n_hgt * LANES), jnp.bfloat16),
            pltpu.VMEM((n_hgt * LANES, 2 * PTS), jnp.bfloat16),
            vmem(n_hgt, heights[2] - (n_col - 2) * cap, PTS),
            sem,
        ],
    )
    both = pltpu.HBM((n_hgt, cut_of(cap) + cap + table_rows(2, cap), PTS), F32)
    mine = pl.pallas_call(
        functools.partial(own_kernel, cap, heights[0]),
        out_shape=both,
        in_specs=[WHOLE],
        out_specs=FAR,
        scratch_shapes=[sem((n_hgt,))],
        compiler_params=params(VMEM_MIB),
        cost_estimate=cost(cells, cells * 20),
        name="own",
    )(flat)
    mine = pl.pallas_call(
        functools.partial(merge_kernel, cap, heights[0]),
        out_shape=both,
        in_specs=[WHOLE, WHOLE, FAR],
        out_specs=FAR,
        input_output_aliases={2: 0},
        scratch_shapes=[vmem(n_hgt, table_rows(2, cap), PTS), sem((2, n_hgt))],
        compiler_params=params(VMEM_MIB),
        cost_estimate=cost(1, 1),
        name="merge",
    )(flat, from_pair, mine)
    mine_blocks = swap(mine, "hgt")
    own = kernel(
        functools.partial(collect_mine_kernel, cap),
        node_rows,
        [WHOLE],
        [mine_blocks],
        "collect_mine",
        1,
        scratch=one_hot_space(2 * n_hgt),
    )
    node_temp = kernel(
        finish_kernel, node_rows, [WHOLE] * (3 + len(parts)), [node_enthalpy, own, tail, *parts], "finish", 1
    )
    return e_out, h_out, node_temp


def solution(mesh):
    placed = (
        P(None, "col", "hgt", None),
        P(None, "col", "hgt", None),
        P("col", "hgt", None),
        P("col", "hgt", None),
        P("col", "hgt", None, None, None, None),
        P("col", "hgt", None, None, None),
        P(("col", "hgt"), None),
    )
    return jax.shard_map(
        per_device,
        mesh=mesh,
        in_specs=placed,
        out_specs=(
            P(None, "col", "hgt", None),
            P(None, "col", "hgt", None),
            P(("col", "hgt"), None),
        ),
        check_vma=False,
    )
```

```python
import functools

import jax
import jax.numpy as jnp
from jax import lax
from jax.experimental import pallas as pl
from jax.experimental.pallas import tpu as pltpu
from jax.sharding import PartitionSpec as P

PTS = 128
STEPS = 4
COURANT = 0.55
LANES = 128
ROWS = 8
F32 = jnp.float32
VMEM_MIB = 20

WHOLE = pl.BlockSpec(memory_space=pltpu.VMEM)
SCALARS = pl.BlockSpec(memory_space=pltpu.SMEM)
FAR = pl.BlockSpec(memory_space=pltpu.HBM)


def vmem(*shape):
    return pltpu.VMEM(shape, F32)


def far(x):
    return pltpu.with_memory_space_constraint(x, pltpu.HBM)


def params(mib):
    return pltpu.CompilerParams(vmem_limit_bytes=mib << 20)


def cost(flops, moved):
    return pl.CostEstimate(flops=flops, bytes_accessed=moved, transcendentals=0)


def after_y(f):
    lane = lax.broadcasted_iota(jnp.int32, (ROWS, LANES), 1)
    n = f.shape[1] // LANES
    turned = [pltpu.roll(f[:, k * LANES : (k + 1) * LANES], LANES - 1, 1) for k in range(n)]
    turned.append(jnp.zeros((ROWS, LANES), F32))
    return jnp.concatenate([jnp.where(lane < LANES - 1, turned[k], turned[k + 1]) for k in range(n)], 1)


def before_y(f):
    lane = lax.broadcasted_iota(jnp.int32, (ROWS, LANES), 1)
    n = f.shape[1] // LANES
    turned = [jnp.zeros((ROWS, LANES), F32)]
    turned += [pltpu.roll(f[:, k * LANES : (k + 1) * LANES], 1, 1) for k in range(n)]
    return jnp.concatenate([jnp.where(lane > 0, turned[k + 1], turned[k]) for k in range(n)], 1)


def after_row(f, row):
    place = lax.broadcasted_iota(jnp.int32, f.shape, 0)
    return jnp.where(place < ROWS - 1, pltpu.roll(f, ROWS - 1, 0), jnp.broadcast_to(row, f.shape))


def before_row(f, row):
    place = lax.broadcasted_iota(jnp.int32, f.shape, 0)
    return jnp.where(place > 0, pltpu.roll(f, 1, 0), jnp.broadcast_to(row, f.shape))


def edge_kernel(e, to_col, to_hgt, low, sems):
    nx = e.shape[1]
    col_copy = pltpu.make_async_copy(e.at[pl.ds(1, 2), 0], to_col, sems.at[0])
    low_copy = pltpu.make_async_copy(e.at[pl.ds(0, 2), :, pl.ds(0, ROWS)], low, sems.at[1])
    low_copy.start()
    col_copy.start()
    low_copy.wait()
    for x in range(nx):
        for comp in range(2):
            to_hgt[comp, x : x + 1, :] = low[comp, x, 0:1, :]
    col_copy.wait()


def load_kernel(
    temp_far, tags_far, e_far, h_far, order, ca, cb, sigma_out, e, h, media_rows, e_rows, h_rows, temp, tags, sems
):
    nx, nz, _ = temp.shape
    parts = 4
    size = nx // parts
    copies = []
    for part in range(parts):
        here = pl.ds(part * size, size)
        copies.append(pltpu.make_async_copy(temp_far.at[here], temp.at[here], sems.at[0, part]))
        copies.append(pltpu.make_async_copy(tags_far.at[here], tags.at[here], sems.at[1, part]))
    e_copy = pltpu.make_async_copy(e_far, e, sems.at[2, 0])
    h_copy = pltpu.make_async_copy(h_far, h, sems.at[2, 1])
    for copy in copies:
        copy.start()
    e_copy.start()
    h_copy.start()

    def plane(x, carry):
        for z in range(0, nz, ROWS):
            tag = tags[x, z : z + ROWS, :]
            lean = tag == 0
            fat = tag == 1
            frac = 1.0 / (1.0 + jnp.exp(-2.0 * temp[x, z : z + ROWS, :]))
            eps_low = jnp.where(lean, 4.0, jnp.where(fat, 2.5, 5.0))
            eps_rise = jnp.where(lean, 46.0, jnp.where(fat, 3.5, 5.0))
            sig_low = jnp.where(lean, 0.2, jnp.where(fat, 0.05, 0.1))
            sig_rise = jnp.where(lean, 7.8, jnp.where(fat, 0.35, 0.9))
            eps = eps_low + eps_rise * frac
            sigma = sig_low + sig_rise * frac
            half = (0.5 * COURANT) * sigma
            inverse = 1.0 / (eps + half)
            ca[x, z : z + ROWS, :] = (eps - half) * inverse
            cb[x, z : z + ROWS, :] = COURANT * inverse
            sigma_out[x, z : z + ROWS, :] = sigma
        media_rows[0, pl.ds(x, 1), :] = ca[x, 0:1, :]
        media_rows[1, pl.ds(x, 1), :] = cb[x, 0:1, :]
        return carry

    for part in range(parts):
        copies[2 * part].wait()
        copies[2 * part + 1].wait()
        lax.fori_loop(part * size, (part + 1) * size, plane, 0)
    e_copy.wait()
    h_copy.wait()

    def rows(x, carry):
        for comp in range(3):
            e_rows[comp, pl.ds(x, 1), :] = e[comp, x, nz - 1 : nz, :]
        for comp in range(2):
            h_rows[comp, pl.ds(x, 1), :] = h[comp, x, nz - 1 : nz, :]
        return carry

    lax.fori_loop(0, nx, rows, 0)


def over(first, stop, body):
    if stop - first == 1:
        body(first)
    else:

        def step(x, carry):
            body(x)
            return carry

        lax.fori_loop(first, stop, step, 0)


def h_tile(e, h, col, hgt, x, z):
    nz = e.shape[2]
    here = slice(z, z + ROWS)
    ex, ey, ez = (e[comp, x, here, :] for comp in range(3))
    if z + ROWS < nz:
        row_x, row_y = (e[comp, x, z + ROWS : z + ROWS + 1, :] for comp in range(2))
    else:
        row_x, row_y = (hgt[comp, pl.ds(x, 1), :] for comp in range(2))
    if col is None:
        next_y, next_z = (e[comp, x + 1, here, :] for comp in (1, 2))
    else:
        next_y, next_z = (col[comp, here, :] for comp in range(2))
    h[0, x, here, :] = h[0, x, here, :] - COURANT * ((after_y(ez) - ez) - (after_row(ey, row_y) - ey))
    hy = h[1, x, here, :] - COURANT * ((after_row(ex, row_x) - ex) - (next_z - ez))
    hz = h[2, x, here, :] - COURANT * ((next_y - ey) - (after_y(ex) - ex))
    h[1, x, here, :] = hy
    h[2, x, here, :] = hz
    return hy, hz


def e_tile(first, h, e, power, ca, cb, sigma, col, hgt, x, z):
    here = slice(z, z + ROWS)
    hx, hy, hz = (h[comp, x, here, :] for comp in range(3))
    if z > 0:
        row_x, row_y = (h[comp, x, z - 1 : z, :] for comp in range(2))
    else:
        row_x, row_y = (hgt[comp, pl.ds(x, 1), :] for comp in range(2))
    if col is None:
        past_y, past_z = (h[comp, x - 1, here, :] for comp in (1, 2))
    else:
        past_y, past_z = (col[comp, here, :] for comp in range(2))
    keep = ca[x, here, :]
    drive = cb[x, here, :]
    ex = keep * e[0, x, here, :] + drive * ((hz - before_y(hz)) - (hy - before_row(hy, row_y)))
    ey = keep * e[1, x, here, :] + drive * ((hx - before_row(hx, row_x)) - (hz - past_z))
    ez = keep * e[2, x, here, :] + drive * ((hy - past_y) - (hx - before_y(hx)))
    e[0, x, here, :] = ex
    e[1, x, here, :] = ey
    e[2, x, here, :] = ez
    heat = sigma[x, here, :] * (ex * ex + ey * ey + ez * ez)
    power[x, here, :] = heat if first else power[x, here, :] + heat
    return ey, ez


def h_edge_kernel(e, col, hgt, e_rows, rows_old, h_old, h, to_col, to_hgt):
    nx, nz = e.shape[1:3]
    for z in range(0, nz, ROWS):
        hy, hz = h_tile(e, h, col, hgt, nx - 1, z)
        to_col[0, z : z + ROWS, :] = hy
        to_col[1, z : z + ROWS, :] = hz
    for x in range(0, nx, ROWS):
        here = slice(x, x + ROWS)
        ex, ey, ez = (e_rows[comp, here, :] for comp in range(3))
        row = e_rows[2, x + ROWS : x + ROWS + 1, :] if x + ROWS < nx else col[1, nz - 1 : nz, :]
        to_hgt[0, here, :] = rows_old[0, here, :] - COURANT * ((after_y(ez) - ez) - (hgt[1, here, :] - ey))
        to_hgt[1, here, :] = rows_old[1, here, :] - COURANT * ((hgt[0, here, :] - ex) - (after_row(ez, row) - ez))


def h_rest_kernel(e, hgt, h_old, h, *rows):
    nx, nz = e.shape[1:3]

    def keep(x):
        if rows:
            for comp in range(3):
                rows[0][comp, pl.ds(x, 1), :] = h[comp, x, 0:1, :]

    def plane(x):
        for z in range(0, nz, ROWS):
            h_tile(e, h, None, hgt, x, z)
        keep(x)

    over(0, nx - 1, plane)
    keep(nx - 1)


def e_edge_kernel(first, h, ca, cb, sigma, col, hgt, media_rows, h_rows, rows_old, *refs):
    e, power, to_col, to_hgt = refs[-4:]
    nx, nz = e.shape[1:3]
    for z in range(0, nz, ROWS):
        ey, ez = e_tile(first, h, e, power, ca, cb, sigma, col, hgt, 0, z)
        to_col[0, z : z + ROWS, :] = ey
        to_col[1, z : z + ROWS, :] = ez
    for x in range(0, nx, ROWS):
        here = slice(x, x + ROWS)
        hx, hy, hz = (h_rows[comp, here, :] for comp in range(3))
        row = h_rows[2, x - 1 : x, :] if x > 0 else col[1, 0:1, :]
        keep = media_rows[0, here, :]
        drive = media_rows[1, here, :]
        to_hgt[0, here, :] = keep * rows_old[0, here, :] + drive * ((hz - before_y(hz)) - (hy - hgt[1, here, :]))
        to_hgt[1, here, :] = keep * rows_old[1, here, :] + drive * ((hx - hgt[0, here, :]) - (hz - before_row(hz, row)))


def e_rest_kernel(first, h, ca, cb, sigma, hgt, e_old, power_old, e, power, rows):
    nx, nz = e.shape[1:3]

    def keep(x):
        for comp in range(3):
            rows[comp, pl.ds(x, 1), :] = e[comp, x, nz - 1 : nz, :]

    def plane(x):
        for z in range(0, nz, ROWS):
            e_tile(first, h, e, power, ca, cb, sigma, None, hgt, x, z)
        keep(x)

    keep(0)
    over(1, nx, plane)


def e_last_kernel(first, h, ca, cb, sigma, col, hgt, e_old, power_old, e, power, h_out, sem):
    nx, nz = e.shape[1:3]
    copy = pltpu.make_async_copy(h, h_out, sem)
    copy.start()

    def plane(x):
        for z in range(0, nz, ROWS):
            e_tile(first, h, e, power, ca, cb, sigma, col if isinstance(x, int) else None, hgt, x, z)

    plane(0)
    over(1, nx, plane)
    copy.wait()


def places_kernel(n_col, n_hgt, cap, my_col, owner, node, place, flat):
    n_dev = n_col * n_hgt
    count = owner.shape[1]
    width = 256
    rows = lax.broadcasted_iota(jnp.int32, (n_dev, width), 0)
    before = lax.broadcasted_iota(jnp.int32, (width, width), 0)
    after = lax.broadcasted_iota(jnp.int32, (width, width), 1)
    upper = jnp.where(before <= after, 1.0, 0.0).astype(jnp.bfloat16)
    per = -(-cap // LANES)
    room_for = per * LANES
    room = lax.broadcasted_iota(jnp.int32, (room_for, width), 0)
    total = jnp.zeros((n_dev, 1), F32)
    parts_of = jnp.zeros((2 * n_dev, room_for), F32)
    nt = (((1,), (1,)), ((), ()))
    begins, heights = starts_of(n_col, n_hgt, cap)
    cut = cut_of(cap)
    behind = [cut, cap, (n_col - 2) * cap + cap - cut]
    for start in range(0, count, width):
        own = owner[:, start : start + width]
        hit = jnp.where(rows == own, 1.0, 0.0)
        running = total + jnp.dot(hit.astype(jnp.bfloat16), upper, preferred_element_type=F32)
        total = running[:, width - 1 : width]
        rank = jnp.sum(hit * running, axis=0, keepdims=True).astype(jnp.int32) - 1
        turn = lax.bitwise_xor(lax.div(own, n_hgt), my_col[0])
        own_hgt = lax.rem(own, n_hgt)
        begin = jnp.where(
            turn == 0,
            jnp.where(rank < cut, begins[0] + own_hgt * heights[0], begins[2] + own_hgt * heights[2] + behind[2] - cap),
            jnp.where(
                turn == 1,
                begins[1] + own_hgt * heights[1],
                begins[2] + own_hgt * heights[2] + (turn - 2) * cap,
            ),
        )
        place[:, start : start + width] = begin + rank
        number = node[:, start : start + width]
        upper_part = lax.div(number, 16)
        lower_part = number - 16 * upper_part
        seat = jnp.where(room == rank, 1.0, 0.0).astype(jnp.bfloat16)
        both = jnp.concatenate([hit * upper_part.astype(F32), hit * lower_part.astype(F32)], 0)
        parts_of = parts_of + lax.dot_general(both.astype(jnp.bfloat16), seat, nt, preferred_element_type=F32)
    taken = lax.broadcasted_iota(jnp.int32, (n_dev, room_for), 1).astype(F32) < total
    table = jnp.where(taken, 16.0 * parts_of[:n_dev] + parts_of[n_dev:], -1.0)
    chunk = 8 * ROWS

    def clear(i, carry):
        flat[pl.ds(pl.multiple_of(i * chunk, chunk), chunk), :] = jnp.zeros((chunk, PTS), F32)
        return carry

    lax.fori_loop(0, flat.shape[0] // chunk, clear, 0)
    for at in range(flat.shape[0] // chunk * chunk, flat.shape[0], ROWS):
        flat[at : at + ROWS, :] = jnp.zeros((ROWS, PTS), F32)
    for begin, height, skip in zip(begins, heights, behind):
        for part in range(n_hgt):
            at = begin + part * height
            flat[at + skip : at + height, :] = jnp.full((height - skip, PTS), -1.0, F32)
    for group in range(n_col):
        turn = lax.bitwise_xor(jnp.int32(group), my_col[0])
        kind = jnp.minimum(turn, 2)
        begin = jnp.where(kind == 0, begins[0], jnp.where(kind == 1, begins[1], begins[2]))
        height = jnp.where(kind == 0, heights[0], jnp.where(kind == 1, heights[1], heights[2]))
        skip = jnp.where(kind == 0, cut, jnp.where(kind == 1, cap, behind[2] + (turn - 2) * per))
        for part in range(n_hgt):
            at = group * n_hgt + part
            for piece in range(per):
                row = table[at : at + 1, piece * LANES : (piece + 1) * LANES]
                flat[pl.ds(begin + part * height + skip + piece, 1), :] = row

        @pl.when(turn == 0)
        def _():
            piece = cut // LANES
            for part in range(n_hgt):
                row = begins[2] + part * heights[2] + behind[2] + (n_col - 2) * per
                at = group * n_hgt + part
                flat[row : row + 1, :] = table[at : at + 1, piece * LANES : (piece + 1) * LANES]


def cut_of(cap):
    return cap - max(2 * ROWS, cap // 6 // (2 * ROWS) * (2 * ROWS))


def table_rows(parts, cap):
    return -(-parts * -(-cap // LANES) // ROWS) * ROWS


def starts_of(n_col, n_hgt, cap):
    cut = cut_of(cap)
    others = (n_col - 2) * cap + cap - cut + table_rows(n_col - 1, cap)
    heights = [cut + table_rows(1, cap), cap + table_rows(1, cap), others]
    return [0, n_hgt * heights[0], n_hgt * (heights[0] + heights[1])], heights


def pack_kernel(heights, place, power, flat_old, e, pair, other, e_out, flat, sems):
    nx, nz, ny = power.shape
    e_copy = pltpu.make_async_copy(e, e_out, sems.at[0])
    e_copy.start()
    per_row = ny // PTS

    def plane(x, carry):
        for z in range(nz):
            for k in range(per_row):
                spot = place[x * (nz * per_row) + z * per_row + k]
                flat[pl.ds(spot, 1), :] = power[x, z : z + 1, k * PTS : (k + 1) * PTS]
        return carry

    lax.fori_loop(0, nx, plane, 0)
    copies = []
    first = pair.shape[0] * heights[0]
    for out, rows in zip((pair, other), heights[1:]):
        for group in range(out.shape[0]):
            target = out.at[group, pl.ds(0, rows)]
            copies.append(pltpu.make_async_copy(flat.at[pl.ds(first, rows)], target, sems.at[1 + len(copies)]))
            first += rows
    for copy in copies:
        copy.start()
    for copy in copies:
        copy.wait()
    e_copy.wait()


def summed(blocks, first, caps, node_row, chosen, split, node_count):
    ids = lax.broadcasted_iota(jnp.int32, (node_count, LANES), 0).astype(F32)
    n_from, _, pts = blocks.shape
    per = -(-max(caps) // LANES)
    many = len(first)
    for source in range(n_from):
        for i in range(many):
            seat = (source * many + i) * per * LANES
            for piece in range(per):
                row = node_row[i] + piece
                lanes = slice(seat + piece * LANES, seat + (piece + 1) * LANES)
                hit = ids == blocks[source, row : row + 1, :]
                chosen[:, lanes] = jnp.where(hit, 1.0, 0.0).astype(jnp.bfloat16)
            cap = caps[i]
            values = blocks[source, first[i] : first[i] + cap, :]
            high = values.astype(jnp.bfloat16)
            if cap < per * LANES:
                split[seat + cap : seat + per * LANES, :] = jnp.zeros((per * LANES - cap, 2 * pts), split.dtype)
            split[seat : seat + cap, 0:pts] = high
            split[seat : seat + cap, pts : 2 * pts] = (values - high.astype(F32)).astype(jnp.bfloat16)
    both = jnp.dot(chosen[...], split[...], preferred_element_type=F32)
    return both[:, 0:pts] + both[:, pts : 2 * pts]


def collect_kernel(cap, parts, n_part, blocks, *refs):
    *outs, chosen, split, near, sems = refs
    rows = blocks.shape[1]
    per = -(-cap // LANES)
    after = n_part * cap
    table = after + cap - cut_of(cap)
    pieces = [(after, rows - after)] + [(part * cap, cap) for part in parts]
    copies = []
    for i, (begin, size) in enumerate(pieces):
        here = pl.ds(begin, size)
        copies.append(pltpu.make_async_copy(blocks.at[:, here], near.at[:, here], sems.at[i]))
        copies[i].start()
    copies[0].wait()
    for i, (part, out) in enumerate(zip(parts, outs)):
        copies[1 + i].wait()
        out[...] = summed(near, [part * cap], [cap], [table + part * per], chosen, split, out.shape[0])


def collect_tail_kernel(cap, n_part, blocks, out, chosen, split, near, sem):
    n_from, rows, pts = blocks.shape
    cut = cut_of(cap)
    begin = n_part * cap
    copy = pltpu.make_async_copy(blocks.at[:, pl.ds(begin, rows - begin)], near, sem)
    copy.start()
    split[...] = jnp.zeros(split.shape, split.dtype)
    copy.wait()
    ids = lax.broadcasted_iota(jnp.int32, (out.shape[0], LANES), 0).astype(F32)
    row = cap - cut + n_part * -(-cap // LANES)
    for source in range(n_from):
        hit = ids == near[source, row : row + 1, :]
        chosen[:, source * LANES : (source + 1) * LANES] = jnp.where(hit, 1.0, 0.0).astype(jnp.bfloat16)
        values = near[source, 0 : cap - cut, :]
        high = values.astype(jnp.bfloat16)
        here = slice(source * LANES + cut % LANES, source * LANES + cut % LANES + cap - cut)
        split[here, 0:pts] = high
        split[here, pts : 2 * pts] = (values - high.astype(F32)).astype(jnp.bfloat16)
    both = jnp.dot(chosen[...], split[...], preferred_element_type=F32)
    out[...] = both[:, 0:pts] + both[:, pts : 2 * pts]


def add_kernel(*refs):
    n = len(refs) // 3
    for own, other, out in zip(refs[:n], refs[n : 2 * n], refs[2 * n :]):
        out[...] = own[...] + other[...]


def own_kernel(cap, height, flat, mine, sems):
    cap = cut_of(cap)
    copies = [
        pltpu.make_async_copy(flat.at[pl.ds(group * height, cap)], mine.at[group, pl.ds(0, cap)], sems.at[group])
        for group in range(mine.shape[0])
    ]
    for copy in copies:
        copy.start()
    for copy in copies:
        copy.wait()


def merge_kernel(cap, height, flat, pair, mine_old, mine, tile, sems):
    per = -(-cap // LANES)
    cut = cut_of(cap)
    groups = mine.shape[0]
    copies = []
    for group in range(groups):
        target = mine.at[group, pl.ds(cut, cap)]
        copies.append(pltpu.make_async_copy(pair.at[group, pl.ds(0, cap)], target, sems.at[0, group]))
    for copy in copies:
        copy.start()
    rest = tile.shape[1]
    tile[...] = jnp.full(tile.shape, -1.0, F32)
    for group in range(groups):
        tile[group, 0:per, :] = pair[group, cap : cap + per, :]
        tile[group, per : 2 * per, :] = flat[group * height + cut : group * height + cut + per, :]
        target = mine.at[group, pl.ds(cut + cap, rest)]
        copies.append(pltpu.make_async_copy(tile.at[group], target, sems.at[1, group]))
        copies[-1].start()
    for copy in copies:
        copy.wait()


def collect_mine_kernel(cap, blocks, out, chosen, split):
    per = -(-cap // LANES)
    cut = cut_of(cap)
    nodes = [cut + cap + per, cut + cap]
    out[...] = summed(blocks, [0, cut], [cut, cap], nodes, chosen, split, out.shape[0])


def finish_kernel(enthalpy, *refs):
    *parts, out = refs
    heat = parts[0][...]
    for part in parts[1:]:
        heat = heat + part[...]
    content = enthalpy[...] + (0.25 / STEPS) * heat
    out[...] = jnp.where(content < 0.0, content / 2.0, jnp.where(content > 1.0, (content - 1.0) / 3.0, 0.0))


def shifted(block, d_col, d_hgt):
    n_col = lax.axis_size("col")
    n_hgt = lax.axis_size("hgt")
    route = [
        (c * n_hgt + h, (c + d_col) * n_hgt + h + d_hgt)
        for c in range(n_col)
        for h in range(n_hgt)
        if 0 <= c + d_col < n_col and 0 <= h + d_hgt < n_hgt
    ]
    return lax.ppermute(block, ("col", "hgt"), route)


def per_device(
    efield_lattice_vector,
    hfield_lattice_vector,
    cell_temp,
    region_tags,
    block_owner,
    block_node,
    node_enthalpy,
):
    nx, nz, ny = cell_temp.shape
    n_col = lax.axis_size("col")
    n_hgt = lax.axis_size("hgt")
    n_dev = n_col * n_hgt
    count = nx * nz * ny // PTS
    cap = 2 * count // n_dev
    node_count = node_enthalpy.shape[0]
    cells = nx * nz * ny
    sem = pltpu.SemaphoreType.DMA

    def kernel(body, outs, ins, args, name, work, aliases=None, scratch=()):
        return pl.pallas_call(
            body,
            out_shape=outs,
            in_specs=ins,
            out_specs=jax.tree.map(lambda out: WHOLE, outs),
            input_output_aliases=aliases or {},
            scratch_shapes=scratch,
            compiler_params=params(VMEM_MIB),
            cost_estimate=cost(work * cells, work * cells),
            name=name,
        )(*args)

    e_start = far(efield_lattice_vector)
    h_start = far(hfield_lattice_vector)
    my_col = lax.axis_index("col").astype(jnp.int32).reshape(1)
    owners = block_owner.reshape(1, count)
    nodes = block_node.reshape(1, count)
    field = vmem(3, nx, nz, ny)
    whole = vmem(nx, nz, ny)
    planes = vmem(2, nz, ny)
    two_rows = vmem(2, nx, ny)
    three_rows = vmem(3, nx, ny)

    to_col, e_low = kernel(
        edge_kernel, (planes, two_rows), [FAR], [e_start], "edge", 4, scratch=[vmem(2, nx, ROWS, ny), sem((2,))]
    )
    col = shifted(to_col, -1, 0)
    hgt = shifted(e_low, 0, -1)
    ca, cb, sigma, e, h, media_rows, e_rows, h_high = kernel(
        load_kernel,
        (whole, whole, whole, field, field, two_rows, three_rows, two_rows),
        [FAR] * 4 + [WHOLE],
        [far(cell_temp), far(region_tags), e_start, h_start, owners + nodes + my_col],
        "load",
        60,
        scratch=[vmem(nx, nz, ny), pltpu.VMEM((nx, nz, ny), jnp.int32), sem((3, 4))],
    )
    begins, heights = starts_of(n_col, n_hgt, cap)
    place, flat = kernel(
        functools.partial(places_kernel, n_col, n_hgt, cap),
        (jax.ShapeDtypeStruct((1, count), jnp.int32), vmem(n_hgt * sum(heights), PTS)),
        [SCALARS, WHOLE, WHOLE],
        [my_col, owners, nodes],
        "places",
        8,
    )
    power = None
    for step in range(STEPS):
        first = step == 0
        h, to_col, h_high = kernel(
            h_edge_kernel,
            (field, planes, two_rows),
            [WHOLE] * 6,
            [e, col, hgt, e_rows, h_high, h],
            f"h_edge_{step}",
            4,
            {5: 0},
        )
        e_hgt = hgt
        col = shifted(to_col, 1, 0)
        hgt = shifted(h_high, 0, 1)
        last = step == STEPS - 1
        outs = (field,) if last else (field, three_rows)
        h, *h_rows = kernel(h_rest_kernel, outs, [WHOLE] * 3, [e, e_hgt, h], f"h_rest_{step}", 40, {2: 0})
        media = [h, ca, cb, sigma]
        if last:
            e, power, h_out = pl.pallas_call(
                functools.partial(e_last_kernel, first),
                out_shape=(field, whole, pltpu.HBM((3, nx, nz, ny), F32)),
                in_specs=[WHOLE] * 8,
                out_specs=(WHOLE, WHOLE, FAR),
                input_output_aliases={6: 0, 7: 1},
                scratch_shapes=[sem],
                compiler_params=params(VMEM_MIB),
                cost_estimate=cost(cells * 50, cells * 50),
                name="e_last",
            )(*media, col, hgt, e, power)
            break
        args = media + [col, hgt, media_rows, *h_rows, e_low, e] + ([] if first else [power])
        e, power, to_col, e_low = kernel(
            functools.partial(e_edge_kernel, first),
            (field, whole, planes, two_rows),
            [WHOLE] * len(args),
            args,
            f"e_edge_{step}",
            5,
            {9: 0} if first else {9: 0, 10: 1},
        )
        h_hgt = hgt
        col = shifted(to_col, -1, 0)
        hgt = shifted(e_low, 0, -1)
        e, power, e_rows = kernel(
            functools.partial(e_rest_kernel, first),
            (field, whole, three_rows),
            [WHOLE] * 7,
            media + [h_hgt, e, power],
            f"e_rest_{step}",
            45,
            {5: 0, 6: 1},
        )

    pair, other, e_out, flat = pl.pallas_call(
        functools.partial(pack_kernel, heights),
        out_shape=(
            pltpu.HBM((n_hgt, heights[1], PTS), F32),
            pltpu.HBM((n_hgt, heights[2], PTS), F32),
            pltpu.HBM((3, nx, nz, ny), F32),
            vmem(n_hgt * sum(heights), PTS),
        ),
        in_specs=[SCALARS] + [WHOLE] * 3,
        out_specs=(FAR,) * 3 + (WHOLE,),
        input_output_aliases={2: 3},
        scratch_shapes=[sem((1 + 2 * n_hgt,))],
        compiler_params=params(VMEM_MIB),
        cost_estimate=cost(cells, cells * 36),
        name="pack",
    )(place.reshape(count), power, flat, e)

    def swap(x, axis):
        return lax.all_to_all(x, axis, split_axis=0, concat_axis=0, tiled=True)

    def across(x, turn):
        return lax.ppermute(x, "col", [(c, c ^ turn) for c in range(n_col)])

    def one_hot_space(sources):
        seats = sources * -(-cap // LANES) * LANES
        return [pltpu.VMEM((node_count, seats), jnp.bfloat16), pltpu.VMEM((seats, 2 * PTS), jnp.bfloat16)]

    node_rows = jax.ShapeDtypeStruct((node_count, PTS), F32)
    from_pair = across(pair, 1)
    other_blocks = swap(other, "hgt")
    def collect(turns, name):
        return kernel(
            functools.partial(collect_kernel, cap, [turn - 2 for turn in turns], n_col - 2),
            (node_rows,) * len(turns),
            [pl.BlockSpec(memory_space=pl.ANY)],
            [other_blocks],
            name,
            8,
            scratch=one_hot_space(n_hgt) + [vmem(n_hgt, heights[2], PTS), sem((1 + len(turns),))],
        )

    turns = list(range(2, n_col, 2))
    swapped = [across(part, 1) for part in collect([turn + 1 for turn in turns], "collect_odd")]
    kept = collect(turns, "collect_even")
    sums = kernel(
        add_kernel, (node_rows,) * len(turns), [WHOLE] * (2 * len(turns)), [*kept, *swapped], "add", 1
    )
    parts = [across(part, turn) for part, turn in zip(sums, turns)]
    tail = kernel(
        functools.partial(collect_tail_kernel, cap, n_col - 2),
        node_rows,
        [pl.BlockSpec(memory_space=pl.ANY)],
        [other_blocks],
        "collect_tail",
        8,
        scratch=[
            pltpu.VMEM((node_count, n_hgt * LANES), jnp.bfloat16),
            pltpu.VMEM((n_hgt * LANES, 2 * PTS), jnp.bfloat16),
            vmem(n_hgt, heights[2] - (n_col - 2) * cap, PTS),
            sem,
        ],
    )
    both = pltpu.HBM((n_hgt, cut_of(cap) + cap + table_rows(2, cap), PTS), F32)
    mine = pl.pallas_call(
        functools.partial(own_kernel, cap, heights[0]),
        out_shape=both,
        in_specs=[WHOLE],
        out_specs=FAR,
        scratch_shapes=[sem((n_hgt,))],
        compiler_params=params(VMEM_MIB),
        cost_estimate=cost(cells, cells * 20),
        name="own",
    )(flat)
    mine = pl.pallas_call(
        functools.partial(merge_kernel, cap, heights[0]),
        out_shape=both,
        in_specs=[WHOLE, WHOLE, FAR],
        out_specs=FAR,
        input_output_aliases={2: 0},
        scratch_shapes=[vmem(n_hgt, table_rows(2, cap), PTS), sem((2, n_hgt))],
        compiler_params=params(VMEM_MIB),
        cost_estimate=cost(1, 1),
        name="merge",
    )(flat, from_pair, mine)
    mine_blocks = swap(mine, "hgt")
    own = kernel(
        functools.partial(collect_mine_kernel, cap),
        node_rows,
        [WHOLE],
        [mine_blocks],
        "collect_mine",
        1,
        scratch=one_hot_space(2 * n_hgt),
    )
    node_temp = kernel(
        finish_kernel, node_rows, [WHOLE] * (3 + len(parts)), [node_enthalpy, own, tail, *parts], "finish", 1
    )
    return e_out, h_out, node_temp


def solution(mesh):
    placed = (
        P(None, "col", "hgt", None),
        P(None, "col", "hgt", None),
        P("col", "hgt", None),
        P("col", "hgt", None),
        P("col", "hgt", None, None, None, None),
        P("col", "hgt", None, None, None),
        P(("col", "hgt"), None),
    )
    return jax.shard_map(
        per_device,
        mesh=mesh,
        in_specs=placed,
        out_specs=(
            P(None, "col", "hgt", None),
            P(None, "col", "hgt", None),
            P(("col", "hgt"), None),
        ),
        check_vma=False,
    )
```
